32 devices in a mesh: gx: 8 (over y, x, core), gy: 4 (over z).
Axes of the slice: x: 2, y: 2, z: 4, core: 2. Of those that a mesh axis runs over, the one named last changes fastest.
Arguments:
- state: bfloat16 [64, 32, 32, 128], P(None, 'gx', 'gy'), may hold values from -6 to 6
- cotangent: bfloat16 [64, 32, 32, 128], P(None, 'gx', 'gy'), may hold values from -6 to 6
- spectral_weight: bfloat16 [2, 16, 32, 32, 4096], P(None, 'gx', 'gy'), may hold values from -0.5 to 0.5
- stencil_weight: bfloat16 [64, 1728], replicated, may hold values from -0.15625 to 0.15625
- pointwise_weight: bfloat16 [64, 64], replicated, may hold values from -0.75 to 0.75
Outputs:
- output: bfloat16 [64, 32, 32, 128], P(None, 'gx', 'gy')
- grad_state: float32 [64, 32, 32, 128], P(None, 'gx', 'gy')
- grad_modes: float32 [2, 16, 32, 32, 4096], P(None, 'gx', 'gy')
- grad_stencil: float32 [64, 1728], replicated
- grad_point: float32 [64, 64], replicated
The draws below stay inside these ranges and needn't reach their ends.
All inputs are finite; a program needn't handle non-finite values.
Results may differ from the reference program's by a relative error of at most 0.0029.
Values may be sent and summed in bfloat16 or wider, within the bound.
No kernel may reach another device: no remote copies, remote signals or barrier semaphores. Data moves between devices by JAX's collectives and lax.ppermute only.
A program may use at most 192 MiB of HBM per device.

```python
import math
import jax
import jax.numpy as jnp
from jax import lax

C = 64
MX = 32
MY = 32
MZ = 16
Z = 128
X = 32
Y = 32


def level_of(key, extent, split, low, top_value):
    factor_of = 1.0
    for dim, parts in split:
        steps = jax.random.uniform(jax.random.fold_in(jax.random.fold_in(key, 6), dim), (parts,), jnp.float32, low / len(split), top_value / len(split))
        factor_of = factor_of * jnp.repeat(jnp.exp(steps), extent[dim] // parts).reshape((-1,) + (1,) * (len(extent) - 1 - dim))
    return factor_of


def gaussian(stream_key, dims, width, reach, split=(), kind=jnp.bfloat16):
    factor_of = level_of(stream_key, dims, split, -0.22, 0.18) if split else 1.0
    values = jax.random.normal(stream_key, dims, jnp.float32) * width * factor_of
    return jnp.minimum(jnp.maximum(values, -reach), reach).astype(kind)


def setup_inputs(seed: int = 0) -> dict:
    splits = jax.random.split(jax.random.key(seed), 6)
    return {
        "state": gaussian(splits[0], (C, X, Y, Z), 1.0, 6.0, ((1, 8), (2, 4))),
        "cotangent": gaussian(splits[1], (C, X, Y, Z), 1.0, 6.0, ((1, 8), (2, 4))),
        "spectral_weight": gaussian(splits[2], (2, MZ, MX, MY, C * C), (2 * C) ** -0.5, 0.5, ((1, 8), (2, 4))),
        "stencil_weight": gaussian(splits[3], (C, C * 27), (27 * C) ** -0.5, 0.15625),
        "pointwise_weight": gaussian(splits[4], (C, C), C ** -0.5, 0.75),
    }


HIGH = lax.Precision.HIGHEST

def phase_pair(count, offset, freqs, length):
    places = offset + jnp.arange(count, dtype=jnp.int32)
    turns = places[:, None] * freqs[None, :] % length
    angle = turns.astype(jnp.float32) * (2.0 * math.pi / length)
    return (jnp.cos(angle), jnp.sin(angle))

def centred(count):
    steps = jnp.arange(count, dtype=jnp.int32)
    return jnp.where(steps < count // 2, steps, steps - count).astype(jnp.int32)

def along(values, table, position):
    return jnp.moveaxis(jnp.tensordot(values, table, axes=((position,), (0,)), precision=HIGH), -1, position)

def forward_pair(pair, cosine, sine, position):
    real_part, imag_part = (pair[0], pair[1])
    where = position - 1
    out_real = along(real_part, cosine, where) + along(imag_part, sine, where)
    out_imag = along(imag_part, cosine, where) - along(real_part, sine, where)
    return jnp.stack([out_real, out_imag])

def inverse_pair(pair, cosine, sine, position):
    real_part, imag_part = (pair[0], pair[1])
    where = position - 1
    out_real = along(real_part, cosine.T, where) - along(imag_part, sine.T, where)
    out_imag = along(imag_part, cosine.T, where) + along(real_part, sine.T, where)
    return jnp.stack([out_real, out_imag])

def reference(state, cotangent, spectral_weight, stencil_weight, pointwise_weight):
    alpha = 1.0 / math.sqrt(X * Y * Z)
    beta = 1.0 / math.sqrt(2 * MX * MY * MZ)
    z_cos, z_sin = phase_pair(Z, 0, jnp.arange(MZ, dtype=jnp.int32), Z)
    x_cos, x_sin = phase_pair(X, 0, centred(MX), X)
    y_cos, y_sin = phase_pair(Y, 0, centred(MY), Y)
    doubling = jnp.where(jnp.arange(MZ) == 0, 1.0, 2.0).astype(jnp.float32)

    def to_modes(field):
        real_part = jnp.tensordot(field, z_cos, axes=((3,), (0,)), precision=HIGH)
        imag_part = -jnp.tensordot(field, z_sin, axes=((3,), (0,)), precision=HIGH)
        pair = jnp.stack([real_part, imag_part])
        pair = forward_pair(pair, x_cos, x_sin, 2)
        return forward_pair(pair, y_cos, y_sin, 3)

    def to_field(pair):
        pair = inverse_pair(pair, y_cos, y_sin, 3)
        pair = inverse_pair(pair, x_cos, x_sin, 2)
        return jnp.tensordot(pair[0], z_cos, axes=((3,), (1,)), precision=HIGH) - jnp.tensordot(pair[1], z_sin, axes=((3,), (1,)), precision=HIGH)
    weights = spectral_weight.astype(jnp.float32).reshape(2, MZ, MX, MY, C, C)

    def mix(pair):
        fwd = lambda a, b: jnp.einsum('cxyz,zxyco->oxyz', a, b, precision=HIGH)
        return jnp.stack([fwd(pair[0], weights[0]) - fwd(pair[1], weights[1]), fwd(pair[0], weights[1]) + fwd(pair[1], weights[0])])

    def mix_back(pair):
        bwd = lambda a, b: jnp.einsum('oxyz,zxyco->cxyz', a, b, precision=HIGH)
        return jnp.stack([bwd(pair[0], weights[0]) + bwd(pair[1], weights[1]), bwd(pair[1], weights[0]) - bwd(pair[0], weights[1])])
    modes_in = alpha * to_modes(state.astype(jnp.float32))
    mixed_modes = mix(modes_in)
    spectral = to_field(beta * doubling * mixed_modes)
    kernel = stencil_weight.reshape(C, C, 3, 3, 3)
    numbers = ('NCDHW', 'OIDHW', 'NCDHW')
    stencil = lax.conv_general_dilated(state[None], kernel, (1, 1, 1), 'SAME', dimension_numbers=numbers, preferred_element_type=jnp.float32)[0]
    flat_state = state.reshape(C, -1)
    point = jnp.dot(pointwise_weight, flat_state, preferred_element_type=jnp.float32).reshape(state.shape)
    pre = spectral + stencil + point
    activated, pull = jax.vjp(jax.nn.gelu, pre)
    output = activated.astype(jnp.bfloat16)
    grad_pre = pull(cotangent.astype(jnp.float32))[0].astype(jnp.bfloat16)
    back_modes = doubling * to_modes(grad_pre.astype(jnp.float32))
    outer = lambda a, b: jnp.einsum('cxyz,oxyz->zxyco', a, b, precision=HIGH)
    grad_real = outer(modes_in[0], back_modes[0]) + outer(modes_in[1], back_modes[1])
    grad_imag = outer(modes_in[0], back_modes[1]) - outer(modes_in[1], back_modes[0])
    grad_modes = alpha * jnp.stack([grad_real, grad_imag]).reshape(2, MZ, MX, MY, C * C)
    back_in = mix_back(beta * back_modes)
    flipped = jnp.transpose(kernel, (1, 0, 2, 3, 4))[:, :, ::-1, ::-1, ::-1]
    stencil_back = lax.conv_general_dilated(grad_pre[None], flipped, (1, 1, 1), 'SAME', dimension_numbers=numbers, preferred_element_type=jnp.float32)[0]
    flat_grad = grad_pre.reshape(C, -1)
    point_back = jnp.dot(pointwise_weight.T, flat_grad, preferred_element_type=jnp.float32).reshape(state.shape)
    grad_state = alpha * to_field(back_in) + stencil_back + point_back
    padded = jnp.pad(state, ((0, 0), (1, 1), (1, 1), (1, 1)))
    terms = []
    for shift_a in range(3):
        for shift_b in range(3):
            for shift_e in range(3):
                window = padded[:, shift_a:shift_a + X, shift_b:shift_b + Y, shift_e:shift_e + Z].reshape(C, -1)
                terms.append(lax.dot_general(flat_grad, window, (((1,), (1,)), ((), ())), preferred_element_type=jnp.float32))
    grad_stencil = alpha * jnp.stack(terms, axis=2).reshape(C, C * 27)
    grad_point = alpha * lax.dot_general(flat_grad, flat_state, (((1,), (1,)), ((), ())), preferred_element_type=jnp.float32)
    return (output, grad_state, grad_modes, grad_stencil, grad_point)
```

```python
import functools
import math

import jax
import jax.numpy as jnp
import numpy as np
from jax import lax
from jax.experimental import pallas as pl
from jax.experimental.pallas import tpu as pltpu
from jax.sharding import PartitionSpec as P

C = 64
MX = 32
MY = 32
MZ = 16
Z = 128
MIB = 1 << 20

F32 = jnp.float32
BF16 = jnp.bfloat16


def angles(places, freqs, length):
    turns = np.outer(np.asarray(places), np.asarray(freqs)) % length
    return turns * (2.0 * np.pi / length)


def centred(count):
    steps = np.arange(count)
    return np.where(steps < count // 2, steps, steps - count)


def split(table, parts):
    rest = np.asarray(table, np.float64)
    out = []
    for _ in range(parts):
        piece = rest.astype(jnp.bfloat16)
        out.append(piece)
        rest = rest - piece.astype(np.float64)
    return out


def z_forward_table(scale):
    def build(nx, mz):
        theta = angles(np.arange(MZ), np.arange(Z), Z)
        pair = np.stack([np.cos(theta), -np.sin(theta)]) * scale[None, :, None]
        rows = pair.reshape(2, nx, mz, Z).transpose(1, 0, 2, 3).reshape(2 * MZ, Z)
        return np.concatenate(split(rows, 3), axis=0)

    return build


def z_inverse_table(nx, mz, scale):
    theta = angles(np.arange(MZ), np.arange(Z), Z)
    pair = np.stack([np.cos(theta), -np.sin(theta)]) * scale[None, :, None]
    rows = pair.reshape(2, nx, mz, Z).transpose(1, 0, 2, 3).reshape(2 * MZ, Z)
    high, low = split(rows, 2)
    return np.concatenate([high, high, low], axis=0)


def rotation(theta, sign):
    cosine, sine = np.cos(theta), sign * np.sin(theta)
    return np.stack([np.stack([cosine, -sine], 1), np.stack([sine, cosine], 1)])


def x_tables(wide, mz):
    theta = angles(centred(MX), np.arange(wide), wide)
    eye = np.eye(mz)
    forward = np.einsum("rkRx,zZ->krzxRZ", rotation(theta, -1.0), eye)
    inverse = np.einsum("rxRk,zZ->xrzkRZ", rotation(theta.T, 1.0), eye)
    size_k, size_x = MX * 2 * mz, wide * 2 * mz
    return (
        forward.reshape(size_k, size_x).astype(np.float32),
        inverse.reshape(size_x, size_k).astype(np.float32),
    )


def y_tables(wide):
    theta = angles(centred(MY), np.arange(wide), wide)
    forward = rotation(theta, -1.0).reshape(2 * MY, 2 * wide)
    inverse = rotation(theta.T, 1.0).reshape(2 * wide, 2 * MY)
    out = []
    for table in (forward, inverse):
        high, low = split(table, 2)
        out.append(np.concatenate([high, high, low], axis=1))
    return out


def pieces(values):
    high = values.astype(BF16)
    low = (values - high.astype(F32)).astype(BF16)
    return jnp.concatenate([high, low, high], axis=0)


def z_forward(rows, table, out_ref, x, nx):
    got = lax.dot_general(table, rows, (((1,), (1,)), ((), ())), preferred_element_type=F32)
    size = 2 * MZ
    total = got[:size] + (got[size : 2 * size] + got[2 * size :])
    per = size // nx
    for owner in range(nx):
        out_ref[owner, x * per : (x + 1) * per, :] = total[owner * per : (owner + 1) * per]


def z_inverse(in_ref, table, x, nx):
    per = 2 * MZ // nx
    rows = jnp.concatenate(
        [in_ref[owner, x * per : (x + 1) * per, :] for owner in range(nx)], axis=0
    )
    return lax.dot_general(
        pieces(rows), table, (((0,), (0,)), ((), ())), preferred_element_type=F32
    )


def prep_kernel(nx, field_ref, table_ref, turned_ref, slab_ref):
    c, cx, cy, z = field_ref.shape
    for x in range(cx):
        block = jnp.swapaxes(field_ref[:, x].astype(F32), 0, 1)
        turned = block.astype(BF16)
        turned_ref[x] = turned
        z_forward(turned.reshape(cy * c, z), table_ref[...], slab_ref, x, nx)


def plane_rows(p, cx, body_ref, xlo_ref, xhi_ref, ylo_ref, yhi_ref):
    cy = body_ref.shape[1]
    if p == 0:
        middle = [xlo_ref[y] for y in range(cy)]
    elif p == cx + 1:
        middle = [xhi_ref[y] for y in range(cy)]
    else:
        middle = [body_ref[p - 1, y] for y in range(cy)]
    return [ylo_ref[p]] + middle + [yhi_ref[p]]


def fill_shifts(blocks, rim_ref):
    c, z = blocks[0].shape
    lane = lax.broadcasted_iota(jnp.int32, (c, z), 1)
    for y, block in enumerate(blocks):
        wide = block.astype(F32)
        before = jnp.where(lane == 0, 0.0, pltpu.roll(wide, 1, 1))
        after = jnp.where(lane == z - 1, 0.0, pltpu.roll(wide, z - 1, 1))
        columns = slice(y * z, (y + 1) * z)
        rim_ref[0:c, columns] = before.astype(BF16)
        rim_ref[c : 2 * c, columns] = block
        rim_ref[2 * c : 3 * c, columns] = after.astype(BF16)
        rim_ref[3 * c : 4 * c, columns] = block


def conv_kernel(body_ref, xlo_ref, xhi_ref, ylo_ref, yhi_ref, weight_ref, out_ref, rim_ref):
    cx, cy, c, z = body_ref.shape
    for p in range(cx + 2):
        fill_shifts(plane_rows(p, cx, body_ref, xlo_ref, xhi_ref, ylo_ref, yhi_ref), rim_ref)
        first, last = max(0, p - cx + 1), min(2, p)
        got = jnp.dot(
            weight_ref[first * 3 * c : (last + 1) * 3 * c, :],
            rim_ref[...],
            preferred_element_type=F32,
        )
        for a in range(first, last + 1):
            total = None
            for b in range(3):
                row = ((a - first) * 3 + b) * c
                term = got[row : row + c, b * z : (b + cy) * z]
                total = term if total is None else total + term
            if a == 0:
                out_ref[p - a] = total
            else:
                out_ref[p - a] += total


def weight_grad_kernel(
    grad_ref, body_ref, xlo_ref, xhi_ref, ylo_ref, yhi_ref, out_ref, rim_ref, wide_ref
):
    cx, cy, c, z = body_ref.shape
    group = 3 * c
    wide_ref[...] = jnp.zeros_like(wide_ref)
    for x in range(cx):
        for b in range(3):
            for y in range(cy):
                row = x * group + b * c
                wide_ref[row : row + c, (y + b) * z : (y + b + 1) * z] = grad_ref[x, y]
    out_ref[...] = jnp.zeros_like(out_ref)
    for p in range(cx + 2):
        fill_shifts(plane_rows(p, cx, body_ref, xlo_ref, xhi_ref, ylo_ref, yhi_ref), rim_ref)
        first, last = max(0, p - 2), min(cx - 1, p)
        got = lax.dot_general(
            wide_ref[first * group : (last + 1) * group, :],
            rim_ref[...],
            (((1,), (1,)), ((), ())),
            preferred_element_type=F32,
        )
        for x in range(first, last + 1):
            a = p - x
            out_ref[a * group : (a + 1) * group, :] += got[
                (x - first) * group : (x - first + 1) * group, : 3 * c
            ]


def gelu_kernel(
    nx, stencil_ref, slab_ref, cot_ref, inverse_ref, forward_ref, out_ref, turned_ref, back_ref
):
    c, cx, cy, z = cot_ref.shape
    root = math.sqrt(2.0 / math.pi)
    for x in range(cx):
        spectral = z_inverse(slab_ref, inverse_ref[...], x, nx).reshape(cy, c, z)
        stencil = jnp.stack([stencil_ref[x, :, y * z : (y + 1) * z] for y in range(cy)])
        pre = spectral + stencil
        cot = jnp.swapaxes(cot_ref[:, x].astype(F32), 0, 1)
        square = pre * pre
        bent = jnp.tanh(root * (pre * (1.0 + 0.044715 * square)))
        half = 0.5 + 0.5 * bent
        slope = half + (0.5 * pre) * (1.0 - bent * bent) * (root * (1.0 + 0.134145 * square))
        out_ref[:, x] = jnp.swapaxes(pre * half, 0, 1).astype(BF16)
        grad = (cot * slope).astype(BF16)
        turned_ref[x] = grad
        z_forward(grad.reshape(cy * c, z), forward_ref[...], back_ref, x, nx)


def finish_kernel(nx, stencil_ref, slab_ref, inverse_ref, out_ref):
    c, cx, cy, z = out_ref.shape
    for x in range(cx):
        spectral = z_inverse(slab_ref, inverse_ref[...], x, nx).reshape(cy, c, z)
        stencil = jnp.stack([stencil_ref[x, :, y * z : (y + 1) * z] for y in range(cy)])
        out_ref[:, x] = jnp.swapaxes(spectral + stencil, 0, 1)


def y_forward(data_ref, table_ref, modes_ref):
    got = jnp.dot(table_ref[...], pieces(data_ref[...]), preferred_element_type=F32)
    for q in range(modes_ref.shape[0]):
        block = got[:, q * C : (q + 1) * C]
        modes_ref[q] = jnp.concatenate([block[:MY], block[MY:]], axis=1)


def y_inverse(modes_ref, table_ref, out_ref):
    count = modes_ref.shape[0]
    real = jnp.concatenate([modes_ref[q, :, :C] for q in range(count)], axis=1)
    imag = jnp.concatenate([modes_ref[q, :, C:] for q in range(count)], axis=1)
    out_ref[...] = jnp.dot(
        table_ref[...], pieces(jnp.concatenate([real, imag], axis=0)), preferred_element_type=F32
    )


def pick(values, lanes):
    return jnp.take_along_axis(values, lanes, axis=1)


def mix_kernel(data_ref, weight_ref, forward_ref, inverse_ref, modes_ref, out_ref, mixed_ref):
    q = pl.program_id(0)

    @pl.when(q == 0)
    def _():
        y_forward(data_ref, forward_ref, modes_ref)

    rows = 16
    lane = lax.broadcasted_iota(jnp.int32, (rows, 2 * C), 1)
    pair = jnp.where(lane < C, 0, 1)
    for start in range(0, MY, rows):
        here = slice(start, start + rows)
        modes = modes_ref[q, here, :]
        real = jnp.zeros((rows, 2 * C), F32)
        imag = jnp.zeros((rows, 2 * C), F32)
        for t in range(C // 2):
            mode_re = pick(modes, pair + 2 * t)
            mode_im = pick(modes, pair + (2 * t + C))
            columns = slice(t * 2 * C, (t + 1) * 2 * C)
            weight_re = weight_ref[0, 0, 0, here, columns].astype(F32)
            weight_im = weight_ref[1, 0, 0, here, columns].astype(F32)
            real += mode_re * weight_re - mode_im * weight_im
            imag += mode_re * weight_im + mode_im * weight_re
        mixed_ref[q, here, :] = jnp.concatenate(
            [real[:, :C] + real[:, C:], imag[:, :C] + imag[:, C:]], axis=1
        )

    @pl.when(q == pl.num_programs(0) - 1)
    def _():
        y_inverse(mixed_ref, inverse_ref, out_ref)


def twice(half):
    return jnp.concatenate([half, half], axis=1)


def mix_back_kernel(data_ref, weight_ref, forward_ref, inverse_ref, modes_ref, out_ref, mixed_ref):
    q = pl.program_id(0)

    @pl.when(q == 0)
    def _():
        y_forward(data_ref, forward_ref, modes_ref)

    rows = 16
    lane = lax.broadcasted_iota(jnp.int32, (rows, 2 * C), 1)
    channel = lane % C
    order = C * (channel % 2) + 2 * (channel // 2) + jnp.where(lane < C, 0, 1)

    def merge(shift, low, high):
        return jnp.where(
            lane & shift == 0,
            low + pltpu.roll(low, 2 * C - shift, 1),
            high + pltpu.roll(high, shift, 1),
        )

    for start in range(0, MY, rows):
        here = slice(start, start + rows)
        modes = modes_ref[q, here, :]
        mode_re = twice(modes[:, :C])
        mode_im = twice(modes[:, C:])

        def products(t):
            columns = slice(t * 2 * C, (t + 1) * 2 * C)
            weight_re = weight_ref[0, 0, 0, here, columns].astype(F32)
            weight_im = weight_ref[1, 0, 0, here, columns].astype(F32)
            return merge(
                1,
                weight_re * mode_re + weight_im * mode_im,
                weight_re * mode_im - weight_im * mode_re,
            )

        def summed(first, count):
            if count == 1:
                return products(first)
            half = count // 2
            return merge(count, summed(first, half), summed(first + half, half))

        mixed_ref[q, here, :] = pick(summed(0, C // 2), order)

    @pl.when(q == pl.num_programs(0) - 1)
    def _():
        y_inverse(mixed_ref, inverse_ref, out_ref)


def outer_kernel(alpha, modes_ref, back_ref, out_ref):
    rows = 8
    lane = lax.broadcasted_iota(jnp.int32, (rows, 2 * C), 1)
    pair = jnp.where(lane < C, 0, 1)
    for start in range(0, MY, rows):
        here = slice(start, start + rows)
        modes = modes_ref[0, here, :] * alpha
        back = back_ref[0, here, :]
        back_re = twice(back[:, :C])
        back_im = twice(back[:, C:])
        for t in range(C // 2):
            mode_re = pick(modes, pair + 2 * t)
            mode_im = pick(modes, pair + (2 * t + C))
            columns = slice(t * 2 * C, (t + 1) * 2 * C)
            out_ref[0, 0, 0, here, columns] = mode_re * back_re + mode_im * back_im
            out_ref[1, 0, 0, here, columns] = mode_re * back_im - mode_im * back_re


def whole():
    return pl.BlockSpec(memory_space=pltpu.VMEM)


def params(mib):
    return pltpu.CompilerParams(vmem_limit_bytes=mib * MIB)


def cost(flops, moved):
    return pl.CostEstimate(flops=int(flops), bytes_accessed=int(moved), transcendentals=0)


def call(kernel, outs, args, scratch=(), mib=24, flops=0, moved=0):
    return pl.pallas_call(
        kernel,
        out_shape=[jax.ShapeDtypeStruct(*out) for out in outs],
        in_specs=[whole() for _ in args],
        out_specs=[whole() for _ in outs],
        scratch_shapes=list(scratch),
        compiler_params=params(mib),
        cost_estimate=cost(flops, moved),
    )(*args)


def per_mode(kernel, data, weight, forward, inverse):
    _, mz, mx, my, wide = weight.shape
    full = lambda shape: pl.BlockSpec(shape, lambda q: (0,) * len(shape))
    modes_shape = (mz * mx, MY, 2 * C)
    out_shape = (inverse.shape[0], mz * mx * C)
    return pl.pallas_call(
        kernel,
        grid=(mz * mx,),
        in_specs=[
            full(data.shape),
            pl.BlockSpec((2, 1, 1, my, wide), lambda q: (0, q // mx, q % mx, 0, 0)),
            full(forward.shape),
            full(inverse.shape),
        ],
        out_specs=[full(modes_shape), full(out_shape)],
        out_shape=[
            jax.ShapeDtypeStruct(modes_shape, F32),
            jax.ShapeDtypeStruct(out_shape, F32),
        ],
        scratch_shapes=[pltpu.VMEM(modes_shape, F32)],
        compiler_params=params(24),
        cost_estimate=cost(weight.size * 8, weight.size * 2),
    )(data, weight, forward, inverse)


def outer(modes, back, shape, alpha):
    _, mz, mx, my, wide = shape
    small = pl.BlockSpec((1, MY, 2 * C), lambda q: (q, 0, 0))
    return pl.pallas_call(
        functools.partial(outer_kernel, alpha),
        grid=(mz * mx,),
        in_specs=[small, small],
        out_specs=pl.BlockSpec((2, 1, 1, my, wide), lambda q: (0, q // mx, q % mx, 0, 0)),
        out_shape=jax.ShapeDtypeStruct(shape, F32),
        compiler_params=params(16),
        cost_estimate=cost(math.prod(shape) * 4, math.prod(shape) * 4),
    )(modes, back)


def halos(turned):
    def shift(block, axis, step):
        count = lax.axis_size(axis)
        pairs = [(i, i + step) for i in range(count) if 0 <= i + step < count]
        return lax.ppermute(block, axis, pairs)

    xlo = shift(turned[-1], "gx", 1)
    xhi = shift(turned[0], "gx", -1)
    edge = lambda y: jnp.concatenate([xlo[None, y], turned[:, y], xhi[None, y]], axis=0)
    ylo = shift(edge(-1), "gy", 1)
    yhi = shift(edge(0), "gy", -1)
    return xlo, xhi, ylo, yhi


def conv(turned, rim, weight):
    cx, cy, c, z = turned.shape
    return call(
        conv_kernel,
        [((cx, c, cy * z), F32)],
        (turned, *rim, weight),
        [pltpu.VMEM((4 * c, (cy + 2) * z), BF16)],
        mib=32,
        flops=2 * 27 * c * c * cx * cy * z,
        moved=turned.size * 8,
    )[0]


def weight_grad(grad, turned, rim):
    cx, cy, c, z = turned.shape
    return call(
        weight_grad_kernel,
        [((9 * c, 3 * c), F32)],
        (grad, turned, *rim),
        [
            pltpu.VMEM((4 * c, (cy + 2) * z), BF16),
            pltpu.VMEM((cx * 3 * c, (cy + 2) * z), BF16),
        ],
        mib=32,
        flops=2 * 27 * c * c * cx * cy * z,
        moved=turned.size * 8,
    )[0]


def sum_everywhere(part, scale):
    nx, ny = lax.axis_size("gx"), lax.axis_size("gy")
    size = part.size
    rows = -(-size // (128 * nx * ny))
    flat = jnp.pad(part.reshape(-1), (0, rows * 128 * nx * ny - size))
    mine = flat.reshape(nx, ny * rows, 128)
    mine = lax.all_to_all(mine, "gx", split_axis=0, concat_axis=0, tiled=True).sum(0)
    mine = mine.reshape(ny, rows, 128)
    mine = lax.all_to_all(mine, "gy", split_axis=0, concat_axis=0, tiled=True).sum(0)
    full = lax.all_gather(mine * scale, ("gx", "gy"), axis=0, tiled=False)
    return full.reshape(-1)[:size].reshape(part.shape)


def body(state, cotangent, spectral_weight, stencil_weight, pointwise_weight):
    nx, ny = lax.axis_size("gx"), lax.axis_size("gy")
    c, cx, cy, z = state.shape
    _, mz, mx, _, _ = spectral_weight.shape
    wide_x, wide_y = cx * nx, cy * ny
    alpha = 1.0 / math.sqrt(wide_x * wide_y * z)
    beta = 1.0 / math.sqrt(2 * MX * MY * MZ)
    double = np.where(np.arange(MZ) == 0, 1.0, 2.0)
    ones = np.ones(MZ)
    z_state = jnp.asarray(z_forward_table(alpha * ones)(nx, mz))
    z_grad = jnp.asarray(z_forward_table(double)(nx, mz))
    z_spectral = jnp.asarray(z_inverse_table(nx, mz, beta * double))
    z_back = jnp.asarray(z_inverse_table(nx, mz, alpha * beta * ones))
    x_fwd, x_inv = (jnp.asarray(t) for t in x_tables(wide_x, mz))
    y_fwd, y_inv = (jnp.asarray(t) for t in y_tables(wide_y))
    lanes = cy * c
    x_rows = cx * 2 * mz

    def swap(block, axis):
        return lax.all_to_all(block, axis, split_axis=0, concat_axis=0, tiled=True)

    def x_stage(table, block, lead):
        flat = block.reshape(-1, lanes)
        got = jnp.dot(table, flat, precision=lax.Precision.HIGHEST)
        return got.reshape(lead, -1, lanes)

    def to_pencil(slab):
        block = swap(x_stage(x_fwd, swap(slab, "gx"), ny), "gy")
        block = block.reshape(ny, mx, 2, mz, cy, c).transpose(2, 0, 4, 3, 1, 5)
        return block.reshape(2 * wide_y, mz * mx * c)

    def to_slab(pencil):
        block = pencil.reshape(2, ny, cy, mz, mx, c).transpose(1, 4, 0, 3, 2, 5)
        block = swap(block.reshape(ny, mx * 2 * mz, lanes), "gy")
        return swap(x_stage(x_inv, block, nx), "gx")

    slab_shape = ((nx, x_rows, lanes), F32)
    turned_shape = ((cx, cy, c, z), BF16)

    taps = stencil_weight.reshape(c, c, 3, 3, 3)
    none = jnp.zeros((3, 3, c, c), BF16)

    def table_of(tap, point):
        own = none.at[1, 1].set(point).reshape(9 * c, c)
        return jnp.concatenate([tap.reshape(9 * c, 3 * c), own], axis=1)

    conv_table = table_of(jnp.transpose(taps, (2, 3, 0, 4, 1)), pointwise_weight)
    back_table = table_of(
        jnp.transpose(taps[:, :, ::-1, ::-1, ::-1], (2, 3, 1, 4, 0)), pointwise_weight.T
    )

    turned, slab = call(
        functools.partial(prep_kernel, nx),
        [turned_shape, slab_shape],
        (state, z_state),
        flops=2 * 96 * state.size,
        moved=state.size * 5,
    )
    rim = halos(turned)
    pencil = to_pencil(slab)
    stencil = conv(turned, rim, conv_table)
    modes_in, pencil = per_mode(mix_kernel, pencil, spectral_weight, y_fwd, y_inv)
    slab = to_slab(pencil)
    output, grad, slab = call(
        functools.partial(gelu_kernel, nx),
        [((c, cx, cy, z), BF16), turned_shape, slab_shape],
        (stencil, slab, cotangent, z_spectral, z_grad),
        flops=2 * 192 * state.size,
        moved=state.size * 12,
    )
    grad_rim = halos(grad)
    pencil = to_pencil(slab)
    grad_taps = weight_grad(grad, turned, rim)
    back_modes, pencil = per_mode(mix_back_kernel, pencil, spectral_weight, y_fwd, y_inv)
    grad_modes = outer(modes_in, back_modes, spectral_weight.shape, alpha)
    stencil_back = conv(grad, grad_rim, back_table)
    slab = to_slab(pencil)
    grad_state = call(
        functools.partial(finish_kernel, nx),
        [((c, cx, cy, z), F32)],
        (stencil_back, slab, z_back),
        flops=2 * 96 * state.size,
        moved=state.size * 10,
    )[0]
    total = sum_everywhere(grad_taps, alpha).reshape(3, 3, c, 3, c)
    grad_stencil = jnp.transpose(total, (2, 4, 0, 1, 3))
    grad_point = total[1, 1, :, 1, :]
    return (output, grad_state, grad_modes, grad_stencil.reshape(c, 27 * c), grad_point)


def solution(mesh):
    in_specs = (
        P(None, "gx", "gy", None),
        P(None, "gx", "gy", None),
        P(None, "gx", "gy", None, None),
        P(),
        P(),
    )
    out_specs = (
        P(None, "gx", "gy", None),
        P(None, "gx", "gy", None),
        P(None, "gx", "gy", None, None),
        P(),
        P(),
    )
    return jax.shard_map(body, mesh=mesh, in_specs=in_specs, out_specs=out_specs, check_vma=False)
```

```python
import functools
import math

import jax
import jax.numpy as jnp
import numpy as np
from jax import lax
from jax.experimental import pallas as pl
from jax.experimental.pallas import tpu as pltpu
from jax.sharding import PartitionSpec as P

C = 64
MX = 32
MY = 32
MZ = 16
Z = 128
MIB = 1 << 20

F32 = jnp.float32
BF16 = jnp.bfloat16


def angles(places, freqs, length):
    turns = np.outer(np.asarray(places), np.asarray(freqs)) % length
    return turns * (2.0 * np.pi / length)


def centred(count):
    steps = np.arange(count)
    return np.where(steps < count // 2, steps, steps - count)


def split(table, parts):
    rest = np.asarray(table, np.float64)
    out = []
    for _ in range(parts):
        piece = rest.astype(jnp.bfloat16)
        out.append(piece)
        rest = rest - piece.astype(np.float64)
    return out


def z_forward_table(scale):
    def build(nx, mz):
        theta = angles(np.arange(MZ), np.arange(Z), Z)
        pair = np.stack([np.cos(theta), -np.sin(theta)]) * scale[None, :, None]
        rows = pair.reshape(2, nx, mz, Z).transpose(1, 0, 2, 3).reshape(2 * MZ, Z)
        return np.concatenate(split(rows, 3), axis=0)

    return build


def z_inverse_table(nx, mz, scale):
    theta = angles(np.arange(MZ), np.arange(Z), Z)
    pair = np.stack([np.cos(theta), -np.sin(theta)]) * scale[None, :, None]
    rows = pair.reshape(2, nx, mz, Z).transpose(1, 0, 2, 3).reshape(2 * MZ, Z)
    high, low = split(rows, 2)
    return np.concatenate([high, high, low], axis=0)


def rotation(theta, sign):
    cosine, sine = np.cos(theta), sign * np.sin(theta)
    return np.stack([np.stack([cosine, -sine], 1), np.stack([sine, cosine], 1)])


def against_pieces(*tables):
    out = []
    for table in tables:
        high, low = split(table, 2)
        out.append(np.concatenate([high, high, low], axis=1))
    return out


def x_tables(wide, mz):
    theta = angles(centred(MX), np.arange(wide), wide)
    eye = np.eye(mz)
    forward = np.einsum("rkRx,zZ->krzxRZ", rotation(theta, -1.0), eye)
    inverse = np.einsum("rxRk,zZ->xrzkRZ", rotation(theta.T, 1.0), eye)
    size_k, size_x = MX * 2 * mz, wide * 2 * mz
    return against_pieces(forward.reshape(size_k, size_x), inverse.reshape(size_x, size_k))


def y_tables(wide):
    theta = angles(centred(MY), np.arange(wide), wide)
    forward = rotation(theta, -1.0).reshape(2 * MY, 2 * wide)
    inverse = rotation(theta.T, 1.0).reshape(2 * wide, 2 * MY)
    return against_pieces(forward, inverse)


def pieces(values):
    high = values.astype(BF16)
    low = (values - high.astype(F32)).astype(BF16)
    return jnp.concatenate([high, low, high], axis=0)


def z_forward(rows, table, out_ref, x, nx):
    got = lax.dot_general(table, rows, (((1,), (1,)), ((), ())), preferred_element_type=F32)
    size = 2 * MZ
    total = got[:size] + (got[size : 2 * size] + got[2 * size :])
    per = size // nx
    for owner in range(nx):
        out_ref[owner, x * per : (x + 1) * per, :] = total[owner * per : (owner + 1) * per]


def z_inverse(in_ref, table, x, nx):
    per = 2 * MZ // nx
    rows = jnp.concatenate(
        [in_ref[owner, x * per : (x + 1) * per, :] for owner in range(nx)], axis=0
    )
    return lax.dot_general(
        pieces(rows), table, (((0,), (0,)), ((), ())), preferred_element_type=F32
    )


def prep_kernel(nx, field_ref, table_ref, turned_ref, slab_ref):
    c, cx, cy, z = field_ref.shape
    for x in range(cx):
        block = jnp.swapaxes(field_ref[:, x].astype(F32), 0, 1)
        turned = block.astype(BF16)
        turned_ref[x] = turned
        z_forward(turned.reshape(cy * c, z), table_ref[...], slab_ref, x, nx)


def plane_rows(p, cx, body_ref, xlo_ref, xhi_ref, ylo_ref, yhi_ref):
    cy = body_ref.shape[1]
    if p == 0:
        middle = [xlo_ref[y] for y in range(cy)]
    elif p == cx + 1:
        middle = [xhi_ref[y] for y in range(cy)]
    else:
        middle = [body_ref[p - 1, y] for y in range(cy)]
    return [ylo_ref[p]] + middle + [yhi_ref[p]]


def fill_shifts(blocks, rim_ref, flip=False):
    c, z = blocks[0].shape
    lane = lax.broadcasted_iota(jnp.int32, (c, z), 1)
    for y, block in enumerate(blocks):
        wide = block.astype(F32)
        before = jnp.where(lane == 0, 0.0, pltpu.roll(wide, 1, 1))
        after = jnp.where(lane == z - 1, 0.0, pltpu.roll(wide, z - 1, 1))
        if flip:
            before, after = after, before
        columns = slice(y * z, (y + 1) * z)
        rim_ref[0:c, columns] = before.astype(BF16)
        rim_ref[c : 2 * c, columns] = block
        rim_ref[2 * c : 3 * c, columns] = after.astype(BF16)
        rim_ref[3 * c : 4 * c, columns] = block


def conv_kernel(
    flip, body_ref, xlo_ref, xhi_ref, ylo_ref, yhi_ref, weight_ref, out_ref, rim_ref
):
    cx, cy, c, z = body_ref.shape
    for p in range(cx + 2):
        blocks = plane_rows(p, cx, body_ref, xlo_ref, xhi_ref, ylo_ref, yhi_ref)
        fill_shifts(blocks, rim_ref, flip)
        places = [a for a in range(3) if 0 <= p - (2 - a if flip else a) < cx]
        first = places[0]
        got = jnp.dot(
            weight_ref[first * 3 * c : (places[-1] + 1) * 3 * c, :],
            rim_ref[...],
            preferred_element_type=F32,
        )
        for a in places:
            x = p - (2 - a if flip else a)
            total = None
            for b in range(3):
                row = ((a - first) * 3 + b) * c
                skip = 2 - b if flip else b
                term = got[row : row + c, skip * z : (skip + cy) * z]
                total = term if total is None else total + term
            if p == x:
                out_ref[x] = total
            else:
                out_ref[x] += total


def weight_grad_kernel(
    grad_ref, body_ref, xlo_ref, xhi_ref, ylo_ref, yhi_ref, out_ref, rim_ref, wide_ref, sum_ref
):
    cx, cy, c, z = body_ref.shape
    group = 3 * c
    wide_ref[...] = jnp.zeros_like(wide_ref)
    for x in range(cx):
        for b in range(3):
            for y in range(cy):
                row = x * group + b * c
                wide_ref[row : row + c, (y + b) * z : (y + b + 1) * z] = grad_ref[x, y]
    sum_ref[...] = jnp.zeros_like(sum_ref)
    for p in range(cx + 2):
        fill_shifts(plane_rows(p, cx, body_ref, xlo_ref, xhi_ref, ylo_ref, yhi_ref), rim_ref)
        first, last = max(0, p - 2), min(cx - 1, p)
        got = lax.dot_general(
            wide_ref[first * group : (last + 1) * group, :],
            rim_ref[...],
            (((1,), (1,)), ((), ())),
            preferred_element_type=F32,
        )
        for x in range(first, last + 1):
            a = p - x
            sum_ref[a * group : (a + 1) * group, :] += got[
                (x - first) * group : (x - first + 1) * group, :
            ]
    out_ref[: 9 * c] = sum_ref[:, : 2 * c]
    last = [sum_ref[k * c : (k + 1) * c, 2 * c : 3 * c] for k in range(9)]
    last.append(jnp.zeros((c, c), F32))
    for k in range(5):
        row = (9 + k) * c
        out_ref[row : row + c] = jnp.concatenate(last[2 * k : 2 * k + 2], axis=1)


def gelu_kernel(
    nx, stencil_ref, slab_ref, cot_ref, inverse_ref, forward_ref, out_ref, turned_ref, back_ref
):
    c, cx, cy, z = cot_ref.shape
    root = math.sqrt(2.0 / math.pi)
    for x in range(cx):
        spectral = z_inverse(slab_ref, inverse_ref[...], x, nx).reshape(cy, c, z)
        stencil = jnp.stack([stencil_ref[x, :, y * z : (y + 1) * z] for y in range(cy)])
        pre = spectral + stencil
        cot = jnp.swapaxes(cot_ref[:, x].astype(F32), 0, 1)
        square = pre * pre
        bent = jnp.tanh(root * (pre * (1.0 + 0.044715 * square)))
        half = 0.5 + 0.5 * bent
        slope = half + (0.5 * pre) * (1.0 - bent * bent) * (root * (1.0 + 0.134145 * square))
        out_ref[:, x] = jnp.swapaxes(pre * half, 0, 1).astype(BF16)
        grad = (cot * slope).astype(BF16)
        turned_ref[x] = grad
        z_forward(grad.reshape(cy * c, z), forward_ref[...], back_ref, x, nx)


def finish_kernel(nx, stencil_ref, slab_ref, inverse_ref, out_ref):
    c, cx, cy, z = out_ref.shape
    for x in range(cx):
        spectral = z_inverse(slab_ref, inverse_ref[...], x, nx).reshape(cy, c, z)
        stencil = jnp.stack([stencil_ref[x, :, y * z : (y + 1) * z] for y in range(cy)])
        out_ref[:, x] = jnp.swapaxes(spectral + stencil, 0, 1)


def x_kernel(table_ref, data_ref, out_ref):
    out_ref[...] = jnp.dot(table_ref[...], pieces(data_ref[...]), preferred_element_type=F32)


def taps_kernel(taps_ref, point_ref, forward_ref, back_ref, turned_ref):
    turned_ref[...] = taps_ref[...].astype(F32).T
    forward_ref[...] = jnp.zeros_like(forward_ref)
    back_ref[...] = jnp.zeros_like(back_ref)
    for tap in range(27):
        rows = slice(tap // 3 * C, (tap // 3 + 1) * C)
        columns = slice(tap % 3 * C, (tap % 3 + 1) * C)
        block = turned_ref[pl.ds(tap, C, stride=27), :]
        back_ref[rows, columns] = block.astype(BF16)
        forward_ref[rows, columns] = block.T.astype(BF16)
    point = point_ref[...].astype(F32)
    forward_ref[4 * C : 5 * C, 3 * C :] = point.astype(BF16)
    back_ref[4 * C : 5 * C, 3 * C :] = point.T.astype(BF16)


def unpack_kernel(scale, packed_ref, taps_ref, point_ref, turned_ref):
    for tap in range(27):
        group, e = tap // 3, tap % 3
        if e < 2:
            block = packed_ref[group * C : (group + 1) * C, e * C : (e + 1) * C]
        else:
            row = (9 + group // 2) * C
            block = packed_ref[row : row + C, group % 2 * C : (group % 2 + 1) * C]
        block = block * scale
        if tap == 13:
            point_ref[...] = block
        turned_ref[pl.ds(tap, C, stride=27), :] = block.T
    taps_ref[...] = turned_ref[...].T


QUAD = 4
SPAN = 8


def y_forward(data_ref, table_ref, store):
    got = jnp.dot(table_ref[...], pieces(data_ref[...]), preferred_element_type=F32)
    for q in range(got.shape[1] // C):
        block = got[:, q * C : (q + 1) * C]
        for part in range(2):
            store(q // QUAD, part, q % QUAD, block[part * MY : (part + 1) * MY])


def y_inverse(load, count, table_ref, out_ref):
    rows = [
        jnp.concatenate([load(q // QUAD, part, q % QUAD) for q in range(count)], axis=1)
        for part in range(2)
    ]
    out_ref[...] = jnp.dot(
        table_ref[...], pieces(jnp.concatenate(rows, axis=0)), preferred_element_type=F32
    )


def place(part, pair):
    start = (part * QUAD + pair) * MY
    return slice(start, start + MY)


def spread_table(step):
    shape = (3 * C, SPAN * C)
    row = lax.broadcasted_iota(jnp.int32, shape, 0) & (C - 1)
    column = lax.broadcasted_iota(jnp.int32, shape, 1) // C + step * SPAN
    return jnp.where(row == column, 1.0, 0.0).astype(BF16)


def gather_table(step):
    shape = (SPAN * C, C)
    row = lax.broadcasted_iota(jnp.int32, shape, 0) // C + step * SPAN
    column = lax.broadcasted_iota(jnp.int32, shape, 1)
    return jnp.where(row == column, 1.0, 0.0).astype(BF16)


def walk(ref):
    mz, mx = ref.shape[1], ref.shape[2]
    for q in range(mz * mx):
        yield q // QUAD, q % QUAD, q // mx, q % mx


def pair_of(ref, kz, kx, tile):
    columns = slice(tile * 2 * C, (tile + 1) * 2 * C)
    return (
        ref[0, kz, kx, :, columns].astype(F32),
        ref[1, kz, kx, :, columns].astype(F32),
    )


def mix_kernel(data_ref, weight_ref, forward_ref, inverse_ref, modes_ref, out_ref, sum_ref):
    step = pl.program_id(0)
    count = weight_ref.shape[1] * weight_ref.shape[2]

    @pl.when(step == 0)
    def _():
        def store(group, part, pair, values):
            high = values.astype(BF16)
            rest = values - high.astype(F32)
            middle = rest.astype(BF16)
            low = (rest - middle.astype(F32)).astype(BF16)
            modes_ref[group, place(part, pair), :] = jnp.concatenate([high, middle, low], axis=1)

        y_forward(data_ref, forward_ref, store)
        sum_ref[...] = jnp.zeros_like(sum_ref)

    table = spread_table(step)
    spread = {}
    for group, pair, kz, kx in walk(weight_ref):
        if pair == 0:
            spread[group] = jnp.dot(modes_ref[group], table, preferred_element_type=F32)
        real = sum_ref[group, place(0, pair), :]
        imag = sum_ref[group, place(1, pair), :]
        for tile in range(SPAN // 2):
            columns = slice(tile * 2 * C, (tile + 1) * 2 * C)
            mode_re = spread[group][place(0, pair), columns]
            mode_im = spread[group][place(1, pair), columns]
            weight_re, weight_im = pair_of(weight_ref, kz, kx, tile)
            real += mode_re * weight_re - mode_im * weight_im
            imag += mode_re * weight_im + mode_im * weight_re
        sum_ref[group, place(0, pair), :] = real
        sum_ref[group, place(1, pair), :] = imag

    @pl.when(step == pl.num_programs(0) - 1)
    def _():
        def load(group, part, pair):
            values = sum_ref[group, place(part, pair), :]
            return values[:, :C] + values[:, C:]

        y_inverse(load, count, inverse_ref, out_ref)


def mix_back_kernel(
    data_ref, weight_ref, forward_ref, inverse_ref, modes_ref, out_ref, sum_ref, term_ref
):
    step = pl.program_id(0)
    count = weight_ref.shape[1] * weight_ref.shape[2]

    @pl.when(step == 0)
    def _():
        def store(group, part, pair, values):
            modes_ref[group, place(part, pair), :] = jnp.concatenate([values, values], axis=1)

        y_forward(data_ref, forward_ref, store)
        sum_ref[...] = jnp.zeros_like(sum_ref)

    table = gather_table(step)
    for group, pair, kz, kx in walk(weight_ref):
        mode_re = modes_ref[group, place(0, pair), :]
        mode_im = modes_ref[group, place(1, pair), :]
        for tile in range(SPAN // 2):
            columns = slice(tile * 2 * C, (tile + 1) * 2 * C)
            weight_re, weight_im = pair_of(weight_ref, kz, kx, tile)
            real = weight_re * mode_re + weight_im * mode_im
            imag = weight_re * mode_im - weight_im * mode_re
            term_ref[group, place(0, pair), columns] = real.astype(BF16)
            term_ref[group, place(1, pair), columns] = imag.astype(BF16)
        if pair == QUAD - 1:
            sum_ref[group] += jnp.dot(term_ref[group], table, preferred_element_type=F32)

    @pl.when(step == pl.num_programs(0) - 1)
    def _():
        load = lambda group, part, pair: sum_ref[group, place(part, pair), :]
        y_inverse(load, count, inverse_ref, out_ref)


def outer_kernel(alpha, modes_ref, back_ref, out_ref):
    table = spread_table(pl.program_id(0))
    spread = {}
    for group, pair, kz, kx in walk(out_ref):
        if pair == 0:
            spread[group] = jnp.dot(modes_ref[group], table, preferred_element_type=F32)
        back_re = back_ref[group, place(0, pair), :] * alpha
        back_im = back_ref[group, place(1, pair), :] * alpha
        for tile in range(SPAN // 2):
            columns = slice(tile * 2 * C, (tile + 1) * 2 * C)
            mode_re = spread[group][place(0, pair), columns]
            mode_im = spread[group][place(1, pair), columns]
            out_ref[0, kz, kx, :, columns] = mode_re * back_re + mode_im * back_im
            out_ref[1, kz, kx, :, columns] = mode_re * back_im - mode_im * back_re


def whole():
    return pl.BlockSpec(memory_space=pltpu.VMEM)


def params(mib):
    return pltpu.CompilerParams(vmem_limit_bytes=mib * MIB)


def cost(flops, moved):
    return pl.CostEstimate(flops=int(flops), bytes_accessed=int(moved), transcendentals=0)


def call(kernel, outs, args, scratch=(), mib=24, flops=0, moved=0):
    return pl.pallas_call(
        kernel,
        out_shape=[jax.ShapeDtypeStruct(*out) for out in outs],
        in_specs=[whole() for _ in args],
        out_specs=[whole() for _ in outs],
        scratch_shapes=list(scratch),
        compiler_params=params(mib),
        cost_estimate=cost(flops, moved),
    )(*args)


def full(shape):
    return pl.BlockSpec(shape, lambda step: (0,) * len(shape))


def channels(shape):
    return pl.BlockSpec(shape[:4] + (SPAN * C,), lambda step: (0, 0, 0, 0, step))


def per_mode(kernel, data, weight, forward, inverse, modes, scratch):
    _, mz, mx, _, _ = weight.shape
    groups = mz * mx // QUAD
    rows = 2 * QUAD * MY
    modes_shape = (groups, rows, modes[0])
    out_shape = (inverse.shape[0], mz * mx * C)
    return pl.pallas_call(
        kernel,
        grid=(C // SPAN,),
        in_specs=[
            full(data.shape),
            channels(weight.shape),
            full(forward.shape),
            full(inverse.shape),
        ],
        out_specs=[full(modes_shape), full(out_shape)],
        out_shape=[
            jax.ShapeDtypeStruct(modes_shape, modes[1]),
            jax.ShapeDtypeStruct(out_shape, F32),
        ],
        scratch_shapes=[pltpu.VMEM((groups, rows, width), kind) for width, kind in scratch],
        compiler_params=params(56),
        cost_estimate=cost(weight.size * 8, weight.size * 2),
    )(data, weight, forward, inverse)


def outer(modes, back, shape, alpha):
    return pl.pallas_call(
        functools.partial(outer_kernel, alpha),
        grid=(C // SPAN,),
        in_specs=[full(modes.shape), full(back.shape)],
        out_specs=channels(shape),
        out_shape=jax.ShapeDtypeStruct(shape, F32),
        compiler_params=params(24),
        cost_estimate=cost(math.prod(shape) * 4, math.prod(shape) * 4),
    )(modes, back)


def halos(turned):
    def shift(block, axis, step):
        count = lax.axis_size(axis)
        pairs = [(i, i + step) for i in range(count) if 0 <= i + step < count]
        return lax.ppermute(block, axis, pairs)

    xlo = shift(turned[-1], "gx", 1)
    xhi = shift(turned[0], "gx", -1)
    edge = lambda y: jnp.concatenate([xlo[None, y], turned[:, y], xhi[None, y]], axis=0)
    ylo = shift(edge(-1), "gy", 1)
    yhi = shift(edge(0), "gy", -1)
    return xlo, xhi, ylo, yhi


def conv(turned, rim, weight, flip):
    cx, cy, c, z = turned.shape
    return call(
        functools.partial(conv_kernel, flip),
        [((cx, c, cy * z), F32)],
        (turned, *rim, weight),
        [pltpu.VMEM((4 * c, (cy + 2) * z), BF16)],
        mib=32,
        flops=2 * 27 * c * c * cx * cy * z,
        moved=turned.size * 8,
    )[0]


def weight_grad(grad, turned, rim):
    cx, cy, c, z = turned.shape
    return call(
        weight_grad_kernel,
        [((14 * c, 2 * c), F32)],
        (grad, turned, *rim),
        [
            pltpu.VMEM((4 * c, (cy + 2) * z), BF16),
            pltpu.VMEM((cx * 3 * c, (cy + 2) * z), BF16),
            pltpu.VMEM((9 * c, 4 * c), F32),
        ],
        mib=32,
        flops=2 * 27 * c * c * cx * cy * z,
        moved=turned.size * 8,
    )[0]


def sum_everywhere(part):
    nx, ny = lax.axis_size("gx"), lax.axis_size("gy")

    def swap(block, axis):
        return lax.all_to_all(block, axis, split_axis=0, concat_axis=0, tiled=True)

    def everyone(block, count):
        return jnp.broadcast_to(block[None], (count, *block.shape))

    mine = swap(part.reshape(nx, -1, part.shape[1]), "gx").sum(0)
    mine = swap(everyone(mine, ny), "gy").sum(0)
    return swap(everyone(mine, nx), "gx").reshape(part.shape)


def body(state, cotangent, spectral_weight, stencil_weight, pointwise_weight):
    nx, ny = lax.axis_size("gx"), lax.axis_size("gy")
    c, cx, cy, z = state.shape
    _, mz, mx, _, _ = spectral_weight.shape
    wide_x, wide_y = cx * nx, cy * ny
    alpha = 1.0 / math.sqrt(wide_x * wide_y * z)
    beta = 1.0 / math.sqrt(2 * MX * MY * MZ)
    double = np.where(np.arange(MZ) == 0, 1.0, 2.0)
    ones = np.ones(MZ)
    z_state = jnp.asarray(z_forward_table(alpha * ones)(nx, mz))
    z_grad = jnp.asarray(z_forward_table(double)(nx, mz))
    z_spectral = jnp.asarray(z_inverse_table(nx, mz, beta * double))
    z_back = jnp.asarray(z_inverse_table(nx, mz, alpha * beta * ones))
    x_fwd, x_inv = (jnp.asarray(t) for t in x_tables(wide_x, mz))
    y_fwd, y_inv = (jnp.asarray(t) for t in y_tables(wide_y))
    lanes = cy * c
    x_rows = cx * 2 * mz

    def swap(block, axis):
        return lax.all_to_all(block, axis, split_axis=0, concat_axis=0, tiled=True)

    def x_stage(table, block, lead):
        flat = block.reshape(-1, lanes)
        got = call(
            x_kernel,
            [((table.shape[0], lanes), F32)],
            (table, flat),
            mib=16,
            flops=2 * table.size * lanes,
            moved=8 * flat.size,
        )[0]
        return got.reshape(lead, -1, lanes)

    def to_pencil(slab):
        block = swap(x_stage(x_fwd, swap(slab, "gx"), ny), "gy")
        block = block.reshape(ny, mx, 2, mz, cy, c).transpose(2, 0, 4, 3, 1, 5)
        return block.reshape(2 * wide_y, mz * mx * c)

    def to_slab(pencil):
        block = pencil.reshape(2, ny, cy, mz, mx, c).transpose(1, 4, 0, 3, 2, 5)
        block = swap(block.reshape(ny, mx * 2 * mz, lanes), "gy")
        return swap(x_stage(x_inv, block, nx), "gx")

    slab_shape = ((nx, x_rows, lanes), F32)
    turned_shape = ((cx, cy, c, z), BF16)

    conv_table, back_table = call(
        taps_kernel,
        [((9 * c, 4 * c), BF16)] * 2,
        (stencil_weight, pointwise_weight),
        [pltpu.VMEM((27 * c, c), F32)],
        moved=stencil_weight.size * 6,
    )
    turned, slab = call(
        functools.partial(prep_kernel, nx),
        [turned_shape, slab_shape],
        (state, z_state),
        flops=2 * 96 * state.size,
        moved=state.size * 5,
    )
    rim = halos(turned)
    pencil = to_pencil(slab)
    stencil = conv(turned, rim, conv_table, False)
    modes_in, pencil = per_mode(
        mix_kernel, pencil, spectral_weight, y_fwd, y_inv, (3 * c, BF16), [(2 * c, F32)]
    )
    slab = to_slab(pencil)
    output, grad, slab = call(
        functools.partial(gelu_kernel, nx),
        [((c, cx, cy, z), BF16), turned_shape, slab_shape],
        (stencil, slab, cotangent, z_spectral, z_grad),
        flops=2 * 192 * state.size,
        moved=state.size * 12,
    )
    grad_rim = halos(grad)
    pencil = to_pencil(slab)
    grad_taps = weight_grad(grad, turned, rim)
    back_modes, pencil = per_mode(
        mix_back_kernel,
        pencil,
        spectral_weight,
        y_fwd,
        y_inv,
        (2 * c, F32),
        [(c, F32), (SPAN * c, BF16)],
    )
    grad_modes = outer(modes_in, back_modes, spectral_weight.shape, alpha)
    stencil_back = conv(grad, grad_rim, back_table, True)
    slab = to_slab(pencil)
    grad_state = call(
        functools.partial(finish_kernel, nx),
        [((c, cx, cy, z), F32)],
        (stencil_back, slab, z_back),
        flops=2 * 96 * state.size,
        moved=state.size * 10,
    )[0]
    grad_stencil, grad_point = call(
        functools.partial(unpack_kernel, alpha),
        [((c, 27 * c), F32), ((c, c), F32)],
        (sum_everywhere(grad_taps),),
        [pltpu.VMEM((27 * c, c), F32)],
        moved=grad_taps.size * 8,
    )
    return (output, grad_state, grad_modes, grad_stencil, grad_point)


def solution(mesh):
    in_specs = (
        P(None, "gx", "gy", None),
        P(None, "gx", "gy", None),
        P(None, "gx", "gy", None, None),
        P(),
        P(),
    )
    out_specs = (
        P(None, "gx", "gy", None),
        P(None, "gx", "gy", None),
        P(None, "gx", "gy", None, None),
        P(),
        P(),
    )
    return jax.shard_map(body, mesh=mesh, in_specs=in_specs, out_specs=out_specs, check_vma=False)
```

```python
import functools
import math

import jax
import jax.numpy as jnp
import numpy as np
from jax import lax
from jax.experimental import pallas as pl
from jax.experimental.pallas import tpu as pltpu
from jax.sharding import PartitionSpec as P

C = 64
MX = 32
MY = 32
MZ = 16
Z = 128
MIB = 1 << 20

F32 = jnp.float32
BF16 = jnp.bfloat16


def angles(places, freqs, length):
    turns = np.outer(np.asarray(places), np.asarray(freqs)) % length
    return turns * (2.0 * np.pi / length)


def centred(count):
    steps = np.arange(count)
    return np.where(steps < count // 2, steps, steps - count)


def split(table, parts):
    rest = np.asarray(table, np.float64)
    out = []
    for _ in range(parts):
        piece = rest.astype(jnp.bfloat16)
        out.append(piece)
        rest = rest - piece.astype(np.float64)
    return out


def z_forward_table(scale):
    def build(nx, mz):
        theta = angles(np.arange(MZ), np.arange(Z), Z)
        pair = np.stack([np.cos(theta), -np.sin(theta)]) * scale[None, :, None]
        rows = pair.reshape(2, nx, mz, Z).transpose(1, 0, 2, 3).reshape(2 * MZ, Z)
        return np.concatenate(split(rows, 3), axis=0)

    return build


def z_inverse_table(nx, mz, scale):
    theta = angles(np.arange(MZ), np.arange(Z), Z)
    pair = np.stack([np.cos(theta), -np.sin(theta)]) * scale[None, :, None]
    rows = pair.reshape(2, nx, mz, Z).transpose(1, 0, 2, 3).reshape(2 * MZ, Z)
    high, low = split(rows, 2)
    return np.concatenate([high, high, low], axis=0)


def rotation(theta, sign):
    cosine, sine = np.cos(theta), sign * np.sin(theta)
    return np.stack([np.stack([cosine, -sine], 1), np.stack([sine, cosine], 1)])


def against_pieces(*tables):
    out = []
    for table in tables:
        high, low = split(table, 2)
        out.append(np.concatenate([high, high, low], axis=1))
    return out


def x_tables(wide, mz):
    theta = angles(centred(MX), np.arange(wide), wide)
    eye = np.eye(mz)
    forward = np.einsum("rkRx,zZ->krzxRZ", rotation(theta, -1.0), eye)
    inverse = np.einsum("rxRk,zZ->xrzkRZ", rotation(theta.T, 1.0), eye)
    size_k, size_x = MX * 2 * mz, wide * 2 * mz
    return against_pieces(forward.reshape(size_k, size_x), inverse.reshape(size_x, size_k))


def y_tables(wide):
    theta = angles(centred(MY), np.arange(wide), wide)
    forward = rotation(theta, -1.0).reshape(2 * MY, 2 * wide)
    inverse = rotation(theta.T, 1.0).reshape(2 * wide, 2 * MY)
    return against_pieces(forward, inverse)


def pieces(values):
    high = values.astype(BF16)
    low = (values - high.astype(F32)).astype(BF16)
    return jnp.concatenate([high, low, high], axis=0)


def z_forward(rows, table, out_ref, x, nx):
    got = lax.dot_general(table, rows, (((1,), (1,)), ((), ())), preferred_element_type=F32)
    size = 2 * MZ
    total = got[:size] + (got[size : 2 * size] + got[2 * size :])
    per = size // nx
    for owner in range(nx):
        out_ref[owner, x * per : (x + 1) * per, :] = total[owner * per : (owner + 1) * per]


def z_inverse(in_ref, table, x, nx):
    per = 2 * MZ // nx
    rows = jnp.concatenate(
        [in_ref[owner, x * per : (x + 1) * per, :] for owner in range(nx)], axis=0
    )
    return lax.dot_general(
        pieces(rows), table, (((0,), (0,)), ((), ())), preferred_element_type=F32
    )


def prep_kernel(nx, field_ref, table_ref, turned_ref, slab_ref):
    c, cx, cy, z = field_ref.shape
    for x in range(cx):
        block = jnp.swapaxes(field_ref[:, x].astype(F32), 0, 1)
        turned = block.astype(BF16)
        turned_ref[x] = turned
        z_forward(turned.reshape(cy * c, z), table_ref[...], slab_ref, x, nx)


def plane_rows(p, cx, body_ref, xlo_ref, xhi_ref, ylo_ref, yhi_ref):
    cy = body_ref.shape[1]
    if p == 0:
        middle = [xlo_ref[y] for y in range(cy)]
    elif p == cx + 1:
        middle = [xhi_ref[y] for y in range(cy)]
    else:
        middle = [body_ref[p - 1, y] for y in range(cy)]
    return [ylo_ref[p]] + middle + [yhi_ref[p]]


def fill_shifts(blocks, rim_ref, flip=False):
    c, z = blocks[0].shape
    lane = lax.broadcasted_iota(jnp.int32, (c, z), 1)
    for y, block in enumerate(blocks):
        wide = block.astype(F32)
        before = jnp.where(lane == 0, 0.0, pltpu.roll(wide, 1, 1))
        after = jnp.where(lane == z - 1, 0.0, pltpu.roll(wide, z - 1, 1))
        if flip:
            before, after = after, before
        columns = slice(y * z, (y + 1) * z)
        rim_ref[0:c, columns] = before.astype(BF16)
        rim_ref[c : 2 * c, columns] = block
        rim_ref[2 * c : 3 * c, columns] = after.astype(BF16)
        rim_ref[3 * c : 4 * c, columns] = block


def conv_kernel(
    flip, body_ref, xlo_ref, xhi_ref, ylo_ref, yhi_ref, weight_ref, out_ref, rim_ref
):
    cx, cy, c, z = body_ref.shape
    for p in range(cx + 2):
        blocks = plane_rows(p, cx, body_ref, xlo_ref, xhi_ref, ylo_ref, yhi_ref)
        fill_shifts(blocks, rim_ref, flip)
        places = [a for a in range(3) if 0 <= p - (2 - a if flip else a) < cx]
        first = places[0]
        got = jnp.dot(
            weight_ref[first * 3 * c : (places[-1] + 1) * 3 * c, :],
            rim_ref[...],
            preferred_element_type=F32,
        )
        for a in places:
            x = p - (2 - a if flip else a)
            total = None
            for b in range(3):
                row = ((a - first) * 3 + b) * c
                skip = 2 - b if flip else b
                term = got[row : row + c, skip * z : (skip + cy) * z]
                total = term if total is None else total + term
            if p == x:
                out_ref[x] = total
            else:
                out_ref[x] += total


def weight_grad_kernel(
    grad_ref, body_ref, xlo_ref, xhi_ref, ylo_ref, yhi_ref, out_ref, rim_ref, wide_ref, sum_ref
):
    cx, cy, c, z = body_ref.shape
    group = 3 * c
    wide_ref[...] = jnp.zeros_like(wide_ref)
    for x in range(cx):
        for b in range(3):
            for y in range(cy):
                row = x * group + b * c
                wide_ref[row : row + c, (y + b) * z : (y + b + 1) * z] = grad_ref[x, y]
    sum_ref[...] = jnp.zeros_like(sum_ref)
    for p in range(cx + 2):
        fill_shifts(plane_rows(p, cx, body_ref, xlo_ref, xhi_ref, ylo_ref, yhi_ref), rim_ref)
        first, last = max(0, p - 2), min(cx - 1, p)
        got = lax.dot_general(
            wide_ref[first * group : (last + 1) * group, :],
            rim_ref[...],
            (((1,), (1,)), ((), ())),
            preferred_element_type=F32,
        )
        for x in range(first, last + 1):
            a = p - x
            sum_ref[a * group : (a + 1) * group, :] += got[
                (x - first) * group : (x - first + 1) * group, :
            ]
    out_ref[: 9 * c] = sum_ref[:, : 2 * c]
    last = [sum_ref[k * c : (k + 1) * c, 2 * c : 3 * c] for k in range(9)]
    last.append(jnp.zeros((c, c), F32))
    for k in range(5):
        row = (9 + k) * c
        out_ref[row : row + c] = jnp.concatenate(last[2 * k : 2 * k + 2], axis=1)
    out_ref[14 * c :] = jnp.zeros((2 * c, 2 * c), F32)


def gelu_kernel(
    nx, stencil_ref, slab_ref, cot_ref, inverse_ref, forward_ref, out_ref, turned_ref, back_ref
):
    c, cx, cy, z = cot_ref.shape
    root = math.sqrt(2.0 / math.pi)
    for x in range(cx):
        spectral = z_inverse(slab_ref, inverse_ref[...], x, nx).reshape(cy, c, z)
        stencil = jnp.stack([stencil_ref[x, :, y * z : (y + 1) * z] for y in range(cy)])
        pre = spectral + stencil
        cot = jnp.swapaxes(cot_ref[:, x].astype(F32), 0, 1)
        square = pre * pre
        bent = jnp.tanh(root * (pre * (1.0 + 0.044715 * square)))
        half = 0.5 + 0.5 * bent
        slope = half + (0.5 * pre) * (1.0 - bent * bent) * (root * (1.0 + 0.134145 * square))
        out_ref[:, x] = jnp.swapaxes(pre * half, 0, 1).astype(BF16)
        grad = (cot * slope).astype(BF16)
        turned_ref[x] = grad
        z_forward(grad.reshape(cy * c, z), forward_ref[...], back_ref, x, nx)


def finish_kernel(nx, stencil_ref, slab_ref, inverse_ref, out_ref):
    c, cx, cy, z = out_ref.shape
    for x in range(cx):
        spectral = z_inverse(slab_ref, inverse_ref[...], x, nx).reshape(cy, c, z)
        stencil = jnp.stack([stencil_ref[x, :, y * z : (y + 1) * z] for y in range(cy)])
        out_ref[:, x] = jnp.swapaxes(spectral + stencil, 0, 1)


def x_kernel(table_ref, data_ref, out_ref):
    data = data_ref[...].astype(F32)
    lanes = data.shape[2]
    rows = table_ref.shape[1] // (3 * data.shape[0])
    flat = pieces(data[:, :rows].reshape(-1, lanes))
    got = jnp.dot(table_ref[...], flat, preferred_element_type=F32).astype(out_ref.dtype)
    count = got.shape[0] // out_ref.shape[0]
    for owner in range(out_ref.shape[0]):
        out_ref[owner, :count] = got[owner * count : (owner + 1) * count]
    if data.shape[1] > rows:
        extra = data[:, rows:].sum(0)
        for owner in range(out_ref.shape[0]):
            out_ref[owner, count:] = extra


def taps_kernel(taps_ref, point_ref, forward_ref, back_ref, turned_ref):
    turned_ref[...] = taps_ref[...].astype(F32).T
    forward_ref[...] = jnp.zeros_like(forward_ref)
    back_ref[...] = jnp.zeros_like(back_ref)
    for tap in range(27):
        rows = slice(tap // 3 * C, (tap // 3 + 1) * C)
        columns = slice(tap % 3 * C, (tap % 3 + 1) * C)
        block = turned_ref[pl.ds(tap, C, stride=27), :]
        back_ref[rows, columns] = block.astype(BF16)
        forward_ref[rows, columns] = block.T.astype(BF16)
    point = point_ref[...].astype(F32)
    forward_ref[4 * C : 5 * C, 3 * C :] = point.astype(BF16)
    back_ref[4 * C : 5 * C, 3 * C :] = point.T.astype(BF16)


def unpack_kernel(scale, skip, message_ref, taps_ref, point_ref, packed_ref, turned_ref):
    devices, rows, lanes = message_ref.shape
    per, tiles_in = rows - skip, lanes // 128
    for owner in range(devices):
        for tile in range(tiles_in):
            row = (owner * tiles_in + tile) * per
            packed_ref[row : row + per] = message_ref[owner, skip:, tile * 128 : (tile + 1) * 128]
    for tap in range(27):
        group, e = tap // 3, tap % 3
        if e < 2:
            block = packed_ref[group * C : (group + 1) * C, e * C : (e + 1) * C]
        else:
            row = (9 + group // 2) * C
            block = packed_ref[row : row + C, group % 2 * C : (group % 2 + 1) * C]
        block = block * scale
        if tap == 13:
            point_ref[...] = block
        turned_ref[pl.ds(tap, C, stride=27), :] = block.T
    taps_ref[...] = turned_ref[...].T


QUAD = 4
SPAN = 8 * C


def y_forward(data_ref, table_ref, store):
    data = pieces(data_ref[...].astype(F32))
    got = jnp.dot(table_ref[...], data, preferred_element_type=F32)
    for q in range(got.shape[1] // C):
        block = got[:, q * C : (q + 1) * C]
        for part in range(2):
            store(q // QUAD, part, q % QUAD, block[part * MY : (part + 1) * MY])


def y_inverse(sum_ref, table_ref, out_ref):
    rows = [
        jnp.concatenate(
            [
                sum_ref[group, place(part, pair), :]
                for group in range(sum_ref.shape[0])
                for pair in range(QUAD)
            ],
            axis=1,
        )
        for part in range(2)
    ]
    out_ref[...] = jnp.dot(
        table_ref[...], pieces(jnp.concatenate(rows, axis=0)), preferred_element_type=F32
    )


def place(part, pair):
    start = (part * QUAD + pair) * MY
    return slice(start, start + MY)


def spread_table():
    return np.tile(np.kron(np.eye(C), np.ones((1, C))), (3, 1)).astype(jnp.bfloat16)


def gather_table():
    return np.kron(np.eye(C), np.ones((C, 1))).astype(jnp.bfloat16)


def tiles():
    for piece in range(C * C // SPAN):
        for tile in range(SPAN // (2 * C)):
            start = piece * SPAN + tile * 2 * C
            yield piece, tile, slice(start, start + 2 * C)


def spread_modes(modes, table_ref):
    count = C * C // SPAN
    made = {}

    def get(piece):
        for p in range(piece, min(piece + 2, count)):
            if p not in made:
                made[p] = jnp.dot(
                    modes, table_ref[:, p * SPAN : (p + 1) * SPAN], preferred_element_type=F32
                )
        return made[piece]

    return get


def mix_kernel(
    data_ref, weight_ref, table_ref, forward_ref, inverse_ref, modes_ref, out_ref, sum_ref
):
    step = pl.program_id(0)

    @pl.when(step == 0)
    def _():
        def store(group, part, pair, values):
            high = values.astype(BF16)
            rest = values - high.astype(F32)
            middle = rest.astype(BF16)
            low = (rest - middle.astype(F32)).astype(BF16)
            modes_ref[group, place(part, pair), :] = jnp.concatenate([high, middle, low], axis=1)

        y_forward(data_ref, forward_ref, store)

    spread = spread_modes(modes_ref[step], table_ref)
    real = [jnp.zeros((MY, 2 * C), F32)] * QUAD
    imag = [jnp.zeros((MY, 2 * C), F32)] * QUAD
    for piece, tile, columns in tiles():
        modes = spread(piece)
        inside = slice(tile * 2 * C, (tile + 1) * 2 * C)
        for pair in range(QUAD):
            mode_re = modes[place(0, pair), inside]
            mode_im = modes[place(1, pair), inside]
            weight_re = weight_ref[0, 0, pair, :, columns].astype(F32)
            weight_im = weight_ref[1, 0, pair, :, columns].astype(F32)
            real[pair] += mode_re * weight_re - mode_im * weight_im
            imag[pair] += mode_re * weight_im + mode_im * weight_re
    for pair in range(QUAD):
        sum_ref[step, place(0, pair), :] = real[pair][:, :C] + real[pair][:, C:]
        sum_ref[step, place(1, pair), :] = imag[pair][:, :C] + imag[pair][:, C:]

    @pl.when(step == pl.num_programs(0) - 1)
    def _():
        y_inverse(sum_ref, inverse_ref, out_ref)


def mix_back_kernel(
    data_ref, weight_ref, table_ref, forward_ref, inverse_ref, modes_ref, out_ref, sum_ref, term_ref
):
    step = pl.program_id(0)

    @pl.when(step == 0)
    def _():
        def store(group, part, pair, values):
            modes_ref[group, place(part, pair), :] = jnp.concatenate([values, values], axis=1)

        y_forward(data_ref, forward_ref, store)

    total = None
    for piece, tile, columns in tiles():
        for pair in range(QUAD):
            mode_re = modes_ref[step, place(0, pair), :]
            mode_im = modes_ref[step, place(1, pair), :]
            weight_re = weight_ref[0, 0, pair, :, columns].astype(F32)
            weight_im = weight_ref[1, 0, pair, :, columns].astype(F32)
            term_ref[place(0, pair), columns] = (
                weight_re * mode_re + weight_im * mode_im
            ).astype(BF16)
            term_ref[place(1, pair), columns] = (
                weight_re * mode_im - weight_im * mode_re
            ).astype(BF16)
        if columns.stop % SPAN == 0:
            whole_piece = slice(piece * SPAN, (piece + 1) * SPAN)
            got = jnp.dot(
                term_ref[:, whole_piece], table_ref[whole_piece, :], preferred_element_type=F32
            )
            total = got if total is None else total + got
    sum_ref[step] = total

    @pl.when(step == pl.num_programs(0) - 1)
    def _():
        y_inverse(sum_ref, inverse_ref, out_ref)


def outer_kernel(alpha, modes_ref, back_ref, table_ref, out_ref):
    spread = spread_modes(modes_ref[0], table_ref)
    for piece, tile, columns in tiles():
        modes = spread(piece)
        inside = slice(tile * 2 * C, (tile + 1) * 2 * C)
        for pair in range(QUAD):
            back_re = back_ref[0, place(0, pair), :] * alpha
            back_im = back_ref[0, place(1, pair), :] * alpha
            mode_re = modes[place(0, pair), inside]
            mode_im = modes[place(1, pair), inside]
            out_ref[0, 0, pair, :, columns] = mode_re * back_re + mode_im * back_im
            out_ref[1, 0, pair, :, columns] = mode_re * back_im - mode_im * back_re


def whole():
    return pl.BlockSpec(memory_space=pltpu.VMEM)


def params(mib):
    return pltpu.CompilerParams(vmem_limit_bytes=mib * MIB)


def cost(flops, moved):
    return pl.CostEstimate(flops=int(flops), bytes_accessed=int(moved), transcendentals=0)


def call(kernel, outs, args, scratch=(), mib=24, flops=0, moved=0):
    return pl.pallas_call(
        kernel,
        out_shape=[jax.ShapeDtypeStruct(*out) for out in outs],
        in_specs=[whole() for _ in args],
        out_specs=[whole() for _ in outs],
        scratch_shapes=list(scratch),
        compiler_params=params(mib),
        cost_estimate=cost(flops, moved),
    )(*args)


def full(shape):
    return pl.BlockSpec(shape, lambda step: (0,) * len(shape))


def group_block(shape):
    per = shape[2] // QUAD
    return pl.BlockSpec(
        (2, 1, QUAD) + shape[3:], lambda step: (0, step // per, step % per, 0, 0)
    )


def per_mode(kernel, data, weight, tables, modes, scratch=()):
    _, mz, mx, _, _ = weight.shape
    groups = mz * mx // QUAD
    rows = 2 * QUAD * MY
    modes_shape = (groups, rows, modes[0])
    out_shape = (tables[-1].shape[0], mz * mx * C)
    return pl.pallas_call(
        kernel,
        grid=(groups,),
        in_specs=[full(data.shape), group_block(weight.shape)] + [full(t.shape) for t in tables],
        out_specs=[full(modes_shape), full(out_shape)],
        out_shape=[
            jax.ShapeDtypeStruct(modes_shape, modes[1]),
            jax.ShapeDtypeStruct(out_shape, F32),
        ],
        scratch_shapes=[pltpu.VMEM((groups, rows, C), F32), *scratch],
        compiler_params=params(56),
        cost_estimate=cost(weight.size * 8, weight.size * 2),
    )(data, weight, *tables)


def outer(modes, back, table, shape, alpha):
    group = lambda ref: pl.BlockSpec((1,) + ref.shape[1:], lambda step: (step, 0, 0))
    return pl.pallas_call(
        functools.partial(outer_kernel, alpha),
        grid=(modes.shape[0],),
        in_specs=[group(modes), group(back), full(table.shape)],
        out_specs=group_block(shape),
        out_shape=jax.ShapeDtypeStruct(shape, F32),
        compiler_params=params(32),
        cost_estimate=cost(math.prod(shape) * 4, math.prod(shape) * 4),
    )(modes, back, table)


def shift(block, axis, step):
    count = lax.axis_size(axis)
    pairs = [(i, i + step) for i in range(count) if 0 <= i + step < count]
    return lax.ppermute(block, axis, pairs)


def x_halos(turned):
    return shift(turned[-1], "gx", 1), shift(turned[0], "gx", -1)


def y_halos(turned, xlo, xhi):
    edge = lambda y: jnp.concatenate([xlo[None, y], turned[:, y], xhi[None, y]], axis=0)
    return shift(edge(-1), "gy", 1), shift(edge(0), "gy", -1)


def conv(turned, rim, weight, flip):
    cx, cy, c, z = turned.shape
    return call(
        functools.partial(conv_kernel, flip),
        [((cx, c, cy * z), F32)],
        (turned, *rim, weight),
        [pltpu.VMEM((4 * c, (cy + 2) * z), BF16)],
        mib=32,
        flops=2 * 27 * c * c * cx * cy * z,
        moved=turned.size * 8,
    )[0]


def weight_grad(grad, turned, rim):
    cx, cy, c, z = turned.shape
    return call(
        weight_grad_kernel,
        [((16 * c, 2 * c), F32)],
        (grad, turned, *rim),
        [
            pltpu.VMEM((4 * c, (cy + 2) * z), BF16),
            pltpu.VMEM((cx * 3 * c, (cy + 2) * z), BF16),
            pltpu.VMEM((9 * c, 4 * c), F32),
        ],
        mib=32,
        flops=2 * 27 * c * c * cx * cy * z,
        moved=turned.size * 8,
    )[0]


def swap(block, axis):
    return lax.all_to_all(block, axis, split_axis=0, concat_axis=0, tiled=True)


def together(*values):
    return lax.optimization_barrier(values)


def body(state, cotangent, spectral_weight, stencil_weight, pointwise_weight):
    nx, ny = lax.axis_size("gx"), lax.axis_size("gy")
    c, cx, cy, z = state.shape
    _, mz, mx, _, _ = spectral_weight.shape
    wide_x, wide_y = cx * nx, cy * ny
    alpha = 1.0 / math.sqrt(wide_x * wide_y * z)
    beta = 1.0 / math.sqrt(2 * MX * MY * MZ)
    double = np.where(np.arange(MZ) == 0, 1.0, 2.0)
    ones = np.ones(MZ)
    z_state = jnp.asarray(z_forward_table(alpha * ones)(nx, mz))
    z_grad = jnp.asarray(z_forward_table(double)(nx, mz))
    z_spectral = jnp.asarray(z_inverse_table(nx, mz, beta * double))
    z_back = jnp.asarray(z_inverse_table(nx, mz, alpha * beta * ones))
    x_fwd, x_inv = (jnp.asarray(t) for t in x_tables(wide_x, mz))
    y_fwd, y_inv = (jnp.asarray(t) for t in y_tables(wide_y))
    spread, gather = jnp.asarray(spread_table()), jnp.asarray(gather_table())
    lanes = cy * c
    x_rows = cx * 2 * mz

    def x_stage(table, block, lead, kind=F32, extra=0):
        rows = table.shape[0] // lead + extra
        return call(
            x_kernel,
            [((lead, rows, lanes), kind)],
            (table, block),
            mib=16,
            flops=2 * table.size * lanes,
            moved=8 * block.size,
        )[0]

    def to_rows(block):
        block = block.reshape(ny, mx, 2, mz, cy, c).transpose(2, 0, 4, 3, 1, 5)
        return block.reshape(2 * wide_y, mz * mx * c)

    def to_blocks(rows):
        block = rows.reshape(2, ny, cy, mz, mx, c).transpose(1, 4, 0, 3, 2, 5)
        return block.reshape(ny, mx * 2 * mz, lanes)

    slab_shape = ((nx, x_rows, lanes), F32)
    turned_shape = ((cx, cy, c, z), BF16)

    conv_table, back_table = call(
        taps_kernel,
        [((9 * c, 4 * c), BF16)] * 2,
        (stencil_weight, pointwise_weight),
        [pltpu.VMEM((27 * c, c), F32)],
        moved=stencil_weight.size * 6,
    )
    turned, slab = call(
        functools.partial(prep_kernel, nx),
        [turned_shape, slab_shape],
        (state, z_state),
        flops=2 * 96 * state.size,
        moved=state.size * 5,
    )
    block = x_stage(x_fwd, swap(slab, "gx"), ny)
    block, *faces = together(block, *x_halos(turned))
    rows = to_rows(swap(block, "gy"))
    modes_in, rows = per_mode(
        mix_kernel, rows, spectral_weight, (spread, y_fwd, y_inv), (3 * c, BF16)
    )
    block, *edges = together(to_blocks(rows), *y_halos(turned, *faces))
    rim = (*faces, *edges)
    block = x_stage(x_inv, swap(block, "gy"), nx)
    stencil = conv(turned, rim, conv_table, False)
    output, grad, slab = call(
        functools.partial(gelu_kernel, nx),
        [((c, cx, cy, z), BF16), turned_shape, slab_shape],
        (stencil, swap(block, "gx"), cotangent, z_spectral, z_grad),
        flops=2 * 192 * state.size,
        moved=state.size * 12,
    )

    block = x_stage(x_fwd, swap(slab, "gx"), ny, BF16)
    grad_taps = weight_grad(grad, turned, rim)
    block, *faces = together(block, *x_halos(grad))
    block, grad_taps = together(swap(block, "gy"), grad_taps)
    mine = swap(grad_taps.reshape(nx, -1, 2 * c), "gx").sum(0)
    back_modes, rows = per_mode(
        mix_back_kernel,
        to_rows(block),
        spectral_weight,
        (gather, y_fwd, y_inv),
        (2 * c, F32),
        [pltpu.VMEM((2 * QUAD * MY, c * c), BF16)],
    )
    packed = jnp.concatenate(jnp.split(mine, lanes // (2 * c)), axis=1)
    extra = packed.shape[0]
    packed = jnp.broadcast_to(packed[None], (ny, extra, lanes))
    block = jnp.concatenate([to_blocks(rows), packed], axis=1).astype(BF16)
    block, *edges = together(block, *y_halos(grad, *faces))
    block = x_stage(x_inv, swap(block, "gy"), nx, F32, extra)
    stencil_back = conv(grad, (*faces, *edges), back_table, True)
    block, stencil_back = together(block, stencil_back)
    message = swap(block, "gx")
    grad_modes = outer(modes_in, back_modes, spread, spectral_weight.shape, alpha)
    grad_state = call(
        functools.partial(finish_kernel, nx),
        [((c, cx, cy, z), F32)],
        (stencil_back, message, z_back),
        flops=2 * 96 * state.size,
        moved=state.size * 10,
    )[0]
    grad_stencil, grad_point = call(
        functools.partial(unpack_kernel, alpha, x_rows),
        [((c, 27 * c), F32), ((c, c), F32)],
        (message,),
        [pltpu.VMEM(grad_taps.shape, F32), pltpu.VMEM((27 * c, c), F32)],
        moved=grad_taps.size * 8,
    )
    return (output, grad_state, grad_modes, grad_stencil, grad_point)


def solution(mesh):
    in_specs = (
        P(None, "gx", "gy", None),
        P(None, "gx", "gy", None),
        P(None, "gx", "gy", None, None),
        P(),
        P(),
    )
    out_specs = (
        P(None, "gx", "gy", None),
        P(None, "gx", "gy", None),
        P(None, "gx", "gy", None, None),
        P(),
        P(),
    )
    return jax.shard_map(body, mesh=mesh, in_specs=in_specs, out_specs=out_specs, check_vma=False)
```

```python
import functools
import math

import jax
import jax.numpy as jnp
import numpy as np
from jax import lax
from jax.experimental import pallas as pl
from jax.experimental.pallas import tpu as pltpu
from jax.sharding import PartitionSpec as P

C = 64
MX = 32
MY = 32
MZ = 16
Z = 128
MIB = 1 << 20

F32 = jnp.float32
BF16 = jnp.bfloat16


def angles(places, freqs, length):
    turns = np.outer(np.asarray(places), np.asarray(freqs)) % length
    return turns * (2.0 * np.pi / length)


def centred(count):
    steps = np.arange(count)
    return np.where(steps < count // 2, steps, steps - count)


def split(table, parts):
    rest = np.asarray(table, np.float64)
    out = []
    for _ in range(parts):
        piece = rest.astype(jnp.bfloat16)
        out.append(piece)
        rest = rest - piece.astype(np.float64)
    return out


def z_forward_table(scale):
    def build(nx, mz):
        theta = angles(np.arange(MZ), np.arange(Z), Z)
        pair = np.stack([np.cos(theta), -np.sin(theta)]) * scale[None, :, None]
        rows = pair.reshape(2, nx, mz, Z).transpose(1, 0, 2, 3).reshape(2 * MZ, Z)
        return np.concatenate(split(rows, 3), axis=0)

    return build


def z_inverse_table(nx, mz, scale):
    theta = angles(np.arange(MZ), np.arange(Z), Z)
    pair = np.stack([np.cos(theta), -np.sin(theta)]) * scale[None, :, None]
    rows = pair.reshape(2, nx, mz, Z).transpose(1, 0, 2, 3).reshape(2 * MZ, Z)
    high, low = split(rows, 2)
    return np.concatenate([high, high, low], axis=0)


def rotation(theta, sign):
    cosine, sine = np.cos(theta), sign * np.sin(theta)
    return np.stack([np.stack([cosine, -sine], 1), np.stack([sine, cosine], 1)])


def against_pieces(*tables):
    out = []
    for table in tables:
        high, low = split(table, 2)
        out.append(np.concatenate([high, high, low], axis=1))
    return out


def x_tables(wide, mz, mx):
    theta = angles(centred(MX), np.arange(wide), wide)
    eye = np.eye(mz)
    forward = np.einsum("rkRx,zZ->krzxRZ", rotation(theta, -1.0), eye)
    inverse = np.einsum("rxRk,zZ->xrzkRZ", rotation(theta.T, 1.0), eye)
    size_k, size_x = MX * 2 * mz, wide * 2 * mz
    forward = forward.reshape(MX // mx, mx, 2, mz, size_x).transpose(0, 2, 3, 1, 4)
    inverse = inverse.reshape(size_x, MX // mx, mx, 2, mz).transpose(0, 1, 3, 4, 2)
    return against_pieces(forward.reshape(size_k, size_x), inverse.reshape(size_x, size_k))


def y_tables(wide):
    theta = angles(centred(MY), np.arange(wide), wide)
    forward = rotation(theta, -1.0).reshape(2 * MY, 2 * wide)
    inverse = rotation(theta.T, 1.0).reshape(2 * wide, 2 * MY)
    return against_pieces(forward, inverse)


def pieces(values):
    high = values.astype(BF16)
    low = (values - high.astype(F32)).astype(BF16)
    return jnp.concatenate([high, low, high], axis=0)


def z_forward(rows, table, out_ref, x, nx):
    got = lax.dot_general(table, rows, (((1,), (1,)), ((), ())), preferred_element_type=F32)
    size = 2 * MZ
    total = got[:size] + (got[size : 2 * size] + got[2 * size :])
    per = size // nx
    for owner in range(nx):
        out_ref[owner, x * per : (x + 1) * per, :] = total[owner * per : (owner + 1) * per]


def z_inverse(in_ref, table, x, nx):
    per = 2 * MZ // nx
    rows = jnp.concatenate(
        [in_ref[owner, x * per : (x + 1) * per, :] for owner in range(nx)], axis=0
    )
    return lax.dot_general(
        pieces(rows), table, (((0,), (0,)), ((), ())), preferred_element_type=F32
    )


def prep_kernel(nx, field_ref, table_ref, turned_ref, slab_ref):
    c, cx, cy, z = field_ref.shape
    for x in range(cx):
        block = jnp.swapaxes(field_ref[:, x].astype(F32), 0, 1)
        turned = block.astype(BF16)
        turned_ref[x] = turned
        z_forward(turned.reshape(cy * c, z), table_ref[...], slab_ref, x, nx)


def plane_rows(p, cx, body_ref, xlo_ref, xhi_ref, ylo_ref, yhi_ref):
    cy = body_ref.shape[1]
    if p == 0:
        middle = [xlo_ref[y] for y in range(cy)]
    elif p == cx + 1:
        middle = [xhi_ref[y] for y in range(cy)]
    else:
        middle = [body_ref[p - 1, y] for y in range(cy)]
    return [ylo_ref[p]] + middle + [yhi_ref[p]]


def fill_shifts(blocks, rim_ref, flip=False):
    c, z = blocks[0].shape
    lane = lax.broadcasted_iota(jnp.int32, (c, z), 1)
    for y, block in enumerate(blocks):
        wide = block.astype(F32)
        before = jnp.where(lane == 0, 0.0, pltpu.roll(wide, 1, 1))
        after = jnp.where(lane == z - 1, 0.0, pltpu.roll(wide, z - 1, 1))
        if flip:
            before, after = after, before
        columns = slice(y * z, (y + 1) * z)
        rim_ref[0:c, columns] = before.astype(BF16)
        rim_ref[c : 2 * c, columns] = block
        rim_ref[2 * c : 3 * c, columns] = after.astype(BF16)
        rim_ref[3 * c : 4 * c, columns] = block


def conv_kernel(
    flip, body_ref, xlo_ref, xhi_ref, ylo_ref, yhi_ref, weight_ref, out_ref, rim_ref
):
    cx, cy, c, z = body_ref.shape
    for p in range(cx + 2):
        blocks = plane_rows(p, cx, body_ref, xlo_ref, xhi_ref, ylo_ref, yhi_ref)
        fill_shifts(blocks, rim_ref, flip)
        places = [a for a in range(3) if 0 <= p - (2 - a if flip else a) < cx]
        first = places[0]
        got = jnp.dot(
            weight_ref[first * 3 * c : (places[-1] + 1) * 3 * c, :],
            rim_ref[...],
            preferred_element_type=F32,
        )
        for a in places:
            x = p - (2 - a if flip else a)
            total = None
            for b in range(3):
                row = ((a - first) * 3 + b) * c
                skip = 2 - b if flip else b
                term = got[row : row + c, skip * z : (skip + cy) * z]
                total = term if total is None else total + term
            if p == x:
                out_ref[x] = total
            else:
                out_ref[x] += total


def weight_grad_kernel(
    grad_ref, body_ref, xlo_ref, xhi_ref, ylo_ref, yhi_ref, out_ref, rim_ref, wide_ref, sum_ref
):
    cx, cy, c, z = body_ref.shape
    group = 3 * c
    wide_ref[...] = jnp.zeros_like(wide_ref)
    for x in range(cx):
        for b in range(3):
            for y in range(cy):
                row = x * group + b * c
                wide_ref[row : row + c, (y + b) * z : (y + b + 1) * z] = grad_ref[x, y]
    sum_ref[...] = jnp.zeros_like(sum_ref)
    for p in range(cx + 2):
        fill_shifts(plane_rows(p, cx, body_ref, xlo_ref, xhi_ref, ylo_ref, yhi_ref), rim_ref)
        first, last = max(0, p - 2), min(cx - 1, p)
        got = lax.dot_general(
            wide_ref[first * group : (last + 1) * group, :],
            rim_ref[...],
            (((1,), (1,)), ((), ())),
            preferred_element_type=F32,
        )
        for x in range(first, last + 1):
            a = p - x
            sum_ref[a * group : (a + 1) * group, :] += got[
                (x - first) * group : (x - first + 1) * group, :
            ]
    out_ref[: 9 * c] = sum_ref[:, : 2 * c]
    last = [sum_ref[k * c : (k + 1) * c, 2 * c : 3 * c] for k in range(9)]
    last.append(jnp.zeros((c, c), F32))
    for k in range(5):
        row = (9 + k) * c
        out_ref[row : row + c] = jnp.concatenate(last[2 * k : 2 * k + 2], axis=1)
    out_ref[14 * c :] = jnp.zeros((2 * c, 2 * c), F32)


def gelu_kernel(
    nx, stencil_ref, slab_ref, cot_ref, inverse_ref, forward_ref, out_ref, turned_ref, back_ref
):
    c, cx, cy, z = cot_ref.shape
    root = math.sqrt(2.0 / math.pi)
    for x in range(cx):
        spectral = z_inverse(slab_ref, inverse_ref[...], x, nx).reshape(cy, c, z)
        stencil = jnp.stack([stencil_ref[x, :, y * z : (y + 1) * z] for y in range(cy)])
        pre = spectral + stencil
        cot = jnp.swapaxes(cot_ref[:, x].astype(F32), 0, 1)
        square = pre * pre
        bent = jnp.tanh(root * (pre * (1.0 + 0.044715 * square)))
        half = 0.5 + 0.5 * bent
        slope = half + (0.5 * pre) * (1.0 - bent * bent) * (root * (1.0 + 0.134145 * square))
        out_ref[:, x] = jnp.swapaxes(pre * half, 0, 1).astype(BF16)
        grad = (cot * slope).astype(BF16)
        turned_ref[x] = grad
        z_forward(grad.reshape(cy * c, z), forward_ref[...], back_ref, x, nx)


def finish_kernel(nx, stencil_ref, slab_ref, inverse_ref, out_ref):
    c, cx, cy, z = out_ref.shape
    for x in range(cx):
        spectral = z_inverse(slab_ref, inverse_ref[...], x, nx).reshape(cy, c, z)
        stencil = jnp.stack([stencil_ref[x, :, y * z : (y + 1) * z] for y in range(cy)])
        out_ref[:, x] = jnp.swapaxes(spectral + stencil, 0, 1)


def x_kernel(table_ref, data_ref, out_ref):
    data = data_ref[...].astype(F32)
    lanes = data.shape[2]
    rows = table_ref.shape[1] // (3 * data.shape[0])
    flat = pieces(data[:, :rows].reshape(-1, lanes))
    got = jnp.dot(table_ref[...], flat, preferred_element_type=F32).astype(out_ref.dtype)
    count = got.shape[0] // out_ref.shape[0]
    for owner in range(out_ref.shape[0]):
        out_ref[owner, :count] = got[owner * count : (owner + 1) * count]
    if data.shape[1] > rows:
        extra = data[:, rows:].sum(0)
        for owner in range(out_ref.shape[0]):
            out_ref[owner, count:] = extra


def taps_kernel(taps_ref, point_ref, forward_ref, back_ref, turned_ref):
    turned_ref[...] = taps_ref[...].astype(F32).T
    forward_ref[...] = jnp.zeros_like(forward_ref)
    back_ref[...] = jnp.zeros_like(back_ref)
    for tap in range(27):
        rows = slice(tap // 3 * C, (tap // 3 + 1) * C)
        columns = slice(tap % 3 * C, (tap % 3 + 1) * C)
        block = turned_ref[pl.ds(tap, C, stride=27), :]
        back_ref[rows, columns] = block.astype(BF16)
        forward_ref[rows, columns] = block.T.astype(BF16)
    point = point_ref[...].astype(F32)
    forward_ref[4 * C : 5 * C, 3 * C :] = point.astype(BF16)
    back_ref[4 * C : 5 * C, 3 * C :] = point.T.astype(BF16)


def unpack_kernel(scale, skip, message_ref, taps_ref, point_ref, packed_ref, turned_ref):
    devices, rows, lanes = message_ref.shape
    per, tiles_in = rows - skip, lanes // 128
    for owner in range(devices):
        for tile in range(tiles_in):
            row = (owner * tiles_in + tile) * per
            packed_ref[row : row + per] = message_ref[owner, skip:, tile * 128 : (tile + 1) * 128]
    for tap in range(27):
        group, e = tap // 3, tap % 3
        if e < 2:
            block = packed_ref[group * C : (group + 1) * C, e * C : (e + 1) * C]
        else:
            row = (9 + group // 2) * C
            block = packed_ref[row : row + C, group % 2 * C : (group % 2 + 1) * C]
        block = block * scale
        if tap == 13:
            point_ref[...] = block
        turned_ref[pl.ds(tap, C, stride=27), :] = block.T
    taps_ref[...] = turned_ref[...].T


QUAD = 4
SPAN = 8 * C


def y_forward(mz, data_ref, table_ref, rows_ref, store):
    ny, _, lanes = data_ref.shape
    cy = lanes // C
    count = rows_ref.shape[1] // C
    for owner in range(ny):
        data = data_ref[owner].astype(F32)
        for part in range(2):
            for kz in range(mz):
                mx = count // mz
                start = (part * mz + kz) * mx
                block = data[start : start + mx]
                block = jnp.stack([block[:, y * C : (y + 1) * C] for y in range(cy)])
                block = jnp.swapaxes(block, 0, 1)
                row = (part * ny + owner) * cy
                for kx in range(mx):
                    column = (kz * mx + kx) * C
                    rows_ref[row : row + cy, column : column + C] = block[kx]
    got = jnp.dot(table_ref[...], pieces(rows_ref[...]), preferred_element_type=F32)
    for q in range(count):
        block = got[:, q * C : (q + 1) * C]
        for part in range(2):
            store(q // QUAD, part, q % QUAD, block[part * MY : (part + 1) * MY])


def y_inverse(mz, sum_ref, table_ref, out_ref, block_ref):
    rows = [
        jnp.concatenate(
            [
                sum_ref[group, place(part, pair), :]
                for group in range(sum_ref.shape[0])
                for pair in range(QUAD)
            ],
            axis=1,
        )
        for part in range(2)
    ]
    got = jnp.dot(
        table_ref[...], pieces(jnp.concatenate(rows, axis=0)), preferred_element_type=F32
    )
    ny, _, lanes = out_ref.shape
    cy = lanes // C
    count = got.shape[1] // C
    mx = count // mz
    for owner in range(ny):
        for part in range(2):
            for kz in range(mz):
                row = (part * ny + owner) * cy
                block = got[row : row + cy, kz * mx * C : (kz + 1) * mx * C]
                block = jnp.stack([block[:, kx * C : (kx + 1) * C] for kx in range(mx)])
                block = jnp.swapaxes(block, 0, 1)
                start = (part * mz + kz) * mx
                for y in range(cy):
                    block_ref[owner, start : start + mx, y * C : (y + 1) * C] = block[y]
    out_ref[...] = block_ref[...].astype(out_ref.dtype)


def place(part, pair):
    start = (part * QUAD + pair) * MY
    return slice(start, start + MY)


def spread_table():
    return np.tile(np.kron(np.eye(C), np.ones((1, C))), (2, 1)).astype(jnp.bfloat16)


def gather_table():
    return np.kron(np.eye(SPAN // C), np.ones((1, C))).astype(jnp.bfloat16)


def tiles():
    for piece in range(C * C // SPAN):
        for tile in range(SPAN // (2 * C)):
            start = piece * SPAN + tile * 2 * C
            yield piece, tile, slice(start, start + 2 * C)


def spread_modes(modes, table_ref):
    count = C * C // SPAN
    made = {}

    def get(piece):
        for p in range(piece, min(piece + 2, count)):
            if p not in made:
                made[p] = jnp.dot(
                    modes, table_ref[:, p * SPAN : (p + 1) * SPAN], preferred_element_type=F32
                )
        return made[piece]

    return get


def mix_kernel(
    mz,
    data_ref,
    weight_ref,
    table_ref,
    forward_ref,
    inverse_ref,
    modes_ref,
    out_ref,
    sum_ref,
    rows_ref,
    block_ref,
):
    step = pl.program_id(0)

    @pl.when(step == 0)
    def _():
        def store(group, part, pair, values):
            high = values.astype(BF16)
            low = (values - high.astype(F32)).astype(BF16)
            modes_ref[group, place(part, pair), :] = jnp.concatenate([high, low], axis=1)

        y_forward(mz, data_ref, forward_ref, rows_ref, store)

    spread = spread_modes(modes_ref[step], table_ref)
    real = [jnp.zeros((MY, 2 * C), F32)] * QUAD
    imag = [jnp.zeros((MY, 2 * C), F32)] * QUAD
    for piece, tile, columns in tiles():
        modes = spread(piece)
        inside = slice(tile * 2 * C, (tile + 1) * 2 * C)
        for pair in range(QUAD):
            mode_re = modes[place(0, pair), inside]
            mode_im = modes[place(1, pair), inside]
            weight_re = weight_ref[0, 0, pair, :, columns].astype(F32)
            weight_im = weight_ref[1, 0, pair, :, columns].astype(F32)
            real[pair] += mode_re * weight_re - mode_im * weight_im
            imag[pair] += mode_re * weight_im + mode_im * weight_re
    for pair in range(QUAD):
        sum_ref[step, place(0, pair), :] = real[pair][:, :C] + real[pair][:, C:]
        sum_ref[step, place(1, pair), :] = imag[pair][:, :C] + imag[pair][:, C:]

    @pl.when(step == pl.num_programs(0) - 1)
    def _():
        y_inverse(mz, sum_ref, inverse_ref, out_ref, block_ref)


def mix_back_kernel(
    mz,
    data_ref,
    weight_ref,
    table_ref,
    forward_ref,
    inverse_ref,
    modes_ref,
    out_ref,
    sum_ref,
    rows_ref,
    block_ref,
    term_ref,
):
    step = pl.program_id(0)

    @pl.when(step == 0)
    def _():
        def store(group, part, pair, values):
            modes_ref[group, place(part, pair), :] = jnp.concatenate([values, values], axis=1)

        y_forward(mz, data_ref, forward_ref, rows_ref, store)

    total = []
    for piece, tile, columns in tiles():
        for pair in range(QUAD):
            mode_re = modes_ref[step, place(0, pair), :]
            mode_im = modes_ref[step, place(1, pair), :]
            weight_re = weight_ref[0, 0, pair, :, columns].astype(F32)
            weight_im = weight_ref[1, 0, pair, :, columns].astype(F32)
            term_ref[place(0, pair), columns] = (
                weight_re * mode_re + weight_im * mode_im
            ).astype(BF16)
            term_ref[place(1, pair), columns] = (
                weight_re * mode_im - weight_im * mode_re
            ).astype(BF16)
        if columns.stop % SPAN == 0:
            whole_piece = slice(piece * SPAN, (piece + 1) * SPAN)
            total.append(
                lax.dot_general(
                    table_ref[...],
                    term_ref[:, whole_piece],
                    (((1,), (1,)), ((), ())),
                    preferred_element_type=F32,
                )
            )
    sum_ref[step] = jnp.concatenate(total, axis=0).T

    @pl.when(step == pl.num_programs(0) - 1)
    def _():
        y_inverse(mz, sum_ref, inverse_ref, out_ref, block_ref)


def outer_kernel(alpha, modes_ref, back_ref, table_ref, out_ref):
    spread = spread_modes(modes_ref[0], table_ref)
    for piece, tile, columns in tiles():
        modes = spread(piece)
        inside = slice(tile * 2 * C, (tile + 1) * 2 * C)
        for pair in range(QUAD):
            back_re = back_ref[0, place(0, pair), :] * alpha
            back_im = back_ref[0, place(1, pair), :] * alpha
            mode_re = modes[place(0, pair), inside]
            mode_im = modes[place(1, pair), inside]
            out_ref[0, 0, pair, :, columns] = mode_re * back_re + mode_im * back_im
            out_ref[1, 0, pair, :, columns] = mode_re * back_im - mode_im * back_re


def whole():
    return pl.BlockSpec(memory_space=pltpu.VMEM)


def params(mib):
    return pltpu.CompilerParams(vmem_limit_bytes=mib * MIB)


def cost(flops, moved):
    return pl.CostEstimate(flops=int(flops), bytes_accessed=int(moved), transcendentals=0)


def call(kernel, outs, args, scratch=(), mib=24, flops=0, moved=0):
    return pl.pallas_call(
        kernel,
        out_shape=[jax.ShapeDtypeStruct(*out) for out in outs],
        in_specs=[whole() for _ in args],
        out_specs=[whole() for _ in outs],
        scratch_shapes=list(scratch),
        compiler_params=params(mib),
        cost_estimate=cost(flops, moved),
    )(*args)


def full(shape):
    return pl.BlockSpec(shape, lambda step: (0,) * len(shape))


def group_block(shape, start=0):
    per = shape[2] // QUAD
    return pl.BlockSpec(
        (2, 1, QUAD) + shape[3:],
        lambda step: (0, (step + start) // per, (step + start) % per, 0, 0),
    )


def per_mode(kernel, data, weight, tables, modes, kind, scratch=()):
    _, mz, mx, _, _ = weight.shape
    groups = mz * mx // QUAD
    rows = 2 * QUAD * MY
    modes_shape = (groups, rows, modes[0])
    return pl.pallas_call(
        functools.partial(kernel, mz),
        grid=(groups,),
        in_specs=[full(data.shape), group_block(weight.shape)] + [full(t.shape) for t in tables],
        out_specs=[full(modes_shape), full(data.shape)],
        out_shape=[
            jax.ShapeDtypeStruct(modes_shape, modes[1]),
            jax.ShapeDtypeStruct(data.shape, kind),
        ],
        scratch_shapes=[
            pltpu.VMEM((groups, rows, C), F32),
            pltpu.VMEM((tables[-1].shape[0], mz * mx * C), F32),
            pltpu.VMEM(data.shape, F32),
            *scratch,
        ],
        compiler_params=params(48),
        cost_estimate=cost(weight.size * 8, weight.size * 2),
    )(data, weight, *tables)


def outer(modes, back, table, shape, alpha, start, count, prior=None):
    def kernel(*refs):
        outer_kernel(alpha, *refs[:3], refs[-1])

    group = lambda ref: pl.BlockSpec((1,) + ref.shape[1:], lambda step: (step + start, 0, 0))
    given = () if prior is None else (prior,)
    return pl.pallas_call(
        kernel,
        grid=(count,),
        in_specs=[group(modes), group(back), full(table.shape)]
        + [pl.BlockSpec(memory_space=pl.ANY)] * len(given),
        out_specs=group_block(shape, start),
        out_shape=jax.ShapeDtypeStruct(shape, F32),
        input_output_aliases={3: 0} if given else {},
        compiler_params=params(24),
        cost_estimate=cost(math.prod(shape) * 4, math.prod(shape) * 4),
    )(modes, back, table, *given)


def shift(block, axis, step):
    count = lax.axis_size(axis)
    pairs = [(i, i + step) for i in range(count) if 0 <= i + step < count]
    return lax.ppermute(block, axis, pairs)


def x_halos(turned):
    return shift(turned[-1], "gx", 1), shift(turned[0], "gx", -1)


def y_halos(turned, xlo, xhi):
    edge = lambda y: jnp.concatenate([xlo[None, y], turned[:, y], xhi[None, y]], axis=0)
    return shift(edge(-1), "gy", 1), shift(edge(0), "gy", -1)


def conv(turned, rim, weight, flip):
    cx, cy, c, z = turned.shape
    return call(
        functools.partial(conv_kernel, flip),
        [((cx, c, cy * z), F32)],
        (turned, *rim, weight),
        [pltpu.VMEM((4 * c, (cy + 2) * z), BF16)],
        mib=32,
        flops=2 * 27 * c * c * cx * cy * z,
        moved=turned.size * 8,
    )[0]


def weight_grad(grad, turned, rim):
    cx, cy, c, z = turned.shape
    return call(
        weight_grad_kernel,
        [((16 * c, 2 * c), F32)],
        (grad, turned, *rim),
        [
            pltpu.VMEM((4 * c, (cy + 2) * z), BF16),
            pltpu.VMEM((cx * 3 * c, (cy + 2) * z), BF16),
            pltpu.VMEM((9 * c, 4 * c), F32),
        ],
        mib=32,
        flops=2 * 27 * c * c * cx * cy * z,
        moved=turned.size * 8,
    )[0]


def swap(block, axis):
    return lax.all_to_all(block, axis, split_axis=0, concat_axis=0, tiled=True)


def together(*values):
    return lax.optimization_barrier(values)


def body(state, cotangent, spectral_weight, stencil_weight, pointwise_weight):
    nx, ny = lax.axis_size("gx"), lax.axis_size("gy")
    c, cx, cy, z = state.shape
    _, mz, mx, _, _ = spectral_weight.shape
    wide_x, wide_y = cx * nx, cy * ny
    alpha = 1.0 / math.sqrt(wide_x * wide_y * z)
    beta = 1.0 / math.sqrt(2 * MX * MY * MZ)
    double = np.where(np.arange(MZ) == 0, 1.0, 2.0)
    ones = np.ones(MZ)
    z_state = jnp.asarray(z_forward_table(alpha * ones)(nx, mz))
    z_grad = jnp.asarray(z_forward_table(double)(nx, mz))
    z_spectral = jnp.asarray(z_inverse_table(nx, mz, beta * double))
    z_back = jnp.asarray(z_inverse_table(nx, mz, alpha * beta * ones))
    x_fwd, x_inv = (jnp.asarray(t) for t in x_tables(wide_x, mz, mx))
    y_fwd, y_inv = (jnp.asarray(t) for t in y_tables(wide_y))
    spread, gather = jnp.asarray(spread_table()), jnp.asarray(gather_table())
    lanes = cy * c
    x_rows = cx * 2 * mz

    def x_stage(table, block, lead, kind=F32, extra=0):
        rows = table.shape[0] // lead + extra
        return call(
            x_kernel,
            [((lead, rows, lanes), kind)],
            (table, block),
            mib=16,
            flops=2 * table.size * lanes,
            moved=8 * block.size,
        )[0]

    slab_shape = ((nx, x_rows, lanes), F32)
    turned_shape = ((cx, cy, c, z), BF16)

    conv_table, back_table = call(
        taps_kernel,
        [((9 * c, 4 * c), BF16)] * 2,
        (stencil_weight, pointwise_weight),
        [pltpu.VMEM((27 * c, c), F32)],
        moved=stencil_weight.size * 6,
    )
    turned, slab = call(
        functools.partial(prep_kernel, nx),
        [turned_shape, slab_shape],
        (state, z_state),
        flops=2 * 96 * state.size,
        moved=state.size * 5,
    )
    block = x_stage(x_fwd, swap(slab, "gx"), ny)
    block, *faces = together(block, *x_halos(turned))
    modes_in, block = per_mode(
        mix_kernel,
        swap(block, "gy"),
        spectral_weight,
        (spread, y_fwd, y_inv),
        (2 * c, BF16),
        F32,
    )
    block, *faces = together(block, *faces)
    edges = y_halos(turned, *faces)
    block = x_stage(x_inv, swap(block, "gy"), nx)
    block, *edges = together(block, *edges)
    rim = (*faces, *edges)
    stencil = conv(turned, rim, conv_table, False)
    output, grad, slab = call(
        functools.partial(gelu_kernel, nx),
        [((c, cx, cy, z), BF16), turned_shape, slab_shape],
        (stencil, swap(block, "gx"), cotangent, z_spectral, z_grad),
        flops=2 * 192 * state.size,
        moved=state.size * 12,
    )

    grad_taps = weight_grad(grad, turned, rim)
    block = x_stage(x_fwd, swap(slab, "gx"), ny, BF16)
    block, *faces = together(block, *x_halos(grad))
    edges = y_halos(grad, *faces)
    block, grad_taps, *edges = together(swap(block, "gy"), grad_taps, *edges)
    mine = swap(grad_taps.reshape(nx, -1, 2 * c), "gx").sum(0)
    back_modes, block = per_mode(
        mix_back_kernel,
        block,
        spectral_weight,
        (gather, y_fwd, y_inv),
        (2 * c, F32),
        BF16,
        [pltpu.VMEM((2 * QUAD * MY, c * c), BF16)],
    )
    packed = jnp.concatenate(jnp.split(mine, lanes // (2 * c)), axis=1).astype(BF16)
    extra = packed.shape[0]
    packed = jnp.broadcast_to(packed[None], (ny, extra, lanes))
    block = x_stage(
        x_inv, swap(jnp.concatenate([block, packed], axis=1), "gy"), nx, F32, extra
    )
    stencil_back = conv(grad, (*faces, *edges), back_table, True)
    shape = spectral_weight.shape
    groups = modes_in.shape[0]
    early = groups // 2
    grad_modes = None
    if early:
        grad_modes = outer(modes_in, back_modes, spread, shape, alpha, 0, early)
        block, stencil_back, grad_modes = together(block, stencil_back, grad_modes)
    message = swap(block, "gx")
    grad_modes = outer(
        modes_in, back_modes, spread, shape, alpha, early, groups - early, grad_modes
    )
    grad_state = call(
        functools.partial(finish_kernel, nx),
        [((c, cx, cy, z), F32)],
        (stencil_back, message, z_back),
        flops=2 * 96 * state.size,
        moved=state.size * 10,
    )[0]
    grad_stencil, grad_point = call(
        functools.partial(unpack_kernel, alpha, x_rows),
        [((c, 27 * c), F32), ((c, c), F32)],
        (message,),
        [pltpu.VMEM(grad_taps.shape, F32), pltpu.VMEM((27 * c, c), F32)],
        moved=grad_taps.size * 8,
    )
    return (output, grad_state, grad_modes, grad_stencil, grad_point)


def solution(mesh):
    in_specs = (
        P(None, "gx", "gy", None),
        P(None, "gx", "gy", None),
        P(None, "gx", "gy", None, None),
        P(),
        P(),
    )
    out_specs = (
        P(None, "gx", "gy", None),
        P(None, "gx", "gy", None),
        P(None, "gx", "gy", None, None),
        P(),
        P(),
    )
    return jax.shard_map(body, mesh=mesh, in_specs=in_specs, out_specs=out_specs, check_vma=False)
```

```python
import functools
import math

import jax
import jax.numpy as jnp
import numpy as np
from jax import lax
from jax.experimental import pallas as pl
from jax.experimental.pallas import tpu as pltpu
from jax.sharding import PartitionSpec as P

C = 64
MX = 32
MY = 32
MZ = 16
Z = 128
MIB = 1 << 20

F32 = jnp.float32
BF16 = jnp.bfloat16


def angles(places, freqs, length):
    turns = np.outer(np.asarray(places), np.asarray(freqs)) % length
    return turns * (2.0 * np.pi / length)


def centred(count):
    steps = np.arange(count)
    return np.where(steps < count // 2, steps, steps - count)


def split(table, parts):
    rest = np.asarray(table, np.float64)
    out = []
    for _ in range(parts):
        piece = rest.astype(jnp.bfloat16)
        out.append(piece)
        rest = rest - piece.astype(np.float64)
    return out


def z_forward_table(scale):
    def build(nx, mz):
        theta = angles(np.arange(MZ), np.arange(Z), Z)
        pair = np.stack([np.cos(theta), -np.sin(theta)]) * scale[None, :, None]
        rows = pair.reshape(2, nx, mz, Z).transpose(1, 0, 2, 3).reshape(2 * MZ, Z)
        return np.concatenate(split(rows, 3), axis=0)

    return build


def z_inverse_table(nx, mz, scale):
    theta = angles(np.arange(MZ), np.arange(Z), Z)
    pair = np.stack([np.cos(theta), -np.sin(theta)]) * scale[None, :, None]
    rows = pair.reshape(2, nx, mz, Z).transpose(1, 0, 2, 3).reshape(2 * MZ, Z)
    high, low = split(rows, 2)
    return np.concatenate([high, high, low], axis=0)


def rotation(theta, sign):
    cosine, sine = np.cos(theta), sign * np.sin(theta)
    return np.stack([np.stack([cosine, -sine], 1), np.stack([sine, cosine], 1)])


def against_pieces(*tables):
    out = []
    for table in tables:
        high, low = split(table, 2)
        out.append(np.concatenate([high, high, low], axis=1))
    return out


def x_tables(wide, mz, mx):
    theta = angles(centred(MX), np.arange(wide), wide)
    eye = np.eye(mz)
    forward = np.einsum("rkRx,zZ->krzxRZ", rotation(theta, -1.0), eye)
    inverse = np.einsum("rxRk,zZ->xrzkRZ", rotation(theta.T, 1.0), eye)
    size_k, size_x = MX * 2 * mz, wide * 2 * mz
    forward = forward.reshape(MX // mx, mx, 2, mz, size_x).transpose(0, 2, 3, 1, 4)
    inverse = inverse.reshape(size_x, MX // mx, mx, 2, mz).transpose(0, 1, 3, 4, 2)
    return against_pieces(forward.reshape(size_k, size_x), inverse.reshape(size_x, size_k))


def y_tables(wide):
    theta = angles(centred(MY), np.arange(wide), wide)
    forward = rotation(theta, -1.0).reshape(2 * MY, 2 * wide)
    inverse = rotation(theta.T, 1.0).reshape(2 * wide, 2 * MY)
    return against_pieces(forward, inverse)


def pieces(values):
    high = values.astype(BF16)
    low = (values - high.astype(F32)).astype(BF16)
    return jnp.concatenate([high, low, high], axis=0)


def z_forward(rows, table, out_ref, x, nx):
    got = lax.dot_general(table, rows, (((1,), (1,)), ((), ())), preferred_element_type=F32)
    size = 2 * MZ
    total = got[:size] + (got[size : 2 * size] + got[2 * size :])
    per = size // nx
    for owner in range(nx):
        out_ref[owner, x * per : (x + 1) * per, :] = total[owner * per : (owner + 1) * per]


def z_inverse(in_ref, table, x, nx):
    per = 2 * MZ // nx
    rows = jnp.concatenate(
        [in_ref[owner].astype(F32)[x * per : (x + 1) * per] for owner in range(nx)], axis=0
    )
    return lax.dot_general(
        pieces(rows), table, (((0,), (0,)), ((), ())), preferred_element_type=F32
    )


def prep_kernel(nx, field_ref, table_ref, turned_ref, slab_ref):
    c, cx, cy, z = field_ref.shape
    for x in range(cx):
        block = jnp.swapaxes(field_ref[:, x].astype(F32), 0, 1)
        turned = block.astype(BF16)
        turned_ref[x] = turned
        z_forward(turned.reshape(cy * c, z), table_ref[...], slab_ref, x, nx)


def plane_rows(p, cx, body_ref, xlo_ref, xhi_ref, ylo_ref, yhi_ref):
    cy = body_ref.shape[1]
    if p == 0:
        middle = [xlo_ref[y] for y in range(cy)]
    elif p == cx + 1:
        middle = [xhi_ref[y] for y in range(cy)]
    else:
        middle = [body_ref[p - 1, y] for y in range(cy)]
    return [ylo_ref[p]] + middle + [yhi_ref[p]]


def fill_shifts(blocks, rim_ref, flip=False):
    c, z = blocks[0].shape
    lane = lax.broadcasted_iota(jnp.int32, (c, z), 1)
    for y, block in enumerate(blocks):
        wide = block.astype(F32)
        before = jnp.where(lane == 0, 0.0, pltpu.roll(wide, 1, 1))
        after = jnp.where(lane == z - 1, 0.0, pltpu.roll(wide, z - 1, 1))
        if flip:
            before, after = after, before
        columns = slice(y * z, (y + 1) * z)
        rim_ref[0:c, columns] = before.astype(BF16)
        rim_ref[c : 2 * c, columns] = block
        rim_ref[2 * c : 3 * c, columns] = after.astype(BF16)
        rim_ref[3 * c : 4 * c, columns] = block


def conv_kernel(
    flip, body_ref, xlo_ref, xhi_ref, ylo_ref, yhi_ref, weight_ref, out_ref, rim_ref
):
    cx, cy, c, z = body_ref.shape
    for p in range(cx + 2):
        blocks = plane_rows(p, cx, body_ref, xlo_ref, xhi_ref, ylo_ref, yhi_ref)
        fill_shifts(blocks, rim_ref, flip)
        places = [a for a in range(3) if 0 <= p - (2 - a if flip else a) < cx]
        first = places[0]
        got = jnp.dot(
            weight_ref[first * 3 * c : (places[-1] + 1) * 3 * c, :],
            rim_ref[...],
            preferred_element_type=F32,
        )
        for a in places:
            x = p - (2 - a if flip else a)
            total = None
            for b in range(3):
                row = ((a - first) * 3 + b) * c
                skip = 2 - b if flip else b
                term = got[row : row + c, skip * z : (skip + cy) * z]
                total = term if total is None else total + term
            if p == x:
                out_ref[x] = total
            else:
                out_ref[x] += total


def weight_grad_kernel(
    grad_ref, body_ref, xlo_ref, xhi_ref, ylo_ref, yhi_ref, out_ref, rim_ref, wide_ref, sum_ref
):
    cx, cy, c, z = body_ref.shape
    group = 3 * c
    wide_ref[...] = jnp.zeros_like(wide_ref)
    for x in range(cx):
        for b in range(3):
            for y in range(cy):
                row = x * group + b * c
                wide_ref[row : row + c, (y + b) * z : (y + b + 1) * z] = grad_ref[x, y]
    sum_ref[...] = jnp.zeros_like(sum_ref)
    for p in range(cx + 2):
        fill_shifts(plane_rows(p, cx, body_ref, xlo_ref, xhi_ref, ylo_ref, yhi_ref), rim_ref)
        first, last = max(0, p - 2), min(cx - 1, p)
        got = lax.dot_general(
            wide_ref[first * group : (last + 1) * group, :],
            rim_ref[...],
            (((1,), (1,)), ((), ())),
            preferred_element_type=F32,
        )
        for x in range(first, last + 1):
            a = p - x
            sum_ref[a * group : (a + 1) * group, :] += got[
                (x - first) * group : (x - first + 1) * group, :
            ]
    out_ref[: 9 * c] = sum_ref[:, : 2 * c]
    last = [sum_ref[k * c : (k + 1) * c, 2 * c : 3 * c] for k in range(9)]
    last.append(jnp.zeros((c, c), F32))
    for k in range(5):
        row = (9 + k) * c
        out_ref[row : row + c] = jnp.concatenate(last[2 * k : 2 * k + 2], axis=1)
    out_ref[14 * c :] = jnp.zeros((2 * c, 2 * c), F32)


def gelu_kernel(
    nx, stencil_ref, slab_ref, cot_ref, inverse_ref, forward_ref, out_ref, turned_ref, back_ref
):
    c, cx, cy, z = cot_ref.shape
    root = math.sqrt(2.0 / math.pi)
    for x in range(cx):
        spectral = z_inverse(slab_ref, inverse_ref[...], x, nx).reshape(cy, c, z)
        stencil = jnp.stack([stencil_ref[x, :, y * z : (y + 1) * z] for y in range(cy)])
        pre = spectral + stencil
        cot = jnp.swapaxes(cot_ref[:, x].astype(F32), 0, 1)
        square = pre * pre
        bent = jnp.tanh(root * (pre * (1.0 + 0.044715 * square)))
        half = 0.5 + 0.5 * bent
        slope = half + (0.5 * pre) * (1.0 - bent * bent) * (root * (1.0 + 0.134145 * square))
        out_ref[:, x] = jnp.swapaxes(pre * half, 0, 1).astype(BF16)
        grad = (cot * slope).astype(BF16)
        turned_ref[x] = grad
        z_forward(grad.reshape(cy * c, z), forward_ref[...], back_ref, x, nx)


def finish_kernel(
    nx,
    scale,
    stencil_ref,
    message_ref,
    inverse_ref,
    out_ref,
    taps_ref,
    point_ref,
    packed_ref,
    turned_ref,
):
    c, cx, cy, z = out_ref.shape
    for x in range(cx):
        spectral = z_inverse(message_ref, inverse_ref[...], x, nx).reshape(cy, c, z)
        stencil = jnp.stack([stencil_ref[x, :, y * z : (y + 1) * z] for y in range(cy)])
        out_ref[:, x] = jnp.swapaxes(spectral + stencil, 0, 1)
    skip = 2 * MZ * cx // nx
    unpack(scale, skip, message_ref, taps_ref, point_ref, packed_ref, turned_ref)


def x_kernel(table_ref, data_ref, out_ref):
    data = data_ref[...].astype(F32)
    lanes = data.shape[2]
    rows = table_ref.shape[1] // (3 * data.shape[0])
    flat = pieces(data[:, :rows].reshape(-1, lanes))
    got = jnp.dot(table_ref[...], flat, preferred_element_type=F32).astype(out_ref.dtype)
    count = got.shape[0] // out_ref.shape[0]
    for owner in range(out_ref.shape[0]):
        out_ref[owner, :count] = got[owner * count : (owner + 1) * count]
    if data.shape[1] > rows:
        extra = data[:, rows:].sum(0)
        extra = extra.astype(out_ref.dtype)
        for owner in range(out_ref.shape[0]):
            out_ref[owner, count:] = extra


def taps_kernel(taps_ref, point_ref, forward_ref, back_ref, turned_ref):
    turned_ref[...] = taps_ref[...].astype(F32).T
    forward_ref[...] = jnp.zeros_like(forward_ref)
    back_ref[...] = jnp.zeros_like(back_ref)
    for tap in range(27):
        rows = slice(tap // 3 * C, (tap // 3 + 1) * C)
        columns = slice(tap % 3 * C, (tap % 3 + 1) * C)
        block = turned_ref[pl.ds(tap, C, stride=27), :]
        back_ref[rows, columns] = block.astype(BF16)
        forward_ref[rows, columns] = block.T.astype(BF16)
    point = point_ref[...].astype(F32)
    forward_ref[4 * C : 5 * C, 3 * C :] = point.astype(BF16)
    back_ref[4 * C : 5 * C, 3 * C :] = point.T.astype(BF16)


def unpack(scale, skip, message_ref, taps_ref, point_ref, packed_ref, turned_ref):
    devices, rows, lanes = message_ref.shape
    per, tiles_in = rows - skip, lanes // 128
    for owner in range(devices):
        message = message_ref[owner].astype(F32)
        for tile in range(tiles_in):
            row = (owner * tiles_in + tile) * per
            packed_ref[row : row + per] = message[skip:, tile * 128 : (tile + 1) * 128]
    for tap in range(27):
        group, e = tap // 3, tap % 3
        if e < 2:
            block = packed_ref[group * C : (group + 1) * C, e * C : (e + 1) * C]
        else:
            row = (9 + group // 2) * C
            block = packed_ref[row : row + C, group % 2 * C : (group % 2 + 1) * C]
        block = block * scale
        if tap == 13:
            point_ref[...] = block
        turned_ref[pl.ds(tap, C, stride=27), :] = block.T
    taps_ref[...] = turned_ref[...].T


QUAD = 4
SPAN = 8 * C


def y_forward(mz, data_ref, table_ref, rows_ref, store):
    ny, _, lanes = data_ref.shape
    cy = lanes // C
    count = rows_ref.shape[1] // C
    for owner in range(ny):
        data = data_ref[owner].astype(F32)
        for part in range(2):
            for kz in range(mz):
                mx = count // mz
                start = (part * mz + kz) * mx
                block = data[start : start + mx]
                block = jnp.stack([block[:, y * C : (y + 1) * C] for y in range(cy)])
                block = jnp.swapaxes(block, 0, 1)
                row = (part * ny + owner) * cy
                for kx in range(mx):
                    column = (kz * mx + kx) * C
                    rows_ref[row : row + cy, column : column + C] = block[kx]
    got = jnp.dot(table_ref[...], pieces(rows_ref[...]), preferred_element_type=F32)
    for q in range(count):
        block = got[:, q * C : (q + 1) * C]
        for part in range(2):
            store(q // QUAD, part, q % QUAD, block[part * MY : (part + 1) * MY])


def y_inverse(mz, sum_ref, table_ref, out_ref, block_ref):
    rows = [
        jnp.concatenate(
            [
                sum_ref[group, place(part, pair), :]
                for group in range(sum_ref.shape[0])
                for pair in range(QUAD)
            ],
            axis=1,
        )
        for part in range(2)
    ]
    got = jnp.dot(
        table_ref[...], pieces(jnp.concatenate(rows, axis=0)), preferred_element_type=F32
    )
    ny, _, lanes = out_ref.shape
    cy = lanes // C
    count = got.shape[1] // C
    mx = count // mz
    for owner in range(ny):
        for part in range(2):
            for kz in range(mz):
                row = (part * ny + owner) * cy
                block = got[row : row + cy, kz * mx * C : (kz + 1) * mx * C]
                block = jnp.stack([block[:, kx * C : (kx + 1) * C] for kx in range(mx)])
                block = jnp.swapaxes(block, 0, 1)
                start = (part * mz + kz) * mx
                for y in range(cy):
                    block_ref[owner, start : start + mx, y * C : (y + 1) * C] = block[y]
    out_ref[...] = block_ref[...].astype(out_ref.dtype)


def place(part, pair):
    start = (part * QUAD + pair) * MY
    return slice(start, start + MY)


def spread_table():
    return np.tile(np.kron(np.eye(C), np.ones((1, C))), (2, 1)).astype(jnp.bfloat16)


def gather_table():
    return np.kron(np.eye(SPAN // C), np.ones((1, C))).astype(jnp.bfloat16)


def tiles():
    for piece in range(C * C // SPAN):
        for tile in range(SPAN // (2 * C)):
            start = piece * SPAN + tile * 2 * C
            yield piece, tile, slice(start, start + 2 * C)


def spread_modes(modes, table_ref, spread_refs):
    count = C * C // SPAN
    made = set()

    def get(piece):
        for p in range(piece, min(piece + 2, count)):
            if p not in made:
                made.add(p)
                spread_refs[p % 2][...] = jnp.dot(
                    modes, table_ref[:, p * SPAN : (p + 1) * SPAN], preferred_element_type=F32
                )
        return spread_refs[piece % 2]

    return get


def mix_kernel(
    mz,
    data_ref,
    weight_ref,
    table_ref,
    forward_ref,
    inverse_ref,
    modes_ref,
    out_ref,
    sum_ref,
    rows_ref,
    block_ref,
    even_ref,
    odd_ref,
    total_ref,
):
    step = pl.program_id(0)

    @pl.when(step == 0)
    def _():
        def store(group, part, pair, values):
            high = values.astype(BF16)
            low = (values - high.astype(F32)).astype(BF16)
            modes_ref[group, place(part, pair), :] = jnp.concatenate([high, low], axis=1)

        y_forward(mz, data_ref, forward_ref, rows_ref, store)

    spread = spread_modes(modes_ref[step], table_ref, (even_ref, odd_ref))
    for piece in range(C * C // SPAN):
        modes = spread(piece)
        for pair in range(QUAD):
            real = imag = None
            for tile in range(SPAN // (2 * C)):
                inside = slice(tile * 2 * C, (tile + 1) * 2 * C)
                columns = slice(piece * SPAN + inside.start, piece * SPAN + inside.stop)
                mode_re = modes[place(0, pair), inside]
                mode_im = modes[place(1, pair), inside]
                weight_re = weight_ref[0, 0, pair, :, columns].astype(F32)
                weight_im = weight_ref[1, 0, pair, :, columns].astype(F32)
                term_re = mode_re * weight_re - mode_im * weight_im
                term_im = mode_re * weight_im + mode_im * weight_re
                real = term_re if real is None else real + term_re
                imag = term_im if imag is None else imag + term_im
            if piece:
                real += total_ref[place(0, pair), :]
                imag += total_ref[place(1, pair), :]
            total_ref[place(0, pair), :] = real
            total_ref[place(1, pair), :] = imag
    total = total_ref[...]
    sum_ref[step] = total[:, :C] + total[:, C:]

    @pl.when(step == pl.num_programs(0) - 1)
    def _():
        y_inverse(mz, sum_ref, inverse_ref, out_ref, block_ref)


def mix_back_kernel(
    mz,
    data_ref,
    weight_ref,
    table_ref,
    forward_ref,
    inverse_ref,
    modes_ref,
    out_ref,
    sum_ref,
    rows_ref,
    block_ref,
    term_ref,
):
    step = pl.program_id(0)

    @pl.when(step == 0)
    def _():
        def store(group, part, pair, values):
            modes_ref[group, place(part, pair), :] = jnp.concatenate([values, values], axis=1)

        y_forward(mz, data_ref, forward_ref, rows_ref, store)

    total = []
    for piece, tile, columns in tiles():
        for pair in range(QUAD):
            mode_re = modes_ref[step, place(0, pair), :]
            mode_im = modes_ref[step, place(1, pair), :]
            weight_re = weight_ref[0, 0, pair, :, columns].astype(F32)
            weight_im = weight_ref[1, 0, pair, :, columns].astype(F32)
            term_ref[place(0, pair), columns] = (
                weight_re * mode_re + weight_im * mode_im
            ).astype(BF16)
            term_ref[place(1, pair), columns] = (
                weight_re * mode_im - weight_im * mode_re
            ).astype(BF16)
        if columns.stop % SPAN == 0:
            whole_piece = slice(piece * SPAN, (piece + 1) * SPAN)
            total.append(
                lax.dot_general(
                    table_ref[...],
                    term_ref[:, whole_piece],
                    (((1,), (1,)), ((), ())),
                    preferred_element_type=F32,
                )
            )
    sum_ref[step] = jnp.concatenate(total, axis=0).T

    @pl.when(step == pl.num_programs(0) - 1)
    def _():
        y_inverse(mz, sum_ref, inverse_ref, out_ref, block_ref)


def outer_kernel(alpha, modes_ref, back_ref, table_ref, out_ref, even_ref, odd_ref):
    spread = spread_modes(modes_ref[0], table_ref, (even_ref, odd_ref))
    for piece in range(C * C // SPAN):
        modes = spread(piece)
        for pair in range(QUAD):
            back_re = back_ref[0, place(0, pair), :] * alpha
            back_im = back_ref[0, place(1, pair), :] * alpha
            for tile in range(SPAN // (2 * C)):
                inside = slice(tile * 2 * C, (tile + 1) * 2 * C)
                columns = slice(piece * SPAN + inside.start, piece * SPAN + inside.stop)
                mode_re = modes[place(0, pair), inside]
                mode_im = modes[place(1, pair), inside]
                out_ref[0, 0, pair, :, columns] = mode_re * back_re + mode_im * back_im
                out_ref[1, 0, pair, :, columns] = mode_re * back_im - mode_im * back_re


def in_hbm(value):
    return pltpu.with_memory_space_constraint(value, pltpu.HBM)


def whole():
    return pl.BlockSpec(memory_space=pltpu.VMEM)


def params(mib):
    return pltpu.CompilerParams(vmem_limit_bytes=mib * MIB)


def cost(flops, moved):
    return pl.CostEstimate(flops=int(flops), bytes_accessed=int(moved), transcendentals=0)


def call(kernel, outs, args, scratch=(), mib=24, flops=0, moved=0):
    return pl.pallas_call(
        kernel,
        out_shape=[jax.ShapeDtypeStruct(*out) for out in outs],
        in_specs=[whole() for _ in args],
        out_specs=[whole() for _ in outs],
        scratch_shapes=list(scratch),
        compiler_params=params(mib),
        cost_estimate=cost(flops, moved),
    )(*args)


def full(shape):
    return pl.BlockSpec(shape, lambda step: (0,) * len(shape))


def group_block(shape, start=0):
    per = shape[2] // QUAD
    return pl.BlockSpec(
        (2, 1, QUAD) + shape[3:],
        lambda step: (0, (step + start) // per, (step + start) % per, 0, 0),
    )


def per_mode(kernel, data, weight, tables, modes, kind, scratch=()):
    _, mz, mx, _, _ = weight.shape
    groups = mz * mx // QUAD
    rows = 2 * QUAD * MY
    modes_shape = (groups, rows, modes[0])
    return pl.pallas_call(
        functools.partial(kernel, mz),
        grid=(groups,),
        in_specs=[full(data.shape), group_block(weight.shape)] + [full(t.shape) for t in tables],
        out_specs=[full(modes_shape), full(data.shape)],
        out_shape=[
            jax.ShapeDtypeStruct(modes_shape, modes[1]),
            jax.ShapeDtypeStruct(data.shape, kind),
        ],
        scratch_shapes=[
            pltpu.VMEM((groups, rows, C), F32),
            pltpu.VMEM((tables[-1].shape[0], mz * mx * C), F32),
            pltpu.VMEM(data.shape, F32),
            *scratch,
        ],
        compiler_params=params(20),
        cost_estimate=cost(weight.size * 8, weight.size * 2),
    )(data, in_hbm(weight), *map(in_hbm, tables))


def outer(modes, back, table, shape, alpha, start, count, prior=None):
    def kernel(*refs):
        outer_kernel(alpha, *refs[:3], *refs[-3:])

    group = lambda ref: pl.BlockSpec((1,) + ref.shape[1:], lambda step: (step + start, 0, 0))
    given = () if prior is None else (prior,)
    return pl.pallas_call(
        kernel,
        grid=(count,),
        in_specs=[group(modes), group(back), full(table.shape)]
        + [pl.BlockSpec(memory_space=pl.ANY)] * len(given),
        out_specs=group_block(shape, start),
        out_shape=jax.ShapeDtypeStruct(shape, F32),
        input_output_aliases={3: 0} if given else {},
        scratch_shapes=[pltpu.VMEM((2 * QUAD * MY, SPAN), F32)] * 2,
        compiler_params=params(20),
        cost_estimate=cost(math.prod(shape) * 4, math.prod(shape) * 4),
    )(modes, back, in_hbm(table), *given)


def shift(block, axis, step):
    count = lax.axis_size(axis)
    pairs = [(i, i + step) for i in range(count) if 0 <= i + step < count]
    return lax.ppermute(block, axis, pairs)


def x_halos(turned):
    return shift(turned[-1], "gx", 1), shift(turned[0], "gx", -1)


def y_halos(turned, xlo, xhi):
    edge = lambda y: jnp.concatenate([xlo[None, y], turned[:, y], xhi[None, y]], axis=0)
    return shift(edge(-1), "gy", 1), shift(edge(0), "gy", -1)


def conv(turned, rim, weight, flip):
    cx, cy, c, z = turned.shape
    return call(
        functools.partial(conv_kernel, flip),
        [((cx, c, cy * z), F32)],
        (turned, *rim, weight),
        [pltpu.VMEM((4 * c, (cy + 2) * z), BF16)],
        mib=32,
        flops=2 * 27 * c * c * cx * cy * z,
        moved=turned.size * 8,
    )[0]


def weight_grad(grad, turned, rim):
    cx, cy, c, z = turned.shape
    return call(
        weight_grad_kernel,
        [((16 * c, 2 * c), F32)],
        (grad, turned, *rim),
        [
            pltpu.VMEM((4 * c, (cy + 2) * z), BF16),
            pltpu.VMEM((cx * 3 * c, (cy + 2) * z), BF16),
            pltpu.VMEM((9 * c, 4 * c), F32),
        ],
        mib=32,
        flops=2 * 27 * c * c * cx * cy * z,
        moved=turned.size * 8,
    )[0]


def swap(block, axis):
    return lax.all_to_all(block, axis, split_axis=0, concat_axis=0, tiled=True)


def together(*values):
    return lax.optimization_barrier(values)


def body(state, cotangent, spectral_weight, stencil_weight, pointwise_weight):
    nx, ny = lax.axis_size("gx"), lax.axis_size("gy")
    c, cx, cy, z = state.shape
    _, mz, mx, _, _ = spectral_weight.shape
    wide_x, wide_y = cx * nx, cy * ny
    alpha = 1.0 / math.sqrt(wide_x * wide_y * z)
    beta = 1.0 / math.sqrt(2 * MX * MY * MZ)
    double = np.where(np.arange(MZ) == 0, 1.0, 2.0)
    ones = np.ones(MZ)
    z_state = jnp.asarray(z_forward_table(alpha * ones)(nx, mz))
    z_grad = jnp.asarray(z_forward_table(double)(nx, mz))
    z_spectral = jnp.asarray(z_inverse_table(nx, mz, beta * double))
    z_back = jnp.asarray(z_inverse_table(nx, mz, alpha * beta * ones))
    x_fwd, x_inv = (jnp.asarray(t) for t in x_tables(wide_x, mz, mx))
    y_fwd, y_inv = (jnp.asarray(t) for t in y_tables(wide_y))
    spread, gather = jnp.asarray(spread_table()), jnp.asarray(gather_table())
    lanes = cy * c
    x_rows = cx * 2 * mz

    def x_stage(table, block, lead, kind=F32, extra=0):
        rows = table.shape[0] // lead + extra
        return call(
            x_kernel,
            [((lead, rows, lanes), kind)],
            (in_hbm(table), block),
            mib=16,
            flops=2 * table.size * lanes,
            moved=8 * block.size,
        )[0]

    slab_shape = ((nx, x_rows, lanes), F32)
    turned_shape = ((cx, cy, c, z), BF16)

    conv_table, back_table = call(
        taps_kernel,
        [((9 * c, 4 * c), BF16)] * 2,
        (in_hbm(stencil_weight), in_hbm(pointwise_weight)),
        [pltpu.VMEM((27 * c, c), F32)],
        moved=stencil_weight.size * 6,
    )
    turned, slab = call(
        functools.partial(prep_kernel, nx),
        [turned_shape, slab_shape],
        (in_hbm(state), in_hbm(z_state)),
        flops=2 * 96 * state.size,
        moved=state.size * 5,
    )
    block = x_stage(x_fwd, swap(slab, "gx"), ny)
    block, conv_table, back_table, *faces = together(
        block, conv_table, back_table, *x_halos(turned)
    )
    modes_in, block = per_mode(
        mix_kernel,
        swap(block, "gy"),
        spectral_weight,
        (spread, y_fwd, y_inv),
        (2 * c, BF16),
        F32,
        [pltpu.VMEM((2 * QUAD * MY, SPAN), F32)] * 2 + [pltpu.VMEM((2 * QUAD * MY, 2 * c), F32)],
    )
    block, *faces = together(block, *faces)
    edges = y_halos(turned, *faces)
    block = x_stage(x_inv, swap(block, "gy"), nx)
    block, *edges = together(block, *edges)
    rim = (*faces, *edges)
    stencil = conv(turned, rim, conv_table, False)
    output, grad, slab = call(
        functools.partial(gelu_kernel, nx),
        [((c, cx, cy, z), BF16), turned_shape, slab_shape],
        (stencil, swap(block, "gx"), cotangent, in_hbm(z_spectral), in_hbm(z_grad)),
        flops=2 * 192 * state.size,
        moved=state.size * 12,
    )

    grad_taps = weight_grad(grad, turned, rim)
    block = x_stage(x_fwd, swap(slab, "gx"), ny, BF16)
    block, *faces = together(block, *x_halos(grad))
    edges = y_halos(grad, *faces)
    block, grad_taps, *edges = together(swap(block, "gy"), grad_taps, *edges)
    mine = swap(grad_taps.reshape(nx, -1, 2 * c), "gx").sum(0)
    back_modes, block = per_mode(
        mix_back_kernel,
        block,
        spectral_weight,
        (gather, y_fwd, y_inv),
        (2 * c, F32),
        BF16,
        [pltpu.VMEM((2 * QUAD * MY, c * c), BF16)],
    )
    packed = jnp.concatenate(jnp.split(mine, lanes // (2 * c)), axis=1).astype(BF16)
    extra = packed.shape[0]
    packed = jnp.broadcast_to(packed[None], (ny, extra, lanes))
    block = x_stage(
        x_inv, swap(jnp.concatenate([block, packed], axis=1), "gy"), nx, BF16, extra
    )
    stencil_back = conv(grad, (*faces, *edges), back_table, True)
    shape = spectral_weight.shape
    groups = modes_in.shape[0]
    early = groups // 2
    grad_modes = None
    if early:
        grad_modes = outer(modes_in, back_modes, spread, shape, alpha, 0, early)
        block, stencil_back, grad_modes = together(block, stencil_back, grad_modes)
    message = swap(block, "gx")
    grad_modes = outer(
        modes_in, back_modes, spread, shape, alpha, early, groups - early, grad_modes
    )
    grad_state, grad_stencil, grad_point = call(
        functools.partial(finish_kernel, nx, alpha),
        [((c, cx, cy, z), F32), ((c, 27 * c), F32), ((c, c), F32)],
        (stencil_back, message, in_hbm(z_back)),
        [pltpu.VMEM(grad_taps.shape, F32), pltpu.VMEM((27 * c, c), F32)],
        flops=2 * 96 * state.size,
        moved=state.size * 10,
    )
    return (output, grad_state, grad_modes, grad_stencil, grad_point)


def solution(mesh):
    in_specs = (
        P(None, "gx", "gy", None),
        P(None, "gx", "gy", None),
        P(None, "gx", "gy", None, None),
        P(),
        P(),
    )
    out_specs = (
        P(None, "gx", "gy", None),
        P(None, "gx", "gy", None),
        P(None, "gx", "gy", None, None),
        P(),
        P(),
    )
    return jax.shard_map(body, mesh=mesh, in_specs=in_specs, out_specs=out_specs, check_vma=False)
```

```python
import functools
import math

import jax
import jax.numpy as jnp
import numpy as np
from jax import lax
from jax.experimental import pallas as pl
from jax.experimental.pallas import tpu as pltpu
from jax.sharding import PartitionSpec as P

C = 64
MX = 32
MY = 32
MZ = 16
Z = 128
MIB = 1 << 20

F32 = jnp.float32
BF16 = jnp.bfloat16


def angles(places, freqs, length):
    turns = np.outer(np.asarray(places), np.asarray(freqs)) % length
    return turns * (2.0 * np.pi / length)


def centred(count):
    steps = np.arange(count)
    return np.where(steps < count // 2, steps, steps - count)


def split(table, parts):
    rest = np.asarray(table, np.float64)
    out = []
    for _ in range(parts):
        piece = rest.astype(jnp.bfloat16)
        out.append(piece)
        rest = rest - piece.astype(np.float64)
    return out


def z_forward_table(scale):
    def build(nx, mz):
        theta = angles(np.arange(MZ), np.arange(Z), Z)
        pair = np.stack([np.cos(theta), -np.sin(theta)]) * scale[None, :, None]
        rows = pair.reshape(2, nx, mz, Z).transpose(1, 0, 2, 3).reshape(2 * MZ, Z)
        return np.concatenate(split(rows, 3), axis=0)

    return build


def z_inverse_table(nx, mz, scale):
    theta = angles(np.arange(MZ), np.arange(Z), Z)
    pair = np.stack([np.cos(theta), -np.sin(theta)]) * scale[None, :, None]
    rows = pair.reshape(2, nx, mz, Z).transpose(1, 0, 2, 3).reshape(2 * MZ, Z)
    high, low = split(rows, 2)
    return np.concatenate([high, high, low], axis=0)


def rotation(theta, sign):
    cosine, sine = np.cos(theta), sign * np.sin(theta)
    return np.stack([np.stack([cosine, -sine], 1), np.stack([sine, cosine], 1)])


def against_pieces(*tables):
    out = []
    for table in tables:
        high, low = split(table, 2)
        out.append(np.concatenate([high, high, low], axis=1))
    return out


def x_tables(wide, mz, mx):
    theta = angles(centred(MX), np.arange(wide), wide)
    eye = np.eye(mz)
    forward = np.einsum("rkRx,zZ->krzxRZ", rotation(theta, -1.0), eye)
    inverse = np.einsum("rxRk,zZ->xrzkRZ", rotation(theta.T, 1.0), eye)
    size_k, size_x = MX * 2 * mz, wide * 2 * mz
    forward = forward.reshape(MX // mx, mx, 2, mz, size_x).transpose(0, 2, 3, 1, 4)
    inverse = inverse.reshape(size_x, MX // mx, mx, 2, mz).transpose(0, 1, 3, 4, 2)
    return against_pieces(forward.reshape(size_k, size_x), inverse.reshape(size_x, size_k))


def y_tables(wide):
    theta = angles(centred(MY), np.arange(wide), wide)
    forward = rotation(theta, -1.0).reshape(2 * MY, 2 * wide)
    inverse = rotation(theta.T, 1.0).reshape(2 * wide, 2 * MY)
    return against_pieces(forward, inverse)


def pieces(values):
    high = values.astype(BF16)
    low = (values - high.astype(F32)).astype(BF16)
    return jnp.concatenate([high, low, high], axis=0)


def z_forward(rows, table, out_ref, x, nx):
    got = lax.dot_general(table, rows, (((1,), (1,)), ((), ())), preferred_element_type=F32)
    size = 2 * MZ
    total = got[:size] + (got[size : 2 * size] + got[2 * size :])
    per = size // nx
    for owner in range(nx):
        out_ref[owner, x * per : (x + 1) * per, :] = total[owner * per : (owner + 1) * per]


def z_inverse(in_ref, table, x, nx):
    per = 2 * MZ // nx
    rows = jnp.concatenate(
        [in_ref[owner].astype(F32)[x * per : (x + 1) * per] for owner in range(nx)], axis=0
    )
    return lax.dot_general(
        pieces(rows), table, (((0,), (0,)), ((), ())), preferred_element_type=F32
    )


def prep_kernel(nx, field_ref, table_ref, turned_ref, slab_ref):
    c, cx, cy, z = field_ref.shape
    for x in range(cx):
        block = jnp.swapaxes(field_ref[:, x].astype(F32), 0, 1)
        turned = block.astype(BF16)
        turned_ref[x] = turned
        z_forward(turned.reshape(cy * c, z), table_ref[...], slab_ref, x, nx)


def plane_rows(p, cx, body_ref, ylo_ref, yhi_ref, xlo_ref, xhi_ref):
    cy = body_ref.shape[1]
    if p in (0, cx + 1):
        face_ref = xhi_ref if p else xlo_ref
        return [face_ref[y] for y in range(cy + 2)]
    return [ylo_ref[p - 1]] + [body_ref[p - 1, y] for y in range(cy)] + [yhi_ref[p - 1]]


def fill_shifts(blocks, rim_ref, flip=False):
    c, z = blocks[0].shape
    lane = lax.broadcasted_iota(jnp.int32, (c, z), 1)
    for y, block in enumerate(blocks):
        wide = block.astype(F32)
        before = jnp.where(lane == 0, 0.0, pltpu.roll(wide, 1, 1))
        after = jnp.where(lane == z - 1, 0.0, pltpu.roll(wide, z - 1, 1))
        if flip:
            before, after = after, before
        columns = slice(y * z, (y + 1) * z)
        rim_ref[0:c, columns] = before.astype(BF16)
        rim_ref[c : 2 * c, columns] = block
        rim_ref[2 * c : 3 * c, columns] = after.astype(BF16)
        rim_ref[3 * c : 4 * c, columns] = block


def conv_kernel(
    flip, body_ref, ylo_ref, yhi_ref, xlo_ref, xhi_ref, weight_ref, out_ref, rim_ref
):
    cx, cy, c, z = body_ref.shape
    for p in range(cx + 2):
        blocks = plane_rows(p, cx, body_ref, ylo_ref, yhi_ref, xlo_ref, xhi_ref)
        fill_shifts(blocks, rim_ref, flip)
        places = [a for a in range(3) if 0 <= p - (2 - a if flip else a) < cx]
        first = places[0]
        got = jnp.dot(
            weight_ref[first * 3 * c : (places[-1] + 1) * 3 * c, :],
            rim_ref[...],
            preferred_element_type=F32,
        )
        for a in places:
            x = p - (2 - a if flip else a)
            total = None
            for b in range(3):
                row = ((a - first) * 3 + b) * c
                skip = 2 - b if flip else b
                term = got[row : row + c, skip * z : (skip + cy) * z]
                total = term if total is None else total + term
            if p == x:
                out_ref[x] = total
            else:
                out_ref[x] += total


def weight_grad_kernel(
    grad_ref, body_ref, ylo_ref, yhi_ref, xlo_ref, xhi_ref, out_ref, rim_ref, wide_ref, sum_ref
):
    cx, cy, c, z = body_ref.shape
    group = 3 * c
    wide_ref[...] = jnp.zeros_like(wide_ref)
    for x in range(cx):
        for b in range(3):
            for y in range(cy):
                row = x * group + b * c
                wide_ref[row : row + c, (y + b) * z : (y + b + 1) * z] = grad_ref[x, y]
    sum_ref[...] = jnp.zeros_like(sum_ref)
    for p in range(cx + 2):
        fill_shifts(plane_rows(p, cx, body_ref, ylo_ref, yhi_ref, xlo_ref, xhi_ref), rim_ref)
        first, last = max(0, p - 2), min(cx - 1, p)
        got = lax.dot_general(
            wide_ref[first * group : (last + 1) * group, :],
            rim_ref[...],
            (((1,), (1,)), ((), ())),
            preferred_element_type=F32,
        )
        for x in range(first, last + 1):
            a = p - x
            sum_ref[a * group : (a + 1) * group, :] += got[
                (x - first) * group : (x - first + 1) * group, :
            ]
    out_ref[: 9 * c] = sum_ref[:, : 2 * c]
    last = [sum_ref[k * c : (k + 1) * c, 2 * c : 3 * c] for k in range(9)]
    last.append(jnp.zeros((c, c), F32))
    for k in range(5):
        row = (9 + k) * c
        out_ref[row : row + c] = jnp.concatenate(last[2 * k : 2 * k + 2], axis=1)
    out_ref[14 * c :] = jnp.zeros((2 * c, 2 * c), F32)


def gelu_kernel(
    nx, stencil_ref, slab_ref, cot_ref, inverse_ref, forward_ref, out_ref, turned_ref, back_ref
):
    c, cx, cy, z = cot_ref.shape
    root = math.sqrt(2.0 / math.pi)
    for x in range(cx):
        spectral = z_inverse(slab_ref, inverse_ref[...], x, nx).reshape(cy, c, z)
        stencil = jnp.stack([stencil_ref[x, :, y * z : (y + 1) * z] for y in range(cy)])
        pre = spectral + stencil
        cot = jnp.swapaxes(cot_ref[:, x].astype(F32), 0, 1)
        square = pre * pre
        bent = jnp.tanh(root * (pre * (1.0 + 0.044715 * square)))
        half = 0.5 + 0.5 * bent
        slope = half + (0.5 * pre) * (1.0 - bent * bent) * (root * (1.0 + 0.134145 * square))
        out_ref[:, x] = jnp.swapaxes(pre * half, 0, 1).astype(BF16)
        grad = (cot * slope).astype(BF16)
        turned_ref[x] = grad
        z_forward(grad.reshape(cy * c, z), forward_ref[...], back_ref, x, nx)


def finish_kernel(
    nx,
    scale,
    stencil_ref,
    message_ref,
    inverse_ref,
    out_ref,
    taps_ref,
    point_ref,
    packed_ref,
    turned_ref,
):
    c, cx, cy, z = out_ref.shape
    for x in range(cx):
        spectral = z_inverse(message_ref, inverse_ref[...], x, nx).reshape(cy, c, z)
        stencil = jnp.stack([stencil_ref[x, :, y * z : (y + 1) * z] for y in range(cy)])
        out_ref[:, x] = jnp.swapaxes(spectral + stencil, 0, 1)
    skip = 2 * MZ * cx // nx
    unpack(scale, skip, message_ref, taps_ref, point_ref, packed_ref, turned_ref)


def x_kernel(table_ref, data_ref, out_ref):
    data = data_ref[...].astype(F32)
    lanes = data.shape[2]
    rows = table_ref.shape[1] // (3 * data.shape[0])
    flat = pieces(data[:, :rows].reshape(-1, lanes))
    got = jnp.dot(table_ref[...], flat, preferred_element_type=F32).astype(out_ref.dtype)
    count = got.shape[0] // out_ref.shape[0]
    for owner in range(out_ref.shape[0]):
        out_ref[owner, :count] = got[owner * count : (owner + 1) * count]
    if data.shape[1] > rows:
        extra = data[:, rows:].sum(0)
        extra = extra.astype(out_ref.dtype)
        for owner in range(out_ref.shape[0]):
            out_ref[owner, count:] = extra


def taps_kernel(taps_ref, point_ref, forward_ref, back_ref, turned_ref):
    turned_ref[...] = taps_ref[...].astype(F32).T
    forward_ref[...] = jnp.zeros_like(forward_ref)
    back_ref[...] = jnp.zeros_like(back_ref)
    for tap in range(27):
        rows = slice(tap // 3 * C, (tap // 3 + 1) * C)
        columns = slice(tap % 3 * C, (tap % 3 + 1) * C)
        block = turned_ref[pl.ds(tap, C, stride=27), :]
        back_ref[rows, columns] = block.astype(BF16)
        forward_ref[rows, columns] = block.T.astype(BF16)
    point = point_ref[...].astype(F32)
    forward_ref[4 * C : 5 * C, 3 * C :] = point.astype(BF16)
    back_ref[4 * C : 5 * C, 3 * C :] = point.T.astype(BF16)


def unpack(scale, skip, message_ref, taps_ref, point_ref, packed_ref, turned_ref):
    devices, rows, lanes = message_ref.shape
    per, tiles_in = rows - skip, lanes // 128
    for owner in range(devices):
        message = message_ref[owner].astype(F32)
        for tile in range(tiles_in):
            row = (owner * tiles_in + tile) * per
            packed_ref[row : row + per] = message[skip:, tile * 128 : (tile + 1) * 128]
    for tap in range(27):
        group, e = tap // 3, tap % 3
        if e < 2:
            block = packed_ref[group * C : (group + 1) * C, e * C : (e + 1) * C]
        else:
            row = (9 + group // 2) * C
            block = packed_ref[row : row + C, group % 2 * C : (group % 2 + 1) * C]
        block = block * scale
        if tap == 13:
            point_ref[...] = block
        turned_ref[pl.ds(tap, C, stride=27), :] = block.T
    taps_ref[...] = turned_ref[...].T


QUAD = 4
SPAN = 8 * C


def y_forward(mz, data_ref, table_ref, rows_ref, store):
    ny, _, lanes = data_ref.shape
    cy = lanes // C
    count = rows_ref.shape[1] // C
    for owner in range(ny):
        data = data_ref[owner].astype(F32)
        for part in range(2):
            for kz in range(mz):
                mx = count // mz
                start = (part * mz + kz) * mx
                block = data[start : start + mx]
                block = jnp.stack([block[:, y * C : (y + 1) * C] for y in range(cy)])
                block = jnp.swapaxes(block, 0, 1)
                row = (part * ny + owner) * cy
                for kx in range(mx):
                    column = (kz * mx + kx) * C
                    rows_ref[row : row + cy, column : column + C] = block[kx]
    got = jnp.dot(table_ref[...], pieces(rows_ref[...]), preferred_element_type=F32)
    for q in range(count):
        block = got[:, q * C : (q + 1) * C]
        for part in range(2):
            store(q // QUAD, part, q % QUAD, block[part * MY : (part + 1) * MY])


def y_inverse(mz, sum_ref, table_ref, out_ref, block_ref):
    rows = [
        jnp.concatenate(
            [
                sum_ref[group, place(part, pair), :]
                for group in range(sum_ref.shape[0])
                for pair in range(QUAD)
            ],
            axis=1,
        )
        for part in range(2)
    ]
    got = jnp.dot(
        table_ref[...], pieces(jnp.concatenate(rows, axis=0)), preferred_element_type=F32
    )
    ny, _, lanes = out_ref.shape
    cy = lanes // C
    count = got.shape[1] // C
    mx = count // mz
    for owner in range(ny):
        for part in range(2):
            for kz in range(mz):
                row = (part * ny + owner) * cy
                block = got[row : row + cy, kz * mx * C : (kz + 1) * mx * C]
                block = jnp.stack([block[:, kx * C : (kx + 1) * C] for kx in range(mx)])
                block = jnp.swapaxes(block, 0, 1)
                start = (part * mz + kz) * mx
                for y in range(cy):
                    block_ref[owner, start : start + mx, y * C : (y + 1) * C] = block[y]
    out_ref[...] = block_ref[...].astype(out_ref.dtype)


def place(part, pair):
    start = (part * QUAD + pair) * MY
    return slice(start, start + MY)


def spread_table():
    return np.tile(np.kron(np.eye(C), np.ones((1, C))), (2, 1)).astype(jnp.bfloat16)


def gather_table():
    return np.kron(np.eye(SPAN // C), np.ones((1, C))).astype(jnp.bfloat16)


def tiles():
    for piece in range(C * C // SPAN):
        for tile in range(SPAN // (2 * C)):
            start = piece * SPAN + tile * 2 * C
            yield piece, tile, slice(start, start + 2 * C)


def spread_modes(modes, table_ref, spread_refs):
    count = C * C // SPAN
    made = set()

    def get(piece):
        for p in range(piece, min(piece + 2, count)):
            if p not in made:
                made.add(p)
                spread_refs[p % 2][...] = jnp.dot(
                    modes, table_ref[:, p * SPAN : (p + 1) * SPAN], preferred_element_type=F32
                )
        return spread_refs[piece % 2]

    return get


def mix_kernel(
    mz,
    data_ref,
    weight_ref,
    table_ref,
    forward_ref,
    inverse_ref,
    modes_ref,
    out_ref,
    sum_ref,
    rows_ref,
    block_ref,
    even_ref,
    odd_ref,
    total_ref,
):
    step = pl.program_id(0)

    @pl.when(step == 0)
    def _():
        def store(group, part, pair, values):
            high = values.astype(BF16)
            low = (values - high.astype(F32)).astype(BF16)
            modes_ref[group, place(part, pair), :] = jnp.concatenate([high, low], axis=1)

        y_forward(mz, data_ref, forward_ref, rows_ref, store)

    spread = spread_modes(modes_ref[step], table_ref, (even_ref, odd_ref))
    for piece in range(C * C // SPAN):
        modes = spread(piece)
        for pair in range(QUAD):
            real = imag = None
            for tile in range(SPAN // (2 * C)):
                inside = slice(tile * 2 * C, (tile + 1) * 2 * C)
                columns = slice(piece * SPAN + inside.start, piece * SPAN + inside.stop)
                mode_re = modes[place(0, pair), inside]
                mode_im = modes[place(1, pair), inside]
                weight_re = weight_ref[0, 0, pair, :, columns].astype(F32)
                weight_im = weight_ref[1, 0, pair, :, columns].astype(F32)
                term_re = mode_re * weight_re - mode_im * weight_im
                term_im = mode_re * weight_im + mode_im * weight_re
                real = term_re if real is None else real + term_re
                imag = term_im if imag is None else imag + term_im
            if piece:
                real += total_ref[place(0, pair), :]
                imag += total_ref[place(1, pair), :]
            total_ref[place(0, pair), :] = real
            total_ref[place(1, pair), :] = imag
    total = total_ref[...]
    sum_ref[step] = total[:, :C] + total[:, C:]

    @pl.when(step == pl.num_programs(0) - 1)
    def _():
        y_inverse(mz, sum_ref, inverse_ref, out_ref, block_ref)


def mix_back_kernel(
    mz,
    data_ref,
    weight_ref,
    table_ref,
    forward_ref,
    inverse_ref,
    modes_ref,
    out_ref,
    sum_ref,
    rows_ref,
    block_ref,
    term_ref,
):
    step = pl.program_id(0)

    @pl.when(step == 0)
    def _():
        def store(group, part, pair, values):
            modes_ref[group, place(part, pair), :] = jnp.concatenate([values, values], axis=1)

        y_forward(mz, data_ref, forward_ref, rows_ref, store)

    total = []
    for piece, tile, columns in tiles():
        for pair in range(QUAD):
            mode_re = modes_ref[step, place(0, pair), :]
            mode_im = modes_ref[step, place(1, pair), :]
            weight_re = weight_ref[0, 0, pair, :, columns].astype(F32)
            weight_im = weight_ref[1, 0, pair, :, columns].astype(F32)
            term_ref[place(0, pair), columns] = (
                weight_re * mode_re + weight_im * mode_im
            ).astype(BF16)
            term_ref[place(1, pair), columns] = (
                weight_re * mode_im - weight_im * mode_re
            ).astype(BF16)
        if columns.stop % SPAN == 0:
            whole_piece = slice(piece * SPAN, (piece + 1) * SPAN)
            total.append(
                lax.dot_general(
                    table_ref[...],
                    term_ref[:, whole_piece],
                    (((1,), (1,)), ((), ())),
                    preferred_element_type=F32,
                )
            )
    sum_ref[step] = jnp.concatenate(total, axis=0).T

    @pl.when(step == pl.num_programs(0) - 1)
    def _():
        y_inverse(mz, sum_ref, inverse_ref, out_ref, block_ref)


def outer_kernel(alpha, modes_ref, back_ref, table_ref, out_ref):
    spread = jnp.dot(modes_ref[0], table_ref[...], preferred_element_type=F32)
    for pair in range(QUAD):
        back_re = back_ref[0, place(0, pair), :] * alpha
        back_im = back_ref[0, place(1, pair), :] * alpha
        for tile in range(out_ref.shape[4] // (2 * C)):
            columns = slice(tile * 2 * C, (tile + 1) * 2 * C)
            mode_re = spread[place(0, pair), columns]
            mode_im = spread[place(1, pair), columns]
            out_ref[0, 0, pair, :, columns] = mode_re * back_re + mode_im * back_im
            out_ref[1, 0, pair, :, columns] = mode_re * back_im - mode_im * back_re


def in_hbm(value):
    return pltpu.with_memory_space_constraint(value, pltpu.HBM)


def whole():
    return pl.BlockSpec(memory_space=pltpu.VMEM)


def params(mib):
    return pltpu.CompilerParams(vmem_limit_bytes=mib * MIB)


def cost(flops, moved):
    return pl.CostEstimate(flops=int(flops), bytes_accessed=int(moved), transcendentals=0)


def call(kernel, outs, args, scratch=(), mib=24, flops=0, moved=0):
    return pl.pallas_call(
        kernel,
        out_shape=[jax.ShapeDtypeStruct(*out) for out in outs],
        in_specs=[whole() for _ in args],
        out_specs=[whole() for _ in outs],
        scratch_shapes=list(scratch),
        compiler_params=params(mib),
        cost_estimate=cost(flops, moved),
    )(*args)


def full(shape):
    return pl.BlockSpec(shape, lambda step: (0,) * len(shape))


def group_block(shape):
    per = shape[2] // QUAD
    return pl.BlockSpec(
        (2, 1, QUAD) + shape[3:], lambda step: (0, step // per, step % per, 0, 0)
    )


def per_mode(kernel, data, weight, tables, modes, kind, scratch=()):
    _, mz, mx, _, _ = weight.shape
    groups = mz * mx // QUAD
    rows = 2 * QUAD * MY
    modes_shape = (groups, rows, modes[0])
    return pl.pallas_call(
        functools.partial(kernel, mz),
        grid=(groups,),
        in_specs=[full(data.shape), group_block(weight.shape)] + [full(t.shape) for t in tables],
        out_specs=[full(modes_shape), full(data.shape)],
        out_shape=[
            jax.ShapeDtypeStruct(modes_shape, modes[1]),
            jax.ShapeDtypeStruct(data.shape, kind),
        ],
        scratch_shapes=[
            pltpu.VMEM((groups, rows, C), F32),
            pltpu.VMEM((tables[-1].shape[0], mz * mx * C), F32),
            pltpu.VMEM(data.shape, F32),
            *scratch,
        ],
        compiler_params=params(20),
        cost_estimate=cost(weight.size * 8, weight.size * 2),
    )(data, in_hbm(weight), *map(in_hbm, tables))


def outer(modes, back, table, shape, alpha, start, count, prior=None):
    def kernel(*refs):
        outer_kernel(alpha, *refs[:3], refs[-1])

    per = shape[2] // QUAD
    width = 2 * SPAN
    group = lambda ref: pl.BlockSpec((1,) + ref.shape[1:], lambda q, piece: (q + start, 0, 0))
    given = () if prior is None else (prior,)
    return pl.pallas_call(
        kernel,
        grid=(count, shape[4] // width),
        in_specs=[
            group(modes),
            group(back),
            pl.BlockSpec((table.shape[0], width), lambda q, piece: (0, piece)),
        ]
        + [pl.BlockSpec(memory_space=pl.ANY)] * len(given),
        out_specs=pl.BlockSpec(
            (2, 1, QUAD, shape[3], width),
            lambda q, piece: (0, (q + start) // per, (q + start) % per, 0, piece),
        ),
        out_shape=jax.ShapeDtypeStruct(shape, F32),
        input_output_aliases={3: 0} if given else {},
        compiler_params=params(16),
        cost_estimate=cost(math.prod(shape) * 4, math.prod(shape) * 4),
    )(modes, back, in_hbm(table), *given)


def shift(block, axis, step):
    count = lax.axis_size(axis)
    pairs = [(i, i + step) for i in range(count) if 0 <= i + step < count]
    return lax.ppermute(block, axis, pairs)


def y_halos(turned):
    return shift(turned[:, -1], "gy", 1), shift(turned[:, 0], "gy", -1)


def x_halos(turned, ylo, yhi):
    edge = lambda x: jnp.concatenate([ylo[x][None], turned[x], yhi[x][None]], axis=0)
    return shift(edge(-1), "gx", 1), shift(edge(0), "gx", -1)


def conv(turned, rim, weight, flip):
    cx, cy, c, z = turned.shape
    return call(
        functools.partial(conv_kernel, flip),
        [((cx, c, cy * z), F32)],
        (turned, *map(in_hbm, rim), in_hbm(weight)),
        [pltpu.VMEM((4 * c, (cy + 2) * z), BF16)],
        mib=32,
        flops=2 * 27 * c * c * cx * cy * z,
        moved=turned.size * 8,
    )[0]


def weight_grad(grad, turned, rim):
    cx, cy, c, z = turned.shape
    return call(
        weight_grad_kernel,
        [((16 * c, 2 * c), F32)],
        (grad, turned, *map(in_hbm, rim)),
        [
            pltpu.VMEM((4 * c, (cy + 2) * z), BF16),
            pltpu.VMEM((cx * 3 * c, (cy + 2) * z), BF16),
            pltpu.VMEM((9 * c, 4 * c), F32),
        ],
        mib=32,
        flops=2 * 27 * c * c * cx * cy * z,
        moved=turned.size * 8,
    )[0]


def swap(block, axis):
    return lax.all_to_all(block, axis, split_axis=0, concat_axis=0, tiled=True)


def together(*values):
    return lax.optimization_barrier(values)


def body(state, cotangent, spectral_weight, stencil_weight, pointwise_weight):
    nx, ny = lax.axis_size("gx"), lax.axis_size("gy")
    c, cx, cy, z = state.shape
    _, mz, mx, _, _ = spectral_weight.shape
    wide_x, wide_y = cx * nx, cy * ny
    alpha = 1.0 / math.sqrt(wide_x * wide_y * z)
    beta = 1.0 / math.sqrt(2 * MX * MY * MZ)
    double = np.where(np.arange(MZ) == 0, 1.0, 2.0)
    ones = np.ones(MZ)
    z_state = jnp.asarray(z_forward_table(alpha * ones)(nx, mz))
    z_grad = jnp.asarray(z_forward_table(double)(nx, mz))
    z_spectral = jnp.asarray(z_inverse_table(nx, mz, beta * double))
    z_back = jnp.asarray(z_inverse_table(nx, mz, alpha * beta * ones))
    x_fwd, x_inv = (jnp.asarray(t) for t in x_tables(wide_x, mz, mx))
    y_fwd, y_inv = (jnp.asarray(t) for t in y_tables(wide_y))
    spread, gather = jnp.asarray(spread_table()), jnp.asarray(gather_table())
    lanes = cy * c
    x_rows = cx * 2 * mz

    def x_stage(table, block, lead, kind=F32, extra=0):
        rows = table.shape[0] // lead + extra
        return call(
            x_kernel,
            [((lead, rows, lanes), kind)],
            (table, block),
            mib=16,
            flops=2 * table.size * lanes,
            moved=8 * block.size,
        )[0]

    slab_shape = ((nx, x_rows, lanes), F32)
    turned_shape = ((cx, cy, c, z), BF16)

    conv_table, back_table = call(
        taps_kernel,
        [((9 * c, 4 * c), BF16)] * 2,
        (in_hbm(stencil_weight), in_hbm(pointwise_weight)),
        [pltpu.VMEM((27 * c, c), F32)],
        moved=stencil_weight.size * 6,
    )
    turned, slab = call(
        functools.partial(prep_kernel, nx),
        [turned_shape, slab_shape],
        (in_hbm(state), in_hbm(z_state)),
        flops=2 * 96 * state.size,
        moved=state.size * 5,
    )
    block = x_stage(x_fwd, swap(slab, "gx"), ny)
    block, conv_table, back_table, *faces = together(
        block, conv_table, back_table, *y_halos(turned)
    )
    modes_in, block = per_mode(
        mix_kernel,
        swap(block, "gy"),
        spectral_weight,
        (spread, y_fwd, y_inv),
        (2 * c, BF16),
        F32,
        [pltpu.VMEM((2 * QUAD * MY, SPAN), F32)] * 2 + [pltpu.VMEM((2 * QUAD * MY, 2 * c), F32)],
    )
    block, *edges = together(block, *x_halos(turned, *faces))
    rim = (*faces, *edges)
    block = x_stage(x_inv, swap(block, "gy"), nx)
    stencil = conv(turned, rim, conv_table, False)
    output, grad, slab = call(
        functools.partial(gelu_kernel, nx),
        [((c, cx, cy, z), BF16), turned_shape, slab_shape],
        (stencil, swap(block, "gx"), cotangent, z_spectral, z_grad),
        flops=2 * 192 * state.size,
        moved=state.size * 12,
    )

    grad_taps = weight_grad(grad, turned, rim)
    block = x_stage(x_fwd, swap(slab, "gx"), ny, BF16)
    grad, grad_taps = together(grad, grad_taps)
    faces = y_halos(grad)
    block, grad_taps = together(block, grad_taps)
    edges = x_halos(grad, *faces)
    block, grad_taps, *edges = together(swap(block, "gy"), grad_taps, *edges)
    mine = swap(grad_taps.reshape(nx, -1, 2 * c), "gx").sum(0)
    back_modes, block = per_mode(
        mix_back_kernel,
        block,
        spectral_weight,
        (gather, y_fwd, y_inv),
        (2 * c, F32),
        BF16,
        [pltpu.VMEM((2 * QUAD * MY, c * c), BF16)],
    )
    packed = jnp.concatenate(jnp.split(mine, lanes // (2 * c)), axis=1).astype(BF16)
    extra = packed.shape[0]
    packed = jnp.broadcast_to(packed[None], (ny, extra, lanes))
    block = x_stage(
        x_inv, swap(jnp.concatenate([block, packed], axis=1), "gy"), nx, BF16, extra
    )
    stencil_back = conv(grad, (*faces, *edges), back_table, True)
    shape = spectral_weight.shape
    groups = modes_in.shape[0]
    early = groups // 2
    grad_modes = None
    if early:
        grad_modes = outer(modes_in, back_modes, spread, shape, alpha, 0, early)
        block, stencil_back, grad_modes = together(block, stencil_back, grad_modes)
    message = swap(block, "gx")
    grad_modes = outer(
        modes_in, back_modes, spread, shape, alpha, early, groups - early, grad_modes
    )
    grad_state, grad_stencil, grad_point = call(
        functools.partial(finish_kernel, nx, alpha),
        [((c, cx, cy, z), F32), ((c, 27 * c), F32), ((c, c), F32)],
        (stencil_back, message, z_back),
        [pltpu.VMEM(grad_taps.shape, F32), pltpu.VMEM((27 * c, c), F32)],
        flops=2 * 96 * state.size,
        moved=state.size * 10,
    )
    return (output, grad_state, grad_modes, grad_stencil, grad_point)


def solution(mesh):
    in_specs = (
        P(None, "gx", "gy", None),
        P(None, "gx", "gy", None),
        P(None, "gx", "gy", None, None),
        P(),
        P(),
    )
    out_specs = (
        P(None, "gx", "gy", None),
        P(None, "gx", "gy", None),
        P(None, "gx", "gy", None, None),
        P(),
        P(),
    )
    return jax.shard_map(body, mesh=mesh, in_specs=in_specs, out_specs=out_specs, check_vma=False)
```

```python
import functools
import math

import jax
import jax.numpy as jnp
import numpy as np
from jax import lax
from jax.experimental import pallas as pl
from jax.experimental.pallas import tpu as pltpu
from jax.sharding import PartitionSpec as P

C = 64
MX = 32
MY = 32
MZ = 16
Z = 128
MIB = 1 << 20

F32 = jnp.float32
BF16 = jnp.bfloat16


def angles(places, freqs, length):
    turns = np.outer(np.asarray(places), np.asarray(freqs)) % length
    return turns * (2.0 * np.pi / length)


def centred(count):
    steps = np.arange(count)
    return np.where(steps < count // 2, steps, steps - count)


def split(table, parts):
    rest = np.asarray(table, np.float64)
    out = []
    for _ in range(parts):
        piece = rest.astype(jnp.bfloat16)
        out.append(piece)
        rest = rest - piece.astype(np.float64)
    return out


def z_forward_table(scale):
    def build(nx, mz):
        theta = angles(np.arange(MZ), np.arange(Z), Z)
        pair = np.stack([np.cos(theta), -np.sin(theta)]) * scale[None, :, None]
        rows = pair.reshape(2, nx, mz, Z).transpose(1, 0, 2, 3).reshape(2 * MZ, Z)
        return np.concatenate(split(rows, 3), axis=0)

    return build


def z_inverse_table(nx, mz, scale):
    theta = angles(np.arange(MZ), np.arange(Z), Z)
    pair = np.stack([np.cos(theta), -np.sin(theta)]) * scale[None, :, None]
    rows = pair.reshape(2, nx, mz, Z).transpose(1, 0, 2, 3).reshape(2 * MZ, Z)
    high, low = split(rows, 2)
    return np.concatenate([high, high, low], axis=0)


def rotation(theta, sign):
    cosine, sine = np.cos(theta), sign * np.sin(theta)
    return np.stack([np.stack([cosine, -sine], 1), np.stack([sine, cosine], 1)])


def against_pieces(*tables):
    out = []
    for table in tables:
        high, low = split(table, 2)
        out.append(np.concatenate([high, high, low], axis=1))
    return out


def x_tables(wide, mz, mx):
    theta = angles(centred(MX), np.arange(wide), wide)
    eye = np.eye(mz)
    forward = np.einsum("rkRx,zZ->krzxRZ", rotation(theta, -1.0), eye)
    inverse = np.einsum("rxRk,zZ->xrzkRZ", rotation(theta.T, 1.0), eye)
    size_k, size_x = MX * 2 * mz, wide * 2 * mz
    forward = forward.reshape(MX // mx, mx, 2, mz, size_x).transpose(0, 2, 3, 1, 4)
    inverse = inverse.reshape(size_x, MX // mx, mx, 2, mz).transpose(0, 1, 3, 4, 2)
    return against_pieces(forward.reshape(size_k, size_x), inverse.reshape(size_x, size_k))


def y_tables(wide):
    theta = angles(centred(MY), np.arange(wide), wide)
    forward = rotation(theta, -1.0).reshape(2 * MY, 2 * wide)
    inverse = rotation(theta.T, 1.0).reshape(2 * wide, 2 * MY)
    return against_pieces(forward, inverse)


def pieces(values):
    high = values.astype(BF16)
    low = (values - high.astype(F32)).astype(BF16)
    return jnp.concatenate([high, low, high], axis=0)


def z_forward(rows, table, out_ref, x, nx):
    got = lax.dot_general(table, rows, (((1,), (1,)), ((), ())), preferred_element_type=F32)
    size = 2 * MZ
    total = got[:size] + (got[size : 2 * size] + got[2 * size :])
    per = size // nx
    for owner in range(nx):
        out_ref[owner, x * per : (x + 1) * per, :] = total[owner * per : (owner + 1) * per]


def z_inverse(in_ref, table, x, nx):
    per = 2 * MZ // nx
    rows = jnp.concatenate(
        [in_ref[owner].astype(F32)[x * per : (x + 1) * per] for owner in range(nx)], axis=0
    )
    return lax.dot_general(
        pieces(rows), table, (((0,), (0,)), ((), ())), preferred_element_type=F32
    )


def prep_kernel(nx, field_ref, table_ref, turned_ref, slab_ref):
    c, cx, cy, z = field_ref.shape
    for x in range(cx):
        block = jnp.swapaxes(field_ref[:, x].astype(F32), 0, 1)
        turned = block.astype(BF16)
        turned_ref[x] = turned
        z_forward(turned.reshape(cy * c, z), table_ref[...], slab_ref, x, nx)


def plane_rows(p, cx, body_ref, xlo_ref, xhi_ref, ylo_ref, yhi_ref):
    cy = body_ref.shape[1]
    if p == 0:
        middle = [xlo_ref[y] for y in range(cy)]
    elif p == cx + 1:
        middle = [xhi_ref[y] for y in range(cy)]
    else:
        middle = [body_ref[p - 1, y] for y in range(cy)]
    return [ylo_ref[p]] + middle + [yhi_ref[p]]


def fill_shifts(blocks, rim_ref, flip=False):
    c, z = blocks[0].shape
    lane = lax.broadcasted_iota(jnp.int32, (c, z), 1)
    for y, block in enumerate(blocks):
        wide = block.astype(F32)
        before = jnp.where(lane == 0, 0.0, pltpu.roll(wide, 1, 1))
        after = jnp.where(lane == z - 1, 0.0, pltpu.roll(wide, z - 1, 1))
        if flip:
            before, after = after, before
        columns = slice(y * z, (y + 1) * z)
        rim_ref[0:c, columns] = before.astype(BF16)
        rim_ref[c : 2 * c, columns] = block
        rim_ref[2 * c : 3 * c, columns] = after.astype(BF16)
        rim_ref[3 * c : 4 * c, columns] = block


def conv_kernel(
    flip, body_ref, xlo_ref, xhi_ref, ylo_ref, yhi_ref, weight_ref, out_ref, rim_ref
):
    cx, cy, c, z = body_ref.shape
    for p in range(cx + 2):
        blocks = plane_rows(p, cx, body_ref, xlo_ref, xhi_ref, ylo_ref, yhi_ref)
        fill_shifts(blocks, rim_ref, flip)
        places = [a for a in range(3) if 0 <= p - (2 - a if flip else a) < cx]
        first = places[0]
        got = jnp.dot(
            weight_ref[first * 3 * c : (places[-1] + 1) * 3 * c, :],
            rim_ref[...],
            preferred_element_type=F32,
        )
        for a in places:
            x = p - (2 - a if flip else a)
            total = None
            for b in range(3):
                row = ((a - first) * 3 + b) * c
                skip = 2 - b if flip else b
                term = got[row : row + c, skip * z : (skip + cy) * z]
                total = term if total is None else total + term
            if p == x:
                out_ref[x] = total
            else:
                out_ref[x] += total


def weight_grad_kernel(
    grad_ref, body_ref, xlo_ref, xhi_ref, ylo_ref, yhi_ref, out_ref, rim_ref, wide_ref, sum_ref
):
    cx, cy, c, z = body_ref.shape
    group = 3 * c
    wide_ref[...] = jnp.zeros_like(wide_ref)
    for x in range(cx):
        for b in range(3):
            for y in range(cy):
                row = x * group + b * c
                wide_ref[row : row + c, (y + b) * z : (y + b + 1) * z] = grad_ref[x, y]
    sum_ref[...] = jnp.zeros_like(sum_ref)
    for p in range(cx + 2):
        fill_shifts(plane_rows(p, cx, body_ref, xlo_ref, xhi_ref, ylo_ref, yhi_ref), rim_ref)
        first, last = max(0, p - 2), min(cx - 1, p)
        got = lax.dot_general(
            wide_ref[first * group : (last + 1) * group, :],
            rim_ref[...],
            (((1,), (1,)), ((), ())),
            preferred_element_type=F32,
        )
        for x in range(first, last + 1):
            a = p - x
            sum_ref[a * group : (a + 1) * group, :] += got[
                (x - first) * group : (x - first + 1) * group, :
            ]
    out_ref[: 9 * c] = sum_ref[:, : 2 * c]
    last = [sum_ref[k * c : (k + 1) * c, 2 * c : 3 * c] for k in range(9)]
    last.append(jnp.zeros((c, c), F32))
    for k in range(5):
        row = (9 + k) * c
        out_ref[row : row + c] = jnp.concatenate(last[2 * k : 2 * k + 2], axis=1)
    out_ref[14 * c :] = jnp.zeros((2 * c, 2 * c), F32)


def gelu_kernel(
    nx, stencil_ref, slab_ref, cot_ref, inverse_ref, forward_ref, out_ref, turned_ref, back_ref
):
    c, cx, cy, z = cot_ref.shape
    root = math.sqrt(2.0 / math.pi)
    for x in range(cx):
        spectral = z_inverse(slab_ref, inverse_ref[...], x, nx).reshape(cy, c, z)
        stencil = jnp.stack([stencil_ref[x, :, y * z : (y + 1) * z] for y in range(cy)])
        pre = spectral + stencil
        cot = jnp.swapaxes(cot_ref[:, x].astype(F32), 0, 1)
        square = pre * pre
        bent = jnp.tanh(root * (pre * (1.0 + 0.044715 * square)))
        half = 0.5 + 0.5 * bent
        slope = half + (0.5 * pre) * (1.0 - bent * bent) * (root * (1.0 + 0.134145 * square))
        out_ref[:, x] = jnp.swapaxes(pre * half, 0, 1).astype(BF16)
        grad = (cot * slope).astype(BF16)
        turned_ref[x] = grad
        z_forward(grad.reshape(cy * c, z), forward_ref[...], back_ref, x, nx)


def finish_kernel(
    nx,
    scale,
    stencil_ref,
    message_ref,
    inverse_ref,
    out_ref,
    taps_ref,
    point_ref,
    packed_ref,
    turned_ref,
):
    c, cx, cy, z = out_ref.shape
    for x in range(cx):
        spectral = z_inverse(message_ref, inverse_ref[...], x, nx).reshape(cy, c, z)
        stencil = jnp.stack([stencil_ref[x, :, y * z : (y + 1) * z] for y in range(cy)])
        out_ref[:, x] = jnp.swapaxes(spectral + stencil, 0, 1)
    skip = 2 * MZ * cx // nx
    unpack(scale, skip, message_ref, taps_ref, point_ref, packed_ref, turned_ref)


def x_kernel(table_ref, data_ref, out_ref):
    data = data_ref[...].astype(F32)
    lanes = data.shape[2]
    rows = table_ref.shape[1] // (3 * data.shape[0])
    flat = pieces(data[:, :rows].reshape(-1, lanes))
    got = jnp.dot(table_ref[...], flat, preferred_element_type=F32).astype(out_ref.dtype)
    count = got.shape[0] // out_ref.shape[0]
    for owner in range(out_ref.shape[0]):
        out_ref[owner, :count] = got[owner * count : (owner + 1) * count]
    if data.shape[1] > rows:
        extra = data[:, rows:].sum(0)
        extra = extra.astype(out_ref.dtype)
        for owner in range(out_ref.shape[0]):
            out_ref[owner, count:] = extra


def taps_kernel(taps_ref, point_ref, forward_ref, back_ref, turned_ref):
    turned_ref[...] = taps_ref[...].astype(F32).T
    forward_ref[...] = jnp.zeros_like(forward_ref)
    back_ref[...] = jnp.zeros_like(back_ref)
    for tap in range(27):
        rows = slice(tap // 3 * C, (tap // 3 + 1) * C)
        columns = slice(tap % 3 * C, (tap % 3 + 1) * C)
        block = turned_ref[pl.ds(tap, C, stride=27), :]
        back_ref[rows, columns] = block.astype(BF16)
        forward_ref[rows, columns] = block.T.astype(BF16)
    point = point_ref[...].astype(F32)
    forward_ref[4 * C : 5 * C, 3 * C :] = point.astype(BF16)
    back_ref[4 * C : 5 * C, 3 * C :] = point.T.astype(BF16)


def unpack(scale, skip, message_ref, taps_ref, point_ref, packed_ref, turned_ref):
    devices, rows, lanes = message_ref.shape
    per, tiles_in = rows - skip, lanes // 128
    for owner in range(devices):
        message = message_ref[owner].astype(F32)
        for tile in range(tiles_in):
            row = (owner * tiles_in + tile) * per
            packed_ref[row : row + per] = message[skip:, tile * 128 : (tile + 1) * 128]
    for tap in range(27):
        group, e = tap // 3, tap % 3
        if e < 2:
            block = packed_ref[group * C : (group + 1) * C, e * C : (e + 1) * C]
        else:
            row = (9 + group // 2) * C
            block = packed_ref[row : row + C, group % 2 * C : (group % 2 + 1) * C]
        block = block * scale
        if tap == 13:
            point_ref[...] = block
        turned_ref[pl.ds(tap, C, stride=27), :] = block.T
    taps_ref[...] = turned_ref[...].T


QUAD = 4
SPAN = 8 * C


def y_forward(mz, data_ref, table_ref, rows_ref, store):
    ny, _, lanes = data_ref.shape
    cy = lanes // C
    count = rows_ref.shape[1] // C
    for owner in range(ny):
        data = data_ref[owner].astype(F32)
        for part in range(2):
            for kz in range(mz):
                mx = count // mz
                start = (part * mz + kz) * mx
                block = data[start : start + mx]
                block = jnp.stack([block[:, y * C : (y + 1) * C] for y in range(cy)])
                block = jnp.swapaxes(block, 0, 1)
                row = (part * ny + owner) * cy
                for kx in range(mx):
                    column = (kz * mx + kx) * C
                    rows_ref[row : row + cy, column : column + C] = block[kx]
    got = jnp.dot(table_ref[...], pieces(rows_ref[...]), preferred_element_type=F32)
    for q in range(count):
        block = got[:, q * C : (q + 1) * C]
        for part in range(2):
            store(q // QUAD, part, q % QUAD, block[part * MY : (part + 1) * MY])


def y_inverse(mz, sum_ref, table_ref, out_ref, block_ref):
    rows = [
        jnp.concatenate(
            [
                sum_ref[group, place(part, pair), :]
                for group in range(sum_ref.shape[0])
                for pair in range(QUAD)
            ],
            axis=1,
        )
        for part in range(2)
    ]
    got = jnp.dot(
        table_ref[...], pieces(jnp.concatenate(rows, axis=0)), preferred_element_type=F32
    )
    ny, _, lanes = out_ref.shape
    cy = lanes // C
    count = got.shape[1] // C
    mx = count // mz
    for owner in range(ny):
        for part in range(2):
            for kz in range(mz):
                row = (part * ny + owner) * cy
                block = got[row : row + cy, kz * mx * C : (kz + 1) * mx * C]
                block = jnp.stack([block[:, kx * C : (kx + 1) * C] for kx in range(mx)])
                block = jnp.swapaxes(block, 0, 1)
                start = (part * mz + kz) * mx
                for y in range(cy):
                    block_ref[owner, start : start + mx, y * C : (y + 1) * C] = block[y]
    out_ref[...] = block_ref[...].astype(out_ref.dtype)


def place(part, pair):
    start = (part * QUAD + pair) * MY
    return slice(start, start + MY)


def spread_table():
    return np.tile(np.kron(np.eye(C), np.ones((1, C))), (2, 1)).astype(jnp.bfloat16)


def gather_table():
    return np.kron(np.eye(SPAN // C), np.ones((1, C))).astype(jnp.bfloat16)


def spread_modes(modes, table_ref, spread_refs):
    count = C * C // SPAN
    made = set()

    def get(piece):
        for p in range(piece, min(piece + 2, count)):
            if p not in made:
                made.add(p)
                spread_refs[p % 2][...] = jnp.dot(
                    modes, table_ref[:, p * SPAN : (p + 1) * SPAN], preferred_element_type=F32
                )
        return spread_refs[piece % 2]

    return get


def weight_copies(weight_ref, held_ref, sem_ref):
    per = weight_ref.shape[2] // QUAD
    return [
        pltpu.make_async_copy(
            weight_ref.at[:, g // per, g % per * QUAD : (g % per + 1) * QUAD],
            held_ref.at[g],
            sem_ref.at[g],
        )
        for g in range(held_ref.shape[0])
    ]


def mix_kernel(
    mz,
    data_ref,
    weight_ref,
    table_ref,
    forward_ref,
    inverse_ref,
    modes_ref,
    out_ref,
    sum_ref,
    rows_ref,
    block_ref,
    held_ref,
    sem_ref,
    spread_ref,
    spread_sem_ref,
    even_ref,
    odd_ref,
    total_ref,
):
    copies = weight_copies(weight_ref, held_ref, sem_ref)
    table_copy = pltpu.make_async_copy(table_ref, spread_ref, spread_sem_ref)
    table_copy.start()
    for copy in copies:
        copy.start()

    def store(group, part, pair, values):
        high = values.astype(BF16)
        low = (values - high.astype(F32)).astype(BF16)
        modes_ref[group, place(part, pair), :] = jnp.concatenate([high, low], axis=1)

    y_forward(mz, data_ref, forward_ref, rows_ref, store)
    table_copy.wait()
    for group, copy in enumerate(copies):
        copy.wait()
        spread = spread_modes(modes_ref[group], spread_ref, (even_ref, odd_ref))
        for piece in range(C * C // SPAN):
            modes = spread(piece)
            for pair in range(QUAD):
                real = imag = None
                for tile in range(SPAN // (2 * C)):
                    inside = slice(tile * 2 * C, (tile + 1) * 2 * C)
                    columns = slice(piece * SPAN + inside.start, piece * SPAN + inside.stop)
                    mode_re = modes[place(0, pair), inside]
                    mode_im = modes[place(1, pair), inside]
                    weight_re = held_ref[group, 0, pair, :, columns].astype(F32)
                    weight_im = held_ref[group, 1, pair, :, columns].astype(F32)
                    term_re = mode_re * weight_re - mode_im * weight_im
                    term_im = mode_re * weight_im + mode_im * weight_re
                    real = term_re if real is None else real + term_re
                    imag = term_im if imag is None else imag + term_im
                if piece:
                    real += total_ref[place(0, pair), :]
                    imag += total_ref[place(1, pair), :]
                total_ref[place(0, pair), :] = real
                total_ref[place(1, pair), :] = imag
        total = total_ref[...]
        sum_ref[group] = total[:, :C] + total[:, C:]
    y_inverse(mz, sum_ref, inverse_ref, out_ref, block_ref)


def mix_back_kernel(
    mz,
    data_ref,
    weight_ref,
    table_ref,
    forward_ref,
    inverse_ref,
    modes_ref,
    out_ref,
    sum_ref,
    rows_ref,
    block_ref,
    held_ref,
    sem_ref,
    term_ref,
):
    copies = weight_copies(weight_ref, held_ref, sem_ref)
    for copy in copies:
        copy.start()

    def store(group, part, pair, values):
        modes_ref[group, place(part, pair), :] = jnp.concatenate([values, values], axis=1)

    y_forward(mz, data_ref, forward_ref, rows_ref, store)
    for group, copy in enumerate(copies):
        copy.wait()
        total = []
        for piece in range(C * C // SPAN):
            for pair in range(QUAD):
                mode_re = modes_ref[group, place(0, pair), :]
                mode_im = modes_ref[group, place(1, pair), :]
                for tile in range(SPAN // (2 * C)):
                    start = piece * SPAN + tile * 2 * C
                    columns = slice(start, start + 2 * C)
                    weight_re = held_ref[group, 0, pair, :, columns].astype(F32)
                    weight_im = held_ref[group, 1, pair, :, columns].astype(F32)
                    term_ref[place(0, pair), columns] = (
                        weight_re * mode_re + weight_im * mode_im
                    ).astype(BF16)
                    term_ref[place(1, pair), columns] = (
                        weight_re * mode_im - weight_im * mode_re
                    ).astype(BF16)
            total.append(
                lax.dot_general(
                    table_ref[...],
                    term_ref[:, piece * SPAN : (piece + 1) * SPAN],
                    (((1,), (1,)), ((), ())),
                    preferred_element_type=F32,
                )
            )
        sum_ref[group] = jnp.concatenate(total, axis=0).T
    y_inverse(mz, sum_ref, inverse_ref, out_ref, block_ref)


def outer_kernel(alpha, modes_ref, back_ref, table_ref, out_ref):
    count = C * C // SPAN
    made = lambda piece: jnp.dot(
        modes_ref[0],
        table_ref[:, piece * SPAN : (piece + 1) * SPAN],
        preferred_element_type=F32,
    )
    ahead = made(0)
    for piece in range(count):
        modes = ahead
        if piece + 1 < count:
            ahead = made(piece + 1)
        for pair in range(QUAD):
            back_re = back_ref[0, place(0, pair), :] * alpha
            back_im = back_ref[0, place(1, pair), :] * alpha
            for tile in range(SPAN // (2 * C)):
                inside = slice(tile * 2 * C, (tile + 1) * 2 * C)
                columns = slice(piece * SPAN + inside.start, piece * SPAN + inside.stop)
                mode_re = modes[place(0, pair), inside]
                mode_im = modes[place(1, pair), inside]
                out_ref[0, 0, pair, :, columns] = mode_re * back_re + mode_im * back_im
                out_ref[1, 0, pair, :, columns] = mode_re * back_im - mode_im * back_re


def in_hbm(value):
    return pltpu.with_memory_space_constraint(value, pltpu.HBM)


def whole():
    return pl.BlockSpec(memory_space=pltpu.VMEM)


def params(mib):
    return pltpu.CompilerParams(vmem_limit_bytes=mib * MIB)


def cost(flops, moved):
    return pl.CostEstimate(flops=int(flops), bytes_accessed=int(moved), transcendentals=0)


def call(kernel, outs, args, scratch=(), mib=24, flops=0, moved=0):
    return pl.pallas_call(
        kernel,
        out_shape=[jax.ShapeDtypeStruct(*out) for out in outs],
        in_specs=[whole() for _ in args],
        out_specs=[whole() for _ in outs],
        scratch_shapes=list(scratch),
        compiler_params=params(mib),
        cost_estimate=cost(flops, moved),
    )(*args)


def per_mode(kernel, data, weight, table, tables, modes, kind, scratch=()):
    _, mz, mx, my, wide = weight.shape
    groups = mz * mx // QUAD
    rows = 2 * QUAD * MY
    modes_shape = (groups, rows, modes[0])
    return pl.pallas_call(
        functools.partial(kernel, mz),
        in_specs=[
            whole(),
            pl.BlockSpec(memory_space=pl.ANY),
            pl.BlockSpec(memory_space=pl.ANY) if table.size > weight.size // 16 else whole(),
            whole(),
            whole(),
        ],
        out_specs=[whole(), whole()],
        out_shape=[
            jax.ShapeDtypeStruct(modes_shape, modes[1]),
            jax.ShapeDtypeStruct(data.shape, kind),
        ],
        scratch_shapes=[
            pltpu.VMEM((groups, rows, C), F32),
            pltpu.VMEM((tables[-1].shape[0], mz * mx * C), F32),
            pltpu.VMEM(data.shape, F32),
            pltpu.VMEM((groups, 2, QUAD, my, wide), BF16),
            pltpu.SemaphoreType.DMA((groups,)),
            *scratch,
        ],
        compiler_params=params(24),
        cost_estimate=cost(weight.size * 8, weight.size * 2),
    )(data, in_hbm(weight), in_hbm(table), *tables)


def outer(modes, back, table, shape, alpha):
    per = shape[2] // QUAD
    group = lambda ref: pl.BlockSpec((1,) + ref.shape[1:], lambda step: (step, 0, 0))
    return pl.pallas_call(
        functools.partial(outer_kernel, alpha),
        grid=(modes.shape[0],),
        in_specs=[group(modes), group(back), pl.BlockSpec(table.shape, lambda step: (0, 0))],
        out_specs=pl.BlockSpec(
            (2, 1, QUAD) + shape[3:], lambda step: (0, step // per, step % per, 0, 0)
        ),
        out_shape=jax.ShapeDtypeStruct(shape, F32),
        compiler_params=params(20),
        cost_estimate=cost(math.prod(shape) * 4, math.prod(shape) * 4),
    )(modes, back, in_hbm(table))


def shift(block, axis, step):
    count = lax.axis_size(axis)
    pairs = [(i, i + step) for i in range(count) if 0 <= i + step < count]
    return lax.ppermute(block, axis, pairs)


def x_halos(turned):
    return shift(turned[-1], "gx", 1), shift(turned[0], "gx", -1)


def y_halos(turned, xlo, xhi):
    edge = lambda y: jnp.concatenate([xlo[None, y], turned[:, y], xhi[None, y]], axis=0)
    return shift(edge(-1), "gy", 1), shift(edge(0), "gy", -1)


def conv(turned, rim, weight, flip):
    cx, cy, c, z = turned.shape
    return call(
        functools.partial(conv_kernel, flip),
        [((cx, c, cy * z), F32)],
        (turned, *map(in_hbm, rim), in_hbm(weight)),
        [pltpu.VMEM((4 * c, (cy + 2) * z), BF16)],
        mib=32,
        flops=2 * 27 * c * c * cx * cy * z,
        moved=turned.size * 8,
    )[0]


def weight_grad(grad, turned, rim):
    cx, cy, c, z = turned.shape
    return call(
        weight_grad_kernel,
        [((16 * c, 2 * c), F32)],
        (grad, turned, *map(in_hbm, rim)),
        [
            pltpu.VMEM((4 * c, (cy + 2) * z), BF16),
            pltpu.VMEM((cx * 3 * c, (cy + 2) * z), BF16),
            pltpu.VMEM((9 * c, 4 * c), F32),
        ],
        mib=32,
        flops=2 * 27 * c * c * cx * cy * z,
        moved=turned.size * 8,
    )[0]


def swap(block, axis):
    return lax.all_to_all(block, axis, split_axis=0, concat_axis=0, tiled=True)


def together(*values):
    return lax.optimization_barrier(values)


def body(state, cotangent, spectral_weight, stencil_weight, pointwise_weight):
    nx, ny = lax.axis_size("gx"), lax.axis_size("gy")
    c, cx, cy, z = state.shape
    _, mz, mx, _, _ = spectral_weight.shape
    wide_x, wide_y = cx * nx, cy * ny
    alpha = 1.0 / math.sqrt(wide_x * wide_y * z)
    beta = 1.0 / math.sqrt(2 * MX * MY * MZ)
    double = np.where(np.arange(MZ) == 0, 1.0, 2.0)
    ones = np.ones(MZ)
    z_state = jnp.asarray(z_forward_table(alpha * ones)(nx, mz))
    z_grad = jnp.asarray(z_forward_table(double)(nx, mz))
    z_spectral = jnp.asarray(z_inverse_table(nx, mz, beta * double))
    z_back = jnp.asarray(z_inverse_table(nx, mz, alpha * beta * ones))
    x_fwd, x_inv = (jnp.asarray(t) for t in x_tables(wide_x, mz, mx))
    y_fwd, y_inv = (jnp.asarray(t) for t in y_tables(wide_y))
    spread, gather = jnp.asarray(spread_table()), jnp.asarray(gather_table())
    lanes = cy * c
    x_rows = cx * 2 * mz

    def x_stage(table, block, lead, kind=F32, extra=0):
        rows = table.shape[0] // lead + extra
        return call(
            x_kernel,
            [((lead, rows, lanes), kind)],
            (table, block),
            mib=16,
            flops=2 * table.size * lanes,
            moved=8 * block.size,
        )[0]

    slab_shape = ((nx, x_rows, lanes), F32)
    turned_shape = ((cx, cy, c, z), BF16)

    conv_table, back_table = call(
        taps_kernel,
        [((9 * c, 4 * c), BF16)] * 2,
        (in_hbm(stencil_weight), in_hbm(pointwise_weight)),
        [pltpu.VMEM((27 * c, c), F32)],
        moved=stencil_weight.size * 6,
    )
    turned, slab = call(
        functools.partial(prep_kernel, nx),
        [turned_shape, slab_shape],
        (in_hbm(state), in_hbm(z_state)),
        flops=2 * 96 * state.size,
        moved=state.size * 5,
    )
    block = x_stage(x_fwd, swap(slab, "gx"), ny)
    block, conv_table, back_table, *faces = together(
        block, conv_table, back_table, *x_halos(turned)
    )
    modes_in, block = per_mode(
        mix_kernel,
        swap(block, "gy"),
        spectral_weight,
        spread,
        (y_fwd, y_inv),
        (2 * c, BF16),
        F32,
        [pltpu.VMEM(spread.shape, BF16), pltpu.SemaphoreType.DMA]
        + [pltpu.VMEM((2 * QUAD * MY, SPAN), F32)] * 2
        + [pltpu.VMEM((2 * QUAD * MY, 2 * c), F32)],
    )
    block, *edges = together(block, *y_halos(turned, *faces))
    rim = (*faces, *edges)
    block = x_stage(x_inv, swap(block, "gy"), nx)
    stencil = conv(turned, rim, conv_table, False)
    output, grad, slab = call(
        functools.partial(gelu_kernel, nx),
        [((c, cx, cy, z), BF16), turned_shape, slab_shape],
        (stencil, swap(block, "gx"), cotangent, z_spectral, z_grad),
        flops=2 * 192 * state.size,
        moved=state.size * 12,
    )

    grad_taps = weight_grad(grad, turned, rim)
    block = x_stage(x_fwd, swap(slab, "gx"), ny, BF16)
    block, grad_taps, *faces = together(block, grad_taps, *x_halos(grad))
    edges = y_halos(grad, *faces)
    block, grad_taps, *edges = together(swap(block, "gy"), grad_taps, *edges)
    mine = swap(grad_taps.reshape(nx, -1, 2 * c), "gx").sum(0)
    back_modes, block = per_mode(
        mix_back_kernel,
        block,
        spectral_weight,
        gather,
        (y_fwd, y_inv),
        (2 * c, F32),
        BF16,
        [pltpu.VMEM((2 * QUAD * MY, c * c), BF16)],
    )
    packed = jnp.concatenate(jnp.split(mine, lanes // (2 * c)), axis=1).astype(BF16)
    extra = packed.shape[0]
    packed = jnp.broadcast_to(packed[None], (ny, extra, lanes))
    block = x_stage(
        x_inv, swap(jnp.concatenate([block, packed], axis=1), "gy"), nx, BF16, extra
    )
    stencil_back = conv(grad, (*faces, *edges), back_table, True)
    block, stencil_back = together(block, stencil_back)
    message = swap(block, "gx")
    grad_modes = outer(modes_in, back_modes, spread, spectral_weight.shape, alpha)
    grad_state, grad_stencil, grad_point = call(
        functools.partial(finish_kernel, nx, alpha),
        [((c, cx, cy, z), F32), ((c, 27 * c), F32), ((c, c), F32)],
        (stencil_back, message, z_back),
        [pltpu.VMEM(grad_taps.shape, F32), pltpu.VMEM((27 * c, c), F32)],
        flops=2 * 96 * state.size,
        moved=state.size * 10,
    )
    return (output, grad_state, grad_modes, grad_stencil, grad_point)


def solution(mesh):
    in_specs = (
        P(None, "gx", "gy", None),
        P(None, "gx", "gy", None),
        P(None, "gx", "gy", None, None),
        P(),
        P(),
    )
    out_specs = (
        P(None, "gx", "gy", None),
        P(None, "gx", "gy", None),
        P(None, "gx", "gy", None, None),
        P(),
        P(),
    )
    return jax.shard_map(body, mesh=mesh, in_specs=in_specs, out_specs=out_specs, check_vma=False)
```

```python
import functools
import math

import jax
import jax.numpy as jnp
import numpy as np
from jax import lax
from jax.experimental import pallas as pl
from jax.experimental.pallas import tpu as pltpu
from jax.sharding import PartitionSpec as P

C = 64
MX = 32
MY = 32
MZ = 16
Z = 128
MIB = 1 << 20

F32 = jnp.float32
BF16 = jnp.bfloat16


def angles(places, freqs, length):
    turns = np.outer(np.asarray(places), np.asarray(freqs)) % length
    return turns * (2.0 * np.pi / length)


def centred(count):
    steps = np.arange(count)
    return np.where(steps < count // 2, steps, steps - count)


def split(table, parts):
    rest = np.asarray(table, np.float64)
    out = []
    for _ in range(parts):
        piece = rest.astype(jnp.bfloat16)
        out.append(piece)
        rest = rest - piece.astype(np.float64)
    return out


def z_forward_table(scale):
    def build(nx, mz):
        theta = angles(np.arange(MZ), np.arange(Z), Z)
        pair = np.stack([np.cos(theta), -np.sin(theta)]) * scale[None, :, None]
        rows = pair.reshape(2, nx, mz, Z).transpose(1, 0, 2, 3).reshape(2 * MZ, Z)
        return np.concatenate(split(rows, 3), axis=0)

    return build


def z_inverse_table(nx, mz, scale):
    theta = angles(np.arange(MZ), np.arange(Z), Z)
    pair = np.stack([np.cos(theta), -np.sin(theta)]) * scale[None, :, None]
    rows = pair.reshape(2, nx, mz, Z).transpose(1, 0, 2, 3).reshape(2 * MZ, Z)
    high, low = split(rows, 2)
    return np.concatenate([high, high, low], axis=0)


def rotation(theta, sign):
    cosine, sine = np.cos(theta), sign * np.sin(theta)
    return np.stack([np.stack([cosine, -sine], 1), np.stack([sine, cosine], 1)])


def against_pieces(*tables):
    out = []
    for table in tables:
        high, low = split(table, 2)
        out.append(np.concatenate([high, high, low], axis=1))
    return out


def x_tables(wide, mz, mx):
    theta = angles(centred(MX), np.arange(wide), wide)
    eye = np.eye(mz)
    forward = np.einsum("rkRx,zZ->krzxRZ", rotation(theta, -1.0), eye)
    inverse = np.einsum("rxRk,zZ->xrzkRZ", rotation(theta.T, 1.0), eye)
    size_k, size_x = MX * 2 * mz, wide * 2 * mz
    forward = forward.reshape(MX // mx, mx, 2, mz, size_x).transpose(0, 2, 3, 1, 4)
    inverse = inverse.reshape(size_x, MX // mx, mx, 2, mz).transpose(0, 1, 3, 4, 2)
    return against_pieces(forward.reshape(size_k, size_x), inverse.reshape(size_x, size_k))


def y_table(wide):
    theta = angles(centred(MY), np.arange(wide), wide)
    forward = rotation(theta, -1.0).reshape(2 * MY, 2 * wide)
    inverse = rotation(theta.T, 1.0).reshape(2 * wide, 2 * MY)
    forward, inverse = against_pieces(forward, inverse)
    inverse = np.pad(inverse, ((0, 0), (0, forward.shape[1] - inverse.shape[1])))
    return np.concatenate([forward, inverse], axis=0)


def pieces(values):
    high = values.astype(BF16)
    low = (values - high.astype(F32)).astype(BF16)
    return jnp.concatenate([high, low, high], axis=0)


def z_forward(rows, table, out_ref, x, nx):
    got = lax.dot_general(table, rows, (((1,), (1,)), ((), ())), preferred_element_type=F32)
    size = 2 * MZ
    total = got[:size] + (got[size : 2 * size] + got[2 * size :])
    per = size // nx
    for owner in range(nx):
        out_ref[owner, x * per : (x + 1) * per, :] = total[owner * per : (owner + 1) * per]


def z_inverse(in_ref, table, x, nx):
    per = 2 * MZ // nx
    rows = jnp.concatenate(
        [in_ref[owner].astype(F32)[x * per : (x + 1) * per] for owner in range(nx)], axis=0
    )
    return lax.dot_general(
        pieces(rows), table, (((0,), (0,)), ((), ())), preferred_element_type=F32
    )


def prep_kernel(nx, field_ref, table_ref, turned_ref, slab_ref):
    c, cx, cy, z = field_ref.shape
    for x in range(cx):
        block = jnp.swapaxes(field_ref[:, x].astype(F32), 0, 1)
        turned = block.astype(BF16)
        turned_ref[x] = turned
        z_forward(turned.reshape(cy * c, z), table_ref[...], slab_ref, x, nx)


def plane_rows(p, cx, body_ref, xlo_ref, xhi_ref, ylo_ref, yhi_ref):
    cy = body_ref.shape[1]
    if p == 0:
        middle = [xlo_ref[y] for y in range(cy)]
    elif p == cx + 1:
        middle = [xhi_ref[y] for y in range(cy)]
    else:
        middle = [body_ref[p - 1, y] for y in range(cy)]
    return [ylo_ref[p]] + middle + [yhi_ref[p]]


def fill_shifts(blocks, rim_ref, flip=False):
    c, z = blocks[0].shape
    lane = lax.broadcasted_iota(jnp.int32, (c, z), 1)
    for y, block in enumerate(blocks):
        wide = block.astype(F32)
        before = jnp.where(lane == 0, 0.0, pltpu.roll(wide, 1, 1))
        after = jnp.where(lane == z - 1, 0.0, pltpu.roll(wide, z - 1, 1))
        if flip:
            before, after = after, before
        columns = slice(y * z, (y + 1) * z)
        rim_ref[0:c, columns] = before.astype(BF16)
        rim_ref[c : 2 * c, columns] = block
        rim_ref[2 * c : 3 * c, columns] = after.astype(BF16)
        rim_ref[3 * c : 4 * c, columns] = block


def conv_kernel(
    flip, body_ref, xlo_ref, xhi_ref, ylo_ref, yhi_ref, weight_ref, out_ref, rim_ref
):
    cx, cy, c, z = body_ref.shape
    for p in range(cx + 2):
        blocks = plane_rows(p, cx, body_ref, xlo_ref, xhi_ref, ylo_ref, yhi_ref)
        fill_shifts(blocks, rim_ref, flip)
        places = [a for a in range(3) if 0 <= p - (2 - a if flip else a) < cx]
        first = places[0]
        got = jnp.dot(
            weight_ref[first * 3 * c : (places[-1] + 1) * 3 * c, :],
            rim_ref[...],
            preferred_element_type=F32,
        )
        for a in places:
            x = p - (2 - a if flip else a)
            total = None
            for b in range(3):
                row = ((a - first) * 3 + b) * c
                skip = 2 - b if flip else b
                term = got[row : row + c, skip * z : (skip + cy) * z]
                total = term if total is None else total + term
            if p == x:
                out_ref[x] = total
            else:
                out_ref[x] += total


def weight_grad_kernel(
    grad_ref,
    body_ref,
    xlo_any,
    xhi_any,
    ylo_any,
    yhi_any,
    out_ref,
    rim_ref,
    wide_ref,
    sum_ref,
    xlo_ref,
    xhi_ref,
    ylo_ref,
    yhi_ref,
    sem_ref,
):
    cx, cy, c, z = body_ref.shape
    group = 3 * c
    held = (xlo_ref, xhi_ref, ylo_ref, yhi_ref)
    copies = [
        pltpu.make_async_copy(given, ref, sem_ref.at[i])
        for i, (given, ref) in enumerate(zip((xlo_any, xhi_any, ylo_any, yhi_any), held))
    ]
    for copy in copies:
        copy.start()
    wide_ref[...] = jnp.zeros_like(wide_ref)
    for x in range(cx):
        for b in range(3):
            for y in range(cy):
                row = x * group + b * c
                wide_ref[row : row + c, (y + b) * z : (y + b + 1) * z] = grad_ref[x, y]
    sum_ref[...] = jnp.zeros_like(sum_ref)
    for copy in copies:
        copy.wait()
    for p in range(cx + 2):
        fill_shifts(plane_rows(p, cx, body_ref, xlo_ref, xhi_ref, ylo_ref, yhi_ref), rim_ref)
        first, last = max(0, p - 2), min(cx - 1, p)
        got = lax.dot_general(
            wide_ref[first * group : (last + 1) * group, :],
            rim_ref[...],
            (((1,), (1,)), ((), ())),
            preferred_element_type=F32,
        )
        for x in range(first, last + 1):
            a = p - x
            sum_ref[a * group : (a + 1) * group, :] += got[
                (x - first) * group : (x - first + 1) * group, :
            ]
    out_ref[: 9 * c] = sum_ref[:, : 2 * c]
    last = [sum_ref[k * c : (k + 1) * c, 2 * c : 3 * c] for k in range(9)]
    last.append(jnp.zeros((c, c), F32))
    for k in range(5):
        row = (9 + k) * c
        out_ref[row : row + c] = jnp.concatenate(last[2 * k : 2 * k + 2], axis=1)
    out_ref[14 * c :] = jnp.zeros((2 * c, 2 * c), F32)


def gelu_kernel(
    nx, stencil_ref, slab_ref, cot_ref, inverse_ref, forward_ref, out_ref, turned_ref, back_ref
):
    c, cx, cy, z = cot_ref.shape
    root = math.sqrt(2.0 / math.pi)
    for x in range(cx):
        spectral = z_inverse(slab_ref, inverse_ref[...], x, nx).reshape(cy, c, z)
        stencil = jnp.stack([stencil_ref[x, :, y * z : (y + 1) * z] for y in range(cy)])
        pre = spectral + stencil
        cot = jnp.swapaxes(cot_ref[:, x].astype(F32), 0, 1)
        square = pre * pre
        bent = jnp.tanh(root * (pre * (1.0 + 0.044715 * square)))
        half = 0.5 + 0.5 * bent
        slope = half + (0.5 * pre) * (1.0 - bent * bent) * (root * (1.0 + 0.134145 * square))
        out_ref[:, x] = jnp.swapaxes(pre * half, 0, 1).astype(BF16)
        grad = (cot * slope).astype(BF16)
        turned_ref[x] = grad
        z_forward(grad.reshape(cy * c, z), forward_ref[...], back_ref, x, nx)


def finish_kernel(
    nx,
    scale,
    stencil_ref,
    message_ref,
    inverse_ref,
    out_ref,
    taps_ref,
    point_ref,
    packed_ref,
    turned_ref,
):
    c, cx, cy, z = out_ref.shape
    for x in range(cx):
        spectral = z_inverse(message_ref, inverse_ref[...], x, nx).reshape(cy, c, z)
        stencil = jnp.stack([stencil_ref[x, :, y * z : (y + 1) * z] for y in range(cy)])
        out_ref[:, x] = jnp.swapaxes(spectral + stencil, 0, 1)
    skip = 2 * MZ * cx // nx
    unpack(scale, skip, message_ref, taps_ref, point_ref, packed_ref, turned_ref)


def x_kernel(table_ref, data_ref, out_ref):
    data = data_ref[...].astype(F32)
    lanes = data.shape[2]
    rows = table_ref.shape[1] // (3 * data.shape[0])
    flat = pieces(data[:, :rows].reshape(-1, lanes))
    got = jnp.dot(table_ref[...], flat, preferred_element_type=F32).astype(out_ref.dtype)
    count = got.shape[0] // out_ref.shape[0]
    for owner in range(out_ref.shape[0]):
        out_ref[owner, :count] = got[owner * count : (owner + 1) * count]
    if data.shape[1] > rows:
        extra = data[:, rows:].sum(0)
        extra = extra.astype(out_ref.dtype)
        for owner in range(out_ref.shape[0]):
            out_ref[owner, count:] = extra


def taps_kernel(taps_ref, point_ref, forward_ref, back_ref, turned_ref):
    turned_ref[...] = taps_ref[...].astype(F32).T
    forward_ref[...] = jnp.zeros_like(forward_ref)
    back_ref[...] = jnp.zeros_like(back_ref)
    for tap in range(27):
        rows = slice(tap // 3 * C, (tap // 3 + 1) * C)
        columns = slice(tap % 3 * C, (tap % 3 + 1) * C)
        block = turned_ref[pl.ds(tap, C, stride=27), :]
        back_ref[rows, columns] = block.astype(BF16)
        forward_ref[rows, columns] = block.T.astype(BF16)
    point = point_ref[...].astype(F32)
    forward_ref[4 * C : 5 * C, 3 * C :] = point.astype(BF16)
    back_ref[4 * C : 5 * C, 3 * C :] = point.T.astype(BF16)


def unpack(scale, skip, message_ref, taps_ref, point_ref, packed_ref, turned_ref):
    devices, rows, lanes = message_ref.shape
    per, tiles_in = rows - skip, lanes // 128
    for owner in range(devices):
        message = message_ref[owner].astype(F32)
        for tile in range(tiles_in):
            row = (owner * tiles_in + tile) * per
            packed_ref[row : row + per] = message[skip:, tile * 128 : (tile + 1) * 128]
    for tap in range(27):
        group, e = tap // 3, tap % 3
        if e < 2:
            block = packed_ref[group * C : (group + 1) * C, e * C : (e + 1) * C]
        else:
            row = (9 + group // 2) * C
            block = packed_ref[row : row + C, group % 2 * C : (group % 2 + 1) * C]
        block = block * scale
        if tap == 13:
            point_ref[...] = block
        turned_ref[pl.ds(tap, C, stride=27), :] = block.T
    taps_ref[...] = turned_ref[...].T


QUAD = 4
SPAN = 8 * C


def y_forward(mz, data_ref, table_ref, rows_ref, store):
    ny, _, lanes = data_ref.shape
    cy = lanes // C
    count = rows_ref.shape[1] // C
    for owner in range(ny):
        data = data_ref[owner].astype(F32)
        for part in range(2):
            for kz in range(mz):
                mx = count // mz
                start = (part * mz + kz) * mx
                block = data[start : start + mx]
                block = jnp.stack([block[:, y * C : (y + 1) * C] for y in range(cy)])
                block = jnp.swapaxes(block, 0, 1)
                row = (part * ny + owner) * cy
                for kx in range(mx):
                    column = (kz * mx + kx) * C
                    rows_ref[row : row + cy, column : column + C] = block[kx]
    got = jnp.dot(table_ref[: 2 * MY], pieces(rows_ref[...]), preferred_element_type=F32)
    for q in range(count):
        block = got[:, q * C : (q + 1) * C]
        for part in range(2):
            store(q // QUAD, part, q % QUAD, block[part * MY : (part + 1) * MY])


def y_inverse(mz, sum_ref, table_ref, out_ref, block_ref):
    rows = [
        jnp.concatenate(
            [
                sum_ref[group, place(part, pair), :]
                for group in range(sum_ref.shape[0])
                for pair in range(QUAD)
            ],
            axis=1,
        )
        for part in range(2)
    ]
    got = jnp.dot(
        table_ref[2 * MY :, : 6 * MY],
        pieces(jnp.concatenate(rows, axis=0)),
        preferred_element_type=F32,
    )
    ny, _, lanes = out_ref.shape
    cy = lanes // C
    count = got.shape[1] // C
    mx = count // mz
    for owner in range(ny):
        for part in range(2):
            for kz in range(mz):
                row = (part * ny + owner) * cy
                block = got[row : row + cy, kz * mx * C : (kz + 1) * mx * C]
                block = jnp.stack([block[:, kx * C : (kx + 1) * C] for kx in range(mx)])
                block = jnp.swapaxes(block, 0, 1)
                start = (part * mz + kz) * mx
                for y in range(cy):
                    block_ref[owner, start : start + mx, y * C : (y + 1) * C] = block[y]
    out_ref[...] = block_ref[...].astype(out_ref.dtype)


def place(part, pair):
    start = (part * QUAD + pair) * MY
    return slice(start, start + MY)


def spread_table():
    return np.tile(np.kron(np.eye(C), np.ones((1, C))), (2, 1)).astype(jnp.bfloat16)


def gather_table():
    return np.kron(np.eye(SPAN // C), np.ones((1, C))).astype(jnp.bfloat16)


def spread_modes(modes, table_ref, spread_refs):
    count = C * C // SPAN
    made = set()

    def get(piece):
        for p in range(piece, min(piece + 2, count)):
            if p not in made:
                made.add(p)
                spread_refs[p % 2][...] = jnp.dot(
                    modes, table_ref[:, p * SPAN : (p + 1) * SPAN], preferred_element_type=F32
                )
        return spread_refs[piece % 2]

    return get


def weight_copies(weight_ref, held_ref, sem_ref):
    per = weight_ref.shape[2] // QUAD
    return [
        pltpu.make_async_copy(
            weight_ref.at[:, g // per, g % per * QUAD : (g % per + 1) * QUAD],
            held_ref.at[g],
            sem_ref.at[g],
        )
        for g in range(held_ref.shape[0])
    ]


def mix_kernel(
    mz,
    data_ref,
    weight_ref,
    table_ref,
    turn_ref,
    modes_ref,
    out_ref,
    sum_ref,
    rows_ref,
    block_ref,
    held_ref,
    sem_ref,
    spread_ref,
    spread_sem_ref,
    even_ref,
    odd_ref,
    total_ref,
):
    copies = weight_copies(weight_ref, held_ref, sem_ref)
    table_copy = pltpu.make_async_copy(table_ref, spread_ref, spread_sem_ref)
    table_copy.start()
    for copy in copies:
        copy.start()

    def store(group, part, pair, values):
        high = values.astype(BF16)
        low = (values - high.astype(F32)).astype(BF16)
        modes_ref[group, place(part, pair), :] = jnp.concatenate([high, low], axis=1)

    y_forward(mz, data_ref, turn_ref, rows_ref, store)
    table_copy.wait()
    for group, copy in enumerate(copies):
        copy.wait()
        spread = spread_modes(modes_ref[group], spread_ref, (even_ref, odd_ref))
        for piece in range(C * C // SPAN):
            modes = spread(piece)
            for pair in range(QUAD):
                real = imag = None
                for tile in range(SPAN // (2 * C)):
                    inside = slice(tile * 2 * C, (tile + 1) * 2 * C)
                    columns = slice(piece * SPAN + inside.start, piece * SPAN + inside.stop)
                    mode_re = modes[place(0, pair), inside]
                    mode_im = modes[place(1, pair), inside]
                    weight_re = held_ref[group, 0, pair, :, columns].astype(F32)
                    weight_im = held_ref[group, 1, pair, :, columns].astype(F32)
                    term_re = mode_re * weight_re - mode_im * weight_im
                    term_im = mode_re * weight_im + mode_im * weight_re
                    real = term_re if real is None else real + term_re
                    imag = term_im if imag is None else imag + term_im
                if piece:
                    real += total_ref[place(0, pair), :]
                    imag += total_ref[place(1, pair), :]
                total_ref[place(0, pair), :] = real
                total_ref[place(1, pair), :] = imag
        total = total_ref[...]
        sum_ref[group] = total[:, :C] + total[:, C:]
    y_inverse(mz, sum_ref, turn_ref, out_ref, block_ref)


def mix_back_kernel(
    mz,
    data_ref,
    weight_ref,
    table_ref,
    turn_ref,
    modes_ref,
    out_ref,
    sum_ref,
    rows_ref,
    block_ref,
    held_ref,
    sem_ref,
    term_ref,
):
    copies = weight_copies(weight_ref, held_ref, sem_ref)
    for copy in copies:
        copy.start()

    def store(group, part, pair, values):
        modes_ref[group, place(part, pair), :] = jnp.concatenate([values, values], axis=1)

    y_forward(mz, data_ref, turn_ref, rows_ref, store)
    for group, copy in enumerate(copies):
        copy.wait()
        total = []
        for piece in range(C * C // SPAN):
            for pair in range(QUAD):
                mode_re = modes_ref[group, place(0, pair), :]
                mode_im = modes_ref[group, place(1, pair), :]
                for tile in range(SPAN // (2 * C)):
                    start = piece * SPAN + tile * 2 * C
                    columns = slice(start, start + 2 * C)
                    weight_re = held_ref[group, 0, pair, :, columns].astype(F32)
                    weight_im = held_ref[group, 1, pair, :, columns].astype(F32)
                    term_ref[place(0, pair), columns] = (
                        weight_re * mode_re + weight_im * mode_im
                    ).astype(BF16)
                    term_ref[place(1, pair), columns] = (
                        weight_re * mode_im - weight_im * mode_re
                    ).astype(BF16)
            total.append(
                lax.dot_general(
                    table_ref[...],
                    term_ref[:, piece * SPAN : (piece + 1) * SPAN],
                    (((1,), (1,)), ((), ())),
                    preferred_element_type=F32,
                )
            )
        sum_ref[group] = jnp.concatenate(total, axis=0).T
    y_inverse(mz, sum_ref, turn_ref, out_ref, block_ref)


def outer_kernel(alpha, modes_ref, back_ref, table_ref, out_ref):
    count = C * C // SPAN
    made = lambda piece: jnp.dot(
        modes_ref[0],
        table_ref[:, piece * SPAN : (piece + 1) * SPAN],
        preferred_element_type=F32,
    )
    ahead = made(0)
    for piece in range(count):
        modes = ahead
        if piece + 1 < count:
            ahead = made(piece + 1)
        for pair in range(QUAD):
            back_re = back_ref[0, place(0, pair), :] * alpha
            back_im = back_ref[0, place(1, pair), :] * alpha
            for tile in range(SPAN // (2 * C)):
                inside = slice(tile * 2 * C, (tile + 1) * 2 * C)
                columns = slice(piece * SPAN + inside.start, piece * SPAN + inside.stop)
                mode_re = modes[place(0, pair), inside]
                mode_im = modes[place(1, pair), inside]
                out_ref[0, 0, pair, :, columns] = mode_re * back_re + mode_im * back_im
                out_ref[1, 0, pair, :, columns] = mode_re * back_im - mode_im * back_re


def in_hbm(value):
    return pltpu.with_memory_space_constraint(value, pltpu.HBM)


def whole():
    return pl.BlockSpec(memory_space=pltpu.VMEM)


def params(mib):
    return pltpu.CompilerParams(vmem_limit_bytes=mib * MIB)


def cost(flops, moved):
    return pl.CostEstimate(flops=int(flops), bytes_accessed=int(moved), transcendentals=0)


def call(kernel, outs, args, scratch=(), mib=24, flops=0, moved=0, anywhere=()):
    return pl.pallas_call(
        kernel,
        out_shape=[jax.ShapeDtypeStruct(*out) for out in outs],
        in_specs=[
            pl.BlockSpec(memory_space=pl.ANY) if i in anywhere else whole()
            for i in range(len(args))
        ],
        out_specs=[whole() for _ in outs],
        scratch_shapes=list(scratch),
        compiler_params=params(mib),
        cost_estimate=cost(flops, moved),
    )(*args)


def per_mode(kernel, data, weight, table, turn, modes, kind, scratch=()):
    _, mz, mx, my, wide = weight.shape
    groups = mz * mx // QUAD
    rows = 2 * QUAD * MY
    modes_shape = (groups, rows, modes[0])
    return pl.pallas_call(
        functools.partial(kernel, mz),
        in_specs=[
            whole(),
            pl.BlockSpec(memory_space=pl.ANY),
            pl.BlockSpec(memory_space=pl.ANY) if kernel is mix_kernel else whole(),
            whole(),
        ],
        out_specs=[whole(), whole()],
        out_shape=[
            jax.ShapeDtypeStruct(modes_shape, modes[1]),
            jax.ShapeDtypeStruct(data.shape, kind),
        ],
        scratch_shapes=[
            pltpu.VMEM((groups, rows, C), F32),
            pltpu.VMEM((turn.shape[0] - 2 * MY, mz * mx * C), F32),
            pltpu.VMEM(data.shape, F32),
            pltpu.VMEM((groups, 2, QUAD, my, wide), BF16),
            pltpu.SemaphoreType.DMA((groups,)),
            *scratch,
        ],
        compiler_params=params(24),
        cost_estimate=cost(weight.size * 8, weight.size * 2),
    )(data, in_hbm(weight), in_hbm(table), turn)


def outer(modes, back, table, shape, alpha):
    per = shape[2] // QUAD
    group = lambda ref: pl.BlockSpec((1,) + ref.shape[1:], lambda step: (step, 0, 0))
    return pl.pallas_call(
        functools.partial(outer_kernel, alpha),
        grid=(modes.shape[0],),
        in_specs=[group(modes), group(back), pl.BlockSpec(table.shape, lambda step: (0, 0))],
        out_specs=pl.BlockSpec(
            (2, 1, QUAD) + shape[3:], lambda step: (0, step // per, step % per, 0, 0)
        ),
        out_shape=jax.ShapeDtypeStruct(shape, F32),
        compiler_params=params(20),
        cost_estimate=cost(math.prod(shape) * 4, math.prod(shape) * 4),
    )(modes, back, table)


def shift(block, axis, step):
    count = lax.axis_size(axis)
    pairs = [(i, i + step) for i in range(count) if 0 <= i + step < count]
    return lax.ppermute(block, axis, pairs)


def x_halos(turned):
    return shift(turned[-1], "gx", 1), shift(turned[0], "gx", -1)


def y_halos(turned, xlo, xhi):
    edge = lambda y: jnp.concatenate([xlo[None, y], turned[:, y], xhi[None, y]], axis=0)
    return shift(edge(-1), "gy", 1), shift(edge(0), "gy", -1)


def conv(turned, rim, weight, flip):
    cx, cy, c, z = turned.shape
    return call(
        functools.partial(conv_kernel, flip),
        [((cx, c, cy * z), F32)],
        (turned, *map(in_hbm, rim), in_hbm(weight)),
        [pltpu.VMEM((4 * c, (cy + 2) * z), BF16)],
        mib=32,
        flops=2 * 27 * c * c * cx * cy * z,
        moved=turned.size * 8,
    )[0]


def weight_grad(grad, turned, rim):
    cx, cy, c, z = turned.shape
    return call(
        weight_grad_kernel,
        [((16 * c, 2 * c), F32)],
        (grad, turned, *map(in_hbm, rim)),
        [
            pltpu.VMEM((4 * c, (cy + 2) * z), BF16),
            pltpu.VMEM((cx * 3 * c, (cy + 2) * z), BF16),
            pltpu.VMEM((9 * c, 4 * c), F32),
            *(pltpu.VMEM(halo.shape, BF16) for halo in rim),
            pltpu.SemaphoreType.DMA((len(rim),)),
        ],
        anywhere=(2, 3, 4, 5),
        mib=32,
        flops=2 * 27 * c * c * cx * cy * z,
        moved=turned.size * 8,
    )[0]


def swap(block, axis):
    return lax.all_to_all(block, axis, split_axis=0, concat_axis=0, tiled=True)


def together(*values):
    return lax.optimization_barrier(values)


def body(state, cotangent, spectral_weight, stencil_weight, pointwise_weight):
    nx, ny = lax.axis_size("gx"), lax.axis_size("gy")
    c, cx, cy, z = state.shape
    _, mz, mx, _, _ = spectral_weight.shape
    wide_x, wide_y = cx * nx, cy * ny
    alpha = 1.0 / math.sqrt(wide_x * wide_y * z)
    beta = 1.0 / math.sqrt(2 * MX * MY * MZ)
    double = np.where(np.arange(MZ) == 0, 1.0, 2.0)
    ones = np.ones(MZ)
    z_state = jnp.asarray(z_forward_table(alpha * ones)(nx, mz))
    z_grad = jnp.asarray(z_forward_table(double)(nx, mz))
    z_spectral = jnp.asarray(z_inverse_table(nx, mz, beta * double))
    z_back = jnp.asarray(z_inverse_table(nx, mz, alpha * beta * ones))
    x_fwd, x_inv = (jnp.asarray(t) for t in x_tables(wide_x, mz, mx))
    y_turn = jnp.asarray(y_table(wide_y))
    spread, gather = jnp.asarray(spread_table()), jnp.asarray(gather_table())
    lanes = cy * c
    x_rows = cx * 2 * mz

    def x_stage(table, block, lead, kind=F32, extra=0):
        rows = table.shape[0] // lead + extra
        return call(
            x_kernel,
            [((lead, rows, lanes), kind)],
            (table, block),
            mib=16,
            flops=2 * table.size * lanes,
            moved=8 * block.size,
        )[0]

    slab_shape = ((nx, x_rows, lanes), F32)
    turned_shape = ((cx, cy, c, z), BF16)

    conv_table, back_table = call(
        taps_kernel,
        [((9 * c, 4 * c), BF16)] * 2,
        (in_hbm(stencil_weight), in_hbm(pointwise_weight)),
        [pltpu.VMEM((27 * c, c), F32)],
        moved=stencil_weight.size * 6,
    )
    turned, slab = call(
        functools.partial(prep_kernel, nx),
        [turned_shape, slab_shape],
        (in_hbm(state), in_hbm(z_state)),
        flops=2 * 96 * state.size,
        moved=state.size * 5,
    )
    block = x_stage(x_fwd, swap(slab, "gx"), ny)
    block, conv_table, back_table, *faces = together(
        block, conv_table, back_table, *x_halos(turned)
    )
    modes_in, block = per_mode(
        mix_kernel,
        swap(block, "gy"),
        spectral_weight,
        spread,
        y_turn,
        (2 * c, BF16),
        F32,
        [pltpu.VMEM(spread.shape, BF16), pltpu.SemaphoreType.DMA]
        + [pltpu.VMEM((2 * QUAD * MY, SPAN), F32)] * 2
        + [pltpu.VMEM((2 * QUAD * MY, 2 * c), F32)],
    )
    block, *edges = together(block, *y_halos(turned, *faces))
    rim = (*faces, *edges)
    block = x_stage(x_inv, swap(block, "gy"), nx)
    stencil = conv(turned, rim, conv_table, False)
    output, grad, slab = call(
        functools.partial(gelu_kernel, nx),
        [((c, cx, cy, z), BF16), turned_shape, slab_shape],
        (stencil, swap(block, "gx"), cotangent, z_spectral, z_grad),
        flops=2 * 192 * state.size,
        moved=state.size * 12,
    )

    grad_taps = weight_grad(grad, turned, rim)
    block = x_stage(x_fwd, swap(slab, "gx"), ny, BF16)
    block, grad_taps, *faces = together(block, grad_taps, *x_halos(grad))
    edges = y_halos(grad, *faces)
    block, grad_taps, ylo = together(swap(block, "gy"), grad_taps, edges[0])
    edges = (ylo, edges[1])
    mine = swap(grad_taps.reshape(nx, -1, 2 * c), "gx").sum(0)
    back_modes, block = per_mode(
        mix_back_kernel,
        block,
        spectral_weight,
        gather,
        y_turn,
        (2 * c, F32),
        BF16,
        [pltpu.VMEM((2 * QUAD * MY, c * c), BF16)],
    )
    packed = jnp.concatenate(jnp.split(mine, lanes // (2 * c)), axis=1).astype(BF16)
    extra = packed.shape[0]
    packed = jnp.broadcast_to(packed[None], (ny, extra, lanes))
    block = x_stage(
        x_inv, swap(jnp.concatenate([block, packed], axis=1), "gy"), nx, BF16, extra
    )
    stencil_back = conv(grad, (*faces, *edges), back_table, True)
    block, stencil_back = together(block, stencil_back)
    message = swap(block, "gx")
    grad_modes = outer(modes_in, back_modes, spread, spectral_weight.shape, alpha)
    grad_state, grad_stencil, grad_point = call(
        functools.partial(finish_kernel, nx, alpha),
        [((c, cx, cy, z), F32), ((c, 27 * c), F32), ((c, c), F32)],
        (stencil_back, message, z_back),
        [pltpu.VMEM(grad_taps.shape, F32), pltpu.VMEM((27 * c, c), F32)],
        flops=2 * 96 * state.size,
        moved=state.size * 10,
    )
    return (output, grad_state, grad_modes, grad_stencil, grad_point)


def solution(mesh):
    in_specs = (
        P(None, "gx", "gy", None),
        P(None, "gx", "gy", None),
        P(None, "gx", "gy", None, None),
        P(),
        P(),
    )
    out_specs = (
        P(None, "gx", "gy", None),
        P(None, "gx", "gy", None),
        P(None, "gx", "gy", None, None),
        P(),
        P(),
    )
    return jax.shard_map(body, mesh=mesh, in_specs=in_specs, out_specs=out_specs, check_vma=False)
```

```python
import functools
import math

import jax
import jax.numpy as jnp
import numpy as np
from jax import lax
from jax.experimental import pallas as pl
from jax.experimental.pallas import tpu as pltpu
from jax.sharding import PartitionSpec as P

C = 64
MX = 32
MY = 32
MZ = 16
Z = 128
MIB = 1 << 20

F32 = jnp.float32
BF16 = jnp.bfloat16


def angles(places, freqs, length):
    turns = np.outer(np.asarray(places), np.asarray(freqs)) % length
    return turns * (2.0 * np.pi / length)


def centred(count):
    steps = np.arange(count)
    return np.where(steps < count // 2, steps, steps - count)


def split(table, parts):
    rest = np.asarray(table, np.float64)
    out = []
    for _ in range(parts):
        piece = rest.astype(jnp.bfloat16)
        out.append(piece)
        rest = rest - piece.astype(np.float64)
    return out


def z_forward_table(scale):
    def build(nx, mz):
        theta = angles(np.arange(MZ), np.arange(Z), Z)
        pair = np.stack([np.cos(theta), -np.sin(theta)]) * scale[None, :, None]
        rows = pair.reshape(2, nx, mz, Z).transpose(1, 0, 2, 3).reshape(2 * MZ, Z)
        return np.concatenate(split(rows, 3), axis=0)

    return build


def z_inverse_table(nx, mz, scale):
    theta = angles(np.arange(MZ), np.arange(Z), Z)
    pair = np.stack([np.cos(theta), -np.sin(theta)]) * scale[None, :, None]
    rows = pair.reshape(2, nx, mz, Z).transpose(1, 0, 2, 3).reshape(2 * MZ, Z)
    high, low = split(rows, 2)
    return np.concatenate([high, high, low], axis=0)


def rotation(theta, sign):
    cosine, sine = np.cos(theta), sign * np.sin(theta)
    return np.stack([np.stack([cosine, -sine], 1), np.stack([sine, cosine], 1)])


def against_pieces(*tables):
    out = []
    for table in tables:
        high, low = split(table, 2)
        out.append(np.concatenate([high, high, low], axis=1))
    return out


def x_tables(wide, mz, mx):
    theta = angles(centred(MX), np.arange(wide), wide)
    eye = np.eye(mz)
    forward = np.einsum("rkRx,zZ->krzxRZ", rotation(theta, -1.0), eye)
    inverse = np.einsum("rxRk,zZ->xrzkRZ", rotation(theta.T, 1.0), eye)
    size_k, size_x = MX * 2 * mz, wide * 2 * mz
    forward = forward.reshape(MX // mx, mx, 2, mz, size_x).transpose(0, 2, 3, 1, 4)
    inverse = inverse.reshape(size_x, MX // mx, mx, 2, mz).transpose(0, 1, 3, 4, 2)
    return against_pieces(forward.reshape(size_k, size_x), inverse.reshape(size_x, size_k))


def y_table(wide):
    theta = angles(centred(MY), np.arange(wide), wide)
    forward = rotation(theta, -1.0).reshape(2 * MY, 2 * wide)
    inverse = rotation(theta.T, 1.0).reshape(2 * wide, 2 * MY)
    forward, inverse = against_pieces(forward, inverse)
    inverse = np.pad(inverse, ((0, 0), (0, forward.shape[1] - inverse.shape[1])))
    return np.concatenate([forward, inverse], axis=0)


def pieces(values):
    high = values.astype(BF16)
    low = (values - high.astype(F32)).astype(BF16)
    return jnp.concatenate([high, low, high], axis=0)


def z_forward(rows, table, out_ref, x, nx):
    got = lax.dot_general(table, rows, (((1,), (1,)), ((), ())), preferred_element_type=F32)
    size = 2 * MZ
    total = got[:size] + (got[size : 2 * size] + got[2 * size :])
    per = size // nx
    for owner in range(nx):
        out_ref[owner, x * per : (x + 1) * per, :] = total[owner * per : (owner + 1) * per]


def z_inverse(in_ref, table, x, nx):
    per = 2 * MZ // nx
    rows = jnp.concatenate(
        [in_ref[owner].astype(F32)[x * per : (x + 1) * per] for owner in range(nx)], axis=0
    )
    return lax.dot_general(
        pieces(rows), table, (((0,), (0,)), ((), ())), preferred_element_type=F32
    )


def prep_kernel(nx, field_ref, table_ref, turned_ref, slab_ref):
    c, cx, cy, z = field_ref.shape
    for x in range(cx):
        block = jnp.swapaxes(field_ref[:, x].astype(F32), 0, 1)
        turned = block.astype(BF16)
        turned_ref[x] = turned
        z_forward(turned.reshape(cy * c, z), table_ref[...], slab_ref, x, nx)


def plane_rows(p, cx, body_ref, xlo_ref, xhi_ref, ylo_ref, yhi_ref):
    cy = body_ref.shape[1]
    if p == 0:
        middle = [xlo_ref[y] for y in range(cy)]
    elif p == cx + 1:
        middle = [xhi_ref[y] for y in range(cy)]
    else:
        middle = [body_ref[p - 1, y] for y in range(cy)]
    return [ylo_ref[p]] + middle + [yhi_ref[p]]


def fill_shifts(blocks, rim_ref, flip=False):
    c, z = blocks[0].shape
    lane = lax.broadcasted_iota(jnp.int32, (c, z), 1)
    for y, block in enumerate(blocks):
        wide = block.astype(F32)
        before = jnp.where(lane == 0, 0.0, pltpu.roll(wide, 1, 1))
        after = jnp.where(lane == z - 1, 0.0, pltpu.roll(wide, z - 1, 1))
        if flip:
            before, after = after, before
        columns = slice(y * z, (y + 1) * z)
        rim_ref[0:c, columns] = before.astype(BF16)
        rim_ref[c : 2 * c, columns] = block
        rim_ref[2 * c : 3 * c, columns] = after.astype(BF16)
        rim_ref[3 * c : 4 * c, columns] = block


def conv_kernel(
    flip, body_ref, xlo_ref, xhi_ref, ylo_ref, yhi_ref, weight_ref, out_ref, rim_ref
):
    cx, cy, c, z = body_ref.shape
    for p in range(cx + 2):
        blocks = plane_rows(p, cx, body_ref, xlo_ref, xhi_ref, ylo_ref, yhi_ref)
        fill_shifts(blocks, rim_ref, flip)
        places = [a for a in range(3) if 0 <= p - (2 - a if flip else a) < cx]
        first = places[0]
        got = jnp.dot(
            weight_ref[first * 3 * c : (places[-1] + 1) * 3 * c, :],
            rim_ref[...],
            preferred_element_type=F32,
        )
        for a in places:
            x = p - (2 - a if flip else a)
            total = None
            for b in range(3):
                row = ((a - first) * 3 + b) * c
                skip = 2 - b if flip else b
                term = got[row : row + c, skip * z : (skip + cy) * z]
                total = term if total is None else total + term
            if p == x:
                out_ref[x] = total
            else:
                out_ref[x] += total


def weight_grad_kernel(
    grad_ref,
    body_ref,
    xlo_any,
    xhi_any,
    ylo_any,
    yhi_any,
    out_ref,
    rim_ref,
    wide_ref,
    sum_ref,
    xlo_ref,
    xhi_ref,
    ylo_ref,
    yhi_ref,
    sem_ref,
):
    cx, cy, c, z = body_ref.shape
    group = 3 * c
    held = (xlo_ref, xhi_ref, ylo_ref, yhi_ref)
    copies = [
        pltpu.make_async_copy(given, ref, sem_ref.at[i])
        for i, (given, ref) in enumerate(zip((xlo_any, xhi_any, ylo_any, yhi_any), held))
    ]
    for copy in copies:
        copy.start()
    wide_ref[...] = jnp.zeros_like(wide_ref)
    for x in range(cx):
        for b in range(3):
            for y in range(cy):
                row = x * group + b * c
                wide_ref[row : row + c, (y + b) * z : (y + b + 1) * z] = grad_ref[x, y]
    sum_ref[...] = jnp.zeros_like(sum_ref)
    for copy in copies:
        copy.wait()
    for p in range(cx + 2):
        fill_shifts(plane_rows(p, cx, body_ref, xlo_ref, xhi_ref, ylo_ref, yhi_ref), rim_ref)
        first, last = max(0, p - 2), min(cx - 1, p)
        got = lax.dot_general(
            wide_ref[first * group : (last + 1) * group, :],
            rim_ref[...],
            (((1,), (1,)), ((), ())),
            preferred_element_type=F32,
        )
        for x in range(first, last + 1):
            a = p - x
            sum_ref[a * group : (a + 1) * group, :] += got[
                (x - first) * group : (x - first + 1) * group, :
            ]
    out_ref[: 9 * c] = sum_ref[:, : 2 * c]
    last = [sum_ref[k * c : (k + 1) * c, 2 * c : 3 * c] for k in range(9)]
    last.append(jnp.zeros((c, c), F32))
    for k in range(5):
        row = (9 + k) * c
        out_ref[row : row + c] = jnp.concatenate(last[2 * k : 2 * k + 2], axis=1)
    out_ref[14 * c :] = jnp.zeros((2 * c, 2 * c), F32)


def gelu_kernel(
    nx,
    stencil_ref,
    slab_ref,
    cot_ref,
    inverse_ref,
    forward_ref,
    out_ref,
    turned_ref,
    message_ref,
    back_ref,
):
    c, cx, cy, z = cot_ref.shape
    root = math.sqrt(2.0 / math.pi)
    for x in range(cx):
        spectral = z_inverse(slab_ref, inverse_ref[...], x, nx).reshape(cy, c, z)
        stencil = jnp.stack([stencil_ref[x, :, y * z : (y + 1) * z] for y in range(cy)])
        pre = spectral + stencil
        cot = jnp.swapaxes(cot_ref[:, x].astype(F32), 0, 1)
        square = pre * pre
        bent = jnp.tanh(root * (pre * (1.0 + 0.044715 * square)))
        half = 0.5 + 0.5 * bent
        slope = half + (0.5 * pre) * (1.0 - bent * bent) * (root * (1.0 + 0.134145 * square))
        out_ref[:, x] = jnp.swapaxes(pre * half, 0, 1).astype(BF16)
        grad = (cot * slope).astype(BF16)
        turned_ref[x] = grad
        z_forward(grad.reshape(cy * c, z), forward_ref[...], back_ref, x, nx)
    ny = message_ref.shape[0] // nx
    for owner in range(nx):
        block = back_ref[owner].astype(BF16)
        for copy in range(ny):
            message_ref[owner * ny + copy] = block


def finish_kernel(
    nx,
    scale,
    stencil_ref,
    message_ref,
    inverse_ref,
    out_ref,
    taps_ref,
    point_ref,
    packed_ref,
    turned_ref,
):
    c, cx, cy, z = out_ref.shape
    for x in range(cx):
        spectral = z_inverse(message_ref, inverse_ref[...], x, nx).reshape(cy, c, z)
        stencil = jnp.stack([stencil_ref[x, :, y * z : (y + 1) * z] for y in range(cy)])
        out_ref[:, x] = jnp.swapaxes(spectral + stencil, 0, 1)
    skip = 2 * MZ * cx // nx
    unpack(scale, skip, message_ref, taps_ref, point_ref, packed_ref, turned_ref)


def x_kernel(table_ref, data_ref, out_ref):
    data = data_ref[...].astype(F32)
    lanes = data.shape[2]
    rows = table_ref.shape[1] // (3 * data.shape[0])
    flat = pieces(data[:, :rows].reshape(-1, lanes))
    got = jnp.dot(table_ref[...], flat, preferred_element_type=F32).astype(out_ref.dtype)
    count = got.shape[0] // out_ref.shape[0]
    for owner in range(out_ref.shape[0]):
        out_ref[owner, :count] = got[owner * count : (owner + 1) * count]
    if data.shape[1] > rows:
        extra = data[:, rows:].sum(0)
        extra = extra.astype(out_ref.dtype)
        for owner in range(out_ref.shape[0]):
            out_ref[owner, count:] = extra


def taps_kernel(taps_ref, point_ref, forward_ref, back_ref, turned_ref):
    turned_ref[...] = taps_ref[...].astype(F32).T
    forward_ref[...] = jnp.zeros_like(forward_ref)
    back_ref[...] = jnp.zeros_like(back_ref)
    for tap in range(27):
        rows = slice(tap // 3 * C, (tap // 3 + 1) * C)
        columns = slice(tap % 3 * C, (tap % 3 + 1) * C)
        block = turned_ref[pl.ds(tap, C, stride=27), :]
        back_ref[rows, columns] = block.astype(BF16)
        forward_ref[rows, columns] = block.T.astype(BF16)
    point = point_ref[...].astype(F32)
    forward_ref[4 * C : 5 * C, 3 * C :] = point.astype(BF16)
    back_ref[4 * C : 5 * C, 3 * C :] = point.T.astype(BF16)


def unpack(scale, skip, message_ref, taps_ref, point_ref, packed_ref, turned_ref):
    devices, rows, lanes = message_ref.shape
    per, tiles_in = rows - skip, lanes // 128
    for owner in range(devices):
        message = message_ref[owner].astype(F32)
        for tile in range(tiles_in):
            row = (owner * tiles_in + tile) * per
            packed_ref[row : row + per] = message[skip:, tile * 128 : (tile + 1) * 128]
    for tap in range(27):
        group, e = tap // 3, tap % 3
        if e < 2:
            block = packed_ref[group * C : (group + 1) * C, e * C : (e + 1) * C]
        else:
            row = (9 + group // 2) * C
            block = packed_ref[row : row + C, group % 2 * C : (group % 2 + 1) * C]
        block = block * scale
        if tap == 13:
            point_ref[...] = block
        turned_ref[pl.ds(tap, C, stride=27), :] = block.T
    taps_ref[...] = turned_ref[...].T


QUAD = 4
SPAN = 8 * C


def y_forward(mz, blocks, table_ref, rows_ref, store):
    ny, cy = len(blocks), blocks[0].shape[1] // C
    count = rows_ref.shape[1] // C
    for owner in range(ny):
        data = blocks[owner]
        for part in range(2):
            for kz in range(mz):
                mx = count // mz
                start = (part * mz + kz) * mx
                block = data[start : start + mx]
                block = jnp.stack([block[:, y * C : (y + 1) * C] for y in range(cy)])
                block = jnp.swapaxes(block, 0, 1)
                row = (part * ny + owner) * cy
                for kx in range(mx):
                    column = (kz * mx + kx) * C
                    rows_ref[row : row + cy, column : column + C] = block[kx]
    got = jnp.dot(table_ref[: 2 * MY], pieces(rows_ref[...]), preferred_element_type=F32)
    for q in range(count):
        block = got[:, q * C : (q + 1) * C]
        for part in range(2):
            store(q // QUAD, part, q % QUAD, block[part * MY : (part + 1) * MY])


def y_inverse(mz, sum_ref, table_ref, out_ref, block_ref):
    rows = [
        jnp.concatenate(
            [
                sum_ref[group, place(part, pair), :]
                for group in range(sum_ref.shape[0])
                for pair in range(QUAD)
            ],
            axis=1,
        )
        for part in range(2)
    ]
    got = jnp.dot(
        table_ref[2 * MY :, : 6 * MY],
        pieces(jnp.concatenate(rows, axis=0)),
        preferred_element_type=F32,
    )
    ny, _, lanes = out_ref.shape
    cy = lanes // C
    count = got.shape[1] // C
    mx = count // mz
    for owner in range(ny):
        for part in range(2):
            for kz in range(mz):
                row = (part * ny + owner) * cy
                block = got[row : row + cy, kz * mx * C : (kz + 1) * mx * C]
                block = jnp.stack([block[:, kx * C : (kx + 1) * C] for kx in range(mx)])
                block = jnp.swapaxes(block, 0, 1)
                start = (part * mz + kz) * mx
                for y in range(cy):
                    block_ref[owner, start : start + mx, y * C : (y + 1) * C] = block[y]
    out_ref[...] = block_ref[...].astype(out_ref.dtype)


def place(part, pair):
    start = (part * QUAD + pair) * MY
    return slice(start, start + MY)


def spread_table():
    return np.tile(np.kron(np.eye(C), np.ones((1, C))), (2, 1)).astype(jnp.bfloat16)


def gather_table():
    return np.kron(np.eye(SPAN // C), np.ones((1, C))).astype(jnp.bfloat16)


def spread_modes(modes, table_ref, spread_refs):
    count = C * C // SPAN
    made = set()

    def get(piece):
        for p in range(piece, min(piece + 2, count)):
            if p not in made:
                made.add(p)
                spread_refs[p % 2][...] = jnp.dot(
                    modes, table_ref[:, p * SPAN : (p + 1) * SPAN], preferred_element_type=F32
                )
        return spread_refs[piece % 2]

    return get


def weight_copies(weight_ref, held_ref, sem_ref):
    per = weight_ref.shape[2] // QUAD
    return [
        pltpu.make_async_copy(
            weight_ref.at[:, g // per, g % per * QUAD : (g % per + 1) * QUAD],
            held_ref.at[g],
            sem_ref.at[g],
        )
        for g in range(held_ref.shape[0])
    ]


def mix_kernel(
    mz,
    data_ref,
    weight_ref,
    table_ref,
    turn_ref,
    modes_ref,
    out_ref,
    sum_ref,
    rows_ref,
    block_ref,
    held_ref,
    sem_ref,
    spread_ref,
    spread_sem_ref,
    even_ref,
    odd_ref,
    total_ref,
):
    copies = weight_copies(weight_ref, held_ref, sem_ref)
    table_copy = pltpu.make_async_copy(table_ref, spread_ref, spread_sem_ref)
    table_copy.start()
    for copy in copies:
        copy.start()

    def store(group, part, pair, values):
        high = values.astype(BF16)
        low = (values - high.astype(F32)).astype(BF16)
        modes_ref[group, place(part, pair), :] = jnp.concatenate([high, low], axis=1)

    blocks = [data_ref[owner] for owner in range(data_ref.shape[0])]
    y_forward(mz, blocks, turn_ref, rows_ref, store)
    table_copy.wait()
    for group, copy in enumerate(copies):
        copy.wait()
        spread = spread_modes(modes_ref[group], spread_ref, (even_ref, odd_ref))
        for piece in range(C * C // SPAN):
            modes = spread(piece)
            for pair in range(QUAD):
                real = imag = None
                for tile in range(SPAN // (2 * C)):
                    inside = slice(tile * 2 * C, (tile + 1) * 2 * C)
                    columns = slice(piece * SPAN + inside.start, piece * SPAN + inside.stop)
                    mode_re = modes[place(0, pair), inside]
                    mode_im = modes[place(1, pair), inside]
                    weight_re = held_ref[group, 0, pair, :, columns].astype(F32)
                    weight_im = held_ref[group, 1, pair, :, columns].astype(F32)
                    term_re = mode_re * weight_re - mode_im * weight_im
                    term_im = mode_re * weight_im + mode_im * weight_re
                    real = term_re if real is None else real + term_re
                    imag = term_im if imag is None else imag + term_im
                if piece:
                    real += total_ref[place(0, pair), :]
                    imag += total_ref[place(1, pair), :]
                total_ref[place(0, pair), :] = real
                total_ref[place(1, pair), :] = imag
        total = total_ref[...]
        sum_ref[group] = total[:, :C] + total[:, C:]
    y_inverse(mz, sum_ref, turn_ref, out_ref, block_ref)


def mix_back_kernel(
    mz,
    data_ref,
    weight_ref,
    table_ref,
    turn_ref,
    x_ref,
    modes_ref,
    out_ref,
    sum_ref,
    rows_ref,
    block_ref,
    held_ref,
    sem_ref,
    term_ref,
):
    copies = weight_copies(weight_ref, held_ref, sem_ref)
    for copy in copies:
        copy.start()

    def store(group, part, pair, values):
        modes_ref[group, place(part, pair), :] = jnp.concatenate([values, values], axis=1)

    ny = block_ref.shape[0]
    size = x_ref.shape[1] // 3
    blocks = []
    for owner in range(ny):
        rows = jnp.concatenate(
            [data_ref[i].astype(F32) for i in range(owner, data_ref.shape[0], ny)], axis=0
        ).astype(BF16)
        blocks.append(
            jnp.dot(x_ref[:, :size], rows, preferred_element_type=F32)
            + jnp.dot(x_ref[:, 2 * size :], rows, preferred_element_type=F32)
        )
    y_forward(mz, blocks, turn_ref, rows_ref, store)
    for group, copy in enumerate(copies):
        copy.wait()
        total = []
        for piece in range(C * C // SPAN):
            for pair in range(QUAD):
                mode_re = modes_ref[group, place(0, pair), :]
                mode_im = modes_ref[group, place(1, pair), :]
                for tile in range(SPAN // (2 * C)):
                    start = piece * SPAN + tile * 2 * C
                    columns = slice(start, start + 2 * C)
                    weight_re = held_ref[group, 0, pair, :, columns].astype(F32)
                    weight_im = held_ref[group, 1, pair, :, columns].astype(F32)
                    term_ref[place(0, pair), columns] = (
                        weight_re * mode_re + weight_im * mode_im
                    ).astype(BF16)
                    term_ref[place(1, pair), columns] = (
                        weight_re * mode_im - weight_im * mode_re
                    ).astype(BF16)
            total.append(
                lax.dot_general(
                    table_ref[...],
                    term_ref[:, piece * SPAN : (piece + 1) * SPAN],
                    (((1,), (1,)), ((), ())),
                    preferred_element_type=F32,
                )
            )
        sum_ref[group] = jnp.concatenate(total, axis=0).T
    y_inverse(mz, sum_ref, turn_ref, out_ref, block_ref)


def outer_kernel(alpha, modes_ref, back_ref, table_ref, out_ref):
    count = C * C // SPAN
    made = lambda piece: jnp.dot(
        modes_ref[0],
        table_ref[:, piece * SPAN : (piece + 1) * SPAN],
        preferred_element_type=F32,
    )
    ahead = made(0)
    for piece in range(count):
        modes = ahead
        if piece + 1 < count:
            ahead = made(piece + 1)
        for pair in range(QUAD):
            back_re = back_ref[0, place(0, pair), :] * alpha
            back_im = back_ref[0, place(1, pair), :] * alpha
            for tile in range(SPAN // (2 * C)):
                inside = slice(tile * 2 * C, (tile + 1) * 2 * C)
                columns = slice(piece * SPAN + inside.start, piece * SPAN + inside.stop)
                mode_re = modes[place(0, pair), inside]
                mode_im = modes[place(1, pair), inside]
                out_ref[0, 0, pair, :, columns] = mode_re * back_re + mode_im * back_im
                out_ref[1, 0, pair, :, columns] = mode_re * back_im - mode_im * back_re


def in_hbm(value):
    return pltpu.with_memory_space_constraint(value, pltpu.HBM)


def whole():
    return pl.BlockSpec(memory_space=pltpu.VMEM)


def params(mib):
    return pltpu.CompilerParams(vmem_limit_bytes=mib * MIB)


def cost(flops, moved):
    return pl.CostEstimate(flops=int(flops), bytes_accessed=int(moved), transcendentals=0)


def call(kernel, outs, args, scratch=(), mib=24, flops=0, moved=0, anywhere=()):
    return pl.pallas_call(
        kernel,
        out_shape=[jax.ShapeDtypeStruct(*out) for out in outs],
        in_specs=[
            pl.BlockSpec(memory_space=pl.ANY) if i in anywhere else whole()
            for i in range(len(args))
        ],
        out_specs=[whole() for _ in outs],
        scratch_shapes=list(scratch),
        compiler_params=params(mib),
        cost_estimate=cost(flops, moved),
    )(*args)


def per_mode(kernel, data, weight, table, tables, modes, kind, scratch=()):
    _, mz, mx, my, wide = weight.shape
    groups = mz * mx // QUAD
    rows = 2 * QUAD * MY
    modes_shape = (groups, rows, modes[0])
    block = (MX // mx, 2 * mz * mx, data.shape[2])
    return pl.pallas_call(
        functools.partial(kernel, mz),
        in_specs=[
            whole(),
            pl.BlockSpec(memory_space=pl.ANY),
            pl.BlockSpec(memory_space=pl.ANY) if kernel is mix_kernel else whole(),
        ]
        + [whole() for _ in tables],
        out_specs=[whole(), whole()],
        out_shape=[
            jax.ShapeDtypeStruct(modes_shape, modes[1]),
            jax.ShapeDtypeStruct(block, kind),
        ],
        scratch_shapes=[
            pltpu.VMEM((groups, rows, C), F32),
            pltpu.VMEM((tables[0].shape[0] - 2 * MY, mz * mx * C), F32),
            pltpu.VMEM(block, F32),
            pltpu.VMEM((groups, 2, QUAD, my, wide), BF16),
            pltpu.SemaphoreType.DMA((groups,)),
            *scratch,
        ],
        compiler_params=params(24),
        cost_estimate=cost(weight.size * 8, weight.size * 2),
    )(data, in_hbm(weight), in_hbm(table), *tables)


def outer(modes, back, table, shape, alpha):
    per = shape[2] // QUAD
    group = lambda ref: pl.BlockSpec((1,) + ref.shape[1:], lambda step: (step, 0, 0))
    return pl.pallas_call(
        functools.partial(outer_kernel, alpha),
        grid=(modes.shape[0],),
        in_specs=[group(modes), group(back), pl.BlockSpec(table.shape, lambda step: (0, 0))],
        out_specs=pl.BlockSpec(
            (2, 1, QUAD) + shape[3:], lambda step: (0, step // per, step % per, 0, 0)
        ),
        out_shape=jax.ShapeDtypeStruct(shape, F32),
        compiler_params=params(20),
        cost_estimate=cost(math.prod(shape) * 4, math.prod(shape) * 4),
    )(modes, back, in_hbm(table))


def shift(block, axis, step):
    count = lax.axis_size(axis)
    pairs = [(i, i + step) for i in range(count) if 0 <= i + step < count]
    return lax.ppermute(block, axis, pairs)


def x_halos(turned):
    return shift(turned[-1], "gx", 1), shift(turned[0], "gx", -1)


def y_halos(turned, xlo, xhi):
    edge = lambda y: jnp.concatenate([xlo[None, y], turned[:, y], xhi[None, y]], axis=0)
    return shift(edge(-1), "gy", 1), shift(edge(0), "gy", -1)


def conv(turned, rim, weight, flip):
    cx, cy, c, z = turned.shape
    return call(
        functools.partial(conv_kernel, flip),
        [((cx, c, cy * z), F32)],
        (turned, *map(in_hbm, rim), in_hbm(weight)),
        [pltpu.VMEM((4 * c, (cy + 2) * z), BF16)],
        mib=32,
        flops=2 * 27 * c * c * cx * cy * z,
        moved=turned.size * 8,
    )[0]


def weight_grad(grad, turned, rim):
    cx, cy, c, z = turned.shape
    return call(
        weight_grad_kernel,
        [((16 * c, 2 * c), F32)],
        (grad, turned, *map(in_hbm, rim)),
        [
            pltpu.VMEM((4 * c, (cy + 2) * z), BF16),
            pltpu.VMEM((cx * 3 * c, (cy + 2) * z), BF16),
            pltpu.VMEM((9 * c, 4 * c), F32),
            *(pltpu.VMEM(halo.shape, BF16) for halo in rim),
            pltpu.SemaphoreType.DMA((len(rim),)),
        ],
        anywhere=(2, 3, 4, 5),
        mib=32,
        flops=2 * 27 * c * c * cx * cy * z,
        moved=turned.size * 8,
    )[0]


def swap(block, axis):
    return lax.all_to_all(block, axis, split_axis=0, concat_axis=0, tiled=True)


def together(*values):
    return lax.optimization_barrier(values)


def body(state, cotangent, spectral_weight, stencil_weight, pointwise_weight):
    nx, ny = lax.axis_size("gx"), lax.axis_size("gy")
    c, cx, cy, z = state.shape
    _, mz, mx, _, _ = spectral_weight.shape
    wide_x, wide_y = cx * nx, cy * ny
    alpha = 1.0 / math.sqrt(wide_x * wide_y * z)
    beta = 1.0 / math.sqrt(2 * MX * MY * MZ)
    double = np.where(np.arange(MZ) == 0, 1.0, 2.0)
    ones = np.ones(MZ)
    z_state = jnp.asarray(z_forward_table(alpha * ones)(nx, mz))
    z_grad = jnp.asarray(z_forward_table(double)(nx, mz))
    z_spectral = jnp.asarray(z_inverse_table(nx, mz, beta * double))
    z_back = jnp.asarray(z_inverse_table(nx, mz, alpha * beta * ones))
    x_fwd, x_inv = (jnp.asarray(t) for t in x_tables(wide_x, mz, mx))
    y_turn = jnp.asarray(y_table(wide_y))
    spread, gather = jnp.asarray(spread_table()), jnp.asarray(gather_table())
    lanes = cy * c
    x_rows = cx * 2 * mz

    def x_stage(table, block, lead, kind=F32, extra=0):
        rows = table.shape[0] // lead + extra
        return call(
            x_kernel,
            [((lead, rows, lanes), kind)],
            (table, block),
            mib=16,
            flops=2 * table.size * lanes,
            moved=8 * block.size,
        )[0]

    slab_shape = ((nx, x_rows, lanes), F32)
    turned_shape = ((cx, cy, c, z), BF16)

    conv_table, back_table = call(
        taps_kernel,
        [((9 * c, 4 * c), BF16)] * 2,
        (in_hbm(stencil_weight), in_hbm(pointwise_weight)),
        [pltpu.VMEM((27 * c, c), F32)],
        moved=stencil_weight.size * 6,
    )
    turned, slab = call(
        functools.partial(prep_kernel, nx),
        [turned_shape, slab_shape],
        (in_hbm(state), in_hbm(z_state)),
        flops=2 * 96 * state.size,
        moved=state.size * 5,
    )
    block = x_stage(x_fwd, swap(slab, "gx"), ny)
    block, conv_table, back_table, *faces = together(
        block, conv_table, back_table, *x_halos(turned)
    )
    modes_in, block = per_mode(
        mix_kernel,
        swap(block, "gy"),
        spectral_weight,
        spread,
        (y_turn,),
        (2 * c, BF16),
        F32,
        [pltpu.VMEM(spread.shape, BF16), pltpu.SemaphoreType.DMA]
        + [pltpu.VMEM((2 * QUAD * MY, SPAN), F32)] * 2
        + [pltpu.VMEM((2 * QUAD * MY, 2 * c), F32)],
    )
    block, *edges = together(block, *y_halos(turned, *faces))
    rim = (*faces, *edges)
    block = x_stage(x_inv, swap(block, "gy"), nx)
    stencil = conv(turned, rim, conv_table, False)
    output, grad, slab = call(
        functools.partial(gelu_kernel, nx),
        [((c, cx, cy, z), BF16), turned_shape, ((nx * ny, x_rows, lanes), BF16)],
        (stencil, swap(block, "gx"), cotangent, z_spectral, z_grad),
        [pltpu.VMEM(slab_shape[0], F32)],
        flops=2 * 192 * state.size,
        moved=state.size * 12,
    )

    grad_taps = weight_grad(grad, turned, rim)
    faces = x_halos(grad)
    edges = y_halos(grad, *faces)
    x_mine = x_fwd.reshape(ny, -1, x_fwd.shape[1])
    x_mine = lax.dynamic_index_in_dim(x_mine, lax.axis_index("gy"), 0, keepdims=False)
    block = swap(slab, ("gx", "gy"))
    block, grad_taps, *edges = together(block, grad_taps, *edges)
    mine = swap(grad_taps.reshape(nx, -1, 2 * c), "gx").sum(0)
    back_modes, block = per_mode(
        mix_back_kernel,
        block,
        spectral_weight,
        gather,
        (y_turn, x_mine),
        (2 * c, F32),
        BF16,
        [pltpu.VMEM((2 * QUAD * MY, c * c), BF16)],
    )
    packed = jnp.concatenate(jnp.split(mine, lanes // (2 * c)), axis=1).astype(BF16)
    extra = packed.shape[0]
    packed = jnp.broadcast_to(packed[None], (ny, extra, lanes))
    block = x_stage(
        x_inv, swap(jnp.concatenate([block, packed], axis=1), "gy"), nx, BF16, extra
    )
    stencil_back = conv(grad, (*faces, *edges), back_table, True)
    block, stencil_back = together(block, stencil_back)
    message = swap(block, "gx")
    grad_modes = outer(modes_in, back_modes, spread, spectral_weight.shape, alpha)
    grad_state, grad_stencil, grad_point = call(
        functools.partial(finish_kernel, nx, alpha),
        [((c, cx, cy, z), F32), ((c, 27 * c), F32), ((c, c), F32)],
        (stencil_back, message, z_back),
        [pltpu.VMEM(grad_taps.shape, F32), pltpu.VMEM((27 * c, c), F32)],
        flops=2 * 96 * state.size,
        moved=state.size * 10,
    )
    return (output, grad_state, grad_modes, grad_stencil, grad_point)


def solution(mesh):
    in_specs = (
        P(None, "gx", "gy", None),
        P(None, "gx", "gy", None),
        P(None, "gx", "gy", None, None),
        P(),
        P(),
    )
    out_specs = (
        P(None, "gx", "gy", None),
        P(None, "gx", "gy", None),
        P(None, "gx", "gy", None, None),
        P(),
        P(),
    )
    return jax.shard_map(body, mesh=mesh, in_specs=in_specs, out_specs=out_specs, check_vma=False)
```

```python
import functools
import math

import jax
import jax.numpy as jnp
import numpy as np
from jax import lax
from jax.experimental import pallas as pl
from jax.experimental.pallas import tpu as pltpu
from jax.sharding import PartitionSpec as P

C = 64
MX = 32
MY = 32
MZ = 16
Z = 128
MIB = 1 << 20

F32 = jnp.float32
BF16 = jnp.bfloat16


def angles(places, freqs, length):
    turns = np.outer(np.asarray(places), np.asarray(freqs)) % length
    return turns * (2.0 * np.pi / length)


def centred(count):
    steps = np.arange(count)
    return np.where(steps < count // 2, steps, steps - count)


def split(table, parts):
    rest = np.asarray(table, np.float64)
    out = []
    for _ in range(parts):
        piece = rest.astype(jnp.bfloat16)
        out.append(piece)
        rest = rest - piece.astype(np.float64)
    return out


def z_forward_table(scale):
    def build(nx, mz):
        theta = angles(np.arange(MZ), np.arange(Z), Z)
        pair = np.stack([np.cos(theta), -np.sin(theta)]) * scale[None, :, None]
        rows = pair.reshape(2, nx, mz, Z).transpose(1, 0, 2, 3).reshape(2 * MZ, Z)
        return np.concatenate(split(rows, 3), axis=0)

    return build


def z_inverse_table(nx, mz, scale):
    theta = angles(np.arange(MZ), np.arange(Z), Z)
    pair = np.stack([np.cos(theta), -np.sin(theta)]) * scale[None, :, None]
    rows = pair.reshape(2, nx, mz, Z).transpose(1, 0, 2, 3).reshape(2 * MZ, Z)
    high, low = split(rows, 2)
    return np.concatenate([high, high, low], axis=0)


def rotation(theta, sign):
    cosine, sine = np.cos(theta), sign * np.sin(theta)
    return np.stack([np.stack([cosine, -sine], 1), np.stack([sine, cosine], 1)])


def against_pieces(*tables):
    out = []
    for table in tables:
        high, low = split(table, 2)
        out.append(np.concatenate([high, high, low], axis=1))
    return out


def x_tables(wide, mz, mx):
    theta = angles(centred(MX), np.arange(wide), wide)
    eye = np.eye(mz)
    forward = np.einsum("rkRx,zZ->krzxRZ", rotation(theta, -1.0), eye)
    inverse = np.einsum("rxRk,zZ->xrzkRZ", rotation(theta.T, 1.0), eye)
    size_k, size_x = MX * 2 * mz, wide * 2 * mz
    forward = forward.reshape(MX // mx, mx, 2, mz, size_x).transpose(0, 2, 3, 1, 4)
    inverse = inverse.reshape(size_x, MX // mx, mx, 2, mz).transpose(0, 1, 3, 4, 2)
    return against_pieces(forward.reshape(size_k, size_x), inverse.reshape(size_x, size_k))


def y_table(wide):
    theta = angles(centred(MY), np.arange(wide), wide)
    forward = rotation(theta, -1.0).reshape(2 * MY, 2 * wide)
    inverse = rotation(theta.T, 1.0).reshape(2 * wide, 2 * MY)
    forward, inverse = against_pieces(forward, inverse)
    inverse = np.pad(inverse, ((0, 0), (0, forward.shape[1] - inverse.shape[1])))
    return np.concatenate([forward, inverse], axis=0)


def pieces(values):
    high = values.astype(BF16)
    low = (values - high.astype(F32)).astype(BF16)
    return jnp.concatenate([high, low, high], axis=0)


def z_forward(rows, table, out_ref, x, nx):
    got = lax.dot_general(table, rows, (((1,), (1,)), ((), ())), preferred_element_type=F32)
    size = 2 * MZ
    total = got[:size] + (got[size : 2 * size] + got[2 * size :])
    per = size // nx
    for owner in range(nx):
        out_ref[owner, x * per : (x + 1) * per, :] = total[owner * per : (owner + 1) * per]


def z_inverse(in_ref, table, x, nx):
    per = 2 * MZ // nx
    rows = jnp.concatenate(
        [in_ref[owner].astype(F32)[x * per : (x + 1) * per] for owner in range(nx)], axis=0
    )
    return lax.dot_general(
        pieces(rows), table, (((0,), (0,)), ((), ())), preferred_element_type=F32
    )


def prep_kernel(nx, field_ref, table_ref, turned_ref, slab_ref):
    c, cx, cy, z = field_ref.shape
    for x in range(cx):
        block = jnp.swapaxes(field_ref[:, x].astype(F32), 0, 1)
        turned = block.astype(BF16)
        turned_ref[x] = turned
        z_forward(turned.reshape(cy * c, z), table_ref[...], slab_ref, x, nx)


def plane_rows(p, cx, body_ref, xlo_ref, xhi_ref, ylo_ref, yhi_ref):
    cy = body_ref.shape[1]
    if p == 0:
        middle = [xlo_ref[y] for y in range(cy)]
    elif p == cx + 1:
        middle = [xhi_ref[y] for y in range(cy)]
    else:
        middle = [body_ref[p - 1, y] for y in range(cy)]
    return [ylo_ref[p]] + middle + [yhi_ref[p]]


def fill_shifts(blocks, rim_ref, flip=False):
    c, z = blocks[0].shape
    lane = lax.broadcasted_iota(jnp.int32, (c, z), 1)
    for y, block in enumerate(blocks):
        wide = block.astype(F32)
        before = jnp.where(lane == 0, 0.0, pltpu.roll(wide, 1, 1))
        after = jnp.where(lane == z - 1, 0.0, pltpu.roll(wide, z - 1, 1))
        if flip:
            before, after = after, before
        columns = slice(y * z, (y + 1) * z)
        rim_ref[0:c, columns] = before.astype(BF16)
        rim_ref[c : 2 * c, columns] = block
        rim_ref[2 * c : 3 * c, columns] = after.astype(BF16)
        rim_ref[3 * c : 4 * c, columns] = block


def conv_kernel(
    flip, body_ref, xlo_ref, xhi_ref, ylo_ref, yhi_ref, weight_ref, out_ref, rim_ref
):
    cx, cy, c, z = body_ref.shape
    for p in range(cx + 2):
        blocks = plane_rows(p, cx, body_ref, xlo_ref, xhi_ref, ylo_ref, yhi_ref)
        fill_shifts(blocks, rim_ref, flip)
        places = [a for a in range(3) if 0 <= p - (2 - a if flip else a) < cx]
        first = places[0]
        got = jnp.dot(
            weight_ref[first * 3 * c : (places[-1] + 1) * 3 * c, :],
            rim_ref[...],
            preferred_element_type=F32,
        )
        for a in places:
            x = p - (2 - a if flip else a)
            total = None
            for b in range(3):
                row = ((a - first) * 3 + b) * c
                skip = 2 - b if flip else b
                term = got[row : row + c, skip * z : (skip + cy) * z]
                total = term if total is None else total + term
            if p == x:
                out_ref[x] = total
            else:
                out_ref[x] += total


def weight_grad_kernel(
    grad_ref,
    body_ref,
    xlo_any,
    xhi_any,
    ylo_any,
    yhi_any,
    slab_ref,
    message_ref,
    out_ref,
    rim_ref,
    wide_ref,
    sum_ref,
    xlo_ref,
    xhi_ref,
    ylo_ref,
    yhi_ref,
    sem_ref,
):
    cx, cy, c, z = body_ref.shape
    group = 3 * c
    held = (xlo_ref, xhi_ref, ylo_ref, yhi_ref)
    copies = [
        pltpu.make_async_copy(given, ref, sem_ref.at[i])
        for i, (given, ref) in enumerate(zip((xlo_any, xhi_any, ylo_any, yhi_any), held))
    ]
    for copy in copies:
        copy.start()
    wide_ref[...] = jnp.zeros_like(wide_ref)
    for x in range(cx):
        for b in range(3):
            for y in range(cy):
                row = x * group + b * c
                wide_ref[row : row + c, (y + b) * z : (y + b + 1) * z] = grad_ref[x, y]
    sum_ref[...] = jnp.zeros_like(sum_ref)
    for copy in copies:
        copy.wait()
    for p in range(cx + 2):
        fill_shifts(plane_rows(p, cx, body_ref, xlo_ref, xhi_ref, ylo_ref, yhi_ref), rim_ref)
        first, last = max(0, p - 2), min(cx - 1, p)
        got = lax.dot_general(
            wide_ref[first * group : (last + 1) * group, :],
            rim_ref[...],
            (((1,), (1,)), ((), ())),
            preferred_element_type=F32,
        )
        for x in range(first, last + 1):
            a = p - x
            sum_ref[a * group : (a + 1) * group, :] += got[
                (x - first) * group : (x - first + 1) * group, :
            ]
    out_ref[: 9 * c] = sum_ref[:, : 2 * c]
    last = [sum_ref[k * c : (k + 1) * c, 2 * c : 3 * c] for k in range(9)]
    last.append(jnp.zeros((c, c), F32))
    for k in range(5):
        row = (9 + k) * c
        out_ref[row : row + c] = jnp.concatenate(last[2 * k : 2 * k + 2], axis=1)
    out_ref[14 * c :] = jnp.zeros((2 * c, 2 * c), F32)
    devices, rows, lanes = message_ref.shape
    nx, skip, _ = slab_ref.shape
    per, tiles_in = rows - skip, lanes // (2 * c)
    for device in range(devices):
        start = device * per * tiles_in
        share = [out_ref[start + t * per : start + (t + 1) * per] for t in range(tiles_in)]
        message_ref[device] = jnp.concatenate(
            [slab_ref[device // (devices // nx)], jnp.concatenate(share, axis=1)], axis=0
        ).astype(BF16)


def gelu_kernel(
    nx,
    stencil_ref,
    slab_ref,
    cot_ref,
    inverse_ref,
    forward_ref,
    out_ref,
    turned_ref,
    back_ref,
):
    c, cx, cy, z = cot_ref.shape
    root = math.sqrt(2.0 / math.pi)
    for x in range(cx):
        spectral = z_inverse(slab_ref, inverse_ref[...], x, nx).reshape(cy, c, z)
        stencil = jnp.stack([stencil_ref[x, :, y * z : (y + 1) * z] for y in range(cy)])
        pre = spectral + stencil
        cot = jnp.swapaxes(cot_ref[:, x].astype(F32), 0, 1)
        square = pre * pre
        bent = jnp.tanh(root * (pre * (1.0 + 0.044715 * square)))
        half = 0.5 + 0.5 * bent
        slope = half + (0.5 * pre) * (1.0 - bent * bent) * (root * (1.0 + 0.134145 * square))
        out_ref[:, x] = jnp.swapaxes(pre * half, 0, 1).astype(BF16)
        grad = (cot * slope).astype(BF16)
        turned_ref[x] = grad
        z_forward(grad.reshape(cy * c, z), forward_ref[...], back_ref, x, nx)


def finish_kernel(
    nx,
    scale,
    stencil_ref,
    message_ref,
    inverse_ref,
    out_ref,
    taps_ref,
    point_ref,
    packed_ref,
    turned_ref,
    slab_ref,
):
    c, cx, cy, z = out_ref.shape
    ny = message_ref.shape[0] // nx
    for owner in range(nx):
        parts = [message_ref[owner * ny + j].astype(F32) for j in range(ny)]
        slab_ref[owner] = sum(parts[1:], parts[0])[: slab_ref.shape[1]]
    for x in range(cx):
        spectral = z_inverse(slab_ref, inverse_ref[...], x, nx).reshape(cy, c, z)
        stencil = jnp.stack([stencil_ref[x, :, y * z : (y + 1) * z] for y in range(cy)])
        out_ref[:, x] = jnp.swapaxes(spectral + stencil, 0, 1)
    skip = slab_ref.shape[1]
    unpack(scale, skip, message_ref, taps_ref, point_ref, packed_ref, turned_ref)


def x_kernel(table_ref, data_ref, out_ref):
    flat = pieces(data_ref[...].reshape(-1, data_ref.shape[2]))
    got = jnp.dot(table_ref[...], flat, preferred_element_type=F32)
    count = got.shape[0] // out_ref.shape[0]
    for owner in range(out_ref.shape[0]):
        out_ref[owner] = got[owner * count : (owner + 1) * count]


def taps_kernel(taps_ref, point_ref, forward_ref, back_ref, turned_ref):
    turned_ref[...] = taps_ref[...].astype(F32).T
    forward_ref[...] = jnp.zeros_like(forward_ref)
    back_ref[...] = jnp.zeros_like(back_ref)
    for tap in range(27):
        rows = slice(tap // 3 * C, (tap // 3 + 1) * C)
        columns = slice(tap % 3 * C, (tap % 3 + 1) * C)
        block = turned_ref[pl.ds(tap, C, stride=27), :]
        back_ref[rows, columns] = block.astype(BF16)
        forward_ref[rows, columns] = block.T.astype(BF16)
    point = point_ref[...].astype(F32)
    forward_ref[4 * C : 5 * C, 3 * C :] = point.astype(BF16)
    back_ref[4 * C : 5 * C, 3 * C :] = point.T.astype(BF16)


def unpack(scale, skip, message_ref, taps_ref, point_ref, packed_ref, turned_ref):
    devices, rows, lanes = message_ref.shape
    per, tiles_in = rows - skip, lanes // 128
    for owner in range(devices):
        message = message_ref[owner].astype(F32)[skip:]
        for tile in range(tiles_in):
            row = (owner * tiles_in + tile) * per
            packed_ref[row : row + per] = message[:, tile * 128 : (tile + 1) * 128]
    for tap in range(27):
        group, e = tap // 3, tap % 3
        if e < 2:
            block = packed_ref[group * C : (group + 1) * C, e * C : (e + 1) * C]
        else:
            row = (9 + group // 2) * C
            block = packed_ref[row : row + C, group % 2 * C : (group % 2 + 1) * C]
        block = block * scale
        if tap == 13:
            point_ref[...] = block
        turned_ref[pl.ds(tap, C, stride=27), :] = block.T
    taps_ref[...] = turned_ref[...].T


QUAD = 4
SPAN = 8 * C


def y_forward(mz, blocks, table_ref, rows_ref, store):
    ny, cy = len(blocks), blocks[0].shape[1] // C
    count = rows_ref.shape[1] // C
    for owner in range(ny):
        data = blocks[owner]
        for part in range(2):
            for kz in range(mz):
                mx = count // mz
                start = (part * mz + kz) * mx
                block = data[start : start + mx]
                block = jnp.stack([block[:, y * C : (y + 1) * C] for y in range(cy)])
                block = jnp.swapaxes(block, 0, 1)
                row = (part * ny + owner) * cy
                for kx in range(mx):
                    column = (kz * mx + kx) * C
                    rows_ref[row : row + cy, column : column + C] = block[kx]
    got = jnp.dot(table_ref[: 2 * MY], pieces(rows_ref[...]), preferred_element_type=F32)
    for q in range(count):
        block = got[:, q * C : (q + 1) * C]
        for part in range(2):
            store(q // QUAD, part, q % QUAD, block[part * MY : (part + 1) * MY])


def y_inverse(mz, sum_ref, table_ref, block_ref):
    rows = [
        jnp.concatenate(
            [
                sum_ref[group, place(part, pair), :]
                for group in range(sum_ref.shape[0])
                for pair in range(QUAD)
            ],
            axis=1,
        )
        for part in range(2)
    ]
    got = jnp.dot(
        table_ref[2 * MY :, : 6 * MY],
        pieces(jnp.concatenate(rows, axis=0)),
        preferred_element_type=F32,
    )
    ny, _, lanes = block_ref.shape
    cy = lanes // C
    count = got.shape[1] // C
    mx = count // mz
    for owner in range(ny):
        for part in range(2):
            for kz in range(mz):
                row = (part * ny + owner) * cy
                block = got[row : row + cy, kz * mx * C : (kz + 1) * mx * C]
                block = jnp.stack([block[:, kx * C : (kx + 1) * C] for kx in range(mx)])
                block = jnp.swapaxes(block, 0, 1)
                start = (part * mz + kz) * mx
                for y in range(cy):
                    block_ref[owner, start : start + mx, y * C : (y + 1) * C] = block[y]


def place(part, pair):
    start = (part * QUAD + pair) * MY
    return slice(start, start + MY)


def spread_table():
    return np.tile(np.kron(np.eye(C), np.ones((1, C))), (2, 1)).astype(jnp.bfloat16)


def gather_table():
    return np.kron(np.eye(SPAN // C), np.ones((1, C))).astype(jnp.bfloat16)


def spread_modes(modes, table_ref, spread_refs):
    count = C * C // SPAN
    made = set()

    def get(piece):
        for p in range(piece, min(piece + 2, count)):
            if p not in made:
                made.add(p)
                spread_refs[p % 2][...] = jnp.dot(
                    modes, table_ref[:, p * SPAN : (p + 1) * SPAN], preferred_element_type=F32
                )
        return spread_refs[piece % 2]

    return get


def weight_copies(weight_ref, held_ref, sem_ref):
    per = weight_ref.shape[2] // QUAD
    return [
        pltpu.make_async_copy(
            weight_ref.at[:, g // per, g % per * QUAD : (g % per + 1) * QUAD],
            held_ref.at[g],
            sem_ref.at[g],
        )
        for g in range(held_ref.shape[0])
    ]


def mix_kernel(
    mz,
    data_ref,
    weight_ref,
    table_ref,
    turn_ref,
    modes_ref,
    out_ref,
    sum_ref,
    rows_ref,
    held_ref,
    sem_ref,
    spread_ref,
    spread_sem_ref,
    even_ref,
    odd_ref,
    total_ref,
):
    copies = weight_copies(weight_ref, held_ref, sem_ref)
    table_copy = pltpu.make_async_copy(table_ref, spread_ref, spread_sem_ref)
    table_copy.start()
    for copy in copies:
        copy.start()

    def store(group, part, pair, values):
        high = values.astype(BF16)
        low = (values - high.astype(F32)).astype(BF16)
        modes_ref[group, place(part, pair), :] = jnp.concatenate([high, low], axis=1)

    blocks = [data_ref[owner] for owner in range(data_ref.shape[0])]
    y_forward(mz, blocks, turn_ref, rows_ref, store)
    table_copy.wait()
    for group, copy in enumerate(copies):
        copy.wait()
        spread = spread_modes(modes_ref[group], spread_ref, (even_ref, odd_ref))
        for piece in range(C * C // SPAN):
            modes = spread(piece)
            for pair in range(QUAD):
                real = imag = None
                for tile in range(SPAN // (2 * C)):
                    inside = slice(tile * 2 * C, (tile + 1) * 2 * C)
                    columns = slice(piece * SPAN + inside.start, piece * SPAN + inside.stop)
                    mode_re = modes[place(0, pair), inside]
                    mode_im = modes[place(1, pair), inside]
                    weight_re = held_ref[group, 0, pair, :, columns].astype(F32)
                    weight_im = held_ref[group, 1, pair, :, columns].astype(F32)
                    term_re = mode_re * weight_re - mode_im * weight_im
                    term_im = mode_re * weight_im + mode_im * weight_re
                    real = term_re if real is None else real + term_re
                    imag = term_im if imag is None else imag + term_im
                if piece:
                    real += total_ref[place(0, pair), :]
                    imag += total_ref[place(1, pair), :]
                total_ref[place(0, pair), :] = real
                total_ref[place(1, pair), :] = imag
        total = total_ref[...]
        sum_ref[group] = total[:, :C] + total[:, C:]
    y_inverse(mz, sum_ref, turn_ref, out_ref)


def mix_back_kernel(
    mz,
    data_ref,
    weight_ref,
    table_ref,
    turn_ref,
    x_ref,
    x_back_ref,
    modes_ref,
    out_ref,
    sum_ref,
    rows_ref,
    held_ref,
    sem_ref,
    term_ref,
    block_ref,
):
    copies = weight_copies(weight_ref, held_ref, sem_ref)
    for copy in copies:
        copy.start()

    def store(group, part, pair, values):
        modes_ref[group, place(part, pair), :] = jnp.concatenate([values, values], axis=1)

    devices, ny = data_ref.shape[0], block_ref.shape[0]
    size = x_ref.shape[1] // 3
    skip = size * ny // devices
    share = data_ref[0].astype(F32)[skip:]
    for device in range(1, devices):
        share += data_ref[device].astype(F32)[skip:]
    blocks = []
    for owner in range(ny):
        rows = jnp.concatenate(
            [data_ref[i].astype(F32)[:skip] for i in range(owner, devices, ny)], axis=0
        ).astype(BF16)
        blocks.append(
            jnp.dot(x_ref[:, :size], rows, preferred_element_type=F32)
            + jnp.dot(x_ref[:, 2 * size :], rows, preferred_element_type=F32)
        )
    y_forward(mz, blocks, turn_ref, rows_ref, store)
    for group, copy in enumerate(copies):
        copy.wait()
        total = []
        for piece in range(C * C // SPAN):
            for pair in range(QUAD):
                mode_re = modes_ref[group, place(0, pair), :]
                mode_im = modes_ref[group, place(1, pair), :]
                for tile in range(SPAN // (2 * C)):
                    start = piece * SPAN + tile * 2 * C
                    columns = slice(start, start + 2 * C)
                    weight_re = held_ref[group, 0, pair, :, columns].astype(F32)
                    weight_im = held_ref[group, 1, pair, :, columns].astype(F32)
                    term_ref[place(0, pair), columns] = (
                        weight_re * mode_re + weight_im * mode_im
                    ).astype(BF16)
                    term_ref[place(1, pair), columns] = (
                        weight_re * mode_im - weight_im * mode_re
                    ).astype(BF16)
            total.append(
                lax.dot_general(
                    table_ref[...],
                    term_ref[:, piece * SPAN : (piece + 1) * SPAN],
                    (((1,), (1,)), ((), ())),
                    preferred_element_type=F32,
                )
            )
        sum_ref[group] = jnp.concatenate(total, axis=0).T
    y_inverse(mz, sum_ref, turn_ref, block_ref)
    for owner in range(ny):
        got = jnp.dot(x_back_ref[...], pieces(block_ref[owner]), preferred_element_type=F32)
        for i in range(devices // ny):
            rows = got[i * skip : (i + 1) * skip]
            out_ref[i * ny + owner] = jnp.concatenate([rows, share], axis=0).astype(BF16)


def outer_kernel(alpha, modes_ref, back_ref, table_ref, out_ref):
    count = C * C // SPAN
    made = lambda piece: jnp.dot(
        modes_ref[0],
        table_ref[:, piece * SPAN : (piece + 1) * SPAN],
        preferred_element_type=F32,
    )
    ahead = made(0)
    for piece in range(count):
        modes = ahead
        if piece + 1 < count:
            ahead = made(piece + 1)
        for pair in range(QUAD):
            back_re = back_ref[0, place(0, pair), :] * alpha
            back_im = back_ref[0, place(1, pair), :] * alpha
            for tile in range(SPAN // (2 * C)):
                inside = slice(tile * 2 * C, (tile + 1) * 2 * C)
                columns = slice(piece * SPAN + inside.start, piece * SPAN + inside.stop)
                mode_re = modes[place(0, pair), inside]
                mode_im = modes[place(1, pair), inside]
                out_ref[0, 0, pair, :, columns] = mode_re * back_re + mode_im * back_im
                out_ref[1, 0, pair, :, columns] = mode_re * back_im - mode_im * back_re


def in_hbm(value):
    return pltpu.with_memory_space_constraint(value, pltpu.HBM)


def whole():
    return pl.BlockSpec(memory_space=pltpu.VMEM)


def params(mib):
    return pltpu.CompilerParams(vmem_limit_bytes=mib * MIB)


def cost(flops, moved):
    return pl.CostEstimate(flops=int(flops), bytes_accessed=int(moved), transcendentals=0)


def call(kernel, outs, args, scratch=(), mib=24, flops=0, moved=0, anywhere=()):
    return pl.pallas_call(
        kernel,
        out_shape=[jax.ShapeDtypeStruct(*out) for out in outs],
        in_specs=[
            pl.BlockSpec(memory_space=pl.ANY) if i in anywhere else whole()
            for i in range(len(args))
        ],
        out_specs=[whole() for _ in outs],
        scratch_shapes=list(scratch),
        compiler_params=params(mib),
        cost_estimate=cost(flops, moved),
    )(*args)


def per_mode(kernel, data, weight, table, tables, modes, scratch=()):
    _, mz, mx, my, wide = weight.shape
    groups = mz * mx // QUAD
    rows = 2 * QUAD * MY
    modes_shape = (groups, rows, modes[0])
    return pl.pallas_call(
        functools.partial(kernel, mz),
        in_specs=[
            whole(),
            pl.BlockSpec(memory_space=pl.ANY),
            pl.BlockSpec(memory_space=pl.ANY) if kernel is mix_kernel else whole(),
        ]
        + [whole() for _ in tables],
        out_specs=[whole(), whole()],
        out_shape=[
            jax.ShapeDtypeStruct(modes_shape, modes[1]),
            jax.ShapeDtypeStruct(data.shape, data.dtype),
        ],
        scratch_shapes=[
            pltpu.VMEM((groups, rows, C), F32),
            pltpu.VMEM((tables[0].shape[0] - 2 * MY, mz * mx * C), F32),
            pltpu.VMEM((groups, 2, QUAD, my, wide), BF16),
            pltpu.SemaphoreType.DMA((groups,)),
            *scratch,
        ],
        compiler_params=params(24),
        cost_estimate=cost(weight.size * 8, weight.size * 2),
    )(data, in_hbm(weight), in_hbm(table), *tables)


def outer(modes, back, table, shape, alpha):
    per = shape[2] // QUAD
    group = lambda ref: pl.BlockSpec((1,) + ref.shape[1:], lambda step: (step, 0, 0))
    return pl.pallas_call(
        functools.partial(outer_kernel, alpha),
        grid=(modes.shape[0],),
        in_specs=[group(modes), group(back), pl.BlockSpec(table.shape, lambda step: (0, 0))],
        out_specs=pl.BlockSpec(
            (2, 1, QUAD) + shape[3:], lambda step: (0, step // per, step % per, 0, 0)
        ),
        out_shape=jax.ShapeDtypeStruct(shape, F32),
        compiler_params=params(20),
        cost_estimate=cost(math.prod(shape) * 4, math.prod(shape) * 4),
    )(modes, back, in_hbm(table))


def shift(block, axis, step):
    count = lax.axis_size(axis)
    pairs = [(i, i + step) for i in range(count) if 0 <= i + step < count]
    return lax.ppermute(block, axis, pairs)


def x_halos(turned):
    return shift(turned[-1], "gx", 1), shift(turned[0], "gx", -1)


def y_halos(turned, xlo, xhi):
    edge = lambda y: jnp.concatenate([xlo[None, y], turned[:, y], xhi[None, y]], axis=0)
    return shift(edge(-1), "gy", 1), shift(edge(0), "gy", -1)


def conv(turned, rim, weight, flip):
    cx, cy, c, z = turned.shape
    return call(
        functools.partial(conv_kernel, flip),
        [((cx, c, cy * z), F32)],
        (turned, *map(in_hbm, rim), in_hbm(weight)),
        [pltpu.VMEM((4 * c, (cy + 2) * z), BF16)],
        mib=32,
        flops=2 * 27 * c * c * cx * cy * z,
        moved=turned.size * 8,
    )[0]


def weight_grad(grad, turned, rim, slab, devices):
    cx, cy, c, z = turned.shape
    _, skip, lanes = slab.shape
    extra = 16 * c * 2 * c // (devices * lanes)
    return call(
        weight_grad_kernel,
        [((devices, skip + extra, lanes), BF16)],
        (grad, turned, *map(in_hbm, rim), slab),
        [
            pltpu.VMEM((16 * c, 2 * c), F32),
            pltpu.VMEM((4 * c, (cy + 2) * z), BF16),
            pltpu.VMEM((cx * 3 * c, (cy + 2) * z), BF16),
            pltpu.VMEM((9 * c, 4 * c), F32),
            *(pltpu.VMEM(halo.shape, BF16) for halo in rim),
            pltpu.SemaphoreType.DMA((len(rim),)),
        ],
        mib=32,
        flops=2 * 27 * c * c * cx * cy * z,
        moved=turned.size * 8,
        anywhere=(2, 3, 4, 5),
    )[0]


def swap(block, axis):
    return lax.all_to_all(block, axis, split_axis=0, concat_axis=0, tiled=True)


def together(*values):
    return lax.optimization_barrier(values)


def body(state, cotangent, spectral_weight, stencil_weight, pointwise_weight):
    nx, ny = lax.axis_size("gx"), lax.axis_size("gy")
    c, cx, cy, z = state.shape
    _, mz, mx, _, _ = spectral_weight.shape
    wide_x, wide_y = cx * nx, cy * ny
    alpha = 1.0 / math.sqrt(wide_x * wide_y * z)
    beta = 1.0 / math.sqrt(2 * MX * MY * MZ)
    double = np.where(np.arange(MZ) == 0, 1.0, 2.0)
    ones = np.ones(MZ)
    z_state = jnp.asarray(z_forward_table(alpha * ones)(nx, mz))
    z_grad = jnp.asarray(z_forward_table(double)(nx, mz))
    z_spectral = jnp.asarray(z_inverse_table(nx, mz, beta * double))
    z_back = jnp.asarray(z_inverse_table(nx, mz, alpha * beta * ones))
    x_fwd, x_inv = (jnp.asarray(t) for t in x_tables(wide_x, mz, mx))
    y_turn = jnp.asarray(y_table(wide_y))
    spread, gather = jnp.asarray(spread_table()), jnp.asarray(gather_table())
    lanes = cy * c
    x_rows = cx * 2 * mz

    def x_stage(table, block, lead):
        return call(
            x_kernel,
            [((lead, table.shape[0] // lead, lanes), F32)],
            (table, block),
            mib=16,
            flops=2 * table.size * lanes,
            moved=8 * block.size,
        )[0]

    slab_shape = ((nx, x_rows, lanes), F32)
    turned_shape = ((cx, cy, c, z), BF16)

    conv_table, back_table = call(
        taps_kernel,
        [((9 * c, 4 * c), BF16)] * 2,
        (in_hbm(stencil_weight), in_hbm(pointwise_weight)),
        [pltpu.VMEM((27 * c, c), F32)],
        moved=stencil_weight.size * 6,
    )
    turned, slab = call(
        functools.partial(prep_kernel, nx),
        [turned_shape, slab_shape],
        (in_hbm(state), in_hbm(z_state)),
        flops=2 * 96 * state.size,
        moved=state.size * 5,
    )
    here = lax.axis_index("gy")
    x_mine = x_fwd.reshape(ny, -1, x_fwd.shape[1])
    x_mine = lax.dynamic_index_in_dim(x_mine, here, 0, keepdims=False)
    x_back = x_inv.reshape(x_inv.shape[0], 3, ny, -1)
    x_back = lax.dynamic_index_in_dim(x_back, here, 2, keepdims=False)
    x_back = x_back.reshape(x_inv.shape[0], -1)

    block = x_stage(x_fwd, swap(slab, "gx"), ny)
    block, conv_table, back_table, x_mine, x_back, *faces = together(
        block, conv_table, back_table, x_mine, x_back, *x_halos(turned)
    )
    modes_in, block = per_mode(
        mix_kernel,
        swap(block, "gy"),
        spectral_weight,
        spread,
        (y_turn,),
        (2 * c, BF16),
        [pltpu.VMEM(spread.shape, BF16), pltpu.SemaphoreType.DMA]
        + [pltpu.VMEM((2 * QUAD * MY, SPAN), F32)] * 2
        + [pltpu.VMEM((2 * QUAD * MY, 2 * c), F32)],
    )
    block, *edges = together(block, *y_halos(turned, *faces))
    rim = (*faces, *edges)
    block = x_stage(x_inv, swap(block, "gy"), nx)
    stencil = conv(turned, rim, conv_table, False)
    output, grad, slab = call(
        functools.partial(gelu_kernel, nx),
        [((c, cx, cy, z), BF16), turned_shape, slab_shape],
        (stencil, swap(block, "gx"), cotangent, z_spectral, z_grad),
        flops=2 * 192 * state.size,
        moved=state.size * 12,
    )

    message = weight_grad(grad, turned, rim, slab, nx * ny)
    faces = x_halos(grad)
    edges = y_halos(grad, *faces)
    message, *edges = together(swap(message, ("gx", "gy")), *edges)
    back_modes, message = per_mode(
        mix_back_kernel,
        message,
        spectral_weight,
        gather,
        (y_turn, x_mine, x_back),
        (2 * c, F32),
        [
            pltpu.VMEM((2 * QUAD * MY, c * c), BF16),
            pltpu.VMEM((ny, 2 * mz * mx, lanes), F32),
        ],
    )
    message = swap(message, ("gx", "gy"))
    stencil_back = conv(grad, (*faces, *edges), back_table, True)
    grad_modes = outer(modes_in, back_modes, spread, spectral_weight.shape, alpha)
    grad_state, grad_stencil, grad_point = call(
        functools.partial(finish_kernel, nx, alpha),
        [((c, cx, cy, z), F32), ((c, 27 * c), F32), ((c, c), F32)],
        (stencil_back, message, z_back),
        [
            pltpu.VMEM((16 * c, 2 * c), F32),
            pltpu.VMEM((27 * c, c), F32),
            pltpu.VMEM(slab_shape[0], F32),
        ],
        flops=2 * 96 * state.size,
        moved=state.size * 10,
    )
    return (output, grad_state, grad_modes, grad_stencil, grad_point)


def solution(mesh):
    in_specs = (
        P(None, "gx", "gy", None),
        P(None, "gx", "gy", None),
        P(None, "gx", "gy", None, None),
        P(),
        P(),
    )
    out_specs = (
        P(None, "gx", "gy", None),
        P(None, "gx", "gy", None),
        P(None, "gx", "gy", None, None),
        P(),
        P(),
    )
    return jax.shard_map(body, mesh=mesh, in_specs=in_specs, out_specs=out_specs, check_vma=False)
```

```python
import functools
import math

import jax
import jax.numpy as jnp
import numpy as np
from jax import lax
from jax.experimental import pallas as pl
from jax.experimental.pallas import tpu as pltpu
from jax.sharding import PartitionSpec as P

C = 64
MX = 32
MY = 32
MZ = 16
Z = 128
MIB = 1 << 20

F32 = jnp.float32
BF16 = jnp.bfloat16


def angles(places, freqs, length):
    turns = np.outer(np.asarray(places), np.asarray(freqs)) % length
    return turns * (2.0 * np.pi / length)


def centred(count):
    steps = np.arange(count)
    return np.where(steps < count // 2, steps, steps - count)


def split(table, parts):
    rest = np.asarray(table, np.float64)
    out = []
    for _ in range(parts):
        piece = rest.astype(jnp.bfloat16)
        out.append(piece)
        rest = rest - piece.astype(np.float64)
    return out


def z_forward_table(scale):
    def build(nx, mz):
        theta = angles(np.arange(MZ), np.arange(Z), Z)
        pair = np.stack([np.cos(theta), -np.sin(theta)]) * scale[None, :, None]
        rows = pair.reshape(2, nx, mz, Z).transpose(1, 0, 2, 3).reshape(2 * MZ, Z)
        return np.concatenate(split(rows, 3), axis=0)

    return build


def z_inverse_table(nx, mz, scale):
    theta = angles(np.arange(MZ), np.arange(Z), Z)
    pair = np.stack([np.cos(theta), -np.sin(theta)]) * scale[None, :, None]
    rows = pair.reshape(2, nx, mz, Z).transpose(1, 0, 2, 3).reshape(2 * MZ, Z)
    high, low = split(rows, 2)
    return np.concatenate([high, high, low], axis=0)


def rotation(theta, sign):
    cosine, sine = np.cos(theta), sign * np.sin(theta)
    return np.stack([np.stack([cosine, -sine], 1), np.stack([sine, cosine], 1)])


def against_pieces(*tables):
    out = []
    for table in tables:
        high, low = split(table, 2)
        out.append(np.concatenate([high, high, low], axis=1))
    return out


def x_tables(wide, mz, mx):
    theta = angles(centred(MX), np.arange(wide), wide)
    eye = np.eye(mz)
    forward = np.einsum("rkRx,zZ->krzxRZ", rotation(theta, -1.0), eye)
    inverse = np.einsum("rxRk,zZ->xrzkRZ", rotation(theta.T, 1.0), eye)
    size_k, size_x = MX * 2 * mz, wide * 2 * mz
    forward = forward.reshape(MX // mx, mx, 2, mz, size_x).transpose(0, 2, 3, 1, 4)
    inverse = inverse.reshape(size_x, MX // mx, mx, 2, mz).transpose(0, 1, 3, 4, 2)
    return against_pieces(forward.reshape(size_k, size_x), inverse.reshape(size_x, size_k))


def y_table(wide):
    theta = angles(centred(MY), np.arange(wide), wide)
    forward = rotation(theta, -1.0).reshape(2 * MY, 2 * wide)
    inverse = rotation(theta.T, 1.0).reshape(2 * wide, 2 * MY)
    forward, inverse = against_pieces(forward, inverse)
    inverse = np.pad(inverse, ((0, 0), (0, forward.shape[1] - inverse.shape[1])))
    return np.concatenate([forward, inverse], axis=0)


def pieces(values):
    high = values.astype(BF16)
    low = (values - high.astype(F32)).astype(BF16)
    return jnp.concatenate([high, low, high], axis=0)


def z_forward(rows, table, out_ref, x, nx):
    got = lax.dot_general(table, rows, (((1,), (1,)), ((), ())), preferred_element_type=F32)
    size = 2 * MZ
    total = got[:size] + (got[size : 2 * size] + got[2 * size :])
    per = size // nx
    for owner in range(nx):
        out_ref[owner, x * per : (x + 1) * per, :] = total[owner * per : (owner + 1) * per]


def z_inverse(in_ref, table, x, nx):
    per = 2 * MZ // nx
    rows = jnp.concatenate(
        [in_ref[owner].astype(F32)[x * per : (x + 1) * per] for owner in range(nx)], axis=0
    )
    return lax.dot_general(
        pieces(rows), table, (((0,), (0,)), ((), ())), preferred_element_type=F32
    )


def prep_kernel(nx, field_ref, table_ref, turned_ref, slab_ref):
    c, cx, cy, z = field_ref.shape
    for x in range(cx):
        block = jnp.swapaxes(field_ref[:, x].astype(F32), 0, 1)
        turned = block.astype(BF16)
        turned_ref[x] = turned
        z_forward(turned.reshape(cy * c, z), table_ref[...], slab_ref, x, nx)


def plane_rows(p, cx, body_ref, xlo_ref, xhi_ref, ylo_ref, yhi_ref):
    cy = body_ref.shape[1]
    if p == 0:
        middle = [xlo_ref[y] for y in range(cy)]
    elif p == cx + 1:
        middle = [xhi_ref[y] for y in range(cy)]
    else:
        middle = [body_ref[p - 1, y] for y in range(cy)]
    return [ylo_ref[p]] + middle + [yhi_ref[p]]


def fill_shifts(blocks, rim_ref, flip=False):
    c, z = blocks[0].shape
    lane = lax.broadcasted_iota(jnp.int32, (c, z), 1)
    for y, block in enumerate(blocks):
        wide = block.astype(F32)
        before = jnp.where(lane == 0, 0.0, pltpu.roll(wide, 1, 1))
        after = jnp.where(lane == z - 1, 0.0, pltpu.roll(wide, z - 1, 1))
        if flip:
            before, after = after, before
        columns = slice(y * z, (y + 1) * z)
        rim_ref[0:c, columns] = before.astype(BF16)
        rim_ref[c : 2 * c, columns] = block
        rim_ref[2 * c : 3 * c, columns] = after.astype(BF16)
        rim_ref[3 * c : 4 * c, columns] = block


def conv_kernel(
    flip, body_ref, xlo_ref, xhi_ref, ylo_ref, yhi_ref, weight_ref, out_ref, rim_ref
):
    cx, cy, c, z = body_ref.shape
    for p in range(cx + 2):
        blocks = plane_rows(p, cx, body_ref, xlo_ref, xhi_ref, ylo_ref, yhi_ref)
        fill_shifts(blocks, rim_ref, flip)
        places = [a for a in range(3) if 0 <= p - (2 - a if flip else a) < cx]
        first = places[0]
        got = jnp.dot(
            weight_ref[first * 3 * c : (places[-1] + 1) * 3 * c, :],
            rim_ref[...],
            preferred_element_type=F32,
        )
        for a in places:
            x = p - (2 - a if flip else a)
            total = None
            for b in range(3):
                row = ((a - first) * 3 + b) * c
                skip = 2 - b if flip else b
                term = got[row : row + c, skip * z : (skip + cy) * z]
                total = term if total is None else total + term
            if p == x:
                out_ref[x] = total
            else:
                out_ref[x] += total


def weight_grad_kernel(
    grad_ref,
    body_ref,
    xlo_any,
    xhi_any,
    ylo_any,
    yhi_any,
    out_ref,
    rim_ref,
    wide_ref,
    sum_ref,
    xlo_ref,
    xhi_ref,
    ylo_ref,
    yhi_ref,
    sem_ref,
):
    cx, cy, c, z = body_ref.shape
    group = 3 * c
    held = (xlo_ref, xhi_ref, ylo_ref, yhi_ref)
    copies = [
        pltpu.make_async_copy(given, ref, sem_ref.at[i])
        for i, (given, ref) in enumerate(zip((xlo_any, xhi_any, ylo_any, yhi_any), held))
    ]
    for copy in copies:
        copy.start()
    wide_ref[...] = jnp.zeros_like(wide_ref)
    for x in range(cx):
        for b in range(3):
            for y in range(cy):
                row = x * group + b * c
                wide_ref[row : row + c, (y + b) * z : (y + b + 1) * z] = grad_ref[x, y]
    sum_ref[...] = jnp.zeros_like(sum_ref)
    for copy in copies:
        copy.wait()
    for p in range(cx + 2):
        fill_shifts(plane_rows(p, cx, body_ref, xlo_ref, xhi_ref, ylo_ref, yhi_ref), rim_ref)
        first, last = max(0, p - 2), min(cx - 1, p)
        got = lax.dot_general(
            wide_ref[first * group : (last + 1) * group, :],
            rim_ref[...],
            (((1,), (1,)), ((), ())),
            preferred_element_type=F32,
        )
        for x in range(first, last + 1):
            a = p - x
            sum_ref[a * group : (a + 1) * group, :] += got[
                (x - first) * group : (x - first + 1) * group, :
            ]
    out_ref[: 9 * c] = sum_ref[:, : 2 * c]
    last = [sum_ref[k * c : (k + 1) * c, 2 * c : 3 * c] for k in range(9)]
    last.append(jnp.zeros((c, c), F32))
    for k in range(5):
        row = (9 + k) * c
        out_ref[row : row + c] = jnp.concatenate(last[2 * k : 2 * k + 2], axis=1)
    out_ref[14 * c :] = jnp.zeros((2 * c, 2 * c), F32)


def gelu_kernel(
    nx,
    stencil_ref,
    slab_ref,
    cot_ref,
    inverse_ref,
    forward_ref,
    out_ref,
    turned_ref,
    message_ref,
    back_ref,
):
    c, cx, cy, z = cot_ref.shape
    root = math.sqrt(2.0 / math.pi)
    for x in range(cx):
        spectral = z_inverse(slab_ref, inverse_ref[...], x, nx).reshape(cy, c, z)
        stencil = jnp.stack([stencil_ref[x, :, y * z : (y + 1) * z] for y in range(cy)])
        pre = spectral + stencil
        cot = jnp.swapaxes(cot_ref[:, x].astype(F32), 0, 1)
        square = pre * pre
        bent = jnp.tanh(root * (pre * (1.0 + 0.044715 * square)))
        half = 0.5 + 0.5 * bent
        slope = half + (0.5 * pre) * (1.0 - bent * bent) * (root * (1.0 + 0.134145 * square))
        out_ref[:, x] = jnp.swapaxes(pre * half, 0, 1).astype(BF16)
        grad = (cot * slope).astype(BF16)
        turned_ref[x] = grad
        z_forward(grad.reshape(cy * c, z), forward_ref[...], back_ref, x, nx)
    ny = message_ref.shape[0] // nx
    for owner in range(nx):
        block = back_ref[owner].astype(BF16)
        for copy in range(ny):
            message_ref[owner * ny + copy] = block


def finish_kernel(
    nx,
    scale,
    stencil_ref,
    message_ref,
    inverse_ref,
    out_ref,
    taps_ref,
    point_ref,
    packed_ref,
    turned_ref,
):
    c, cx, cy, z = out_ref.shape
    for x in range(cx):
        spectral = z_inverse(message_ref, inverse_ref[...], x, nx).reshape(cy, c, z)
        stencil = jnp.stack([stencil_ref[x, :, y * z : (y + 1) * z] for y in range(cy)])
        out_ref[:, x] = jnp.swapaxes(spectral + stencil, 0, 1)
    skip = 2 * MZ * cx // nx
    unpack(scale, skip, message_ref, taps_ref, point_ref, packed_ref, turned_ref)


def x_kernel(table_ref, data_ref, out_ref):
    data = data_ref[...].astype(F32)
    lanes = data.shape[2]
    rows = table_ref.shape[1] // (3 * data.shape[0])
    flat = pieces(data[:, :rows].reshape(-1, lanes))
    got = jnp.dot(table_ref[...], flat, preferred_element_type=F32).astype(out_ref.dtype)
    count = got.shape[0] // out_ref.shape[0]
    for owner in range(out_ref.shape[0]):
        out_ref[owner, :count] = got[owner * count : (owner + 1) * count]
    if data.shape[1] > rows:
        extra = data[:, rows:].sum(0)
        extra = extra.astype(out_ref.dtype)
        for owner in range(out_ref.shape[0]):
            out_ref[owner, count:] = extra


def taps_kernel(taps_ref, point_ref, forward_ref, back_ref, turned_ref):
    turned_ref[...] = taps_ref[...].astype(F32).T
    forward_ref[...] = jnp.zeros_like(forward_ref)
    back_ref[...] = jnp.zeros_like(back_ref)
    for tap in range(27):
        rows = slice(tap // 3 * C, (tap // 3 + 1) * C)
        columns = slice(tap % 3 * C, (tap % 3 + 1) * C)
        block = turned_ref[pl.ds(tap, C, stride=27), :]
        back_ref[rows, columns] = block.astype(BF16)
        forward_ref[rows, columns] = block.T.astype(BF16)
    point = point_ref[...].astype(F32)
    forward_ref[4 * C : 5 * C, 3 * C :] = point.astype(BF16)
    back_ref[4 * C : 5 * C, 3 * C :] = point.T.astype(BF16)


def unpack(scale, skip, message_ref, taps_ref, point_ref, packed_ref, turned_ref):
    devices, rows, lanes = message_ref.shape
    per, tiles_in = rows - skip, lanes // 128
    for owner in range(devices):
        message = message_ref[owner].astype(F32)
        for tile in range(tiles_in):
            row = (owner * tiles_in + tile) * per
            packed_ref[row : row + per] = message[skip:, tile * 128 : (tile + 1) * 128]
    for tap in range(27):
        group, e = tap // 3, tap % 3
        if e < 2:
            block = packed_ref[group * C : (group + 1) * C, e * C : (e + 1) * C]
        else:
            row = (9 + group // 2) * C
            block = packed_ref[row : row + C, group % 2 * C : (group % 2 + 1) * C]
        block = block * scale
        if tap == 13:
            point_ref[...] = block
        turned_ref[pl.ds(tap, C, stride=27), :] = block.T
    taps_ref[...] = turned_ref[...].T


QUAD = 4
SPAN = 8 * C


def y_forward(mz, blocks, table_ref, rows_ref, store):
    ny, cy = len(blocks), blocks[0].shape[1] // C
    count = rows_ref.shape[1] // C
    for owner in range(ny):
        data = blocks[owner]
        for part in range(2):
            for kz in range(mz):
                mx = count // mz
                start = (part * mz + kz) * mx
                block = data[start : start + mx]
                block = jnp.stack([block[:, y * C : (y + 1) * C] for y in range(cy)])
                block = jnp.swapaxes(block, 0, 1)
                row = (part * ny + owner) * cy
                for kx in range(mx):
                    column = (kz * mx + kx) * C
                    rows_ref[row : row + cy, column : column + C] = block[kx]
    got = jnp.dot(table_ref[: 2 * MY], pieces(rows_ref[...]), preferred_element_type=F32)
    for q in range(count):
        block = got[:, q * C : (q + 1) * C]
        for part in range(2):
            store(q // QUAD, part, q % QUAD, block[part * MY : (part + 1) * MY])


def y_inverse(mz, sum_ref, table_ref, out_ref, block_ref):
    rows = [
        jnp.concatenate(
            [
                sum_ref[group, place(part, pair), :]
                for group in range(sum_ref.shape[0])
                for pair in range(QUAD)
            ],
            axis=1,
        )
        for part in range(2)
    ]
    got = jnp.dot(
        table_ref[2 * MY :, : 6 * MY],
        pieces(jnp.concatenate(rows, axis=0)),
        preferred_element_type=F32,
    )
    ny, _, lanes = out_ref.shape
    cy = lanes // C
    count = got.shape[1] // C
    mx = count // mz
    for owner in range(ny):
        for part in range(2):
            for kz in range(mz):
                row = (part * ny + owner) * cy
                block = got[row : row + cy, kz * mx * C : (kz + 1) * mx * C]
                block = jnp.stack([block[:, kx * C : (kx + 1) * C] for kx in range(mx)])
                block = jnp.swapaxes(block, 0, 1)
                start = (part * mz + kz) * mx
                for y in range(cy):
                    block_ref[owner, start : start + mx, y * C : (y + 1) * C] = block[y]
    out_ref[...] = block_ref[...].astype(out_ref.dtype)


def place(part, pair):
    start = (part * QUAD + pair) * MY
    return slice(start, start + MY)


def spread_table():
    return np.tile(np.kron(np.eye(C), np.ones((1, C))), (2, 1)).astype(jnp.bfloat16)


def gather_table():
    return np.kron(np.eye(SPAN // C), np.ones((1, C))).astype(jnp.bfloat16)


def spread_modes(modes, table_ref, spread_refs):
    count = C * C // SPAN
    made = set()

    def get(piece):
        for p in range(piece, min(piece + 2, count)):
            if p not in made:
                made.add(p)
                spread_refs[p % 2][...] = jnp.dot(
                    modes, table_ref[:, p * SPAN : (p + 1) * SPAN], preferred_element_type=F32
                )
        return spread_refs[piece % 2]

    return get


def weight_copies(weight_ref, held_ref, sem_ref):
    per = weight_ref.shape[2] // QUAD
    return [
        pltpu.make_async_copy(
            weight_ref.at[:, g // per, g % per * QUAD : (g % per + 1) * QUAD],
            held_ref.at[g],
            sem_ref.at[g],
        )
        for g in range(held_ref.shape[0])
    ]


def mix_kernel(
    mz,
    data_ref,
    weight_ref,
    table_ref,
    turn_ref,
    modes_ref,
    out_ref,
    sum_ref,
    rows_ref,
    block_ref,
    held_ref,
    sem_ref,
    spread_ref,
    spread_sem_ref,
    even_ref,
    odd_ref,
    total_ref,
):
    copies = weight_copies(weight_ref, held_ref, sem_ref)
    table_copy = pltpu.make_async_copy(table_ref, spread_ref, spread_sem_ref)
    table_copy.start()
    for copy in copies:
        copy.start()

    def store(group, part, pair, values):
        high = values.astype(BF16)
        low = (values - high.astype(F32)).astype(BF16)
        modes_ref[group, place(part, pair), :] = jnp.concatenate([high, low], axis=1)

    blocks = [data_ref[owner] for owner in range(data_ref.shape[0])]
    y_forward(mz, blocks, turn_ref, rows_ref, store)
    table_copy.wait()
    for group, copy in enumerate(copies):
        copy.wait()
        spread = spread_modes(modes_ref[group], spread_ref, (even_ref, odd_ref))
        for piece in range(C * C // SPAN):
            modes = spread(piece)
            for pair in range(QUAD):
                real = imag = None
                for tile in range(SPAN // (2 * C)):
                    inside = slice(tile * 2 * C, (tile + 1) * 2 * C)
                    columns = slice(piece * SPAN + inside.start, piece * SPAN + inside.stop)
                    mode_re = modes[place(0, pair), inside]
                    mode_im = modes[place(1, pair), inside]
                    weight_re = held_ref[group, 0, pair, :, columns].astype(F32)
                    weight_im = held_ref[group, 1, pair, :, columns].astype(F32)
                    term_re = mode_re * weight_re - mode_im * weight_im
                    term_im = mode_re * weight_im + mode_im * weight_re
                    real = term_re if real is None else real + term_re
                    imag = term_im if imag is None else imag + term_im
                if piece:
                    real += total_ref[place(0, pair), :]
                    imag += total_ref[place(1, pair), :]
                total_ref[place(0, pair), :] = real
                total_ref[place(1, pair), :] = imag
        total = total_ref[...]
        sum_ref[group] = total[:, :C] + total[:, C:]
    y_inverse(mz, sum_ref, turn_ref, out_ref, block_ref)


def mix_back_kernel(
    mz,
    data_ref,
    weight_ref,
    table_ref,
    turn_ref,
    x_ref,
    modes_ref,
    out_ref,
    sum_ref,
    rows_ref,
    block_ref,
    held_ref,
    sem_ref,
    term_ref,
):
    copies = weight_copies(weight_ref, held_ref, sem_ref)
    for copy in copies:
        copy.start()

    def store(group, part, pair, values):
        modes_ref[group, place(part, pair), :] = jnp.concatenate([values, values], axis=1)

    ny = block_ref.shape[0]
    size = x_ref.shape[1] // 3
    blocks = []
    for owner in range(ny):
        rows = jnp.concatenate(
            [data_ref[i].astype(F32) for i in range(owner, data_ref.shape[0], ny)], axis=0
        ).astype(BF16)
        blocks.append(
            jnp.dot(x_ref[:, :size], rows, preferred_element_type=F32)
            + jnp.dot(x_ref[:, 2 * size :], rows, preferred_element_type=F32)
        )
    y_forward(mz, blocks, turn_ref, rows_ref, store)
    for group, copy in enumerate(copies):
        copy.wait()
        total = []
        for piece in range(C * C // SPAN):
            for pair in range(QUAD):
                mode_re = modes_ref[group, place(0, pair), :]
                mode_im = modes_ref[group, place(1, pair), :]
                for tile in range(SPAN // (2 * C)):
                    start = piece * SPAN + tile * 2 * C
                    columns = slice(start, start + 2 * C)
                    weight_re = held_ref[group, 0, pair, :, columns].astype(F32)
                    weight_im = held_ref[group, 1, pair, :, columns].astype(F32)
                    term_ref[place(0, pair), columns] = (
                        weight_re * mode_re + weight_im * mode_im
                    ).astype(BF16)
                    term_ref[place(1, pair), columns] = (
                        weight_re * mode_im - weight_im * mode_re
                    ).astype(BF16)
            total.append(
                lax.dot_general(
                    table_ref[...],
                    term_ref[:, piece * SPAN : (piece + 1) * SPAN],
                    (((1,), (1,)), ((), ())),
                    preferred_element_type=F32,
                )
            )
        sum_ref[group] = jnp.concatenate(total, axis=0).T
    y_inverse(mz, sum_ref, turn_ref, out_ref, block_ref)


def outer_kernel(alpha, modes_ref, back_ref, table_ref, out_ref):
    count = C * C // SPAN
    made = lambda piece: jnp.dot(
        modes_ref[0],
        table_ref[:, piece * SPAN : (piece + 1) * SPAN],
        preferred_element_type=F32,
    )
    ahead = made(0)
    for piece in range(count):
        modes = ahead
        if piece + 1 < count:
            ahead = made(piece + 1)
        for pair in range(QUAD):
            back_re = back_ref[0, place(0, pair), :] * alpha
            back_im = back_ref[0, place(1, pair), :] * alpha
            for tile in range(SPAN // (2 * C)):
                inside = slice(tile * 2 * C, (tile + 1) * 2 * C)
                columns = slice(piece * SPAN + inside.start, piece * SPAN + inside.stop)
                mode_re = modes[place(0, pair), inside]
                mode_im = modes[place(1, pair), inside]
                out_ref[0, 0, pair, :, columns] = mode_re * back_re + mode_im * back_im
                out_ref[1, 0, pair, :, columns] = mode_re * back_im - mode_im * back_re


def in_hbm(value):
    return pltpu.with_memory_space_constraint(value, pltpu.HBM)


def whole():
    return pl.BlockSpec(memory_space=pltpu.VMEM)


def params(mib):
    return pltpu.CompilerParams(vmem_limit_bytes=mib * MIB)


def cost(flops, moved):
    return pl.CostEstimate(flops=int(flops), bytes_accessed=int(moved), transcendentals=0)


def call(kernel, outs, args, scratch=(), mib=24, flops=0, moved=0, anywhere=()):
    return pl.pallas_call(
        kernel,
        out_shape=[jax.ShapeDtypeStruct(*out) for out in outs],
        in_specs=[
            pl.BlockSpec(memory_space=pl.ANY) if i in anywhere else whole()
            for i in range(len(args))
        ],
        out_specs=[whole() for _ in outs],
        scratch_shapes=list(scratch),
        compiler_params=params(mib),
        cost_estimate=cost(flops, moved),
    )(*args)


def per_mode(kernel, data, weight, table, tables, modes, kind, scratch=()):
    _, mz, mx, my, wide = weight.shape
    groups = mz * mx // QUAD
    rows = 2 * QUAD * MY
    modes_shape = (groups, rows, modes[0])
    block = (MX // mx, 2 * mz * mx, data.shape[2])
    return pl.pallas_call(
        functools.partial(kernel, mz),
        in_specs=[
            whole(),
            pl.BlockSpec(memory_space=pl.ANY),
            pl.BlockSpec(memory_space=pl.ANY) if kernel is mix_kernel else whole(),
        ]
        + [whole() for _ in tables],
        out_specs=[whole(), whole()],
        out_shape=[
            jax.ShapeDtypeStruct(modes_shape, modes[1]),
            jax.ShapeDtypeStruct(block, kind),
        ],
        scratch_shapes=[
            pltpu.VMEM((groups, rows, C), F32),
            pltpu.VMEM((tables[0].shape[0] - 2 * MY, mz * mx * C), F32),
            pltpu.VMEM(block, F32),
            pltpu.VMEM((groups, 2, QUAD, my, wide), BF16),
            pltpu.SemaphoreType.DMA((groups,)),
            *scratch,
        ],
        compiler_params=params(24),
        cost_estimate=cost(weight.size * 8, weight.size * 2),
    )(data, in_hbm(weight), in_hbm(table), *tables)


def outer(modes, back, table, shape, alpha):
    per = shape[2] // QUAD
    group = lambda ref: pl.BlockSpec((1,) + ref.shape[1:], lambda step: (step, 0, 0))
    return pl.pallas_call(
        functools.partial(outer_kernel, alpha),
        grid=(modes.shape[0],),
        in_specs=[group(modes), group(back), pl.BlockSpec(table.shape, lambda step: (0, 0))],
        out_specs=pl.BlockSpec(
            (2, 1, QUAD) + shape[3:], lambda step: (0, step // per, step % per, 0, 0)
        ),
        out_shape=jax.ShapeDtypeStruct(shape, F32),
        compiler_params=params(20),
        cost_estimate=cost(math.prod(shape) * 4, math.prod(shape) * 4),
    )(modes, back, in_hbm(table))


def shift(block, axis, step):
    count = lax.axis_size(axis)
    pairs = [(i, i + step) for i in range(count) if 0 <= i + step < count]
    return lax.ppermute(block, axis, pairs)


def x_halos(turned):
    return shift(turned[-1], "gx", 1), shift(turned[0], "gx", -1)


def y_halos(turned, xlo, xhi):
    edge = lambda y: jnp.concatenate([xlo[None, y], turned[:, y], xhi[None, y]], axis=0)
    return shift(edge(-1), "gy", 1), shift(edge(0), "gy", -1)


def conv(turned, rim, weight, flip):
    cx, cy, c, z = turned.shape
    return call(
        functools.partial(conv_kernel, flip),
        [((cx, c, cy * z), F32)],
        (turned, *map(in_hbm, rim), in_hbm(weight)),
        [pltpu.VMEM((4 * c, (cy + 2) * z), BF16)],
        mib=32,
        flops=2 * 27 * c * c * cx * cy * z,
        moved=turned.size * 8,
    )[0]


def weight_grad(grad, turned, rim):
    cx, cy, c, z = turned.shape
    return call(
        weight_grad_kernel,
        [((16 * c, 2 * c), F32)],
        (grad, turned, *map(in_hbm, rim)),
        [
            pltpu.VMEM((4 * c, (cy + 2) * z), BF16),
            pltpu.VMEM((cx * 3 * c, (cy + 2) * z), BF16),
            pltpu.VMEM((9 * c, 4 * c), F32),
            *(pltpu.VMEM(halo.shape, BF16) for halo in rim),
            pltpu.SemaphoreType.DMA((len(rim),)),
        ],
        anywhere=(2, 3, 4, 5),
        mib=32,
        flops=2 * 27 * c * c * cx * cy * z,
        moved=turned.size * 8,
    )[0]


def swap(block, axis):
    return lax.all_to_all(block, axis, split_axis=0, concat_axis=0, tiled=True)


def together(*values):
    return lax.optimization_barrier(values)


def body(state, cotangent, spectral_weight, stencil_weight, pointwise_weight):
    nx, ny = lax.axis_size("gx"), lax.axis_size("gy")
    c, cx, cy, z = state.shape
    _, mz, mx, _, _ = spectral_weight.shape
    wide_x, wide_y = cx * nx, cy * ny
    alpha = 1.0 / math.sqrt(wide_x * wide_y * z)
    beta = 1.0 / math.sqrt(2 * MX * MY * MZ)
    double = np.where(np.arange(MZ) == 0, 1.0, 2.0)
    ones = np.ones(MZ)
    z_state = jnp.asarray(z_forward_table(alpha * ones)(nx, mz))
    z_grad = jnp.asarray(z_forward_table(double)(nx, mz))
    z_spectral = jnp.asarray(z_inverse_table(nx, mz, beta * double))
    z_back = jnp.asarray(z_inverse_table(nx, mz, alpha * beta * ones))
    x_fwd, x_inv = (jnp.asarray(t) for t in x_tables(wide_x, mz, mx))
    y_turn = jnp.asarray(y_table(wide_y))
    spread, gather = jnp.asarray(spread_table()), jnp.asarray(gather_table())
    lanes = cy * c
    x_rows = cx * 2 * mz

    def x_stage(table, block, lead, kind=F32, extra=0):
        rows = table.shape[0] // lead + extra
        return call(
            x_kernel,
            [((lead, rows, lanes), kind)],
            (table, block),
            mib=16,
            flops=2 * table.size * lanes,
            moved=8 * block.size,
        )[0]

    slab_shape = ((nx, x_rows, lanes), F32)
    turned_shape = ((cx, cy, c, z), BF16)

    conv_table, back_table = call(
        taps_kernel,
        [((9 * c, 4 * c), BF16)] * 2,
        (in_hbm(stencil_weight), in_hbm(pointwise_weight)),
        [pltpu.VMEM((27 * c, c), F32)],
        moved=stencil_weight.size * 6,
    )
    turned, slab = call(
        functools.partial(prep_kernel, nx),
        [turned_shape, slab_shape],
        (in_hbm(state), in_hbm(z_state)),
        flops=2 * 96 * state.size,
        moved=state.size * 5,
    )
    x_mine = x_fwd.reshape(ny, -1, x_fwd.shape[1])
    x_mine = lax.dynamic_index_in_dim(x_mine, lax.axis_index("gy"), 0, keepdims=False)

    block = x_stage(x_fwd, swap(slab, "gx"), ny)
    block, conv_table, back_table, x_mine, *faces = together(
        block, conv_table, back_table, x_mine, *x_halos(turned)
    )
    modes_in, block = per_mode(
        mix_kernel,
        swap(block, "gy"),
        spectral_weight,
        spread,
        (y_turn,),
        (2 * c, BF16),
        F32,
        [pltpu.VMEM(spread.shape, BF16), pltpu.SemaphoreType.DMA]
        + [pltpu.VMEM((2 * QUAD * MY, SPAN), F32)] * 2
        + [pltpu.VMEM((2 * QUAD * MY, 2 * c), F32)],
    )
    block, *edges = together(block, *y_halos(turned, *faces))
    rim = (*faces, *edges)
    block = x_stage(x_inv, swap(block, "gy"), nx)
    stencil = conv(turned, rim, conv_table, False)
    output, grad, slab = call(
        functools.partial(gelu_kernel, nx),
        [((c, cx, cy, z), BF16), turned_shape, ((nx * ny, x_rows, lanes), BF16)],
        (stencil, swap(block, "gx"), cotangent, z_spectral, z_grad),
        [pltpu.VMEM(slab_shape[0], F32)],
        flops=2 * 192 * state.size,
        moved=state.size * 12,
    )

    grad_taps = weight_grad(grad, turned, rim)
    faces = x_halos(grad)
    grad_taps, *faces = together(grad_taps, *faces)
    edges = y_halos(grad, *faces)
    block = swap(slab, ("gx", "gy"))
    block, grad_taps, *edges = together(block, grad_taps, *edges)
    mine = swap(grad_taps.reshape(nx, -1, 2 * c), "gx").sum(0)
    back_modes, block = per_mode(
        mix_back_kernel,
        block,
        spectral_weight,
        gather,
        (y_turn, x_mine),
        (2 * c, F32),
        BF16,
        [pltpu.VMEM((2 * QUAD * MY, c * c), BF16)],
    )
    packed = jnp.concatenate(jnp.split(mine, lanes // (2 * c)), axis=1).astype(BF16)
    extra = packed.shape[0]
    packed = jnp.broadcast_to(packed[None], (ny, extra, lanes))
    block = x_stage(
        x_inv, swap(jnp.concatenate([block, packed], axis=1), "gy"), nx, BF16, extra
    )
    grad_modes = outer(modes_in, back_modes, spread, spectral_weight.shape, alpha)
    block, grad_modes = together(block, grad_modes)
    message = swap(block, "gx")
    stencil_back = conv(grad, (*faces, *edges), back_table, True)
    grad_state, grad_stencil, grad_point = call(
        functools.partial(finish_kernel, nx, alpha),
        [((c, cx, cy, z), F32), ((c, 27 * c), F32), ((c, c), F32)],
        (stencil_back, message, z_back),
        [pltpu.VMEM(grad_taps.shape, F32), pltpu.VMEM((27 * c, c), F32)],
        flops=2 * 96 * state.size,
        moved=state.size * 10,
    )
    return (output, grad_state, grad_modes, grad_stencil, grad_point)


def solution(mesh):
    in_specs = (
        P(None, "gx", "gy", None),
        P(None, "gx", "gy", None),
        P(None, "gx", "gy", None, None),
        P(),
        P(),
    )
    out_specs = (
        P(None, "gx", "gy", None),
        P(None, "gx", "gy", None),
        P(None, "gx", "gy", None, None),
        P(),
        P(),
    )
    return jax.shard_map(body, mesh=mesh, in_specs=in_specs, out_specs=out_specs, check_vma=False)
```

```python
import functools
import math

import jax
import jax.numpy as jnp
import numpy as np
from jax import lax
from jax.experimental import pallas as pl
from jax.experimental.pallas import tpu as pltpu
from jax.sharding import PartitionSpec as P

C = 64
MX = 32
MY = 32
MZ = 16
Z = 128
MIB = 1 << 20

F32 = jnp.float32
BF16 = jnp.bfloat16


def angles(places, freqs, length):
    turns = np.outer(np.asarray(places), np.asarray(freqs)) % length
    return turns * (2.0 * np.pi / length)


def centred(count):
    steps = np.arange(count)
    return np.where(steps < count // 2, steps, steps - count)


def split(table, parts):
    rest = np.asarray(table, np.float64)
    out = []
    for _ in range(parts):
        piece = rest.astype(jnp.bfloat16)
        out.append(piece)
        rest = rest - piece.astype(np.float64)
    return out


def z_forward_table(scale):
    def build(nx, mz):
        theta = angles(np.arange(MZ), np.arange(Z), Z)
        pair = np.stack([np.cos(theta), -np.sin(theta)]) * scale[None, :, None]
        rows = pair.reshape(2, nx, mz, Z).transpose(1, 0, 2, 3).reshape(2 * MZ, Z)
        return np.concatenate(split(rows, 3), axis=0)

    return build


def z_inverse_table(nx, mz, scale):
    theta = angles(np.arange(MZ), np.arange(Z), Z)
    pair = np.stack([np.cos(theta), -np.sin(theta)]) * scale[None, :, None]
    rows = pair.reshape(2, nx, mz, Z).transpose(1, 0, 2, 3).reshape(2 * MZ, Z)
    high, low = split(rows, 2)
    return np.concatenate([high, high, low], axis=0)


def rotation(theta, sign):
    cosine, sine = np.cos(theta), sign * np.sin(theta)
    return np.stack([np.stack([cosine, -sine], 1), np.stack([sine, cosine], 1)])


def against_pieces(*tables):
    out = []
    for table in tables:
        high, low = split(table, 2)
        out.append(np.concatenate([high, high, low], axis=1))
    return out


def x_tables(wide, mz, mx):
    theta = angles(centred(MX), np.arange(wide), wide)
    eye = np.eye(mz)
    forward = np.einsum("rkRx,zZ->krzxRZ", rotation(theta, -1.0), eye)
    inverse = np.einsum("rxRk,zZ->xrzkRZ", rotation(theta.T, 1.0), eye)
    size_k, size_x = MX * 2 * mz, wide * 2 * mz
    forward = forward.reshape(MX // mx, mx, 2, mz, size_x).transpose(0, 2, 3, 1, 4)
    inverse = inverse.reshape(size_x, MX // mx, mx, 2, mz).transpose(0, 1, 3, 4, 2)
    return against_pieces(forward.reshape(size_k, size_x), inverse.reshape(size_x, size_k))


def y_table(wide):
    theta = angles(centred(MY), np.arange(wide), wide)
    forward = rotation(theta, -1.0).reshape(2 * MY, 2 * wide)
    inverse = rotation(theta.T, 1.0).reshape(2 * wide, 2 * MY)
    forward, inverse = against_pieces(forward, inverse)
    inverse = np.pad(inverse, ((0, 0), (0, forward.shape[1] - inverse.shape[1])))
    return np.concatenate([forward, inverse], axis=0)


def pieces(values):
    high = values.astype(BF16)
    low = (values - high.astype(F32)).astype(BF16)
    return jnp.concatenate([high, low, high], axis=0)


def z_forward(rows, table, out_ref, x, nx):
    got = lax.dot_general(table, rows, (((1,), (1,)), ((), ())), preferred_element_type=F32)
    size = 2 * MZ
    total = got[:size] + (got[size : 2 * size] + got[2 * size :])
    per = size // nx
    for owner in range(nx):
        out_ref[owner, x * per : (x + 1) * per, :] = total[owner * per : (owner + 1) * per]


def z_inverse(in_ref, table, x, nx):
    per = 2 * MZ // nx
    rows = jnp.concatenate(
        [in_ref[owner].astype(F32)[x * per : (x + 1) * per] for owner in range(nx)], axis=0
    )
    return lax.dot_general(
        pieces(rows), table, (((0,), (0,)), ((), ())), preferred_element_type=F32
    )


def prep_kernel(
    nx,
    field_ref,
    table_ref,
    forward_ref,
    inverse_ref,
    turn_ref,
    turned_ref,
    slab_ref,
    forward_out_ref,
    inverse_out_ref,
    turn_out_ref,
):
    forward_out_ref[...] = forward_ref[...]
    inverse_out_ref[...] = inverse_ref[...]
    turn_out_ref[...] = turn_ref[...]
    c, cx, cy, z = field_ref.shape
    for x in range(cx):
        block = jnp.swapaxes(field_ref[:, x].astype(F32), 0, 1)
        turned = block.astype(BF16)
        turned_ref[x] = turned
        z_forward(turned.reshape(cy * c, z), table_ref[...], slab_ref, x, nx)


def plane_rows(p, cx, body_ref, xlo_ref, xhi_ref, ylo_ref, yhi_ref):
    cy = body_ref.shape[1]
    if p == 0:
        middle = [xlo_ref[y] for y in range(cy)]
    elif p == cx + 1:
        middle = [xhi_ref[y] for y in range(cy)]
    else:
        middle = [body_ref[p - 1, y] for y in range(cy)]
    return [ylo_ref[p]] + middle + [yhi_ref[p]]


def fill_shifts(blocks, rim_ref, flip=False):
    c, z = blocks[0].shape
    lane = lax.broadcasted_iota(jnp.int32, (c, z), 1)
    for y, block in enumerate(blocks):
        wide = block.astype(F32)
        before = jnp.where(lane == 0, 0.0, pltpu.roll(wide, 1, 1))
        after = jnp.where(lane == z - 1, 0.0, pltpu.roll(wide, z - 1, 1))
        if flip:
            before, after = after, before
        columns = slice(y * z, (y + 1) * z)
        rim_ref[0:c, columns] = before.astype(BF16)
        rim_ref[c : 2 * c, columns] = block
        rim_ref[2 * c : 3 * c, columns] = after.astype(BF16)
        rim_ref[3 * c : 4 * c, columns] = block


def conv_kernel(
    flip, body_ref, xlo_ref, xhi_ref, ylo_ref, yhi_ref, weight_ref, out_ref, rim_ref
):
    cx, cy, c, z = body_ref.shape
    for p in range(cx + 2):
        blocks = plane_rows(p, cx, body_ref, xlo_ref, xhi_ref, ylo_ref, yhi_ref)
        fill_shifts(blocks, rim_ref, flip)
        places = [a for a in range(3) if 0 <= p - (2 - a if flip else a) < cx]
        first = places[0]
        got = jnp.dot(
            weight_ref[first * 3 * c : (places[-1] + 1) * 3 * c, :],
            rim_ref[...],
            preferred_element_type=F32,
        )
        for a in places:
            x = p - (2 - a if flip else a)
            total = None
            for b in range(3):
                row = ((a - first) * 3 + b) * c
                skip = 2 - b if flip else b
                term = got[row : row + c, skip * z : (skip + cy) * z]
                total = term if total is None else total + term
            if p == x:
                out_ref[x] = total
            else:
                out_ref[x] += total


def weight_grad_kernel(
    grad_ref,
    body_ref,
    xlo_any,
    xhi_any,
    ylo_any,
    yhi_any,
    out_ref,
    rim_ref,
    wide_ref,
    sum_ref,
    xlo_ref,
    xhi_ref,
    ylo_ref,
    yhi_ref,
    sem_ref,
):
    cx, cy, c, z = body_ref.shape
    group = 3 * c
    held = (xlo_ref, xhi_ref, ylo_ref, yhi_ref)
    copies = [
        pltpu.make_async_copy(given, ref, sem_ref.at[i])
        for i, (given, ref) in enumerate(zip((xlo_any, xhi_any, ylo_any, yhi_any), held))
    ]
    for copy in copies:
        copy.start()
    wide_ref[...] = jnp.zeros_like(wide_ref)
    for x in range(cx):
        for b in range(3):
            for y in range(cy):
                row = x * group + b * c
                wide_ref[row : row + c, (y + b) * z : (y + b + 1) * z] = grad_ref[x, y]
    sum_ref[...] = jnp.zeros_like(sum_ref)
    for copy in copies:
        copy.wait()
    for p in range(cx + 2):
        fill_shifts(plane_rows(p, cx, body_ref, xlo_ref, xhi_ref, ylo_ref, yhi_ref), rim_ref)
        first, last = max(0, p - 2), min(cx - 1, p)
        got = lax.dot_general(
            wide_ref[first * group : (last + 1) * group, :],
            rim_ref[...],
            (((1,), (1,)), ((), ())),
            preferred_element_type=F32,
        )
        for x in range(first, last + 1):
            a = p - x
            sum_ref[a * group : (a + 1) * group, :] += got[
                (x - first) * group : (x - first + 1) * group, :
            ]
    out_ref[: 9 * c] = sum_ref[:, : 2 * c]
    last = [sum_ref[k * c : (k + 1) * c, 2 * c : 3 * c] for k in range(9)]
    last.append(jnp.zeros((c, c), F32))
    for k in range(5):
        row = (9 + k) * c
        out_ref[row : row + c] = jnp.concatenate(last[2 * k : 2 * k + 2], axis=1)
    out_ref[14 * c :] = jnp.zeros((2 * c, 2 * c), F32)


def gelu_kernel(
    nx,
    stencil_ref,
    slab_ref,
    cot_ref,
    inverse_ref,
    forward_ref,
    out_ref,
    turned_ref,
    message_ref,
    back_ref,
):
    c, cx, cy, z = cot_ref.shape
    root = math.sqrt(2.0 / math.pi)
    for x in range(cx):
        spectral = z_inverse(slab_ref, inverse_ref[...], x, nx).reshape(cy, c, z)
        stencil = jnp.stack([stencil_ref[x, :, y * z : (y + 1) * z] for y in range(cy)])
        pre = spectral + stencil
        cot = jnp.swapaxes(cot_ref[:, x].astype(F32), 0, 1)
        square = pre * pre
        bent = jnp.tanh(root * (pre * (1.0 + 0.044715 * square)))
        half = 0.5 + 0.5 * bent
        slope = half + (0.5 * pre) * (1.0 - bent * bent) * (root * (1.0 + 0.134145 * square))
        out_ref[:, x] = jnp.swapaxes(pre * half, 0, 1).astype(BF16)
        grad = (cot * slope).astype(BF16)
        turned_ref[x] = grad
        z_forward(grad.reshape(cy * c, z), forward_ref[...], back_ref, x, nx)
    ny = message_ref.shape[0] // nx
    for owner in range(nx):
        block = back_ref[owner].astype(BF16)
        for copy in range(ny):
            message_ref[owner * ny + copy] = block


def finish_kernel(
    nx,
    scale,
    stencil_ref,
    message_ref,
    inverse_ref,
    out_ref,
    taps_ref,
    point_ref,
    packed_ref,
    turned_ref,
):
    c, cx, cy, z = out_ref.shape
    for x in range(cx):
        spectral = z_inverse(message_ref, inverse_ref[...], x, nx).reshape(cy, c, z)
        stencil = jnp.stack([stencil_ref[x, :, y * z : (y + 1) * z] for y in range(cy)])
        out_ref[:, x] = jnp.swapaxes(spectral + stencil, 0, 1)
    skip = 2 * MZ * cx // nx
    unpack(scale, skip, message_ref, taps_ref, point_ref, packed_ref, turned_ref)


def x_kernel(table_ref, data_ref, out_ref):
    data = data_ref[...].astype(F32)
    lanes = data.shape[2]
    rows = table_ref.shape[1] // (3 * data.shape[0])
    flat = pieces(data[:, :rows].reshape(-1, lanes))
    got = jnp.dot(table_ref[...], flat, preferred_element_type=F32).astype(out_ref.dtype)
    count = got.shape[0] // out_ref.shape[0]
    for owner in range(out_ref.shape[0]):
        out_ref[owner, :count] = got[owner * count : (owner + 1) * count]
    if data.shape[1] > rows:
        extra = data[:, rows:].sum(0)
        extra = extra.astype(out_ref.dtype)
        for owner in range(out_ref.shape[0]):
            out_ref[owner, count:] = extra


def taps_kernel(taps_ref, point_ref, forward_ref, back_ref, turned_ref):
    turned_ref[...] = taps_ref[...].astype(F32).T
    forward_ref[...] = jnp.zeros_like(forward_ref)
    back_ref[...] = jnp.zeros_like(back_ref)
    for tap in range(27):
        rows = slice(tap // 3 * C, (tap // 3 + 1) * C)
        columns = slice(tap % 3 * C, (tap % 3 + 1) * C)
        block = turned_ref[pl.ds(tap, C, stride=27), :]
        back_ref[rows, columns] = block.astype(BF16)
        forward_ref[rows, columns] = block.T.astype(BF16)
    point = point_ref[...].astype(F32)
    forward_ref[4 * C : 5 * C, 3 * C :] = point.astype(BF16)
    back_ref[4 * C : 5 * C, 3 * C :] = point.T.astype(BF16)


def unpack(scale, skip, message_ref, taps_ref, point_ref, packed_ref, turned_ref):
    devices, rows, lanes = message_ref.shape
    per, tiles_in = rows - skip, lanes // 128
    for owner in range(devices):
        message = message_ref[owner].astype(F32)
        for tile in range(tiles_in):
            row = (owner * tiles_in + tile) * per
            packed_ref[row : row + per] = message[skip:, tile * 128 : (tile + 1) * 128]
    for tap in range(27):
        group, e = tap // 3, tap % 3
        if e < 2:
            block = packed_ref[group * C : (group + 1) * C, e * C : (e + 1) * C]
        else:
            row = (9 + group // 2) * C
            block = packed_ref[row : row + C, group % 2 * C : (group % 2 + 1) * C]
        block = block * scale
        if tap == 13:
            point_ref[...] = block
        turned_ref[pl.ds(tap, C, stride=27), :] = block.T
    taps_ref[...] = turned_ref[...].T


QUAD = 4
SPAN = 8 * C


def y_forward(mz, blocks, table_ref, rows_ref, store):
    ny, cy = len(blocks), blocks[0].shape[1] // C
    count = rows_ref.shape[1] // C
    for owner in range(ny):
        data = blocks[owner]
        for part in range(2):
            for kz in range(mz):
                mx = count // mz
                start = (part * mz + kz) * mx
                block = data[start : start + mx]
                block = jnp.stack([block[:, y * C : (y + 1) * C] for y in range(cy)])
                block = jnp.swapaxes(block, 0, 1)
                row = (part * ny + owner) * cy
                for kx in range(mx):
                    column = (kz * mx + kx) * C
                    rows_ref[row : row + cy, column : column + C] = block[kx]
    got = jnp.dot(table_ref[: 2 * MY], pieces(rows_ref[...]), preferred_element_type=F32)
    for q in range(count):
        block = got[:, q * C : (q + 1) * C]
        for part in range(2):
            store(q // QUAD, part, q % QUAD, block[part * MY : (part + 1) * MY])


def y_inverse(mz, sum_ref, table_ref, out_ref, block_ref):
    rows = [
        jnp.concatenate(
            [
                sum_ref[group, place(part, pair), :]
                for group in range(sum_ref.shape[0])
                for pair in range(QUAD)
            ],
            axis=1,
        )
        for part in range(2)
    ]
    got = jnp.dot(
        table_ref[2 * MY :, : 6 * MY],
        pieces(jnp.concatenate(rows, axis=0)),
        preferred_element_type=F32,
    )
    ny, _, lanes = out_ref.shape
    cy = lanes // C
    count = got.shape[1] // C
    mx = count // mz
    for owner in range(ny):
        for part in range(2):
            for kz in range(mz):
                row = (part * ny + owner) * cy
                block = got[row : row + cy, kz * mx * C : (kz + 1) * mx * C]
                block = jnp.stack([block[:, kx * C : (kx + 1) * C] for kx in range(mx)])
                block = jnp.swapaxes(block, 0, 1)
                start = (part * mz + kz) * mx
                for y in range(cy):
                    block_ref[owner, start : start + mx, y * C : (y + 1) * C] = block[y]
    out_ref[...] = block_ref[...].astype(out_ref.dtype)


def place(part, pair):
    start = (part * QUAD + pair) * MY
    return slice(start, start + MY)


def spread_table():
    return np.tile(np.kron(np.eye(C), np.ones((1, C))), (2, 1)).astype(jnp.bfloat16)


def gather_table():
    return np.kron(np.eye(SPAN // C), np.ones((1, C))).astype(jnp.bfloat16)


def spread_modes(modes, table_ref, spread_refs):
    count = C * C // SPAN
    made = set()

    def get(piece):
        for p in range(piece, min(piece + 2, count)):
            if p not in made:
                made.add(p)
                spread_refs[p % 2][...] = jnp.dot(
                    modes, table_ref[:, p * SPAN : (p + 1) * SPAN], preferred_element_type=F32
                )
        return spread_refs[piece % 2]

    return get


def weight_copies(weight_ref, held_ref, sem_ref):
    per = weight_ref.shape[2] // QUAD
    return [
        pltpu.make_async_copy(
            weight_ref.at[:, g // per, g % per * QUAD : (g % per + 1) * QUAD],
            held_ref.at[g],
            sem_ref.at[g],
        )
        for g in range(held_ref.shape[0])
    ]


def mix_kernel(
    mz,
    data_ref,
    weight_ref,
    table_ref,
    turn_ref,
    modes_ref,
    out_ref,
    sum_ref,
    rows_ref,
    block_ref,
    held_ref,
    sem_ref,
    spread_ref,
    spread_sem_ref,
    even_ref,
    odd_ref,
    total_ref,
):
    copies = weight_copies(weight_ref, held_ref, sem_ref)
    table_copy = pltpu.make_async_copy(table_ref, spread_ref, spread_sem_ref)
    table_copy.start()
    for copy in copies:
        copy.start()

    def store(group, part, pair, values):
        high = values.astype(BF16)
        low = (values - high.astype(F32)).astype(BF16)
        modes_ref[group, place(part, pair), :] = jnp.concatenate([high, low], axis=1)

    blocks = [data_ref[owner] for owner in range(data_ref.shape[0])]
    y_forward(mz, blocks, turn_ref, rows_ref, store)
    table_copy.wait()
    for group, copy in enumerate(copies):
        copy.wait()
        spread = spread_modes(modes_ref[group], spread_ref, (even_ref, odd_ref))
        for piece in range(C * C // SPAN):
            modes = spread(piece)
            for pair in range(QUAD):
                real = imag = None
                for tile in range(SPAN // (2 * C)):
                    inside = slice(tile * 2 * C, (tile + 1) * 2 * C)
                    columns = slice(piece * SPAN + inside.start, piece * SPAN + inside.stop)
                    mode_re = modes[place(0, pair), inside]
                    mode_im = modes[place(1, pair), inside]
                    weight_re = held_ref[group, 0, pair, :, columns].astype(F32)
                    weight_im = held_ref[group, 1, pair, :, columns].astype(F32)
                    term_re = mode_re * weight_re - mode_im * weight_im
                    term_im = mode_re * weight_im + mode_im * weight_re
                    real = term_re if real is None else real + term_re
                    imag = term_im if imag is None else imag + term_im
                if piece:
                    real += total_ref[place(0, pair), :]
                    imag += total_ref[place(1, pair), :]
                total_ref[place(0, pair), :] = real
                total_ref[place(1, pair), :] = imag
        total = total_ref[...]
        sum_ref[group] = total[:, :C] + total[:, C:]
    y_inverse(mz, sum_ref, turn_ref, out_ref, block_ref)


def mix_back_kernel(
    mz,
    data_ref,
    weight_ref,
    table_ref,
    turn_ref,
    x_ref,
    modes_ref,
    out_ref,
    sum_ref,
    rows_ref,
    block_ref,
    held_ref,
    sem_ref,
    term_ref,
):
    copies = weight_copies(weight_ref, held_ref, sem_ref)
    for copy in copies:
        copy.start()

    def store(group, part, pair, values):
        modes_ref[group, place(part, pair), :] = jnp.concatenate([values, values], axis=1)

    ny = block_ref.shape[0]
    size = x_ref.shape[1] // 3
    blocks = []
    for owner in range(ny):
        rows = jnp.concatenate(
            [data_ref[i].astype(F32) for i in range(owner, data_ref.shape[0], ny)], axis=0
        ).astype(BF16)
        blocks.append(
            jnp.dot(x_ref[:, :size], rows, preferred_element_type=F32)
            + jnp.dot(x_ref[:, 2 * size :], rows, preferred_element_type=F32)
        )
    y_forward(mz, blocks, turn_ref, rows_ref, store)
    for group, copy in enumerate(copies):
        copy.wait()
        total = []
        for piece in range(C * C // SPAN):
            for pair in range(QUAD):
                mode_re = modes_ref[group, place(0, pair), :]
                mode_im = modes_ref[group, place(1, pair), :]
                for tile in range(SPAN // (2 * C)):
                    start = piece * SPAN + tile * 2 * C
                    columns = slice(start, start + 2 * C)
                    weight_re = held_ref[group, 0, pair, :, columns].astype(F32)
                    weight_im = held_ref[group, 1, pair, :, columns].astype(F32)
                    term_ref[place(0, pair), columns] = (
                        weight_re * mode_re + weight_im * mode_im
                    ).astype(BF16)
                    term_ref[place(1, pair), columns] = (
                        weight_re * mode_im - weight_im * mode_re
                    ).astype(BF16)
            total.append(
                lax.dot_general(
                    table_ref[...],
                    term_ref[:, piece * SPAN : (piece + 1) * SPAN],
                    (((1,), (1,)), ((), ())),
                    preferred_element_type=F32,
                )
            )
        sum_ref[group] = jnp.concatenate(total, axis=0).T
    y_inverse(mz, sum_ref, turn_ref, out_ref, block_ref)


def outer_kernel(alpha, modes_ref, back_ref, table_ref, out_ref):
    count = C * C // SPAN
    made = lambda piece: jnp.dot(
        modes_ref[0],
        table_ref[:, piece * SPAN : (piece + 1) * SPAN],
        preferred_element_type=F32,
    )
    ahead = made(0)
    for piece in range(count):
        modes = ahead
        if piece + 1 < count:
            ahead = made(piece + 1)
        for pair in range(QUAD):
            back_re = back_ref[0, place(0, pair), :] * alpha
            back_im = back_ref[0, place(1, pair), :] * alpha
            for tile in range(SPAN // (2 * C)):
                inside = slice(tile * 2 * C, (tile + 1) * 2 * C)
                columns = slice(piece * SPAN + inside.start, piece * SPAN + inside.stop)
                mode_re = modes[place(0, pair), inside]
                mode_im = modes[place(1, pair), inside]
                out_ref[0, 0, pair, :, columns] = mode_re * back_re + mode_im * back_im
                out_ref[1, 0, pair, :, columns] = mode_re * back_im - mode_im * back_re


def in_hbm(value):
    return pltpu.with_memory_space_constraint(value, pltpu.HBM)


def whole():
    return pl.BlockSpec(memory_space=pltpu.VMEM)


def params(mib):
    return pltpu.CompilerParams(vmem_limit_bytes=mib * MIB)


def cost(flops, moved):
    return pl.CostEstimate(flops=int(flops), bytes_accessed=int(moved), transcendentals=0)


def call(kernel, outs, args, scratch=(), mib=24, flops=0, moved=0, anywhere=()):
    return pl.pallas_call(
        kernel,
        out_shape=[jax.ShapeDtypeStruct(*out) for out in outs],
        in_specs=[
            pl.BlockSpec(memory_space=pl.ANY) if i in anywhere else whole()
            for i in range(len(args))
        ],
        out_specs=[whole() for _ in outs],
        scratch_shapes=list(scratch),
        compiler_params=params(mib),
        cost_estimate=cost(flops, moved),
    )(*args)


def per_mode(kernel, data, weight, table, tables, modes, kind, scratch=()):
    _, mz, mx, my, wide = weight.shape
    groups = mz * mx // QUAD
    rows = 2 * QUAD * MY
    modes_shape = (groups, rows, modes[0])
    block = (MX // mx, 2 * mz * mx, data.shape[2])
    return pl.pallas_call(
        functools.partial(kernel, mz),
        in_specs=[
            whole(),
            pl.BlockSpec(memory_space=pl.ANY),
            pl.BlockSpec(memory_space=pl.ANY) if kernel is mix_kernel else whole(),
        ]
        + [whole() for _ in tables],
        out_specs=[whole(), whole()],
        out_shape=[
            jax.ShapeDtypeStruct(modes_shape, modes[1]),
            jax.ShapeDtypeStruct(block, kind),
        ],
        scratch_shapes=[
            pltpu.VMEM((groups, rows, C), F32),
            pltpu.VMEM((tables[0].shape[0] - 2 * MY, mz * mx * C), F32),
            pltpu.VMEM(block, F32),
            pltpu.VMEM((groups, 2, QUAD, my, wide), BF16),
            pltpu.SemaphoreType.DMA((groups,)),
            *scratch,
        ],
        compiler_params=params(24),
        cost_estimate=cost(weight.size * 8, weight.size * 2),
    )(data, in_hbm(weight), in_hbm(table), *tables)


def outer(modes, back, table, shape, alpha):
    per = shape[2] // QUAD
    group = lambda ref: pl.BlockSpec((1,) + ref.shape[1:], lambda step: (step, 0, 0))
    return pl.pallas_call(
        functools.partial(outer_kernel, alpha),
        grid=(modes.shape[0],),
        in_specs=[group(modes), group(back), pl.BlockSpec(table.shape, lambda step: (0, 0))],
        out_specs=pl.BlockSpec(
            (2, 1, QUAD) + shape[3:], lambda step: (0, step // per, step % per, 0, 0)
        ),
        out_shape=jax.ShapeDtypeStruct(shape, F32),
        compiler_params=params(20),
        cost_estimate=cost(math.prod(shape) * 4, math.prod(shape) * 4),
    )(modes, back, in_hbm(table))


def shift(block, axis, step):
    count = lax.axis_size(axis)
    pairs = [(i, i + step) for i in range(count) if 0 <= i + step < count]
    return lax.ppermute(block, axis, pairs)


def x_halos(turned):
    return shift(turned[-1], "gx", 1), shift(turned[0], "gx", -1)


def y_halos(turned, xlo, xhi):
    edge = lambda y: jnp.concatenate([xlo[None, y], turned[:, y], xhi[None, y]], axis=0)
    return shift(edge(-1), "gy", 1), shift(edge(0), "gy", -1)


def conv(turned, rim, weight, flip):
    cx, cy, c, z = turned.shape
    return call(
        functools.partial(conv_kernel, flip),
        [((cx, c, cy * z), F32)],
        (turned, *map(in_hbm, rim), in_hbm(weight)),
        [pltpu.VMEM((4 * c, (cy + 2) * z), BF16)],
        mib=32,
        flops=2 * 27 * c * c * cx * cy * z,
        moved=turned.size * 8,
    )[0]


def weight_grad(grad, turned, rim):
    cx, cy, c, z = turned.shape
    return call(
        weight_grad_kernel,
        [((16 * c, 2 * c), F32)],
        (grad, turned, *map(in_hbm, rim)),
        [
            pltpu.VMEM((4 * c, (cy + 2) * z), BF16),
            pltpu.VMEM((cx * 3 * c, (cy + 2) * z), BF16),
            pltpu.VMEM((9 * c, 4 * c), F32),
            *(pltpu.VMEM(halo.shape, BF16) for halo in rim),
            pltpu.SemaphoreType.DMA((len(rim),)),
        ],
        anywhere=(2, 3, 4, 5),
        mib=32,
        flops=2 * 27 * c * c * cx * cy * z,
        moved=turned.size * 8,
    )[0]


def swap(block, axis):
    return lax.all_to_all(block, axis, split_axis=0, concat_axis=0, tiled=True)


def together(*values):
    return lax.optimization_barrier(values)


def body(state, cotangent, spectral_weight, stencil_weight, pointwise_weight):
    nx, ny = lax.axis_size("gx"), lax.axis_size("gy")
    c, cx, cy, z = state.shape
    _, mz, mx, _, _ = spectral_weight.shape
    wide_x, wide_y = cx * nx, cy * ny
    alpha = 1.0 / math.sqrt(wide_x * wide_y * z)
    beta = 1.0 / math.sqrt(2 * MX * MY * MZ)
    double = np.where(np.arange(MZ) == 0, 1.0, 2.0)
    ones = np.ones(MZ)
    z_state = jnp.asarray(z_forward_table(alpha * ones)(nx, mz))
    z_grad = jnp.asarray(z_forward_table(double)(nx, mz))
    z_spectral = jnp.asarray(z_inverse_table(nx, mz, beta * double))
    z_back = jnp.asarray(z_inverse_table(nx, mz, alpha * beta * ones))
    x_fwd, x_inv = (jnp.asarray(t) for t in x_tables(wide_x, mz, mx))
    y_turn = jnp.asarray(y_table(wide_y))
    spread, gather = jnp.asarray(spread_table()), jnp.asarray(gather_table())
    lanes = cy * c
    x_rows = cx * 2 * mz

    def x_stage(table, block, lead, kind=F32, extra=0):
        rows = table.shape[0] // lead + extra
        return call(
            x_kernel,
            [((lead, rows, lanes), kind)],
            (table, block),
            mib=16,
            flops=2 * table.size * lanes,
            moved=8 * block.size,
        )[0]

    slab_shape = ((nx, x_rows, lanes), F32)
    turned_shape = ((cx, cy, c, z), BF16)

    conv_table, back_table = call(
        taps_kernel,
        [((9 * c, 4 * c), BF16)] * 2,
        (in_hbm(stencil_weight), in_hbm(pointwise_weight)),
        [pltpu.VMEM((27 * c, c), F32)],
        moved=stencil_weight.size * 6,
    )
    tables = (x_fwd, x_inv, y_turn)
    turned, slab, *held = call(
        functools.partial(prep_kernel, nx),
        [turned_shape, slab_shape] + [(t.shape, BF16) for t in tables],
        (in_hbm(state), in_hbm(z_state), *map(in_hbm, tables)),
        flops=2 * 96 * state.size,
        moved=state.size * 5,
    )
    x_mine = x_fwd.reshape(ny, -1, x_fwd.shape[1])
    x_mine = lax.dynamic_index_in_dim(x_mine, lax.axis_index("gy"), 0, keepdims=False)
    x_fwd, x_inv, y_turn = held

    block = x_stage(x_fwd, swap(slab, "gx"), ny)
    block, conv_table, back_table, x_mine, *faces = together(
        block, conv_table, back_table, x_mine, *x_halos(turned)
    )
    modes_in, block = per_mode(
        mix_kernel,
        swap(block, "gy"),
        spectral_weight,
        spread,
        (y_turn,),
        (2 * c, BF16),
        F32,
        [pltpu.VMEM(spread.shape, BF16), pltpu.SemaphoreType.DMA]
        + [pltpu.VMEM((2 * QUAD * MY, SPAN), F32)] * 2
        + [pltpu.VMEM((2 * QUAD * MY, 2 * c), F32)],
    )
    block, *edges = together(block, *y_halos(turned, *faces))
    rim = (*faces, *edges)
    block = x_stage(x_inv, swap(block, "gy"), nx)
    stencil = conv(turned, rim, conv_table, False)
    output, grad, slab = call(
        functools.partial(gelu_kernel, nx),
        [((c, cx, cy, z), BF16), turned_shape, ((nx * ny, x_rows, lanes), BF16)],
        (stencil, swap(block, "gx"), cotangent, z_spectral, z_grad),
        [pltpu.VMEM(slab_shape[0], F32)],
        flops=2 * 192 * state.size,
        moved=state.size * 12,
    )

    grad_taps = weight_grad(grad, turned, rim)
    faces = x_halos(grad)
    block = swap(slab, ("gx", "gy"))
    block, grad_taps, *faces = together(block, grad_taps, *faces)
    mine = swap(grad_taps.reshape(nx, -1, 2 * c), "gx").sum(0)
    back_modes, block = per_mode(
        mix_back_kernel,
        block,
        spectral_weight,
        gather,
        (y_turn, x_mine),
        (2 * c, F32),
        BF16,
        [pltpu.VMEM((2 * QUAD * MY, c * c), BF16)],
    )
    packed = jnp.concatenate(jnp.split(mine, lanes // (2 * c)), axis=1).astype(BF16)
    extra = packed.shape[0]
    packed = jnp.broadcast_to(packed[None], (ny, extra, lanes))
    block = x_stage(
        x_inv, swap(jnp.concatenate([block, packed], axis=1), "gy"), nx, BF16, extra
    )
    grad_modes = outer(modes_in, back_modes, spread, spectral_weight.shape, alpha)
    block, grad_modes, *faces = together(block, grad_modes, *faces)
    message = swap(block, "gx")
    edges = y_halos(grad, *faces)
    stencil_back = conv(grad, (*faces, *edges), back_table, True)
    grad_state, grad_stencil, grad_point = call(
        functools.partial(finish_kernel, nx, alpha),
        [((c, cx, cy, z), F32), ((c, 27 * c), F32), ((c, c), F32)],
        (stencil_back, message, z_back),
        [pltpu.VMEM(grad_taps.shape, F32), pltpu.VMEM((27 * c, c), F32)],
        flops=2 * 96 * state.size,
        moved=state.size * 10,
    )
    return (output, grad_state, grad_modes, grad_stencil, grad_point)


def solution(mesh):
    in_specs = (
        P(None, "gx", "gy", None),
        P(None, "gx", "gy", None),
        P(None, "gx", "gy", None, None),
        P(),
        P(),
    )
    out_specs = (
        P(None, "gx", "gy", None),
        P(None, "gx", "gy", None),
        P(None, "gx", "gy", None, None),
        P(),
        P(),
    )
    return jax.shard_map(body, mesh=mesh, in_specs=in_specs, out_specs=out_specs, check_vma=False)
```

```python
import functools
import math

import jax
import jax.numpy as jnp
import numpy as np
from jax import lax
from jax.experimental import pallas as pl
from jax.experimental.pallas import tpu as pltpu
from jax.sharding import PartitionSpec as P

C = 64
MX = 32
MY = 32
MZ = 16
Z = 128
MIB = 1 << 20

F32 = jnp.float32
BF16 = jnp.bfloat16


def angles(places, freqs, length):
    turns = np.outer(np.asarray(places), np.asarray(freqs)) % length
    return turns * (2.0 * np.pi / length)


def centred(count):
    steps = np.arange(count)
    return np.where(steps < count // 2, steps, steps - count)


def split(table, parts):
    rest = np.asarray(table, np.float64)
    out = []
    for _ in range(parts):
        piece = rest.astype(jnp.bfloat16)
        out.append(piece)
        rest = rest - piece.astype(np.float64)
    return out


def z_forward_table(scale):
    def build(nx, mz):
        theta = angles(np.arange(MZ), np.arange(Z), Z)
        pair = np.stack([np.cos(theta), -np.sin(theta)]) * scale[None, :, None]
        rows = pair.reshape(2, nx, mz, Z).transpose(1, 0, 2, 3).reshape(2 * MZ, Z)
        return np.concatenate(split(rows, 3), axis=0)

    return build


def z_inverse_table(nx, mz, scale):
    theta = angles(np.arange(MZ), np.arange(Z), Z)
    pair = np.stack([np.cos(theta), -np.sin(theta)]) * scale[None, :, None]
    rows = pair.reshape(2, nx, mz, Z).transpose(1, 0, 2, 3).reshape(2 * MZ, Z)
    high, low = split(rows, 2)
    return np.concatenate([high, high, low], axis=0)


def rotation(theta, sign):
    cosine, sine = np.cos(theta), sign * np.sin(theta)
    return np.stack([np.stack([cosine, -sine], 1), np.stack([sine, cosine], 1)])


def against_pieces(*tables):
    out = []
    for table in tables:
        high, low = split(table, 2)
        out.append(np.concatenate([high, high, low], axis=1))
    return out


def x_tables(wide, mz, mx):
    theta = angles(centred(MX), np.arange(wide), wide)
    eye = np.eye(mz)
    forward = np.einsum("rkRx,zZ->krzxRZ", rotation(theta, -1.0), eye)
    inverse = np.einsum("rxRk,zZ->xrzkRZ", rotation(theta.T, 1.0), eye)
    size_k, size_x = MX * 2 * mz, wide * 2 * mz
    forward = forward.reshape(MX // mx, mx, 2, mz, size_x).transpose(0, 2, 3, 1, 4)
    inverse = inverse.reshape(size_x, MX // mx, mx, 2, mz).transpose(0, 1, 3, 4, 2)
    return against_pieces(forward.reshape(size_k, size_x), inverse.reshape(size_x, size_k))


def y_table(wide):
    theta = angles(centred(MY), np.arange(wide), wide)
    forward = rotation(theta, -1.0).reshape(2 * MY, 2 * wide)
    inverse = rotation(theta.T, 1.0).reshape(2 * wide, 2 * MY)
    forward, inverse = against_pieces(forward, inverse)
    inverse = np.pad(inverse, ((0, 0), (0, forward.shape[1] - inverse.shape[1])))
    return np.concatenate([forward, inverse], axis=0)


def pieces(values):
    high = values.astype(BF16)
    low = (values - high.astype(F32)).astype(BF16)
    return jnp.concatenate([high, low, high], axis=0)


def z_forward(rows, table, out_ref, x, nx):
    got = lax.dot_general(table, rows, (((1,), (1,)), ((), ())), preferred_element_type=F32)
    size = 2 * MZ
    total = got[:size] + (got[size : 2 * size] + got[2 * size :])
    per = size // nx
    for owner in range(nx):
        out_ref[owner, x * per : (x + 1) * per, :] = total[owner * per : (owner + 1) * per]


def z_inverse(in_ref, table, x, nx):
    per = 2 * MZ // nx
    rows = jnp.concatenate(
        [in_ref[owner].astype(F32)[x * per : (x + 1) * per] for owner in range(nx)], axis=0
    )
    return lax.dot_general(
        pieces(rows), table, (((0,), (0,)), ((), ())), preferred_element_type=F32
    )


def prep_kernel(
    nx,
    field_ref,
    table_ref,
    forward_ref,
    inverse_ref,
    turn_ref,
    turned_ref,
    slab_ref,
    forward_out_ref,
    inverse_out_ref,
    turn_out_ref,
):
    forward_out_ref[...] = forward_ref[...]
    inverse_out_ref[...] = inverse_ref[...]
    turn_out_ref[...] = turn_ref[...]
    c, cx, cy, z = field_ref.shape
    for x in range(cx):
        block = jnp.swapaxes(field_ref[:, x].astype(F32), 0, 1)
        turned = block.astype(BF16)
        turned_ref[x] = turned
        z_forward(turned.reshape(cy * c, z), table_ref[...], slab_ref, x, nx)


def plane_rows(p, cx, body_ref, xlo_ref, xhi_ref, ylo_ref, yhi_ref):
    cy = body_ref.shape[1]
    if p == 0:
        middle = [xlo_ref[y] for y in range(cy)]
    elif p == cx + 1:
        middle = [xhi_ref[y] for y in range(cy)]
    else:
        middle = [body_ref[p - 1, y] for y in range(cy)]
    return [ylo_ref[p]] + middle + [yhi_ref[p]]


def fill_shifts(blocks, rim_ref, flip=False):
    c, z = blocks[0].shape
    lane = lax.broadcasted_iota(jnp.int32, (c, z), 1)
    for y, block in enumerate(blocks):
        wide = block.astype(F32)
        before = jnp.where(lane == 0, 0.0, pltpu.roll(wide, 1, 1))
        after = jnp.where(lane == z - 1, 0.0, pltpu.roll(wide, z - 1, 1))
        if flip:
            before, after = after, before
        columns = slice(y * z, (y + 1) * z)
        rim_ref[0:c, columns] = before.astype(BF16)
        rim_ref[c : 2 * c, columns] = block
        rim_ref[2 * c : 3 * c, columns] = after.astype(BF16)
        rim_ref[3 * c : 4 * c, columns] = block


def conv_kernel(
    flip, body_ref, xlo_ref, xhi_ref, ylo_ref, yhi_ref, weight_ref, out_ref, rim_ref
):
    cx, cy, c, z = body_ref.shape
    for p in range(cx + 2):
        blocks = plane_rows(p, cx, body_ref, xlo_ref, xhi_ref, ylo_ref, yhi_ref)
        fill_shifts(blocks, rim_ref, flip)
        places = [a for a in range(3) if 0 <= p - (2 - a if flip else a) < cx]
        first = places[0]
        got = jnp.dot(
            weight_ref[first * 3 * c : (places[-1] + 1) * 3 * c, :],
            rim_ref[...],
            preferred_element_type=F32,
        )
        for a in places:
            x = p - (2 - a if flip else a)
            total = None
            for b in range(3):
                row = ((a - first) * 3 + b) * c
                skip = 2 - b if flip else b
                term = got[row : row + c, skip * z : (skip + cy) * z]
                total = term if total is None else total + term
            if p == x:
                out_ref[x] = total
            else:
                out_ref[x] += total


def weight_grad_kernel(
    grad_ref,
    body_ref,
    xlo_any,
    xhi_any,
    ylo_any,
    yhi_any,
    out_ref,
    rim_ref,
    wide_ref,
    sum_ref,
    xlo_ref,
    xhi_ref,
    ylo_ref,
    yhi_ref,
    sem_ref,
):
    cx, cy, c, z = body_ref.shape
    group = 3 * c
    held = (xlo_ref, xhi_ref, ylo_ref, yhi_ref)
    copies = [
        pltpu.make_async_copy(given, ref, sem_ref.at[i])
        for i, (given, ref) in enumerate(zip((xlo_any, xhi_any, ylo_any, yhi_any), held))
    ]
    for copy in copies:
        copy.start()
    wide_ref[...] = jnp.zeros_like(wide_ref)
    for x in range(cx):
        for b in range(3):
            for y in range(cy):
                row = x * group + b * c
                wide_ref[row : row + c, (y + b) * z : (y + b + 1) * z] = grad_ref[x, y]
    sum_ref[...] = jnp.zeros_like(sum_ref)
    for copy in copies:
        copy.wait()
    for p in range(cx + 2):
        fill_shifts(plane_rows(p, cx, body_ref, xlo_ref, xhi_ref, ylo_ref, yhi_ref), rim_ref)
        first, last = max(0, p - 2), min(cx - 1, p)
        got = lax.dot_general(
            wide_ref[first * group : (last + 1) * group, :],
            rim_ref[...],
            (((1,), (1,)), ((), ())),
            preferred_element_type=F32,
        )
        for x in range(first, last + 1):
            a = p - x
            sum_ref[a * group : (a + 1) * group, :] += got[
                (x - first) * group : (x - first + 1) * group, :
            ]
    out_ref[: 9 * c] = sum_ref[:, : 2 * c]
    last = [sum_ref[k * c : (k + 1) * c, 2 * c : 3 * c] for k in range(9)]
    last.append(jnp.zeros((c, c), F32))
    for k in range(5):
        row = (9 + k) * c
        out_ref[row : row + c] = jnp.concatenate(last[2 * k : 2 * k + 2], axis=1)
    out_ref[14 * c :] = jnp.zeros((2 * c, 2 * c), F32)


def gelu_kernel(
    nx,
    stencil_ref,
    slab_ref,
    cot_ref,
    inverse_ref,
    forward_ref,
    out_ref,
    turned_ref,
    message_ref,
    back_ref,
):
    c, cx, cy, z = cot_ref.shape
    root = math.sqrt(2.0 / math.pi)
    for x in range(cx):
        spectral = z_inverse(slab_ref, inverse_ref[...], x, nx).reshape(cy, c, z)
        stencil = jnp.stack([stencil_ref[x, :, y * z : (y + 1) * z] for y in range(cy)])
        pre = spectral + stencil
        cot = jnp.swapaxes(cot_ref[:, x].astype(F32), 0, 1)
        square = pre * pre
        bent = jnp.tanh(root * (pre * (1.0 + 0.044715 * square)))
        half = 0.5 + 0.5 * bent
        slope = half + (0.5 * pre) * (1.0 - bent * bent) * (root * (1.0 + 0.134145 * square))
        out_ref[:, x] = jnp.swapaxes(pre * half, 0, 1).astype(BF16)
        grad = (cot * slope).astype(BF16)
        turned_ref[x] = grad
        z_forward(grad.reshape(cy * c, z), forward_ref[...], back_ref, x, nx)
    ny = message_ref.shape[0] // nx
    for owner in range(nx):
        block = back_ref[owner].astype(BF16)
        for copy in range(ny):
            message_ref[owner * ny + copy] = block


def finish_kernel(
    nx,
    scale,
    stencil_ref,
    message_ref,
    inverse_ref,
    out_ref,
    taps_ref,
    point_ref,
    packed_ref,
    turned_ref,
):
    c, cx, cy, z = out_ref.shape
    for x in range(cx):
        spectral = z_inverse(message_ref, inverse_ref[...], x, nx).reshape(cy, c, z)
        stencil = jnp.stack([stencil_ref[x, :, y * z : (y + 1) * z] for y in range(cy)])
        out_ref[:, x] = jnp.swapaxes(spectral + stencil, 0, 1)
    skip = 2 * MZ * cx // nx
    unpack(scale, skip, message_ref, taps_ref, point_ref, packed_ref, turned_ref)


def x_kernel(table_ref, data_ref, out_ref):
    data = data_ref[...].astype(F32)
    lanes = data.shape[2]
    rows = table_ref.shape[1] // (3 * data.shape[0])
    flat = pieces(data[:, :rows].reshape(-1, lanes))
    got = jnp.dot(table_ref[...], flat, preferred_element_type=F32).astype(out_ref.dtype)
    count = got.shape[0] // out_ref.shape[0]
    for owner in range(out_ref.shape[0]):
        out_ref[owner, :count] = got[owner * count : (owner + 1) * count]
    if data.shape[1] > rows:
        extra = data[:, rows:].sum(0)
        extra = extra.astype(out_ref.dtype)
        for owner in range(out_ref.shape[0]):
            out_ref[owner, count:] = extra


def taps_kernel(taps_ref, point_ref, forward_ref, back_ref, turned_ref):
    turned_ref[...] = taps_ref[...].astype(F32).T
    forward_ref[...] = jnp.zeros_like(forward_ref)
    back_ref[...] = jnp.zeros_like(back_ref)
    for tap in range(27):
        rows = slice(tap // 3 * C, (tap // 3 + 1) * C)
        columns = slice(tap % 3 * C, (tap % 3 + 1) * C)
        block = turned_ref[pl.ds(tap, C, stride=27), :]
        back_ref[rows, columns] = block.astype(BF16)
        forward_ref[rows, columns] = block.T.astype(BF16)
    point = point_ref[...].astype(F32)
    forward_ref[4 * C : 5 * C, 3 * C :] = point.astype(BF16)
    back_ref[4 * C : 5 * C, 3 * C :] = point.T.astype(BF16)


def unpack(scale, skip, message_ref, taps_ref, point_ref, packed_ref, turned_ref):
    devices, rows, lanes = message_ref.shape
    per, tiles_in = rows - skip, lanes // 128
    for owner in range(devices):
        message = message_ref[owner].astype(F32)
        for tile in range(tiles_in):
            row = (owner * tiles_in + tile) * per
            packed_ref[row : row + per] = message[skip:, tile * 128 : (tile + 1) * 128]
    for tap in range(27):
        group, e = tap // 3, tap % 3
        if e < 2:
            block = packed_ref[group * C : (group + 1) * C, e * C : (e + 1) * C]
        else:
            row = (9 + group // 2) * C
            block = packed_ref[row : row + C, group % 2 * C : (group % 2 + 1) * C]
        block = block * scale
        if tap == 13:
            point_ref[...] = block
        turned_ref[pl.ds(tap, C, stride=27), :] = block.T
    taps_ref[...] = turned_ref[...].T


QUAD = 4
SPAN = 8 * C


def y_forward(mz, blocks, table_ref, rows_ref, store):
    ny, cy = len(blocks), blocks[0].shape[1] // C
    count = rows_ref.shape[1] // C
    for owner in range(ny):
        data = blocks[owner]
        for part in range(2):
            for kz in range(mz):
                mx = count // mz
                start = (part * mz + kz) * mx
                block = data[start : start + mx]
                block = jnp.stack([block[:, y * C : (y + 1) * C] for y in range(cy)])
                block = jnp.swapaxes(block, 0, 1)
                row = (part * ny + owner) * cy
                for kx in range(mx):
                    column = (kz * mx + kx) * C
                    rows_ref[row : row + cy, column : column + C] = block[kx]
    got = jnp.dot(table_ref[: 2 * MY], pieces(rows_ref[...]), preferred_element_type=F32)
    for q in range(count):
        block = got[:, q * C : (q + 1) * C]
        for part in range(2):
            store(q // QUAD, part, q % QUAD, block[part * MY : (part + 1) * MY])


def y_inverse(mz, sum_ref, table_ref, out_ref, block_ref):
    rows = [
        jnp.concatenate(
            [
                sum_ref[group, place(part, pair), :]
                for group in range(sum_ref.shape[0])
                for pair in range(QUAD)
            ],
            axis=1,
        )
        for part in range(2)
    ]
    got = jnp.dot(
        table_ref[2 * MY :, : 6 * MY],
        pieces(jnp.concatenate(rows, axis=0)),
        preferred_element_type=F32,
    )
    ny, _, lanes = out_ref.shape
    cy = lanes // C
    count = got.shape[1] // C
    mx = count // mz
    for owner in range(ny):
        for part in range(2):
            for kz in range(mz):
                row = (part * ny + owner) * cy
                block = got[row : row + cy, kz * mx * C : (kz + 1) * mx * C]
                block = jnp.stack([block[:, kx * C : (kx + 1) * C] for kx in range(mx)])
                block = jnp.swapaxes(block, 0, 1)
                start = (part * mz + kz) * mx
                for y in range(cy):
                    block_ref[owner, start : start + mx, y * C : (y + 1) * C] = block[y]
    out_ref[...] = block_ref[...].astype(out_ref.dtype)


def place(part, pair):
    start = (part * QUAD + pair) * MY
    return slice(start, start + MY)


def spread_table():
    return np.tile(np.kron(np.eye(C), np.ones((1, C))), (2, 1)).astype(jnp.bfloat16)


def gather_table():
    return np.kron(np.eye(SPAN // C), np.ones((1, C))).astype(jnp.bfloat16)


def spread_modes(modes, table_ref, spread_refs):
    count = C * C // SPAN
    made = set()

    def get(piece):
        for p in range(piece, min(piece + 2, count)):
            if p not in made:
                made.add(p)
                spread_refs[p % 2][...] = jnp.dot(
                    modes, table_ref[:, p * SPAN : (p + 1) * SPAN], preferred_element_type=F32
                )
        return spread_refs[piece % 2]

    return get


def weight_copies(weight_ref, held_ref, sem_ref):
    per = weight_ref.shape[2] // QUAD
    return [
        pltpu.make_async_copy(
            weight_ref.at[:, g // per, g % per * QUAD : (g % per + 1) * QUAD],
            held_ref.at[g],
            sem_ref.at[g],
        )
        for g in range(held_ref.shape[0])
    ]


def mix_kernel(
    mz,
    data_ref,
    weight_ref,
    table_ref,
    turn_ref,
    modes_ref,
    out_ref,
    sum_ref,
    rows_ref,
    block_ref,
    held_ref,
    sem_ref,
    spread_ref,
    spread_sem_ref,
    even_ref,
    odd_ref,
    total_ref,
):
    copies = weight_copies(weight_ref, held_ref, sem_ref)
    table_copy = pltpu.make_async_copy(table_ref, spread_ref, spread_sem_ref)
    table_copy.start()
    for copy in copies:
        copy.start()

    def store(group, part, pair, values):
        high = values.astype(BF16)
        low = (values - high.astype(F32)).astype(BF16)
        modes_ref[group, place(part, pair), :] = jnp.concatenate([high, low], axis=1)

    blocks = [data_ref[owner] for owner in range(data_ref.shape[0])]
    y_forward(mz, blocks, turn_ref, rows_ref, store)
    table_copy.wait()
    for group, copy in enumerate(copies):
        copy.wait()
        spread = spread_modes(modes_ref[group], spread_ref, (even_ref, odd_ref))
        for piece in range(C * C // SPAN):
            modes = spread(piece)
            for pair in range(QUAD):
                real = imag = None
                for tile in range(SPAN // (2 * C)):
                    inside = slice(tile * 2 * C, (tile + 1) * 2 * C)
                    columns = slice(piece * SPAN + inside.start, piece * SPAN + inside.stop)
                    mode_re = modes[place(0, pair), inside]
                    mode_im = modes[place(1, pair), inside]
                    weight_re = held_ref[group, 0, pair, :, columns].astype(F32)
                    weight_im = held_ref[group, 1, pair, :, columns].astype(F32)
                    term_re = mode_re * weight_re - mode_im * weight_im
                    term_im = mode_re * weight_im + mode_im * weight_re
                    real = term_re if real is None else real + term_re
                    imag = term_im if imag is None else imag + term_im
                if piece:
                    real += total_ref[place(0, pair), :]
                    imag += total_ref[place(1, pair), :]
                total_ref[place(0, pair), :] = real
                total_ref[place(1, pair), :] = imag
        total = total_ref[...]
        sum_ref[group] = total[:, :C] + total[:, C:]
    y_inverse(mz, sum_ref, turn_ref, out_ref, block_ref)


def mix_back_kernel(
    mz,
    data_ref,
    weight_ref,
    table_ref,
    turn_ref,
    x_ref,
    modes_ref,
    out_ref,
    sum_ref,
    rows_ref,
    block_ref,
    held_ref,
    sem_ref,
    term_ref,
):
    copies = weight_copies(weight_ref, held_ref, sem_ref)
    for copy in copies:
        copy.start()

    def store(group, part, pair, values):
        modes_ref[group, place(part, pair), :] = jnp.concatenate([values, values], axis=1)

    ny = block_ref.shape[0]
    size = x_ref.shape[1] // 3
    blocks = []
    for owner in range(ny):
        rows = jnp.concatenate(
            [data_ref[i].astype(F32) for i in range(owner, data_ref.shape[0], ny)], axis=0
        ).astype(BF16)
        blocks.append(
            jnp.dot(x_ref[:, :size], rows, preferred_element_type=F32)
            + jnp.dot(x_ref[:, 2 * size :], rows, preferred_element_type=F32)
        )
    y_forward(mz, blocks, turn_ref, rows_ref, store)
    for group, copy in enumerate(copies):
        copy.wait()
        total = []
        for piece in range(C * C // SPAN):
            for pair in range(QUAD):
                mode_re = modes_ref[group, place(0, pair), :]
                mode_im = modes_ref[group, place(1, pair), :]
                for tile in range(SPAN // (2 * C)):
                    start = piece * SPAN + tile * 2 * C
                    columns = slice(start, start + 2 * C)
                    weight_re = held_ref[group, 0, pair, :, columns].astype(F32)
                    weight_im = held_ref[group, 1, pair, :, columns].astype(F32)
                    term_ref[place(0, pair), columns] = (
                        weight_re * mode_re + weight_im * mode_im
                    ).astype(BF16)
                    term_ref[place(1, pair), columns] = (
                        weight_re * mode_im - weight_im * mode_re
                    ).astype(BF16)
            total.append(
                lax.dot_general(
                    table_ref[...],
                    term_ref[:, piece * SPAN : (piece + 1) * SPAN],
                    (((1,), (1,)), ((), ())),
                    preferred_element_type=F32,
                )
            )
        sum_ref[group] = jnp.concatenate(total, axis=0).T
    y_inverse(mz, sum_ref, turn_ref, out_ref, block_ref)


def outer_kernel(alpha, modes_ref, back_ref, table_ref, out_ref):
    count = C * C // SPAN
    made = lambda piece: jnp.dot(
        modes_ref[0],
        table_ref[:, piece * SPAN : (piece + 1) * SPAN],
        preferred_element_type=F32,
    )
    ahead = made(0)
    for piece in range(count):
        modes = ahead
        if piece + 1 < count:
            ahead = made(piece + 1)
        for pair in range(QUAD):
            back_re = back_ref[0, place(0, pair), :] * alpha
            back_im = back_ref[0, place(1, pair), :] * alpha
            for tile in range(SPAN // (2 * C)):
                inside = slice(tile * 2 * C, (tile + 1) * 2 * C)
                columns = slice(piece * SPAN + inside.start, piece * SPAN + inside.stop)
                mode_re = modes[place(0, pair), inside]
                mode_im = modes[place(1, pair), inside]
                out_ref[0, 0, pair, :, columns] = mode_re * back_re + mode_im * back_im
                out_ref[1, 0, pair, :, columns] = mode_re * back_im - mode_im * back_re


def in_hbm(value):
    return pltpu.with_memory_space_constraint(value, pltpu.HBM)


def whole():
    return pl.BlockSpec(memory_space=pltpu.VMEM)


def params(mib):
    return pltpu.CompilerParams(vmem_limit_bytes=mib * MIB)


def cost(flops, moved):
    return pl.CostEstimate(flops=int(flops), bytes_accessed=int(moved), transcendentals=0)


def call(kernel, outs, args, scratch=(), mib=24, flops=0, moved=0, anywhere=()):
    return pl.pallas_call(
        kernel,
        out_shape=[jax.ShapeDtypeStruct(*out) for out in outs],
        in_specs=[
            pl.BlockSpec(memory_space=pl.ANY) if i in anywhere else whole()
            for i in range(len(args))
        ],
        out_specs=[whole() for _ in outs],
        scratch_shapes=list(scratch),
        compiler_params=params(mib),
        cost_estimate=cost(flops, moved),
    )(*args)


def per_mode(kernel, data, weight, table, tables, modes, kind, scratch=()):
    _, mz, mx, my, wide = weight.shape
    groups = mz * mx // QUAD
    rows = 2 * QUAD * MY
    modes_shape = (groups, rows, modes[0])
    block = (MX // mx, 2 * mz * mx, data.shape[2])
    return pl.pallas_call(
        functools.partial(kernel, mz),
        in_specs=[
            whole(),
            pl.BlockSpec(memory_space=pl.ANY),
            pl.BlockSpec(memory_space=pl.ANY) if kernel is mix_kernel else whole(),
        ]
        + [whole() for _ in tables],
        out_specs=[whole(), whole()],
        out_shape=[
            jax.ShapeDtypeStruct(modes_shape, modes[1]),
            jax.ShapeDtypeStruct(block, kind),
        ],
        scratch_shapes=[
            pltpu.VMEM((groups, rows, C), F32),
            pltpu.VMEM((tables[0].shape[0] - 2 * MY, mz * mx * C), F32),
            pltpu.VMEM(block, F32),
            pltpu.VMEM((groups, 2, QUAD, my, wide), BF16),
            pltpu.SemaphoreType.DMA((groups,)),
            *scratch,
        ],
        compiler_params=params(24),
        cost_estimate=cost(weight.size * 8, weight.size * 2),
    )(data, in_hbm(weight), in_hbm(table), *tables)


def outer(modes, back, table, shape, alpha, start, count, prior=None):
    def kernel(*refs):
        outer_kernel(alpha, *refs[:3], refs[-1])

    per = shape[2] // QUAD
    group = lambda ref: pl.BlockSpec((1,) + ref.shape[1:], lambda step: (step + start, 0, 0))
    given = () if prior is None else (prior,)
    return pl.pallas_call(
        kernel,
        grid=(count,),
        in_specs=[group(modes), group(back), pl.BlockSpec(table.shape, lambda step: (0, 0))]
        + [pl.BlockSpec(memory_space=pl.ANY)] * len(given),
        out_specs=pl.BlockSpec(
            (2, 1, QUAD) + shape[3:],
            lambda step: (0, (step + start) // per, (step + start) % per, 0, 0),
        ),
        out_shape=jax.ShapeDtypeStruct(shape, F32),
        input_output_aliases={3: 0} if given else {},
        compiler_params=params(20),
        cost_estimate=cost(
            math.prod(shape) * 4 * count / modes.shape[0],
            math.prod(shape) * 4 * count / modes.shape[0],
        ),
    )(modes, back, in_hbm(table), *given)


def shift(block, axis, step):
    count = lax.axis_size(axis)
    pairs = [(i, i + step) for i in range(count) if 0 <= i + step < count]
    return lax.ppermute(block, axis, pairs)


def x_halos(turned):
    return shift(turned[-1], "gx", 1), shift(turned[0], "gx", -1)


def y_halos(turned, xlo, xhi):
    edge = lambda y: jnp.concatenate([xlo[None, y], turned[:, y], xhi[None, y]], axis=0)
    return shift(edge(-1), "gy", 1), shift(edge(0), "gy", -1)


def conv(turned, rim, weight, flip):
    cx, cy, c, z = turned.shape
    return call(
        functools.partial(conv_kernel, flip),
        [((cx, c, cy * z), F32)],
        (turned, *map(in_hbm, rim), in_hbm(weight)),
        [pltpu.VMEM((4 * c, (cy + 2) * z), BF16)],
        mib=32,
        flops=2 * 27 * c * c * cx * cy * z,
        moved=turned.size * 8,
    )[0]


def weight_grad(grad, turned, rim):
    cx, cy, c, z = turned.shape
    return call(
        weight_grad_kernel,
        [((16 * c, 2 * c), F32)],
        (grad, turned, *map(in_hbm, rim)),
        [
            pltpu.VMEM((4 * c, (cy + 2) * z), BF16),
            pltpu.VMEM((cx * 3 * c, (cy + 2) * z), BF16),
            pltpu.VMEM((9 * c, 4 * c), F32),
            *(pltpu.VMEM(halo.shape, BF16) for halo in rim),
            pltpu.SemaphoreType.DMA((len(rim),)),
        ],
        anywhere=(2, 3, 4, 5),
        mib=32,
        flops=2 * 27 * c * c * cx * cy * z,
        moved=turned.size * 8,
    )[0]


def swap(block, axis):
    return lax.all_to_all(block, axis, split_axis=0, concat_axis=0, tiled=True)


def together(*values):
    return lax.optimization_barrier(values)


def body(state, cotangent, spectral_weight, stencil_weight, pointwise_weight):
    nx, ny = lax.axis_size("gx"), lax.axis_size("gy")
    c, cx, cy, z = state.shape
    _, mz, mx, _, _ = spectral_weight.shape
    wide_x, wide_y = cx * nx, cy * ny
    alpha = 1.0 / math.sqrt(wide_x * wide_y * z)
    beta = 1.0 / math.sqrt(2 * MX * MY * MZ)
    double = np.where(np.arange(MZ) == 0, 1.0, 2.0)
    ones = np.ones(MZ)
    z_state = jnp.asarray(z_forward_table(alpha * ones)(nx, mz))
    z_grad = jnp.asarray(z_forward_table(double)(nx, mz))
    z_spectral = jnp.asarray(z_inverse_table(nx, mz, beta * double))
    z_back = jnp.asarray(z_inverse_table(nx, mz, alpha * beta * ones))
    x_fwd, x_inv = (jnp.asarray(t) for t in x_tables(wide_x, mz, mx))
    y_turn = jnp.asarray(y_table(wide_y))
    spread, gather = jnp.asarray(spread_table()), jnp.asarray(gather_table())
    lanes = cy * c
    x_rows = cx * 2 * mz

    def x_stage(table, block, lead, kind=F32, extra=0):
        rows = table.shape[0] // lead + extra
        return call(
            x_kernel,
            [((lead, rows, lanes), kind)],
            (table, block),
            mib=16,
            flops=2 * table.size * lanes,
            moved=8 * block.size,
        )[0]

    slab_shape = ((nx, x_rows, lanes), F32)
    turned_shape = ((cx, cy, c, z), BF16)

    conv_table, back_table = call(
        taps_kernel,
        [((9 * c, 4 * c), BF16)] * 2,
        (in_hbm(stencil_weight), in_hbm(pointwise_weight)),
        [pltpu.VMEM((27 * c, c), F32)],
        moved=stencil_weight.size * 6,
    )
    tables = (x_fwd, x_inv, y_turn)
    turned, slab, *held = call(
        functools.partial(prep_kernel, nx),
        [turned_shape, slab_shape] + [(t.shape, BF16) for t in tables],
        (in_hbm(state), in_hbm(z_state), *map(in_hbm, tables)),
        flops=2 * 96 * state.size,
        moved=state.size * 5,
    )
    x_mine = x_fwd.reshape(ny, -1, x_fwd.shape[1])
    x_mine = lax.dynamic_index_in_dim(x_mine, lax.axis_index("gy"), 0, keepdims=False)
    x_fwd, x_inv, y_turn = held

    block = x_stage(x_fwd, swap(slab, "gx"), ny)
    block, conv_table, back_table, x_mine, *faces = together(
        block, conv_table, back_table, x_mine, *x_halos(turned)
    )
    modes_in, block = per_mode(
        mix_kernel,
        swap(block, "gy"),
        spectral_weight,
        spread,
        (y_turn,),
        (2 * c, BF16),
        F32,
        [pltpu.VMEM(spread.shape, BF16), pltpu.SemaphoreType.DMA]
        + [pltpu.VMEM((2 * QUAD * MY, SPAN), F32)] * 2
        + [pltpu.VMEM((2 * QUAD * MY, 2 * c), F32)],
    )
    block, *edges = together(block, *y_halos(turned, *faces))
    rim = (*faces, *edges)
    block = x_stage(x_inv, swap(block, "gy"), nx)
    stencil = conv(turned, rim, conv_table, False)
    output, grad, slab = call(
        functools.partial(gelu_kernel, nx),
        [((c, cx, cy, z), BF16), turned_shape, ((nx * ny, x_rows, lanes), BF16)],
        (stencil, swap(block, "gx"), cotangent, z_spectral, z_grad),
        [pltpu.VMEM(slab_shape[0], F32)],
        flops=2 * 192 * state.size,
        moved=state.size * 12,
    )

    grad_taps = weight_grad(grad, turned, rim)
    faces = x_halos(grad)
    block = swap(slab, ("gx", "gy"))
    edges = y_halos(grad, *faces)
    block, grad_taps, ylo, *faces = together(block, grad_taps, edges[0], *faces)
    mine = swap(grad_taps.reshape(nx, -1, 2 * c), "gx").sum(0)
    back_modes, block = per_mode(
        mix_back_kernel,
        block,
        spectral_weight,
        gather,
        (y_turn, x_mine),
        (2 * c, F32),
        BF16,
        [pltpu.VMEM((2 * QUAD * MY, c * c), BF16)],
    )
    packed = jnp.concatenate(jnp.split(mine, lanes // (2 * c)), axis=1).astype(BF16)
    extra = packed.shape[0]
    packed = jnp.broadcast_to(packed[None], (ny, extra, lanes))
    block, yhi = together(jnp.concatenate([block, packed], axis=1), edges[1])
    block = x_stage(x_inv, swap(block, "gy"), nx, BF16, extra)
    shape = spectral_weight.shape
    groups = modes_in.shape[0]
    early = groups * 3 // 4
    grad_modes = None
    if early:
        grad_modes = outer(modes_in, back_modes, spread, shape, alpha, 0, early)
        block, grad_modes = together(block, grad_modes)
    message = swap(block, "gx")
    stencil_back = conv(grad, (*faces, ylo, yhi), back_table, True)
    grad_modes = outer(
        modes_in, back_modes, spread, shape, alpha, early, groups - early, grad_modes
    )
    grad_state, grad_stencil, grad_point = call(
        functools.partial(finish_kernel, nx, alpha),
        [((c, cx, cy, z), F32), ((c, 27 * c), F32), ((c, c), F32)],
        (stencil_back, message, z_back),
        [pltpu.VMEM(grad_taps.shape, F32), pltpu.VMEM((27 * c, c), F32)],
        flops=2 * 96 * state.size,
        moved=state.size * 10,
    )
    return (output, grad_state, grad_modes, grad_stencil, grad_point)


def solution(mesh):
    in_specs = (
        P(None, "gx", "gy", None),
        P(None, "gx", "gy", None),
        P(None, "gx", "gy", None, None),
        P(),
        P(),
    )
    out_specs = (
        P(None, "gx", "gy", None),
        P(None, "gx", "gy", None),
        P(None, "gx", "gy", None, None),
        P(),
        P(),
    )
    return jax.shard_map(body, mesh=mesh, in_specs=in_specs, out_specs=out_specs, check_vma=False)
```

```python
import functools
import math

import jax
import jax.numpy as jnp
import numpy as np
from jax import lax
from jax.experimental import pallas as pl
from jax.experimental.pallas import tpu as pltpu
from jax.sharding import PartitionSpec as P

C = 64
MX = 32
MY = 32
MZ = 16
Z = 128
MIB = 1 << 20

F32 = jnp.float32
BF16 = jnp.bfloat16


def angles(places, freqs, length):
    turns = np.outer(np.asarray(places), np.asarray(freqs)) % length
    return turns * (2.0 * np.pi / length)


def centred(count):
    steps = np.arange(count)
    return np.where(steps < count // 2, steps, steps - count)


def split(table, parts):
    rest = np.asarray(table, np.float64)
    out = []
    for _ in range(parts):
        piece = rest.astype(jnp.bfloat16)
        out.append(piece)
        rest = rest - piece.astype(np.float64)
    return out


def z_forward_table(scale):
    def build(nx, mz):
        theta = angles(np.arange(MZ), np.arange(Z), Z)
        pair = np.stack([np.cos(theta), -np.sin(theta)]) * scale[None, :, None]
        rows = pair.reshape(2, nx, mz, Z).transpose(1, 0, 2, 3).reshape(2 * MZ, Z)
        return np.concatenate(split(rows, 3), axis=0)

    return build


def z_inverse_table(nx, mz, scale):
    theta = angles(np.arange(MZ), np.arange(Z), Z)
    pair = np.stack([np.cos(theta), -np.sin(theta)]) * scale[None, :, None]
    rows = pair.reshape(2, nx, mz, Z).transpose(1, 0, 2, 3).reshape(2 * MZ, Z)
    high, low = split(rows, 2)
    return np.concatenate([high, high, low], axis=0)


def rotation(theta, sign):
    cosine, sine = np.cos(theta), sign * np.sin(theta)
    return np.stack([np.stack([cosine, -sine], 1), np.stack([sine, cosine], 1)])


def against_pieces(*tables):
    out = []
    for table in tables:
        high, low = split(table, 2)
        out.append(np.concatenate([high, high, low], axis=1))
    return out


def x_tables(wide, mz, mx):
    theta = angles(centred(MX), np.arange(wide), wide)
    eye = np.eye(mz)
    forward = np.einsum("rkRx,zZ->krzxRZ", rotation(theta, -1.0), eye)
    inverse = np.einsum("rxRk,zZ->xrzkRZ", rotation(theta.T, 1.0), eye)
    size_k, size_x = MX * 2 * mz, wide * 2 * mz
    forward = forward.reshape(MX // mx, mx, 2, mz, size_x).transpose(0, 2, 3, 1, 4)
    inverse = inverse.reshape(size_x, MX // mx, mx, 2, mz).transpose(0, 1, 3, 4, 2)
    return against_pieces(forward.reshape(size_k, size_x), inverse.reshape(size_x, size_k))


def y_table(wide):
    theta = angles(centred(MY), np.arange(wide), wide)
    forward = rotation(theta, -1.0).reshape(2 * MY, 2 * wide)
    inverse = rotation(theta.T, 1.0).reshape(2 * wide, 2 * MY)
    forward, inverse = against_pieces(forward, inverse)
    inverse = np.pad(inverse, ((0, 0), (0, forward.shape[1] - inverse.shape[1])))
    return np.concatenate([forward, inverse], axis=0)


def pieces(values):
    high = values.astype(BF16)
    low = (values - high.astype(F32)).astype(BF16)
    return jnp.concatenate([high, low, high], axis=0)


def z_forward(rows, table, out_ref, x, nx):
    got = lax.dot_general(table, rows, (((1,), (1,)), ((), ())), preferred_element_type=F32)
    size = 2 * MZ
    total = got[:size] + (got[size : 2 * size] + got[2 * size :])
    per = size // nx
    for owner in range(nx):
        out_ref[owner, x * per : (x + 1) * per, :] = total[owner * per : (owner + 1) * per]


def z_inverse(in_ref, table, x, nx):
    per = 2 * MZ // nx
    rows = jnp.concatenate(
        [in_ref[owner].astype(F32)[x * per : (x + 1) * per] for owner in range(nx)], axis=0
    )
    return lax.dot_general(
        pieces(rows), table, (((0,), (0,)), ((), ())), preferred_element_type=F32
    )


def prep_kernel(
    nx,
    field_ref,
    table_ref,
    forward_ref,
    inverse_ref,
    turn_ref,
    turned_ref,
    slab_ref,
    forward_out_ref,
    inverse_out_ref,
    turn_out_ref,
):
    forward_out_ref[...] = forward_ref[...]
    inverse_out_ref[...] = inverse_ref[...]
    turn_out_ref[...] = turn_ref[...]
    c, cx, cy, z = field_ref.shape
    for x in range(cx):
        block = jnp.swapaxes(field_ref[:, x].astype(F32), 0, 1)
        turned = block.astype(BF16)
        turned_ref[x] = turned
        z_forward(turned.reshape(cy * c, z), table_ref[...], slab_ref, x, nx)


def plane_rows(p, cx, body_ref, xlo_ref, xhi_ref, ylo_ref, yhi_ref):
    cy = body_ref.shape[1]
    if p == 0:
        middle = [xlo_ref[y] for y in range(cy)]
    elif p == cx + 1:
        middle = [xhi_ref[y] for y in range(cy)]
    else:
        middle = [body_ref[p - 1, y] for y in range(cy)]
    return [ylo_ref[p]] + middle + [yhi_ref[p]]


def fill_shifts(blocks, rim_ref, flip=False):
    c, z = blocks[0].shape
    lane = lax.broadcasted_iota(jnp.int32, (c, z), 1)
    for y, block in enumerate(blocks):
        wide = block.astype(F32)
        before = jnp.where(lane == 0, 0.0, pltpu.roll(wide, 1, 1))
        after = jnp.where(lane == z - 1, 0.0, pltpu.roll(wide, z - 1, 1))
        if flip:
            before, after = after, before
        columns = slice(y * z, (y + 1) * z)
        rim_ref[0:c, columns] = before.astype(BF16)
        rim_ref[c : 2 * c, columns] = block
        rim_ref[2 * c : 3 * c, columns] = after.astype(BF16)
        rim_ref[3 * c : 4 * c, columns] = block


def conv_kernel(
    flip, body_ref, xlo_ref, xhi_ref, ylo_ref, yhi_ref, weight_ref, out_ref, rim_ref
):
    cx, cy, c, z = body_ref.shape
    for p in range(cx + 2):
        blocks = plane_rows(p, cx, body_ref, xlo_ref, xhi_ref, ylo_ref, yhi_ref)
        fill_shifts(blocks, rim_ref, flip)
        places = [a for a in range(3) if 0 <= p - (2 - a if flip else a) < cx]
        first = places[0]
        got = jnp.dot(
            weight_ref[first * 3 * c : (places[-1] + 1) * 3 * c, :],
            rim_ref[...],
            preferred_element_type=F32,
        )
        for a in places:
            x = p - (2 - a if flip else a)
            total = None
            for b in range(3):
                row = ((a - first) * 3 + b) * c
                skip = 2 - b if flip else b
                term = got[row : row + c, skip * z : (skip + cy) * z]
                total = term if total is None else total + term
            if p == x:
                out_ref[x] = total
            else:
                out_ref[x] += total


def weight_grad_kernel(
    grad_ref,
    body_ref,
    xlo_any,
    xhi_any,
    ylo_any,
    yhi_any,
    slab_ref,
    message_ref,
    out_ref,
    rim_ref,
    wide_ref,
    sum_ref,
    xlo_ref,
    xhi_ref,
    ylo_ref,
    yhi_ref,
    sem_ref,
):
    cx, cy, c, z = body_ref.shape
    group = 3 * c
    held = (xlo_ref, xhi_ref, ylo_ref, yhi_ref)
    copies = [
        pltpu.make_async_copy(given, ref, sem_ref.at[i])
        for i, (given, ref) in enumerate(zip((xlo_any, xhi_any, ylo_any, yhi_any), held))
    ]
    for copy in copies:
        copy.start()
    wide_ref[...] = jnp.zeros_like(wide_ref)
    for x in range(cx):
        for b in range(3):
            for y in range(cy):
                row = x * group + b * c
                wide_ref[row : row + c, (y + b) * z : (y + b + 1) * z] = grad_ref[x, y]
    sum_ref[...] = jnp.zeros_like(sum_ref)
    for copy in copies:
        copy.wait()
    for p in range(cx + 2):
        fill_shifts(plane_rows(p, cx, body_ref, xlo_ref, xhi_ref, ylo_ref, yhi_ref), rim_ref)
        first, last = max(0, p - 2), min(cx - 1, p)
        got = lax.dot_general(
            wide_ref[first * group : (last + 1) * group, :],
            rim_ref[...],
            (((1,), (1,)), ((), ())),
            preferred_element_type=F32,
        )
        for x in range(first, last + 1):
            a = p - x
            sum_ref[a * group : (a + 1) * group, :] += got[
                (x - first) * group : (x - first + 1) * group, :
            ]
    out_ref[: 9 * c] = sum_ref[:, : 2 * c]
    last = [sum_ref[k * c : (k + 1) * c, 2 * c : 3 * c] for k in range(9)]
    last.append(jnp.zeros((c, c), F32))
    for k in range(5):
        row = (9 + k) * c
        out_ref[row : row + c] = jnp.concatenate(last[2 * k : 2 * k + 2], axis=1)
    out_ref[14 * c :] = jnp.zeros((2 * c, 2 * c), F32)
    devices, rows, lanes = message_ref.shape
    skip = slab_ref.shape[1]
    per, tiles_in = rows - skip, lanes // (2 * c)
    for device in range(devices):
        start = device * per * tiles_in
        share = [out_ref[start + t * per : start + (t + 1) * per] for t in range(tiles_in)]
        message_ref[device] = jnp.concatenate(
            [slab_ref[device].astype(F32), jnp.concatenate(share, axis=1)], axis=0
        ).astype(BF16)


def gelu_kernel(
    nx,
    stencil_ref,
    slab_ref,
    cot_ref,
    inverse_ref,
    forward_ref,
    out_ref,
    turned_ref,
    message_ref,
    back_ref,
):
    c, cx, cy, z = cot_ref.shape
    root = math.sqrt(2.0 / math.pi)
    for x in range(cx):
        spectral = z_inverse(slab_ref, inverse_ref[...], x, nx).reshape(cy, c, z)
        stencil = jnp.stack([stencil_ref[x, :, y * z : (y + 1) * z] for y in range(cy)])
        pre = spectral + stencil
        cot = jnp.swapaxes(cot_ref[:, x].astype(F32), 0, 1)
        square = pre * pre
        bent = jnp.tanh(root * (pre * (1.0 + 0.044715 * square)))
        half = 0.5 + 0.5 * bent
        slope = half + (0.5 * pre) * (1.0 - bent * bent) * (root * (1.0 + 0.134145 * square))
        out_ref[:, x] = jnp.swapaxes(pre * half, 0, 1).astype(BF16)
        grad = (cot * slope).astype(BF16)
        turned_ref[x] = grad
        z_forward(grad.reshape(cy * c, z), forward_ref[...], back_ref, x, nx)
    ny = message_ref.shape[0] // nx
    for owner in range(nx):
        block = back_ref[owner].astype(BF16)
        for copy in range(ny):
            message_ref[owner * ny + copy] = block


def finish_kernel(
    nx,
    shares,
    scale,
    stencil_ref,
    message_ref,
    inverse_ref,
    out_ref,
    taps_ref,
    point_ref,
    packed_ref,
    turned_ref,
):
    c, cx, cy, z = out_ref.shape
    for x in range(cx):
        spectral = z_inverse(message_ref, inverse_ref[...], x, nx).reshape(cy, c, z)
        stencil = jnp.stack([stencil_ref[x, :, y * z : (y + 1) * z] for y in range(cy)])
        out_ref[:, x] = jnp.swapaxes(spectral + stencil, 0, 1)
    skip = 2 * MZ * cx // nx
    unpack(scale, skip, shares, message_ref, taps_ref, point_ref, packed_ref, turned_ref)


def x_kernel(table_ref, data_ref, out_ref):
    data = data_ref[...].astype(F32)
    lanes = data.shape[2]
    rows = table_ref.shape[1] // (3 * data.shape[0])
    flat = pieces(data[:, :rows].reshape(-1, lanes))
    got = jnp.dot(table_ref[...], flat, preferred_element_type=F32).astype(out_ref.dtype)
    count = got.shape[0] // out_ref.shape[0]
    for owner in range(out_ref.shape[0]):
        out_ref[owner, :count] = got[owner * count : (owner + 1) * count]
    if data.shape[1] > rows:
        extra = jnp.concatenate([data[i, rows:] for i in range(data.shape[0])], axis=0)
        extra = extra.astype(out_ref.dtype)
        for owner in range(out_ref.shape[0]):
            out_ref[owner, count:] = extra


def taps_kernel(taps_ref, point_ref, forward_ref, back_ref, turned_ref):
    turned_ref[...] = taps_ref[...].astype(F32).T
    forward_ref[...] = jnp.zeros_like(forward_ref)
    back_ref[...] = jnp.zeros_like(back_ref)
    for tap in range(27):
        rows = slice(tap // 3 * C, (tap // 3 + 1) * C)
        columns = slice(tap % 3 * C, (tap % 3 + 1) * C)
        block = turned_ref[pl.ds(tap, C, stride=27), :]
        back_ref[rows, columns] = block.astype(BF16)
        forward_ref[rows, columns] = block.T.astype(BF16)
    point = point_ref[...].astype(F32)
    forward_ref[4 * C : 5 * C, 3 * C :] = point.astype(BF16)
    back_ref[4 * C : 5 * C, 3 * C :] = point.T.astype(BF16)


def unpack(scale, skip, shares, message_ref, taps_ref, point_ref, packed_ref, turned_ref):
    devices, rows, lanes = message_ref.shape
    per, tiles_in = (rows - skip) // shares, lanes // 128
    for owner in range(devices):
        message = message_ref[owner].astype(F32)[skip:]
        for share in range(shares):
            for tile in range(tiles_in):
                row = ((owner * shares + share) * tiles_in + tile) * per
                packed_ref[row : row + per] = message[
                    share * per : (share + 1) * per, tile * 128 : (tile + 1) * 128
                ]
    for tap in range(27):
        group, e = tap // 3, tap % 3
        if e < 2:
            block = packed_ref[group * C : (group + 1) * C, e * C : (e + 1) * C]
        else:
            row = (9 + group // 2) * C
            block = packed_ref[row : row + C, group % 2 * C : (group % 2 + 1) * C]
        block = block * scale
        if tap == 13:
            point_ref[...] = block
        turned_ref[pl.ds(tap, C, stride=27), :] = block.T
    taps_ref[...] = turned_ref[...].T


QUAD = 4
SPAN = 8 * C


def y_forward(mz, blocks, table_ref, rows_ref, store):
    ny, cy = len(blocks), blocks[0].shape[1] // C
    count = rows_ref.shape[1] // C
    for owner in range(ny):
        data = blocks[owner]
        for part in range(2):
            for kz in range(mz):
                mx = count // mz
                start = (part * mz + kz) * mx
                block = data[start : start + mx]
                block = jnp.stack([block[:, y * C : (y + 1) * C] for y in range(cy)])
                block = jnp.swapaxes(block, 0, 1)
                row = (part * ny + owner) * cy
                for kx in range(mx):
                    column = (kz * mx + kx) * C
                    rows_ref[row : row + cy, column : column + C] = block[kx]
    got = jnp.dot(table_ref[: 2 * MY], pieces(rows_ref[...]), preferred_element_type=F32)
    for q in range(count):
        block = got[:, q * C : (q + 1) * C]
        for part in range(2):
            store(q // QUAD, part, q % QUAD, block[part * MY : (part + 1) * MY])


def y_inverse(mz, sum_ref, table_ref, out_ref, block_ref):
    rows = [
        jnp.concatenate(
            [
                sum_ref[group, place(part, pair), :]
                for group in range(sum_ref.shape[0])
                for pair in range(QUAD)
            ],
            axis=1,
        )
        for part in range(2)
    ]
    got = jnp.dot(
        table_ref[2 * MY :, : 6 * MY],
        pieces(jnp.concatenate(rows, axis=0)),
        preferred_element_type=F32,
    )
    ny, _, lanes = out_ref.shape
    cy = lanes // C
    count = got.shape[1] // C
    mx = count // mz
    for owner in range(ny):
        for part in range(2):
            for kz in range(mz):
                row = (part * ny + owner) * cy
                block = got[row : row + cy, kz * mx * C : (kz + 1) * mx * C]
                block = jnp.stack([block[:, kx * C : (kx + 1) * C] for kx in range(mx)])
                block = jnp.swapaxes(block, 0, 1)
                start = (part * mz + kz) * mx
                for y in range(cy):
                    block_ref[owner, start : start + mx, y * C : (y + 1) * C] = block[y]
    out_ref[...] = block_ref[...].astype(out_ref.dtype)


def place(part, pair):
    start = (part * QUAD + pair) * MY
    return slice(start, start + MY)


def spread_table():
    return np.tile(np.kron(np.eye(C), np.ones((1, C))), (2, 1)).astype(jnp.bfloat16)


def gather_table():
    return np.kron(np.eye(SPAN // C), np.ones((1, C))).astype(jnp.bfloat16)


def spread_modes(modes, table_ref, spread_refs):
    count = C * C // SPAN
    made = set()

    def get(piece):
        for p in range(piece, min(piece + 2, count)):
            if p not in made:
                made.add(p)
                spread_refs[p % 2][...] = jnp.dot(
                    modes, table_ref[:, p * SPAN : (p + 1) * SPAN], preferred_element_type=F32
                )
        return spread_refs[piece % 2]

    return get


def weight_copies(weight_ref, held_ref, sem_ref):
    per = weight_ref.shape[2] // QUAD
    return [
        pltpu.make_async_copy(
            weight_ref.at[:, g // per, g % per * QUAD : (g % per + 1) * QUAD],
            held_ref.at[g],
            sem_ref.at[g],
        )
        for g in range(held_ref.shape[0])
    ]


def mix_kernel(
    mz,
    data_ref,
    weight_ref,
    table_ref,
    turn_ref,
    modes_ref,
    out_ref,
    sum_ref,
    rows_ref,
    block_ref,
    held_ref,
    sem_ref,
    spread_ref,
    spread_sem_ref,
    even_ref,
    odd_ref,
    total_ref,
):
    copies = weight_copies(weight_ref, held_ref, sem_ref)
    table_copy = pltpu.make_async_copy(table_ref, spread_ref, spread_sem_ref)
    table_copy.start()
    for copy in copies:
        copy.start()

    def store(group, part, pair, values):
        high = values.astype(BF16)
        low = (values - high.astype(F32)).astype(BF16)
        modes_ref[group, place(part, pair), :] = jnp.concatenate([high, low], axis=1)

    blocks = [data_ref[owner] for owner in range(data_ref.shape[0])]
    y_forward(mz, blocks, turn_ref, rows_ref, store)
    table_copy.wait()
    for group, copy in enumerate(copies):
        copy.wait()
        spread = spread_modes(modes_ref[group], spread_ref, (even_ref, odd_ref))
        for piece in range(C * C // SPAN):
            modes = spread(piece)
            for pair in range(QUAD):
                real = imag = None
                for tile in range(SPAN // (2 * C)):
                    inside = slice(tile * 2 * C, (tile + 1) * 2 * C)
                    columns = slice(piece * SPAN + inside.start, piece * SPAN + inside.stop)
                    mode_re = modes[place(0, pair), inside]
                    mode_im = modes[place(1, pair), inside]
                    weight_re = held_ref[group, 0, pair, :, columns].astype(F32)
                    weight_im = held_ref[group, 1, pair, :, columns].astype(F32)
                    term_re = mode_re * weight_re - mode_im * weight_im
                    term_im = mode_re * weight_im + mode_im * weight_re
                    real = term_re if real is None else real + term_re
                    imag = term_im if imag is None else imag + term_im
                if piece:
                    real += total_ref[place(0, pair), :]
                    imag += total_ref[place(1, pair), :]
                total_ref[place(0, pair), :] = real
                total_ref[place(1, pair), :] = imag
        total = total_ref[...]
        sum_ref[group] = total[:, :C] + total[:, C:]
    y_inverse(mz, sum_ref, turn_ref, out_ref, block_ref)


def mix_back_kernel(
    mz,
    data_ref,
    weight_ref,
    table_ref,
    turn_ref,
    x_ref,
    modes_ref,
    out_ref,
    sum_ref,
    rows_ref,
    block_ref,
    held_ref,
    sem_ref,
    term_ref,
):
    copies = weight_copies(weight_ref, held_ref, sem_ref)
    for copy in copies:
        copy.start()

    def store(group, part, pair, values):
        modes_ref[group, place(part, pair), :] = jnp.concatenate([values, values], axis=1)

    devices, ny = data_ref.shape[0], block_ref.shape[0]
    size = x_ref.shape[1] // 3
    skip = size * ny // devices
    share = data_ref[0].astype(F32)[skip:]
    for device in range(1, devices):
        share += data_ref[device].astype(F32)[skip:]
    blocks = []
    for owner in range(ny):
        rows = jnp.concatenate(
            [data_ref[i].astype(F32)[:skip] for i in range(owner, devices, ny)], axis=0
        ).astype(BF16)
        blocks.append(
            jnp.dot(x_ref[:, :size], rows, preferred_element_type=F32)
            + jnp.dot(x_ref[:, 2 * size :], rows, preferred_element_type=F32)
        )
    y_forward(mz, blocks, turn_ref, rows_ref, store)
    for group, copy in enumerate(copies):
        copy.wait()
        total = []
        for piece in range(C * C // SPAN):
            for pair in range(QUAD):
                mode_re = modes_ref[group, place(0, pair), :]
                mode_im = modes_ref[group, place(1, pair), :]
                for tile in range(SPAN // (2 * C)):
                    start = piece * SPAN + tile * 2 * C
                    columns = slice(start, start + 2 * C)
                    weight_re = held_ref[group, 0, pair, :, columns].astype(F32)
                    weight_im = held_ref[group, 1, pair, :, columns].astype(F32)
                    term_ref[place(0, pair), columns] = (
                        weight_re * mode_re + weight_im * mode_im
                    ).astype(BF16)
                    term_ref[place(1, pair), columns] = (
                        weight_re * mode_im - weight_im * mode_re
                    ).astype(BF16)
            total.append(
                lax.dot_general(
                    table_ref[...],
                    term_ref[:, piece * SPAN : (piece + 1) * SPAN],
                    (((1,), (1,)), ((), ())),
                    preferred_element_type=F32,
                )
            )
        sum_ref[group] = jnp.concatenate(total, axis=0).T
    y_inverse(mz, sum_ref, turn_ref, block_ref, block_ref)
    for owner in range(ny):
        out_ref[owner] = jnp.concatenate([block_ref[owner], share], axis=0).astype(BF16)


def outer_kernel(alpha, modes_ref, back_ref, table_ref, out_ref):
    count = C * C // SPAN
    made = lambda piece: jnp.dot(
        modes_ref[0],
        table_ref[:, piece * SPAN : (piece + 1) * SPAN],
        preferred_element_type=F32,
    )
    ahead = made(0)
    for piece in range(count):
        modes = ahead
        if piece + 1 < count:
            ahead = made(piece + 1)
        for pair in range(QUAD):
            back_re = back_ref[0, place(0, pair), :] * alpha
            back_im = back_ref[0, place(1, pair), :] * alpha
            for tile in range(SPAN // (2 * C)):
                inside = slice(tile * 2 * C, (tile + 1) * 2 * C)
                columns = slice(piece * SPAN + inside.start, piece * SPAN + inside.stop)
                mode_re = modes[place(0, pair), inside]
                mode_im = modes[place(1, pair), inside]
                out_ref[0, 0, pair, :, columns] = mode_re * back_re + mode_im * back_im
                out_ref[1, 0, pair, :, columns] = mode_re * back_im - mode_im * back_re


def in_hbm(value):
    return pltpu.with_memory_space_constraint(value, pltpu.HBM)


def whole():
    return pl.BlockSpec(memory_space=pltpu.VMEM)


def params(mib):
    return pltpu.CompilerParams(vmem_limit_bytes=mib * MIB)


def cost(flops, moved):
    return pl.CostEstimate(flops=int(flops), bytes_accessed=int(moved), transcendentals=0)


def call(kernel, outs, args, scratch=(), mib=24, flops=0, moved=0, anywhere=()):
    return pl.pallas_call(
        kernel,
        out_shape=[jax.ShapeDtypeStruct(*out) for out in outs],
        in_specs=[
            pl.BlockSpec(memory_space=pl.ANY) if i in anywhere else whole()
            for i in range(len(args))
        ],
        out_specs=[whole() for _ in outs],
        scratch_shapes=list(scratch),
        compiler_params=params(mib),
        cost_estimate=cost(flops, moved),
    )(*args)


def per_mode(kernel, data, weight, table, tables, modes, kind, scratch=(), extra=0):
    _, mz, mx, my, wide = weight.shape
    groups = mz * mx // QUAD
    rows = 2 * QUAD * MY
    modes_shape = (groups, rows, modes[0])
    block = (MX // mx, 2 * mz * mx, data.shape[2])
    return pl.pallas_call(
        functools.partial(kernel, mz),
        in_specs=[
            whole(),
            pl.BlockSpec(memory_space=pl.ANY),
            pl.BlockSpec(memory_space=pl.ANY) if kernel is mix_kernel else whole(),
        ]
        + [whole() for _ in tables],
        out_specs=[whole(), whole()],
        out_shape=[
            jax.ShapeDtypeStruct(modes_shape, modes[1]),
            jax.ShapeDtypeStruct((block[0], block[1] + extra, block[2]), kind),
        ],
        scratch_shapes=[
            pltpu.VMEM((groups, rows, C), F32),
            pltpu.VMEM((tables[0].shape[0] - 2 * MY, mz * mx * C), F32),
            pltpu.VMEM(block, F32),
            pltpu.VMEM((groups, 2, QUAD, my, wide), BF16),
            pltpu.SemaphoreType.DMA((groups,)),
            *scratch,
        ],
        compiler_params=params(24),
        cost_estimate=cost(weight.size * 8, weight.size * 2),
    )(data, in_hbm(weight), in_hbm(table), *tables)


def outer(modes, back, table, shape, alpha, start, count, prior=None):
    def kernel(*refs):
        outer_kernel(alpha, *refs[:3], refs[-1])

    per = shape[2] // QUAD
    group = lambda ref: pl.BlockSpec((1,) + ref.shape[1:], lambda step: (step + start, 0, 0))
    given = () if prior is None else (prior,)
    return pl.pallas_call(
        kernel,
        grid=(count,),
        in_specs=[group(modes), group(back), pl.BlockSpec(table.shape, lambda step: (0, 0))]
        + [pl.BlockSpec(memory_space=pl.ANY)] * len(given),
        out_specs=pl.BlockSpec(
            (2, 1, QUAD) + shape[3:],
            lambda step: (0, (step + start) // per, (step + start) % per, 0, 0),
        ),
        out_shape=jax.ShapeDtypeStruct(shape, F32),
        input_output_aliases={3: 0} if given else {},
        compiler_params=params(20),
        cost_estimate=cost(
            math.prod(shape) * 4 * count / modes.shape[0],
            math.prod(shape) * 4 * count / modes.shape[0],
        ),
    )(modes, back, in_hbm(table), *given)


def shift(block, axis, step):
    count = lax.axis_size(axis)
    pairs = [(i, i + step) for i in range(count) if 0 <= i + step < count]
    return lax.ppermute(block, axis, pairs)


def x_halos(turned):
    return shift(turned[-1], "gx", 1), shift(turned[0], "gx", -1)


def y_halos(turned, xlo, xhi):
    edge = lambda y: jnp.concatenate([xlo[None, y], turned[:, y], xhi[None, y]], axis=0)
    return shift(edge(-1), "gy", 1), shift(edge(0), "gy", -1)


def conv(turned, rim, weight, flip):
    cx, cy, c, z = turned.shape
    return call(
        functools.partial(conv_kernel, flip),
        [((cx, c, cy * z), F32)],
        (turned, *map(in_hbm, rim), in_hbm(weight)),
        [pltpu.VMEM((4 * c, (cy + 2) * z), BF16)],
        mib=32,
        flops=2 * 27 * c * c * cx * cy * z,
        moved=turned.size * 8,
    )[0]


def weight_grad(grad, turned, rim, slab):
    cx, cy, c, z = turned.shape
    devices, skip, lanes = slab.shape
    extra = 16 * c * 2 * c // (devices * lanes)
    return call(
        weight_grad_kernel,
        [((devices, skip + extra, lanes), BF16)],
        (grad, turned, *map(in_hbm, rim), slab),
        [
            pltpu.VMEM((16 * c, 2 * c), F32),
            pltpu.VMEM((4 * c, (cy + 2) * z), BF16),
            pltpu.VMEM((cx * 3 * c, (cy + 2) * z), BF16),
            pltpu.VMEM((9 * c, 4 * c), F32),
            *(pltpu.VMEM(halo.shape, BF16) for halo in rim),
            pltpu.SemaphoreType.DMA((len(rim),)),
        ],
        mib=32,
        flops=2 * 27 * c * c * cx * cy * z,
        moved=turned.size * 8,
        anywhere=(2, 3, 4, 5),
    )[0]


def swap(block, axis):
    return lax.all_to_all(block, axis, split_axis=0, concat_axis=0, tiled=True)


def together(*values):
    return lax.optimization_barrier(values)


def body(state, cotangent, spectral_weight, stencil_weight, pointwise_weight):
    nx, ny = lax.axis_size("gx"), lax.axis_size("gy")
    c, cx, cy, z = state.shape
    _, mz, mx, _, _ = spectral_weight.shape
    wide_x, wide_y = cx * nx, cy * ny
    alpha = 1.0 / math.sqrt(wide_x * wide_y * z)
    beta = 1.0 / math.sqrt(2 * MX * MY * MZ)
    double = np.where(np.arange(MZ) == 0, 1.0, 2.0)
    ones = np.ones(MZ)
    z_state = jnp.asarray(z_forward_table(alpha * ones)(nx, mz))
    z_grad = jnp.asarray(z_forward_table(double)(nx, mz))
    z_spectral = jnp.asarray(z_inverse_table(nx, mz, beta * double))
    z_back = jnp.asarray(z_inverse_table(nx, mz, alpha * beta * ones))
    x_fwd, x_inv = (jnp.asarray(t) for t in x_tables(wide_x, mz, mx))
    y_turn = jnp.asarray(y_table(wide_y))
    spread, gather = jnp.asarray(spread_table()), jnp.asarray(gather_table())
    lanes = cy * c
    x_rows = cx * 2 * mz

    def x_stage(table, block, lead, kind=F32, extra=0):
        rows = table.shape[0] // lead + extra
        return call(
            x_kernel,
            [((lead, rows, lanes), kind)],
            (table, block),
            mib=16,
            flops=2 * table.size * lanes,
            moved=8 * block.size,
        )[0]

    slab_shape = ((nx, x_rows, lanes), F32)
    turned_shape = ((cx, cy, c, z), BF16)

    conv_table, back_table = call(
        taps_kernel,
        [((9 * c, 4 * c), BF16)] * 2,
        (in_hbm(stencil_weight), in_hbm(pointwise_weight)),
        [pltpu.VMEM((27 * c, c), F32)],
        moved=stencil_weight.size * 6,
    )
    tables = (x_fwd, x_inv, y_turn)
    turned, slab, *held = call(
        functools.partial(prep_kernel, nx),
        [turned_shape, slab_shape] + [(t.shape, BF16) for t in tables],
        (in_hbm(state), in_hbm(z_state), *map(in_hbm, tables)),
        flops=2 * 96 * state.size,
        moved=state.size * 5,
    )
    x_mine = x_fwd.reshape(ny, -1, x_fwd.shape[1])
    x_mine = lax.dynamic_index_in_dim(x_mine, lax.axis_index("gy"), 0, keepdims=False)
    x_fwd, x_inv, y_turn = held

    block = x_stage(x_fwd, swap(slab, "gx"), ny)
    block, conv_table, back_table, x_mine, *faces = together(
        block, conv_table, back_table, x_mine, *x_halos(turned)
    )
    modes_in, block = per_mode(
        mix_kernel,
        swap(block, "gy"),
        spectral_weight,
        spread,
        (y_turn,),
        (2 * c, BF16),
        F32,
        [pltpu.VMEM(spread.shape, BF16), pltpu.SemaphoreType.DMA]
        + [pltpu.VMEM((2 * QUAD * MY, SPAN), F32)] * 2
        + [pltpu.VMEM((2 * QUAD * MY, 2 * c), F32)],
    )
    block, *edges = together(block, *y_halos(turned, *faces))
    rim = (*faces, *edges)
    block = x_stage(x_inv, swap(block, "gy"), nx)
    stencil = conv(turned, rim, conv_table, False)
    output, grad, slab = call(
        functools.partial(gelu_kernel, nx),
        [((c, cx, cy, z), BF16), turned_shape, ((nx * ny, x_rows, lanes), BF16)],
        (stencil, swap(block, "gx"), cotangent, z_spectral, z_grad),
        [pltpu.VMEM(slab_shape[0], F32)],
        flops=2 * 192 * state.size,
        moved=state.size * 12,
    )

    message = weight_grad(grad, turned, rim, slab)
    extra = message.shape[1] - x_rows
    faces = x_halos(grad)
    edges = y_halos(grad, *faces)
    message, ylo, yhi = together(swap(message, ("gx", "gy")), *edges)
    back_modes, block = per_mode(
        mix_back_kernel,
        message,
        spectral_weight,
        gather,
        (y_turn, x_mine),
        (2 * c, F32),
        BF16,
        [pltpu.VMEM((2 * QUAD * MY, c * c), BF16)],
        extra,
    )
    block = x_stage(x_inv, swap(block, "gy"), nx, BF16, ny * extra)
    shape = spectral_weight.shape
    groups = modes_in.shape[0]
    early = groups * 3 // 4
    grad_modes = None
    if early:
        grad_modes = outer(modes_in, back_modes, spread, shape, alpha, 0, early)
        block, grad_modes = together(block, grad_modes)
    message = swap(block, "gx")
    stencil_back = conv(grad, (*faces, ylo, yhi), back_table, True)
    grad_modes = outer(
        modes_in, back_modes, spread, shape, alpha, early, groups - early, grad_modes
    )
    grad_state, grad_stencil, grad_point = call(
        functools.partial(finish_kernel, nx, ny, alpha),
        [((c, cx, cy, z), F32), ((c, 27 * c), F32), ((c, c), F32)],
        (stencil_back, message, z_back),
        [pltpu.VMEM((16 * c, 2 * c), F32), pltpu.VMEM((27 * c, c), F32)],
        flops=2 * 96 * state.size,
        moved=state.size * 10,
    )
    return (output, grad_state, grad_modes, grad_stencil, grad_point)


def solution(mesh):
    in_specs = (
        P(None, "gx", "gy", None),
        P(None, "gx", "gy", None),
        P(None, "gx", "gy", None, None),
        P(),
        P(),
    )
    out_specs = (
        P(None, "gx", "gy", None),
        P(None, "gx", "gy", None),
        P(None, "gx", "gy", None, None),
        P(),
        P(),
    )
    return jax.shard_map(body, mesh=mesh, in_specs=in_specs, out_specs=out_specs, check_vma=False)
```

```python
import functools
import math

import jax
import jax.numpy as jnp
import numpy as np
from jax import lax
from jax.experimental import pallas as pl
from jax.experimental.pallas import tpu as pltpu
from jax.sharding import PartitionSpec as P

C = 64
MX = 32
MY = 32
MZ = 16
Z = 128
MIB = 1 << 20

F32 = jnp.float32
BF16 = jnp.bfloat16


def angles(places, freqs, length):
    turns = np.outer(np.asarray(places), np.asarray(freqs)) % length
    return turns * (2.0 * np.pi / length)


def centred(count):
    steps = np.arange(count)
    return np.where(steps < count // 2, steps, steps - count)


def split(table, parts):
    rest = np.asarray(table, np.float64)
    out = []
    for _ in range(parts):
        piece = rest.astype(jnp.bfloat16)
        out.append(piece)
        rest = rest - piece.astype(np.float64)
    return out


def z_forward_table(scale):
    def build(nx, mz):
        theta = angles(np.arange(MZ), np.arange(Z), Z)
        pair = np.stack([np.cos(theta), -np.sin(theta)]) * scale[None, :, None]
        rows = pair.reshape(2, nx, mz, Z).transpose(1, 0, 2, 3).reshape(2 * MZ, Z)
        return np.concatenate(split(rows, 3), axis=0)

    return build


def z_inverse_table(nx, mz, scale):
    theta = angles(np.arange(MZ), np.arange(Z), Z)
    pair = np.stack([np.cos(theta), -np.sin(theta)]) * scale[None, :, None]
    rows = pair.reshape(2, nx, mz, Z).transpose(1, 0, 2, 3).reshape(2 * MZ, Z)
    high, low = split(rows, 2)
    return np.concatenate([high, high, low], axis=0)


def rotation(theta, sign):
    cosine, sine = np.cos(theta), sign * np.sin(theta)
    return np.stack([np.stack([cosine, -sine], 1), np.stack([sine, cosine], 1)])


def against_pieces(*tables):
    out = []
    for table in tables:
        high, low = split(table, 2)
        out.append(np.concatenate([high, high, low], axis=1))
    return out


def x_tables(wide, mz, mx):
    theta = angles(centred(MX), np.arange(wide), wide)
    eye = np.eye(mz)
    forward = np.einsum("rkRx,zZ->krzxRZ", rotation(theta, -1.0), eye)
    inverse = np.einsum("rxRk,zZ->xrzkRZ", rotation(theta.T, 1.0), eye)
    size_k, size_x = MX * 2 * mz, wide * 2 * mz
    forward = forward.reshape(MX // mx, mx, 2, mz, size_x).transpose(0, 2, 3, 1, 4)
    inverse = inverse.reshape(size_x, MX // mx, mx, 2, mz).transpose(0, 1, 3, 4, 2)
    return against_pieces(forward.reshape(size_k, size_x), inverse.reshape(size_x, size_k))


def y_table(wide):
    theta = angles(centred(MY), np.arange(wide), wide)
    forward = rotation(theta, -1.0).reshape(2 * MY, 2 * wide)
    inverse = rotation(theta.T, 1.0).reshape(2 * wide, 2 * MY)
    forward, inverse = against_pieces(forward, inverse)
    inverse = np.pad(inverse, ((0, 0), (0, forward.shape[1] - inverse.shape[1])))
    return np.concatenate([forward, inverse], axis=0)


def pieces(values):
    high = values.astype(BF16)
    low = (values - high.astype(F32)).astype(BF16)
    return jnp.concatenate([high, low, high], axis=0)


def z_forward(rows, table, out_ref, x, nx):
    got = lax.dot_general(table, rows, (((1,), (1,)), ((), ())), preferred_element_type=F32)
    size = 2 * MZ
    total = got[:size] + (got[size : 2 * size] + got[2 * size :])
    per = size // nx
    for owner in range(nx):
        out_ref[owner, x * per : (x + 1) * per, :] = total[owner * per : (owner + 1) * per]


def z_inverse(in_ref, table, x, nx):
    per = 2 * MZ // nx
    rows = jnp.concatenate(
        [in_ref[owner].astype(F32)[x * per : (x + 1) * per] for owner in range(nx)], axis=0
    )
    return lax.dot_general(
        pieces(rows), table, (((0,), (0,)), ((), ())), preferred_element_type=F32
    )


def prep_kernel(
    nx,
    field_ref,
    table_ref,
    forward_ref,
    inverse_ref,
    turn_ref,
    turned_ref,
    slab_ref,
    forward_out_ref,
    inverse_out_ref,
    turn_out_ref,
):
    forward_out_ref[...] = forward_ref[...]
    inverse_out_ref[...] = inverse_ref[...]
    turn_out_ref[...] = turn_ref[...]
    c, cx, cy, z = field_ref.shape
    for x in range(cx):
        block = jnp.swapaxes(field_ref[:, x].astype(F32), 0, 1)
        turned = block.astype(BF16)
        turned_ref[x] = turned
        z_forward(turned.reshape(cy * c, z), table_ref[...], slab_ref, x, nx)


def plane_rows(p, cx, body_ref, xlo_ref, xhi_ref, ylo_ref, yhi_ref):
    cy = body_ref.shape[1]
    if p == 0:
        middle = [xlo_ref[y] for y in range(cy)]
    elif p == cx + 1:
        middle = [xhi_ref[y] for y in range(cy)]
    else:
        middle = [body_ref[p - 1, y] for y in range(cy)]
    return [ylo_ref[p]] + middle + [yhi_ref[p]]


def fill_shifts(blocks, rim_ref, flip=False):
    c, z = blocks[0].shape
    lane = lax.broadcasted_iota(jnp.int32, (c, z), 1)
    for y, block in enumerate(blocks):
        wide = block.astype(F32)
        before = jnp.where(lane == 0, 0.0, pltpu.roll(wide, 1, 1))
        after = jnp.where(lane == z - 1, 0.0, pltpu.roll(wide, z - 1, 1))
        if flip:
            before, after = after, before
        columns = slice(y * z, (y + 1) * z)
        rim_ref[0:c, columns] = before.astype(BF16)
        rim_ref[c : 2 * c, columns] = block
        rim_ref[2 * c : 3 * c, columns] = after.astype(BF16)
        rim_ref[3 * c : 4 * c, columns] = block


def conv_kernel(
    flip, body_ref, xlo_ref, xhi_ref, ylo_ref, yhi_ref, weight_ref, out_ref, rim_ref
):
    cx, cy, c, z = body_ref.shape
    for p in range(cx + 2):
        blocks = plane_rows(p, cx, body_ref, xlo_ref, xhi_ref, ylo_ref, yhi_ref)
        fill_shifts(blocks, rim_ref, flip)
        places = [a for a in range(3) if 0 <= p - (2 - a if flip else a) < cx]
        first = places[0]
        got = jnp.dot(
            weight_ref[first * 3 * c : (places[-1] + 1) * 3 * c, :],
            rim_ref[...],
            preferred_element_type=F32,
        )
        for a in places:
            x = p - (2 - a if flip else a)
            total = None
            for b in range(3):
                row = ((a - first) * 3 + b) * c
                skip = 2 - b if flip else b
                term = got[row : row + c, skip * z : (skip + cy) * z]
                total = term if total is None else total + term
            if p == x:
                out_ref[x] = total
            else:
                out_ref[x] += total


def weight_grad_kernel(
    grad_ref,
    body_ref,
    xlo_any,
    xhi_any,
    ylo_any,
    yhi_any,
    slab_ref,
    message_ref,
    out_ref,
    rim_ref,
    wide_ref,
    sum_ref,
    xlo_ref,
    xhi_ref,
    ylo_ref,
    yhi_ref,
    sem_ref,
):
    cx, cy, c, z = body_ref.shape
    group = 3 * c
    held = (xlo_ref, xhi_ref, ylo_ref, yhi_ref)
    copies = [
        pltpu.make_async_copy(given, ref, sem_ref.at[i])
        for i, (given, ref) in enumerate(zip((xlo_any, xhi_any, ylo_any, yhi_any), held))
    ]
    for copy in copies:
        copy.start()
    wide_ref[...] = jnp.zeros_like(wide_ref)
    for x in range(cx):
        for b in range(3):
            for y in range(cy):
                row = x * group + b * c
                wide_ref[row : row + c, (y + b) * z : (y + b + 1) * z] = grad_ref[x, y]
    sum_ref[...] = jnp.zeros_like(sum_ref)
    for copy in copies:
        copy.wait()
    for p in range(cx + 2):
        fill_shifts(plane_rows(p, cx, body_ref, xlo_ref, xhi_ref, ylo_ref, yhi_ref), rim_ref)
        first, last = max(0, p - 2), min(cx - 1, p)
        got = lax.dot_general(
            wide_ref[first * group : (last + 1) * group, :],
            rim_ref[...],
            (((1,), (1,)), ((), ())),
            preferred_element_type=F32,
        )
        for x in range(first, last + 1):
            a = p - x
            sum_ref[a * group : (a + 1) * group, :] += got[
                (x - first) * group : (x - first + 1) * group, :
            ]
    out_ref[: 9 * c] = sum_ref[:, : 2 * c]
    last = [sum_ref[k * c : (k + 1) * c, 2 * c : 3 * c] for k in range(9)]
    last.append(jnp.zeros((c, c), F32))
    for k in range(5):
        row = (9 + k) * c
        out_ref[row : row + c] = jnp.concatenate(last[2 * k : 2 * k + 2], axis=1)
    out_ref[14 * c :] = jnp.zeros((2 * c, 2 * c), F32)
    devices, rows, lanes = message_ref.shape
    skip = slab_ref.shape[1]
    per, tiles_in = rows - skip, lanes // (2 * c)
    for device in range(devices):
        start = device * per * tiles_in
        share = [out_ref[start + t * per : start + (t + 1) * per] for t in range(tiles_in)]
        message_ref[device] = jnp.concatenate(
            [slab_ref[device].astype(F32), jnp.concatenate(share, axis=1)], axis=0
        ).astype(BF16)


def gelu_kernel(
    nx,
    stencil_ref,
    slab_ref,
    cot_ref,
    inverse_ref,
    forward_ref,
    out_ref,
    turned_ref,
    message_ref,
    back_ref,
):
    c, cx, cy, z = cot_ref.shape
    root = math.sqrt(2.0 / math.pi)
    for x in range(cx):
        spectral = z_inverse(slab_ref, inverse_ref[...], x, nx).reshape(cy, c, z)
        stencil = jnp.stack([stencil_ref[x, :, y * z : (y + 1) * z] for y in range(cy)])
        pre = spectral + stencil
        cot = jnp.swapaxes(cot_ref[:, x].astype(F32), 0, 1)
        square = pre * pre
        bent = jnp.tanh(root * (pre * (1.0 + 0.044715 * square)))
        half = 0.5 + 0.5 * bent
        slope = half + (0.5 * pre) * (1.0 - bent * bent) * (root * (1.0 + 0.134145 * square))
        out_ref[:, x] = jnp.swapaxes(pre * half, 0, 1).astype(BF16)
        grad = (cot * slope).astype(BF16)
        turned_ref[x] = grad
        z_forward(grad.reshape(cy * c, z), forward_ref[...], back_ref, x, nx)
    ny = message_ref.shape[0] // nx
    for owner in range(nx):
        block = back_ref[owner].astype(BF16)
        for copy in range(ny):
            message_ref[owner * ny + copy] = block


def finish_kernel(
    nx,
    shares,
    scale,
    stencil_ref,
    message_ref,
    inverse_ref,
    out_ref,
    taps_ref,
    point_ref,
    packed_ref,
    turned_ref,
):
    c, cx, cy, z = out_ref.shape
    for x in range(cx):
        spectral = z_inverse(message_ref, inverse_ref[...], x, nx).reshape(cy, c, z)
        stencil = jnp.stack([stencil_ref[x, :, y * z : (y + 1) * z] for y in range(cy)])
        out_ref[:, x] = jnp.swapaxes(spectral + stencil, 0, 1)
    skip = 2 * MZ * cx // nx
    unpack(scale, skip, shares, message_ref, taps_ref, point_ref, packed_ref, turned_ref)


def x_kernel(table_ref, data_ref, out_ref):
    data = data_ref[...].astype(F32)
    lanes = data.shape[2]
    rows = table_ref.shape[1] // (3 * data.shape[0])
    flat = pieces(data[:, :rows].reshape(-1, lanes))
    got = jnp.dot(table_ref[...], flat, preferred_element_type=F32).astype(out_ref.dtype)
    count = got.shape[0] // out_ref.shape[0]
    for owner in range(out_ref.shape[0]):
        out_ref[owner, :count] = got[owner * count : (owner + 1) * count]
    if data.shape[1] > rows:
        extra = jnp.concatenate([data[i, rows:] for i in range(data.shape[0])], axis=0)
        extra = extra.astype(out_ref.dtype)
        for owner in range(out_ref.shape[0]):
            out_ref[owner, count:] = extra


def taps_kernel(taps_ref, point_ref, forward_ref, back_ref, turned_ref):
    turned_ref[...] = taps_ref[...].astype(F32).T
    forward_ref[...] = jnp.zeros_like(forward_ref)
    back_ref[...] = jnp.zeros_like(back_ref)
    for tap in range(27):
        rows = slice(tap // 3 * C, (tap // 3 + 1) * C)
        columns = slice(tap % 3 * C, (tap % 3 + 1) * C)
        block = turned_ref[pl.ds(tap, C, stride=27), :]
        back_ref[rows, columns] = block.astype(BF16)
        forward_ref[rows, columns] = block.T.astype(BF16)
    point = point_ref[...].astype(F32)
    forward_ref[4 * C : 5 * C, 3 * C :] = point.astype(BF16)
    back_ref[4 * C : 5 * C, 3 * C :] = point.T.astype(BF16)


def unpack(scale, skip, shares, message_ref, taps_ref, point_ref, packed_ref, turned_ref):
    devices, rows, lanes = message_ref.shape
    per, tiles_in = (rows - skip) // shares, lanes // 128
    for owner in range(devices):
        message = message_ref[owner].astype(F32)[skip:]
        for share in range(shares):
            for tile in range(tiles_in):
                row = ((owner * shares + share) * tiles_in + tile) * per
                packed_ref[row : row + per] = message[
                    share * per : (share + 1) * per, tile * 128 : (tile + 1) * 128
                ]
    for tap in range(27):
        group, e = tap // 3, tap % 3
        if e < 2:
            block = packed_ref[group * C : (group + 1) * C, e * C : (e + 1) * C]
        else:
            row = (9 + group // 2) * C
            block = packed_ref[row : row + C, group % 2 * C : (group % 2 + 1) * C]
        block = block * scale
        if tap == 13:
            point_ref[...] = block
        turned_ref[pl.ds(tap, C, stride=27), :] = block.T
    taps_ref[...] = turned_ref[...].T


QUAD = 4
SPAN = 8 * C


def y_forward(mz, blocks, table_ref, rows_ref, store):
    ny, cy = len(blocks), blocks[0].shape[1] // C
    count = rows_ref.shape[1] // C
    for owner in range(ny):
        data = blocks[owner]
        for part in range(2):
            for kz in range(mz):
                mx = count // mz
                start = (part * mz + kz) * mx
                block = data[start : start + mx]
                block = jnp.stack([block[:, y * C : (y + 1) * C] for y in range(cy)])
                block = jnp.swapaxes(block, 0, 1)
                row = (part * ny + owner) * cy
                for kx in range(mx):
                    column = (kz * mx + kx) * C
                    rows_ref[row : row + cy, column : column + C] = block[kx]
    got = jnp.dot(table_ref[: 2 * MY], pieces(rows_ref[...]), preferred_element_type=F32)
    for q in range(count):
        block = got[:, q * C : (q + 1) * C]
        for part in range(2):
            store(q // QUAD, part, q % QUAD, block[part * MY : (part + 1) * MY])


def y_inverse(mz, sum_ref, table_ref, out_ref, block_ref):
    rows = [
        jnp.concatenate(
            [
                sum_ref[group, place(part, pair), :]
                for group in range(sum_ref.shape[0])
                for pair in range(QUAD)
            ],
            axis=1,
        )
        for part in range(2)
    ]
    got = jnp.dot(
        table_ref[2 * MY :, : 6 * MY],
        pieces(jnp.concatenate(rows, axis=0)),
        preferred_element_type=F32,
    )
    ny, _, lanes = out_ref.shape
    cy = lanes // C
    count = got.shape[1] // C
    mx = count // mz
    for owner in range(ny):
        for part in range(2):
            for kz in range(mz):
                row = (part * ny + owner) * cy
                block = got[row : row + cy, kz * mx * C : (kz + 1) * mx * C]
                block = jnp.stack([block[:, kx * C : (kx + 1) * C] for kx in range(mx)])
                block = jnp.swapaxes(block, 0, 1)
                start = (part * mz + kz) * mx
                for y in range(cy):
                    block_ref[owner, start : start + mx, y * C : (y + 1) * C] = block[y]
    out_ref[...] = block_ref[...].astype(out_ref.dtype)


def place(part, pair):
    start = (part * QUAD + pair) * MY
    return slice(start, start + MY)


def spread_table():
    return np.tile(np.kron(np.eye(C), np.ones((1, C))), (2, 1)).astype(jnp.bfloat16)


def gather_table():
    return np.kron(np.eye(SPAN // C), np.ones((1, C))).astype(jnp.bfloat16)


def spread_modes(modes, table_ref, spread_refs):
    count = C * C // SPAN
    made = set()

    def get(piece):
        for p in range(piece, min(piece + 2, count)):
            if p not in made:
                made.add(p)
                spread_refs[p % 2][...] = jnp.dot(
                    modes, table_ref[:, p * SPAN : (p + 1) * SPAN], preferred_element_type=F32
                )
        return spread_refs[piece % 2]

    return get


def weight_copies(weight_ref, held_ref, sem_ref):
    per = weight_ref.shape[2] // QUAD
    return [
        pltpu.make_async_copy(
            weight_ref.at[:, g // per, g % per * QUAD : (g % per + 1) * QUAD],
            held_ref.at[g],
            sem_ref.at[g],
        )
        for g in range(held_ref.shape[0])
    ]


def mix_kernel(
    mz,
    data_ref,
    weight_ref,
    table_ref,
    turn_ref,
    modes_ref,
    out_ref,
    sum_ref,
    rows_ref,
    block_ref,
    held_ref,
    sem_ref,
    spread_ref,
    spread_sem_ref,
    even_ref,
    odd_ref,
    total_ref,
):
    copies = weight_copies(weight_ref, held_ref, sem_ref)
    table_copy = pltpu.make_async_copy(table_ref, spread_ref, spread_sem_ref)
    table_copy.start()
    for copy in copies:
        copy.start()

    def store(group, part, pair, values):
        high = values.astype(BF16)
        low = (values - high.astype(F32)).astype(BF16)
        modes_ref[group, place(part, pair), :] = jnp.concatenate([high, low], axis=1)

    blocks = [data_ref[owner] for owner in range(data_ref.shape[0])]
    y_forward(mz, blocks, turn_ref, rows_ref, store)
    table_copy.wait()
    for group, copy in enumerate(copies):
        copy.wait()
        spread = spread_modes(modes_ref[group], spread_ref, (even_ref, odd_ref))
        for piece in range(C * C // SPAN):
            modes = spread(piece)
            for pair in range(QUAD):
                real = imag = None
                for tile in range(SPAN // (2 * C)):
                    inside = slice(tile * 2 * C, (tile + 1) * 2 * C)
                    columns = slice(piece * SPAN + inside.start, piece * SPAN + inside.stop)
                    mode_re = modes[place(0, pair), inside]
                    mode_im = modes[place(1, pair), inside]
                    weight_re = held_ref[group, 0, pair, :, columns].astype(F32)
                    weight_im = held_ref[group, 1, pair, :, columns].astype(F32)
                    term_re = mode_re * weight_re - mode_im * weight_im
                    term_im = mode_re * weight_im + mode_im * weight_re
                    real = term_re if real is None else real + term_re
                    imag = term_im if imag is None else imag + term_im
                if piece:
                    real += total_ref[place(0, pair), :]
                    imag += total_ref[place(1, pair), :]
                total_ref[place(0, pair), :] = real
                total_ref[place(1, pair), :] = imag
        total = total_ref[...]
        sum_ref[group] = total[:, :C] + total[:, C:]
    y_inverse(mz, sum_ref, turn_ref, out_ref, block_ref)


def mix_back_kernel(
    mz,
    data_ref,
    weight_ref,
    table_ref,
    turn_ref,
    x_ref,
    modes_ref,
    out_ref,
    sum_ref,
    rows_ref,
    block_ref,
    held_ref,
    sem_ref,
    term_ref,
):
    copies = weight_copies(weight_ref, held_ref, sem_ref)
    for copy in copies:
        copy.start()

    def store(group, part, pair, values):
        modes_ref[group, place(part, pair), :] = jnp.concatenate([values, values], axis=1)

    devices, ny = data_ref.shape[0], block_ref.shape[0]
    size = x_ref.shape[1] // 3
    skip = size * ny // devices
    share = data_ref[0].astype(F32)[skip:]
    for device in range(1, devices):
        share += data_ref[device].astype(F32)[skip:]
    blocks = []
    for owner in range(ny):
        rows = jnp.concatenate(
            [data_ref[i].astype(F32)[:skip] for i in range(owner, devices, ny)], axis=0
        ).astype(BF16)
        blocks.append(
            jnp.dot(x_ref[:, :size], rows, preferred_element_type=F32)
            + jnp.dot(x_ref[:, 2 * size :], rows, preferred_element_type=F32)
        )
    y_forward(mz, blocks, turn_ref, rows_ref, store)
    for group, copy in enumerate(copies):
        copy.wait()
        total = []
        for piece in range(C * C // SPAN):
            for pair in range(QUAD):
                mode_re = modes_ref[group, place(0, pair), :]
                mode_im = modes_ref[group, place(1, pair), :]
                for tile in range(SPAN // (2 * C)):
                    start = piece * SPAN + tile * 2 * C
                    columns = slice(start, start + 2 * C)
                    weight_re = held_ref[group, 0, pair, :, columns].astype(F32)
                    weight_im = held_ref[group, 1, pair, :, columns].astype(F32)
                    term_ref[place(0, pair), columns] = (
                        weight_re * mode_re + weight_im * mode_im
                    ).astype(BF16)
                    term_ref[place(1, pair), columns] = (
                        weight_re * mode_im - weight_im * mode_re
                    ).astype(BF16)
            total.append(
                lax.dot_general(
                    table_ref[...],
                    term_ref[:, piece * SPAN : (piece + 1) * SPAN],
                    (((1,), (1,)), ((), ())),
                    preferred_element_type=F32,
                )
            )
        sum_ref[group] = jnp.concatenate(total, axis=0).T
    y_inverse(mz, sum_ref, turn_ref, block_ref, block_ref)
    for owner in range(ny):
        out_ref[owner] = jnp.concatenate([block_ref[owner], share], axis=0).astype(BF16)


def outer_kernel(alpha, modes_ref, back_ref, table_ref, out_ref):
    count = C * C // SPAN
    made = lambda piece: jnp.dot(
        modes_ref[0],
        table_ref[:, piece * SPAN : (piece + 1) * SPAN],
        preferred_element_type=F32,
    )
    ahead = made(0)
    for piece in range(count):
        modes = ahead
        if piece + 1 < count:
            ahead = made(piece + 1)
        for pair in range(QUAD):
            back_re = back_ref[0, place(0, pair), :] * alpha
            back_im = back_ref[0, place(1, pair), :] * alpha
            for tile in range(SPAN // (2 * C)):
                inside = slice(tile * 2 * C, (tile + 1) * 2 * C)
                columns = slice(piece * SPAN + inside.start, piece * SPAN + inside.stop)
                mode_re = modes[place(0, pair), inside]
                mode_im = modes[place(1, pair), inside]
                out_ref[0, 0, pair, :, columns] = mode_re * back_re + mode_im * back_im
                out_ref[1, 0, pair, :, columns] = mode_re * back_im - mode_im * back_re


def in_hbm(value):
    return pltpu.with_memory_space_constraint(value, pltpu.HBM)


def whole():
    return pl.BlockSpec(memory_space=pltpu.VMEM)


def params(mib):
    return pltpu.CompilerParams(vmem_limit_bytes=mib * MIB)


def cost(flops, moved):
    return pl.CostEstimate(flops=int(flops), bytes_accessed=int(moved), transcendentals=0)


def call(kernel, outs, args, scratch=(), mib=24, flops=0, moved=0, anywhere=()):
    return pl.pallas_call(
        kernel,
        out_shape=[jax.ShapeDtypeStruct(*out) for out in outs],
        in_specs=[
            pl.BlockSpec(memory_space=pl.ANY) if i in anywhere else whole()
            for i in range(len(args))
        ],
        out_specs=[whole() for _ in outs],
        scratch_shapes=list(scratch),
        compiler_params=params(mib),
        cost_estimate=cost(flops, moved),
    )(*args)


def per_mode(kernel, data, weight, table, tables, modes, kind, scratch=(), extra=0):
    _, mz, mx, my, wide = weight.shape
    groups = mz * mx // QUAD
    rows = 2 * QUAD * MY
    modes_shape = (groups, rows, modes[0])
    block = (MX // mx, 2 * mz * mx, data.shape[2])
    return pl.pallas_call(
        functools.partial(kernel, mz),
        in_specs=[
            whole(),
            pl.BlockSpec(memory_space=pl.ANY),
            pl.BlockSpec(memory_space=pl.ANY) if kernel is mix_kernel else whole(),
        ]
        + [whole() for _ in tables],
        out_specs=[whole(), whole()],
        out_shape=[
            jax.ShapeDtypeStruct(modes_shape, modes[1]),
            jax.ShapeDtypeStruct((block[0], block[1] + extra, block[2]), kind),
        ],
        scratch_shapes=[
            pltpu.VMEM((groups, rows, C), F32),
            pltpu.VMEM((tables[0].shape[0] - 2 * MY, mz * mx * C), F32),
            pltpu.VMEM(block, F32),
            pltpu.VMEM((groups, 2, QUAD, my, wide), BF16),
            pltpu.SemaphoreType.DMA((groups,)),
            *scratch,
        ],
        compiler_params=params(24),
        cost_estimate=cost(weight.size * 8, weight.size * 2),
    )(data, in_hbm(weight), in_hbm(table), *tables)


def outer(modes, back, table, shape, alpha, start, count, prior=None):
    def kernel(*refs):
        outer_kernel(alpha, *refs[:3], refs[-1])

    per = shape[2] // QUAD
    group = lambda ref: pl.BlockSpec((1,) + ref.shape[1:], lambda step: (step + start, 0, 0))
    given = () if prior is None else (prior,)
    return pl.pallas_call(
        kernel,
        grid=(count,),
        in_specs=[group(modes), group(back), pl.BlockSpec(table.shape, lambda step: (0, 0))]
        + [pl.BlockSpec(memory_space=pl.ANY)] * len(given),
        out_specs=pl.BlockSpec(
            (2, 1, QUAD) + shape[3:],
            lambda step: (0, (step + start) // per, (step + start) % per, 0, 0),
        ),
        out_shape=jax.ShapeDtypeStruct(shape, F32),
        input_output_aliases={3: 0} if given else {},
        compiler_params=params(20),
        cost_estimate=cost(
            math.prod(shape) * 4 * count / modes.shape[0],
            math.prod(shape) * 4 * count / modes.shape[0],
        ),
    )(modes, back, in_hbm(table), *given)


def shift(block, axis, step):
    count = lax.axis_size(axis)
    pairs = [(i, i + step) for i in range(count) if 0 <= i + step < count]
    return lax.ppermute(block, axis, pairs)


def x_halos(turned):
    return shift(turned[-1], "gx", 1), shift(turned[0], "gx", -1)


def y_halos(turned, xlo, xhi):
    edge = lambda y: jnp.concatenate([xlo[None, y], turned[:, y], xhi[None, y]], axis=0)
    return shift(edge(-1), "gy", 1), shift(edge(0), "gy", -1)


def conv(turned, rim, weight, flip):
    cx, cy, c, z = turned.shape
    return call(
        functools.partial(conv_kernel, flip),
        [((cx, c, cy * z), F32)],
        (turned, *map(in_hbm, rim), in_hbm(weight)),
        [pltpu.VMEM((4 * c, (cy + 2) * z), BF16)],
        mib=32,
        flops=2 * 27 * c * c * cx * cy * z,
        moved=turned.size * 8,
    )[0]


def weight_grad(grad, turned, rim, slab):
    cx, cy, c, z = turned.shape
    devices, skip, lanes = slab.shape
    extra = 16 * c * 2 * c // (devices * lanes)
    return call(
        weight_grad_kernel,
        [((devices, skip + extra, lanes), BF16)],
        (grad, turned, *map(in_hbm, rim), slab),
        [
            pltpu.VMEM((16 * c, 2 * c), F32),
            pltpu.VMEM((4 * c, (cy + 2) * z), BF16),
            pltpu.VMEM((cx * 3 * c, (cy + 2) * z), BF16),
            pltpu.VMEM((9 * c, 4 * c), F32),
            *(pltpu.VMEM(halo.shape, BF16) for halo in rim),
            pltpu.SemaphoreType.DMA((len(rim),)),
        ],
        mib=32,
        flops=2 * 27 * c * c * cx * cy * z,
        moved=turned.size * 8,
        anywhere=(2, 3, 4, 5),
    )[0]


def swap(block, axis):
    return lax.all_to_all(block, axis, split_axis=0, concat_axis=0, tiled=True)


def together(*values):
    return lax.optimization_barrier(values)


def body(state, cotangent, spectral_weight, stencil_weight, pointwise_weight):
    nx, ny = lax.axis_size("gx"), lax.axis_size("gy")
    c, cx, cy, z = state.shape
    _, mz, mx, _, _ = spectral_weight.shape
    wide_x, wide_y = cx * nx, cy * ny
    alpha = 1.0 / math.sqrt(wide_x * wide_y * z)
    beta = 1.0 / math.sqrt(2 * MX * MY * MZ)
    double = np.where(np.arange(MZ) == 0, 1.0, 2.0)
    ones = np.ones(MZ)
    z_state = jnp.asarray(z_forward_table(alpha * ones)(nx, mz))
    z_grad = jnp.asarray(z_forward_table(double)(nx, mz))
    z_spectral = jnp.asarray(z_inverse_table(nx, mz, beta * double))
    z_back = jnp.asarray(z_inverse_table(nx, mz, alpha * beta * ones))
    x_fwd, x_inv = (jnp.asarray(t) for t in x_tables(wide_x, mz, mx))
    y_turn = jnp.asarray(y_table(wide_y))
    spread, gather = jnp.asarray(spread_table()), jnp.asarray(gather_table())
    lanes = cy * c
    x_rows = cx * 2 * mz

    def x_stage(table, block, lead, kind=F32, extra=0):
        rows = table.shape[0] // lead + extra
        return call(
            x_kernel,
            [((lead, rows, lanes), kind)],
            (table, block),
            mib=16,
            flops=2 * table.size * lanes,
            moved=8 * block.size,
        )[0]

    slab_shape = ((nx, x_rows, lanes), F32)
    turned_shape = ((cx, cy, c, z), BF16)

    conv_table, back_table = call(
        taps_kernel,
        [((9 * c, 4 * c), BF16)] * 2,
        (in_hbm(stencil_weight), in_hbm(pointwise_weight)),
        [pltpu.VMEM((27 * c, c), F32)],
        moved=stencil_weight.size * 6,
    )
    tables = (x_fwd, x_inv, y_turn)
    turned, slab, *held = call(
        functools.partial(prep_kernel, nx),
        [turned_shape, slab_shape] + [(t.shape, BF16) for t in tables],
        (in_hbm(state), in_hbm(z_state), *map(in_hbm, tables)),
        flops=2 * 96 * state.size,
        moved=state.size * 5,
    )
    x_mine = x_fwd.reshape(ny, -1, x_fwd.shape[1])
    x_mine = lax.dynamic_index_in_dim(x_mine, lax.axis_index("gy"), 0, keepdims=False)
    x_fwd, x_inv, y_turn = held

    block = x_stage(x_fwd, swap(slab, "gx"), ny)
    block, conv_table, back_table, x_mine, *faces = together(
        block, conv_table, back_table, x_mine, *x_halos(turned)
    )
    modes_in, block = per_mode(
        mix_kernel,
        swap(block, "gy"),
        spectral_weight,
        spread,
        (y_turn,),
        (2 * c, BF16),
        F32,
        [pltpu.VMEM(spread.shape, BF16), pltpu.SemaphoreType.DMA]
        + [pltpu.VMEM((2 * QUAD * MY, SPAN), F32)] * 2
        + [pltpu.VMEM((2 * QUAD * MY, 2 * c), F32)],
    )
    block, *edges = together(block, *y_halos(turned, *faces))
    rim = (*faces, *edges)
    block = x_stage(x_inv, swap(block, "gy"), nx)
    stencil = conv(turned, rim, conv_table, False)
    output, grad, slab = call(
        functools.partial(gelu_kernel, nx),
        [((c, cx, cy, z), BF16), turned_shape, ((nx * ny, x_rows, lanes), BF16)],
        (stencil, swap(block, "gx"), cotangent, z_spectral, z_grad),
        [pltpu.VMEM(slab_shape[0], F32)],
        flops=2 * 192 * state.size,
        moved=state.size * 12,
    )

    message = weight_grad(grad, turned, rim, slab)
    extra = message.shape[1] - x_rows
    faces = x_halos(grad)
    edges = y_halos(grad, *faces)
    message, ylo, yhi = together(swap(message, ("gx", "gy")), *edges)
    back_modes, block = per_mode(
        mix_back_kernel,
        message,
        spectral_weight,
        gather,
        (y_turn, x_mine),
        (2 * c, F32),
        BF16,
        [pltpu.VMEM((2 * QUAD * MY, c * c), BF16)],
        extra,
    )
    block = x_stage(x_inv, swap(block, "gy"), nx, BF16, ny * extra)
    shape = spectral_weight.shape
    groups = modes_in.shape[0]
    early = groups // 2
    grad_modes = None
    if early:
        grad_modes = outer(modes_in, back_modes, spread, shape, alpha, 0, early)
        block, grad_modes = together(block, grad_modes)
    message = swap(block, "gx")
    stencil_back = conv(grad, (*faces, ylo, yhi), back_table, True)
    grad_modes = outer(
        modes_in, back_modes, spread, shape, alpha, early, groups - early, grad_modes
    )
    grad_state, grad_stencil, grad_point = call(
        functools.partial(finish_kernel, nx, ny, alpha),
        [((c, cx, cy, z), F32), ((c, 27 * c), F32), ((c, c), F32)],
        (stencil_back, message, z_back),
        [pltpu.VMEM((16 * c, 2 * c), F32), pltpu.VMEM((27 * c, c), F32)],
        flops=2 * 96 * state.size,
        moved=state.size * 10,
    )
    return (output, grad_state, grad_modes, grad_stencil, grad_point)


def solution(mesh):
    in_specs = (
        P(None, "gx", "gy", None),
        P(None, "gx", "gy", None),
        P(None, "gx", "gy", None, None),
        P(),
        P(),
    )
    out_specs = (
        P(None, "gx", "gy", None),
        P(None, "gx", "gy", None),
        P(None, "gx", "gy", None, None),
        P(),
        P(),
    )
    return jax.shard_map(body, mesh=mesh, in_specs=in_specs, out_specs=out_specs, check_vma=False)
```

```python
import functools
import math

import jax
import jax.numpy as jnp
import numpy as np
from jax import lax
from jax.experimental import pallas as pl
from jax.experimental.pallas import tpu as pltpu
from jax.sharding import PartitionSpec as P

C = 64
MX = 32
MY = 32
MZ = 16
Z = 128
MIB = 1 << 20

F32 = jnp.float32
BF16 = jnp.bfloat16


def angles(places, freqs, length):
    turns = np.outer(np.asarray(places), np.asarray(freqs)) % length
    return turns * (2.0 * np.pi / length)


def centred(count):
    steps = np.arange(count)
    return np.where(steps < count // 2, steps, steps - count)


def split(table, parts):
    rest = np.asarray(table, np.float64)
    out = []
    for _ in range(parts):
        piece = rest.astype(jnp.bfloat16)
        out.append(piece)
        rest = rest - piece.astype(np.float64)
    return out


def z_forward_table(scale):
    def build(nx, mz):
        theta = angles(np.arange(MZ), np.arange(Z), Z)
        pair = np.stack([np.cos(theta), -np.sin(theta)]) * scale[None, :, None]
        rows = pair.reshape(2, nx, mz, Z).transpose(1, 0, 2, 3).reshape(2 * MZ, Z)
        return np.concatenate(split(rows, 3), axis=0)

    return build


def z_inverse_table(nx, mz, scale):
    theta = angles(np.arange(MZ), np.arange(Z), Z)
    pair = np.stack([np.cos(theta), -np.sin(theta)]) * scale[None, :, None]
    rows = pair.reshape(2, nx, mz, Z).transpose(1, 0, 2, 3).reshape(2 * MZ, Z)
    high, low = split(rows, 2)
    return np.concatenate([high, high, low], axis=0)


def rotation(theta, sign):
    cosine, sine = np.cos(theta), sign * np.sin(theta)
    return np.stack([np.stack([cosine, -sine], 1), np.stack([sine, cosine], 1)])


def against_pieces(*tables):
    out = []
    for table in tables:
        high, low = split(table, 2)
        out.append(np.concatenate([high, high, low], axis=1))
    return out


def x_tables(wide, mz, mx):
    theta = angles(centred(MX), np.arange(wide), wide)
    eye = np.eye(mz)
    forward = np.einsum("rkRx,zZ->krzxRZ", rotation(theta, -1.0), eye)
    inverse = np.einsum("rxRk,zZ->xrzkRZ", rotation(theta.T, 1.0), eye)
    size_k, size_x = MX * 2 * mz, wide * 2 * mz
    forward = forward.reshape(MX // mx, mx, 2, mz, size_x).transpose(0, 2, 3, 1, 4)
    inverse = inverse.reshape(size_x, MX // mx, mx, 2, mz).transpose(0, 1, 3, 4, 2)
    return against_pieces(forward.reshape(size_k, size_x), inverse.reshape(size_x, size_k))


def y_table(wide):
    theta = angles(centred(MY), np.arange(wide), wide)
    forward = rotation(theta, -1.0).reshape(2 * MY, 2 * wide)
    inverse = rotation(theta.T, 1.0).reshape(2 * wide, 2 * MY)
    forward, inverse = against_pieces(forward, inverse)
    inverse = np.pad(inverse, ((0, 0), (0, forward.shape[1] - inverse.shape[1])))
    return np.concatenate([forward, inverse], axis=0)


def pieces(values):
    high = values.astype(BF16)
    low = (values - high.astype(F32)).astype(BF16)
    return jnp.concatenate([high, low, high], axis=0)


def z_forward(rows, table, out_ref, x, nx):
    got = lax.dot_general(table, rows, (((1,), (1,)), ((), ())), preferred_element_type=F32)
    size = 2 * MZ
    total = got[:size] + (got[size : 2 * size] + got[2 * size :])
    per = size // nx
    for owner in range(nx):
        out_ref[owner, x * per : (x + 1) * per, :] = total[owner * per : (owner + 1) * per]


def z_inverse(in_ref, table, x, nx):
    per = 2 * MZ // nx
    rows = jnp.concatenate(
        [in_ref[owner].astype(F32)[x * per : (x + 1) * per] for owner in range(nx)], axis=0
    )
    return lax.dot_general(
        pieces(rows), table, (((0,), (0,)), ((), ())), preferred_element_type=F32
    )


def prep_kernel(
    nx,
    field_ref,
    table_ref,
    forward_ref,
    inverse_ref,
    turn_ref,
    turned_ref,
    slab_ref,
    forward_out_ref,
    inverse_out_ref,
    turn_out_ref,
):
    forward_out_ref[...] = forward_ref[...]
    inverse_out_ref[...] = inverse_ref[...]
    turn_out_ref[...] = turn_ref[...]
    c, cx, cy, z = field_ref.shape
    for x in range(cx):
        block = jnp.swapaxes(field_ref[:, x].astype(F32), 0, 1)
        turned = block.astype(BF16)
        turned_ref[x] = turned
        z_forward(turned.reshape(cy * c, z), table_ref[...], slab_ref, x, nx)


def plane_rows(p, cx, body_ref, xlo_ref, xhi_ref, ylo_ref, yhi_ref):
    cy = body_ref.shape[1]
    if p == 0:
        middle = [xlo_ref[y] for y in range(cy)]
    elif p == cx + 1:
        middle = [xhi_ref[y] for y in range(cy)]
    else:
        middle = [body_ref[p - 1, y] for y in range(cy)]
    return [ylo_ref[p]] + middle + [yhi_ref[p]]


def fill_shifts(blocks, rim_ref, flip=False):
    c, z = blocks[0].shape
    lane = lax.broadcasted_iota(jnp.int32, (c, z), 1)
    for y, block in enumerate(blocks):
        wide = block.astype(F32)
        before = jnp.where(lane == 0, 0.0, pltpu.roll(wide, 1, 1))
        after = jnp.where(lane == z - 1, 0.0, pltpu.roll(wide, z - 1, 1))
        if flip:
            before, after = after, before
        columns = slice(y * z, (y + 1) * z)
        rim_ref[0:c, columns] = before.astype(BF16)
        rim_ref[c : 2 * c, columns] = block
        rim_ref[2 * c : 3 * c, columns] = after.astype(BF16)
        rim_ref[3 * c : 4 * c, columns] = block


def conv_kernel(
    flip, body_ref, xlo_ref, xhi_ref, ylo_ref, yhi_ref, weight_ref, out_ref, rim_ref
):
    cx, cy, c, z = body_ref.shape
    for p in range(cx + 2):
        blocks = plane_rows(p, cx, body_ref, xlo_ref, xhi_ref, ylo_ref, yhi_ref)
        fill_shifts(blocks, rim_ref, flip)
        places = [a for a in range(3) if 0 <= p - (2 - a if flip else a) < cx]
        first = places[0]
        got = jnp.dot(
            weight_ref[first * 3 * c : (places[-1] + 1) * 3 * c, :],
            rim_ref[...],
            preferred_element_type=F32,
        )
        for a in places:
            x = p - (2 - a if flip else a)
            total = None
            for b in range(3):
                row = ((a - first) * 3 + b) * c
                skip = 2 - b if flip else b
                term = got[row : row + c, skip * z : (skip + cy) * z]
                total = term if total is None else total + term
            if p == x:
                out_ref[x] = total
            else:
                out_ref[x] += total


def weight_grad_kernel(
    grad_ref,
    body_ref,
    xlo_any,
    xhi_any,
    ylo_any,
    yhi_any,
    slab_ref,
    message_ref,
    out_ref,
    rim_ref,
    wide_ref,
    sum_ref,
    xlo_ref,
    xhi_ref,
    ylo_ref,
    yhi_ref,
    sem_ref,
):
    cx, cy, c, z = body_ref.shape
    group = 3 * c
    held = (xlo_ref, xhi_ref, ylo_ref, yhi_ref)
    copies = [
        pltpu.make_async_copy(given, ref, sem_ref.at[i])
        for i, (given, ref) in enumerate(zip((xlo_any, xhi_any, ylo_any, yhi_any), held))
    ]
    for copy in copies:
        copy.start()
    wide_ref[...] = jnp.zeros_like(wide_ref)
    for x in range(cx):
        for b in range(3):
            for y in range(cy):
                row = x * group + b * c
                wide_ref[row : row + c, (y + b) * z : (y + b + 1) * z] = grad_ref[x, y]
    sum_ref[...] = jnp.zeros_like(sum_ref)
    for copy in copies:
        copy.wait()
    for p in range(cx + 2):
        fill_shifts(plane_rows(p, cx, body_ref, xlo_ref, xhi_ref, ylo_ref, yhi_ref), rim_ref)
        first, last = max(0, p - 2), min(cx - 1, p)
        got = lax.dot_general(
            wide_ref[first * group : (last + 1) * group, :],
            rim_ref[...],
            (((1,), (1,)), ((), ())),
            preferred_element_type=F32,
        )
        for x in range(first, last + 1):
            a = p - x
            sum_ref[a * group : (a + 1) * group, :] += got[
                (x - first) * group : (x - first + 1) * group, :
            ]
    out_ref[: 9 * c] = sum_ref[:, : 2 * c]
    last = [sum_ref[k * c : (k + 1) * c, 2 * c : 3 * c] for k in range(9)]
    last.append(jnp.zeros((c, c), F32))
    for k in range(5):
        row = (9 + k) * c
        out_ref[row : row + c] = jnp.concatenate(last[2 * k : 2 * k + 2], axis=1)
    out_ref[14 * c :] = jnp.zeros((2 * c, 2 * c), F32)
    devices, rows, lanes = message_ref.shape
    skip = slab_ref.shape[1]
    per, tiles_in = rows - skip, lanes // (2 * c)
    for device in range(devices):
        start = device * per * tiles_in
        share = [out_ref[start + t * per : start + (t + 1) * per] for t in range(tiles_in)]
        message_ref[device] = jnp.concatenate(
            [slab_ref[device].astype(F32), jnp.concatenate(share, axis=1)], axis=0
        ).astype(BF16)


def gelu_kernel(
    nx,
    stencil_ref,
    slab_ref,
    cot_ref,
    inverse_ref,
    forward_ref,
    out_ref,
    turned_ref,
    message_ref,
    back_ref,
):
    c, cx, cy, z = cot_ref.shape
    root = math.sqrt(2.0 / math.pi)
    for x in range(cx):
        spectral = z_inverse(slab_ref, inverse_ref[...], x, nx).reshape(cy, c, z)
        stencil = jnp.stack([stencil_ref[x, :, y * z : (y + 1) * z] for y in range(cy)])
        pre = spectral + stencil
        cot = jnp.swapaxes(cot_ref[:, x].astype(F32), 0, 1)
        square = pre * pre
        bent = jnp.tanh(root * (pre * (1.0 + 0.044715 * square)))
        half = 0.5 + 0.5 * bent
        slope = half + (0.5 * pre) * (1.0 - bent * bent) * (root * (1.0 + 0.134145 * square))
        out_ref[:, x] = jnp.swapaxes(pre * half, 0, 1).astype(BF16)
        grad = (cot * slope).astype(BF16)
        turned_ref[x] = grad
        z_forward(grad.reshape(cy * c, z), forward_ref[...], back_ref, x, nx)
    ny = message_ref.shape[0] // nx
    for owner in range(nx):
        block = back_ref[owner].astype(BF16)
        for copy in range(ny):
            message_ref[owner * ny + copy] = block


def finish_kernel(
    nx,
    shares,
    scale,
    stencil_ref,
    message_ref,
    inverse_ref,
    out_ref,
    taps_ref,
    point_ref,
    packed_ref,
    turned_ref,
):
    c, cx, cy, z = out_ref.shape
    for x in range(cx):
        spectral = z_inverse(message_ref, inverse_ref[...], x, nx).reshape(cy, c, z)
        stencil = jnp.stack([stencil_ref[x, :, y * z : (y + 1) * z] for y in range(cy)])
        out_ref[:, x] = jnp.swapaxes(spectral + stencil, 0, 1)
    skip = 2 * MZ * cx // nx
    unpack(scale, skip, shares, message_ref, taps_ref, point_ref, packed_ref, turned_ref)


def x_kernel(table_ref, data_ref, out_ref):
    data = data_ref[...].astype(F32)
    lanes = data.shape[2]
    rows = table_ref.shape[1] // (3 * data.shape[0])
    flat = pieces(data[:, :rows].reshape(-1, lanes))
    got = jnp.dot(table_ref[...], flat, preferred_element_type=F32).astype(out_ref.dtype)
    count = got.shape[0] // out_ref.shape[0]
    for owner in range(out_ref.shape[0]):
        out_ref[owner, :count] = got[owner * count : (owner + 1) * count]
    if data.shape[1] > rows:
        extra = jnp.concatenate([data[i, rows:] for i in range(data.shape[0])], axis=0)
        extra = extra.astype(out_ref.dtype)
        for owner in range(out_ref.shape[0]):
            out_ref[owner, count:] = extra


def taps_kernel(taps_ref, point_ref, forward_ref, back_ref, turned_ref):
    turned_ref[...] = taps_ref[...].astype(F32).T
    forward_ref[...] = jnp.zeros_like(forward_ref)
    back_ref[...] = jnp.zeros_like(back_ref)
    for tap in range(27):
        rows = slice(tap // 3 * C, (tap // 3 + 1) * C)
        columns = slice(tap % 3 * C, (tap % 3 + 1) * C)
        block = turned_ref[pl.ds(tap, C, stride=27), :]
        back_ref[rows, columns] = block.astype(BF16)
        forward_ref[rows, columns] = block.T.astype(BF16)
    point = point_ref[...].astype(F32)
    forward_ref[4 * C : 5 * C, 3 * C :] = point.astype(BF16)
    back_ref[4 * C : 5 * C, 3 * C :] = point.T.astype(BF16)


def unpack(scale, skip, shares, message_ref, taps_ref, point_ref, packed_ref, turned_ref):
    devices, rows, lanes = message_ref.shape
    per, tiles_in = (rows - skip) // shares, lanes // 128
    for owner in range(devices):
        message = message_ref[owner].astype(F32)[skip:]
        for share in range(shares):
            for tile in range(tiles_in):
                row = ((owner * shares + share) * tiles_in + tile) * per
                packed_ref[row : row + per] = message[
                    share * per : (share + 1) * per, tile * 128 : (tile + 1) * 128
                ]
    for tap in range(27):
        group, e = tap // 3, tap % 3
        if e < 2:
            block = packed_ref[group * C : (group + 1) * C, e * C : (e + 1) * C]
        else:
            row = (9 + group // 2) * C
            block = packed_ref[row : row + C, group % 2 * C : (group % 2 + 1) * C]
        block = block * scale
        if tap == 13:
            point_ref[...] = block
        turned_ref[pl.ds(tap, C, stride=27), :] = block.T
    taps_ref[...] = turned_ref[...].T


QUAD = 4
SPAN = 16 * C


def y_forward(mz, blocks, table_ref, rows_ref, store):
    ny, cy = len(blocks), blocks[0].shape[1] // C
    count = rows_ref.shape[1] // C
    for owner in range(ny):
        data = blocks[owner]
        for part in range(2):
            for kz in range(mz):
                mx = count // mz
                start = (part * mz + kz) * mx
                block = data[start : start + mx]
                block = jnp.stack([block[:, y * C : (y + 1) * C] for y in range(cy)])
                block = jnp.swapaxes(block, 0, 1)
                row = (part * ny + owner) * cy
                for kx in range(mx):
                    column = (kz * mx + kx) * C
                    rows_ref[row : row + cy, column : column + C] = block[kx]
    got = jnp.dot(table_ref[: 2 * MY], pieces(rows_ref[...]), preferred_element_type=F32)
    for q in range(count):
        block = got[:, q * C : (q + 1) * C]
        for part in range(2):
            store(q // QUAD, part, q % QUAD, block[part * MY : (part + 1) * MY])


def y_inverse(mz, sum_ref, table_ref, out_ref, block_ref):
    rows = [
        jnp.concatenate(
            [
                sum_ref[group, place(part, pair), :]
                for group in range(sum_ref.shape[0])
                for pair in range(QUAD)
            ],
            axis=1,
        )
        for part in range(2)
    ]
    got = jnp.dot(
        table_ref[2 * MY :, : 6 * MY],
        pieces(jnp.concatenate(rows, axis=0)),
        preferred_element_type=F32,
    )
    ny, _, lanes = out_ref.shape
    cy = lanes // C
    count = got.shape[1] // C
    mx = count // mz
    for owner in range(ny):
        for part in range(2):
            for kz in range(mz):
                row = (part * ny + owner) * cy
                block = got[row : row + cy, kz * mx * C : (kz + 1) * mx * C]
                block = jnp.stack([block[:, kx * C : (kx + 1) * C] for kx in range(mx)])
                block = jnp.swapaxes(block, 0, 1)
                start = (part * mz + kz) * mx
                for y in range(cy):
                    block_ref[owner, start : start + mx, y * C : (y + 1) * C] = block[y]
    out_ref[...] = block_ref[...].astype(out_ref.dtype)


def place(part, pair):
    start = (part * QUAD + pair) * MY
    return slice(start, start + MY)


def spread_table():
    return np.tile(np.kron(np.eye(C), np.ones((1, C))), (2, 1)).astype(jnp.bfloat16)


def gather_table():
    return np.kron(np.eye(SPAN // C), np.ones((1, C))).astype(jnp.bfloat16)


def spread_modes(modes, table_ref, spread_refs):
    count = C * C // SPAN
    made = set()

    def get(piece):
        for p in range(piece, min(piece + 2, count)):
            if p not in made:
                made.add(p)
                spread_refs[p % 2][...] = jnp.dot(
                    modes, table_ref[:, p * SPAN : (p + 1) * SPAN], preferred_element_type=F32
                )
        return spread_refs[piece % 2]

    return get


def weight_copies(weight_ref, held_ref, sem_ref):
    per = weight_ref.shape[2] // QUAD
    return [
        pltpu.make_async_copy(
            weight_ref.at[:, g // per, g % per * QUAD : (g % per + 1) * QUAD],
            held_ref.at[g],
            sem_ref.at[g],
        )
        for g in range(held_ref.shape[0])
    ]


def mix_kernel(
    mz,
    data_ref,
    weight_ref,
    table_ref,
    turn_ref,
    modes_ref,
    out_ref,
    sum_ref,
    rows_ref,
    block_ref,
    held_ref,
    sem_ref,
    spread_ref,
    spread_sem_ref,
    even_ref,
    odd_ref,
    total_ref,
):
    copies = weight_copies(weight_ref, held_ref, sem_ref)
    table_copy = pltpu.make_async_copy(table_ref, spread_ref, spread_sem_ref)
    table_copy.start()
    for copy in copies:
        copy.start()

    def store(group, part, pair, values):
        high = values.astype(BF16)
        low = (values - high.astype(F32)).astype(BF16)
        modes_ref[group, place(part, pair), :] = jnp.concatenate([high, low], axis=1)

    blocks = [data_ref[owner] for owner in range(data_ref.shape[0])]
    y_forward(mz, blocks, turn_ref, rows_ref, store)
    table_copy.wait()
    for group, copy in enumerate(copies):
        copy.wait()
        spread = spread_modes(modes_ref[group], spread_ref, (even_ref, odd_ref))
        for piece in range(C * C // SPAN):
            modes = spread(piece)
            for pair in range(QUAD):
                real = imag = None
                for tile in range(SPAN // (2 * C)):
                    inside = slice(tile * 2 * C, (tile + 1) * 2 * C)
                    columns = slice(piece * SPAN + inside.start, piece * SPAN + inside.stop)
                    mode_re = modes[place(0, pair), inside]
                    mode_im = modes[place(1, pair), inside]
                    weight_re = held_ref[group, 0, pair, :, columns].astype(F32)
                    weight_im = held_ref[group, 1, pair, :, columns].astype(F32)
                    term_re = mode_re * weight_re - mode_im * weight_im
                    term_im = mode_re * weight_im + mode_im * weight_re
                    real = term_re if real is None else real + term_re
                    imag = term_im if imag is None else imag + term_im
                if piece:
                    real += total_ref[place(0, pair), :]
                    imag += total_ref[place(1, pair), :]
                total_ref[place(0, pair), :] = real
                total_ref[place(1, pair), :] = imag
        total = total_ref[...]
        sum_ref[group] = total[:, :C] + total[:, C:]
    y_inverse(mz, sum_ref, turn_ref, out_ref, block_ref)


def mix_back_kernel(
    mz,
    data_ref,
    weight_ref,
    table_ref,
    turn_ref,
    x_ref,
    modes_ref,
    out_ref,
    sum_ref,
    rows_ref,
    block_ref,
    held_ref,
    sem_ref,
    term_ref,
):
    copies = weight_copies(weight_ref, held_ref, sem_ref)
    for copy in copies:
        copy.start()

    def store(group, part, pair, values):
        modes_ref[group, place(part, pair), :] = jnp.concatenate([values, values], axis=1)

    devices, ny = data_ref.shape[0], block_ref.shape[0]
    size = x_ref.shape[1] // 3
    skip = size * ny // devices
    share = data_ref[0].astype(F32)[skip:]
    for device in range(1, devices):
        share += data_ref[device].astype(F32)[skip:]
    blocks = []
    for owner in range(ny):
        rows = jnp.concatenate(
            [data_ref[i].astype(F32)[:skip] for i in range(owner, devices, ny)], axis=0
        ).astype(BF16)
        blocks.append(
            jnp.dot(x_ref[:, :size], rows, preferred_element_type=F32)
            + jnp.dot(x_ref[:, 2 * size :], rows, preferred_element_type=F32)
        )
    y_forward(mz, blocks, turn_ref, rows_ref, store)
    for group, copy in enumerate(copies):
        copy.wait()
        total = []
        for piece in range(C * C // SPAN):
            for pair in range(QUAD):
                mode_re = modes_ref[group, place(0, pair), :]
                mode_im = modes_ref[group, place(1, pair), :]
                for tile in range(SPAN // (2 * C)):
                    start = piece * SPAN + tile * 2 * C
                    columns = slice(start, start + 2 * C)
                    weight_re = held_ref[group, 0, pair, :, columns].astype(F32)
                    weight_im = held_ref[group, 1, pair, :, columns].astype(F32)
                    term_ref[place(0, pair), columns] = (
                        weight_re * mode_re + weight_im * mode_im
                    ).astype(BF16)
                    term_ref[place(1, pair), columns] = (
                        weight_re * mode_im - weight_im * mode_re
                    ).astype(BF16)
            total.append(
                lax.dot_general(
                    table_ref[...],
                    term_ref[:, piece * SPAN : (piece + 1) * SPAN],
                    (((1,), (1,)), ((), ())),
                    preferred_element_type=F32,
                )
            )
        sum_ref[group] = jnp.concatenate(total, axis=0).T
    y_inverse(mz, sum_ref, turn_ref, block_ref, block_ref)
    for owner in range(ny):
        out_ref[owner] = jnp.concatenate([block_ref[owner], share], axis=0).astype(BF16)


def outer_kernel(alpha, modes_ref, back_ref, table_ref, out_ref):
    count = C * C // SPAN
    made = lambda piece: jnp.dot(
        modes_ref[0],
        table_ref[:, piece * SPAN : (piece + 1) * SPAN],
        preferred_element_type=F32,
    )
    ahead = made(0)
    for piece in range(count):
        modes = ahead
        if piece + 1 < count:
            ahead = made(piece + 1)
        for pair in range(QUAD):
            back_re = back_ref[0, place(0, pair), :] * alpha
            back_im = back_ref[0, place(1, pair), :] * alpha
            for tile in range(SPAN // (2 * C)):
                inside = slice(tile * 2 * C, (tile + 1) * 2 * C)
                columns = slice(piece * SPAN + inside.start, piece * SPAN + inside.stop)
                mode_re = modes[place(0, pair), inside]
                mode_im = modes[place(1, pair), inside]
                out_ref[0, 0, pair, :, columns] = mode_re * back_re + mode_im * back_im
                out_ref[1, 0, pair, :, columns] = mode_re * back_im - mode_im * back_re


def in_hbm(value):
    return pltpu.with_memory_space_constraint(value, pltpu.HBM)


def whole():
    return pl.BlockSpec(memory_space=pltpu.VMEM)


def params(mib):
    return pltpu.CompilerParams(vmem_limit_bytes=mib * MIB)


def cost(flops, moved):
    return pl.CostEstimate(flops=int(flops), bytes_accessed=int(moved), transcendentals=0)


def call(kernel, outs, args, scratch=(), mib=24, flops=0, moved=0, anywhere=()):
    return pl.pallas_call(
        kernel,
        out_shape=[jax.ShapeDtypeStruct(*out) for out in outs],
        in_specs=[
            pl.BlockSpec(memory_space=pl.ANY) if i in anywhere else whole()
            for i in range(len(args))
        ],
        out_specs=[whole() for _ in outs],
        scratch_shapes=list(scratch),
        compiler_params=params(mib),
        cost_estimate=cost(flops, moved),
    )(*args)


def per_mode(kernel, data, weight, table, tables, modes, kind, scratch=(), extra=0):
    _, mz, mx, my, wide = weight.shape
    groups = mz * mx // QUAD
    rows = 2 * QUAD * MY
    modes_shape = (groups, rows, modes[0])
    block = (MX // mx, 2 * mz * mx, data.shape[2])
    return pl.pallas_call(
        functools.partial(kernel, mz),
        in_specs=[
            whole(),
            pl.BlockSpec(memory_space=pl.ANY),
            pl.BlockSpec(memory_space=pl.ANY) if kernel is mix_kernel else whole(),
        ]
        + [whole() for _ in tables],
        out_specs=[whole(), whole()],
        out_shape=[
            jax.ShapeDtypeStruct(modes_shape, modes[1]),
            jax.ShapeDtypeStruct((block[0], block[1] + extra, block[2]), kind),
        ],
        scratch_shapes=[
            pltpu.VMEM((groups, rows, C), F32),
            pltpu.VMEM((tables[0].shape[0] - 2 * MY, mz * mx * C), F32),
            pltpu.VMEM(block, F32),
            pltpu.VMEM((groups, 2, QUAD, my, wide), BF16),
            pltpu.SemaphoreType.DMA((groups,)),
            *scratch,
        ],
        compiler_params=params(24),
        cost_estimate=cost(weight.size * 8, weight.size * 2),
    )(data, in_hbm(weight), in_hbm(table), *tables)


def outer(modes, back, table, shape, alpha, start, count, prior=None):
    def kernel(*refs):
        outer_kernel(alpha, *refs[:3], refs[-1])

    per = shape[2] // QUAD
    group = lambda ref: pl.BlockSpec((1,) + ref.shape[1:], lambda step: (step + start, 0, 0))
    given = () if prior is None else (prior,)
    return pl.pallas_call(
        kernel,
        grid=(count,),
        in_specs=[group(modes), group(back), pl.BlockSpec(table.shape, lambda step: (0, 0))]
        + [pl.BlockSpec(memory_space=pl.ANY)] * len(given),
        out_specs=pl.BlockSpec(
            (2, 1, QUAD) + shape[3:],
            lambda step: (0, (step + start) // per, (step + start) % per, 0, 0),
        ),
        out_shape=jax.ShapeDtypeStruct(shape, F32),
        input_output_aliases={3: 0} if given else {},
        compiler_params=params(20),
        cost_estimate=cost(
            math.prod(shape) * 4 * count / modes.shape[0],
            math.prod(shape) * 4 * count / modes.shape[0],
        ),
    )(modes, back, in_hbm(table), *given)


def shift(block, axis, step):
    count = lax.axis_size(axis)
    pairs = [(i, i + step) for i in range(count) if 0 <= i + step < count]
    return lax.ppermute(block, axis, pairs)


def x_halos(turned):
    return shift(turned[-1], "gx", 1), shift(turned[0], "gx", -1)


def y_halos(turned, xlo, xhi):
    edge = lambda y: jnp.concatenate([xlo[None, y], turned[:, y], xhi[None, y]], axis=0)
    return shift(edge(-1), "gy", 1), shift(edge(0), "gy", -1)


def conv(turned, rim, weight, flip):
    cx, cy, c, z = turned.shape
    return call(
        functools.partial(conv_kernel, flip),
        [((cx, c, cy * z), F32)],
        (turned, *map(in_hbm, rim), in_hbm(weight)),
        [pltpu.VMEM((4 * c, (cy + 2) * z), BF16)],
        mib=32,
        flops=2 * 27 * c * c * cx * cy * z,
        moved=turned.size * 8,
    )[0]


def weight_grad(grad, turned, rim, slab):
    cx, cy, c, z = turned.shape
    devices, skip, lanes = slab.shape
    extra = 16 * c * 2 * c // (devices * lanes)
    return call(
        weight_grad_kernel,
        [((devices, skip + extra, lanes), BF16)],
        (grad, turned, *map(in_hbm, rim), slab),
        [
            pltpu.VMEM((16 * c, 2 * c), F32),
            pltpu.VMEM((4 * c, (cy + 2) * z), BF16),
            pltpu.VMEM((cx * 3 * c, (cy + 2) * z), BF16),
            pltpu.VMEM((9 * c, 4 * c), F32),
            *(pltpu.VMEM(halo.shape, BF16) for halo in rim),
            pltpu.SemaphoreType.DMA((len(rim),)),
        ],
        mib=32,
        flops=2 * 27 * c * c * cx * cy * z,
        moved=turned.size * 8,
        anywhere=(2, 3, 4, 5),
    )[0]


def swap(block, axis):
    return lax.all_to_all(block, axis, split_axis=0, concat_axis=0, tiled=True)


def together(*values):
    return lax.optimization_barrier(values)


def body(state, cotangent, spectral_weight, stencil_weight, pointwise_weight):
    nx, ny = lax.axis_size("gx"), lax.axis_size("gy")
    c, cx, cy, z = state.shape
    _, mz, mx, _, _ = spectral_weight.shape
    wide_x, wide_y = cx * nx, cy * ny
    alpha = 1.0 / math.sqrt(wide_x * wide_y * z)
    beta = 1.0 / math.sqrt(2 * MX * MY * MZ)
    double = np.where(np.arange(MZ) == 0, 1.0, 2.0)
    ones = np.ones(MZ)
    z_state = jnp.asarray(z_forward_table(alpha * ones)(nx, mz))
    z_grad = jnp.asarray(z_forward_table(double)(nx, mz))
    z_spectral = jnp.asarray(z_inverse_table(nx, mz, beta * double))
    z_back = jnp.asarray(z_inverse_table(nx, mz, alpha * beta * ones))
    x_fwd, x_inv = (jnp.asarray(t) for t in x_tables(wide_x, mz, mx))
    y_turn = jnp.asarray(y_table(wide_y))
    spread, gather = jnp.asarray(spread_table()), jnp.asarray(gather_table())
    lanes = cy * c
    x_rows = cx * 2 * mz

    def x_stage(table, block, lead, kind=F32, extra=0):
        rows = table.shape[0] // lead + extra
        return call(
            x_kernel,
            [((lead, rows, lanes), kind)],
            (table, block),
            mib=16,
            flops=2 * table.size * lanes,
            moved=8 * block.size,
        )[0]

    slab_shape = ((nx, x_rows, lanes), F32)
    turned_shape = ((cx, cy, c, z), BF16)

    conv_table, back_table = call(
        taps_kernel,
        [((9 * c, 4 * c), BF16)] * 2,
        (in_hbm(stencil_weight), in_hbm(pointwise_weight)),
        [pltpu.VMEM((27 * c, c), F32)],
        moved=stencil_weight.size * 6,
    )
    tables = (x_fwd, x_inv, y_turn)
    turned, slab, *held = call(
        functools.partial(prep_kernel, nx),
        [turned_shape, slab_shape] + [(t.shape, BF16) for t in tables],
        (in_hbm(state), in_hbm(z_state), *map(in_hbm, tables)),
        flops=2 * 96 * state.size,
        moved=state.size * 5,
    )
    x_mine = x_fwd.reshape(ny, -1, x_fwd.shape[1])
    x_mine = lax.dynamic_index_in_dim(x_mine, lax.axis_index("gy"), 0, keepdims=False)
    x_fwd, x_inv, y_turn = held

    block = x_stage(x_fwd, swap(slab, "gx"), ny)
    block, conv_table, back_table, x_mine, *faces = together(
        block, conv_table, back_table, x_mine, *x_halos(turned)
    )
    modes_in, block = per_mode(
        mix_kernel,
        swap(block, "gy"),
        spectral_weight,
        spread,
        (y_turn,),
        (2 * c, BF16),
        F32,
        [pltpu.VMEM(spread.shape, BF16), pltpu.SemaphoreType.DMA]
        + [pltpu.VMEM((2 * QUAD * MY, SPAN), F32)] * 2
        + [pltpu.VMEM((2 * QUAD * MY, 2 * c), F32)],
    )
    block, *edges = together(block, *y_halos(turned, *faces))
    rim = (*faces, *edges)
    block = x_stage(x_inv, swap(block, "gy"), nx)
    stencil = conv(turned, rim, conv_table, False)
    output, grad, slab = call(
        functools.partial(gelu_kernel, nx),
        [((c, cx, cy, z), BF16), turned_shape, ((nx * ny, x_rows, lanes), BF16)],
        (stencil, swap(block, "gx"), cotangent, z_spectral, z_grad),
        [pltpu.VMEM(slab_shape[0], F32)],
        flops=2 * 192 * state.size,
        moved=state.size * 12,
    )

    message = weight_grad(grad, turned, rim, slab)
    extra = message.shape[1] - x_rows
    faces = x_halos(grad)
    edges = y_halos(grad, *faces)
    message, ylo, yhi = together(swap(message, ("gx", "gy")), *edges)
    back_modes, block = per_mode(
        mix_back_kernel,
        message,
        spectral_weight,
        gather,
        (y_turn, x_mine),
        (2 * c, F32),
        BF16,
        [pltpu.VMEM((2 * QUAD * MY, c * c), BF16)],
        extra,
    )
    block = x_stage(x_inv, swap(block, "gy"), nx, BF16, ny * extra)
    shape = spectral_weight.shape
    groups = modes_in.shape[0]
    early = groups // 2
    grad_modes = None
    if early:
        grad_modes = outer(modes_in, back_modes, spread, shape, alpha, 0, early)
        block, grad_modes = together(block, grad_modes)
    message = swap(block, "gx")
    stencil_back = conv(grad, (*faces, ylo, yhi), back_table, True)
    grad_modes = outer(
        modes_in, back_modes, spread, shape, alpha, early, groups - early, grad_modes
    )
    grad_state, grad_stencil, grad_point = call(
        functools.partial(finish_kernel, nx, ny, alpha),
        [((c, cx, cy, z), F32), ((c, 27 * c), F32), ((c, c), F32)],
        (stencil_back, message, z_back),
        [pltpu.VMEM((16 * c, 2 * c), F32), pltpu.VMEM((27 * c, c), F32)],
        flops=2 * 96 * state.size,
        moved=state.size * 10,
    )
    return (output, grad_state, grad_modes, grad_stencil, grad_point)


def solution(mesh):
    in_specs = (
        P(None, "gx", "gy", None),
        P(None, "gx", "gy", None),
        P(None, "gx", "gy", None, None),
        P(),
        P(),
    )
    out_specs = (
        P(None, "gx", "gy", None),
        P(None, "gx", "gy", None),
        P(None, "gx", "gy", None, None),
        P(),
        P(),
    )
    return jax.shard_map(body, mesh=mesh, in_specs=in_specs, out_specs=out_specs, check_vma=False)
```
